32 devices in a mesh: ctx: 8 (over z, x), head: 4 (over y, core).
Axes of the slice: x: 2, y: 2, z: 4, core: 2. Of those that a mesh axis runs over, the one named last changes fastest.
Arguments:
- ssm_input: bfloat16 [2048, 8192], P('ctx', 'head'), may hold values from -32 to 32
- gate_input: bfloat16 [2048, 8192], P('ctx', 'head'), may hold values from -6 to 6
- write_map: bfloat16 [2048, 128], P('ctx'), may hold values from -0.5 to 0.5
- read_map: bfloat16 [2048, 128], P('ctx'), may hold values from -0.5 to 0.5
- log_decay: float32 [2048, 64], P('ctx', 'head'), may hold values from -2.2 to 0
- doc_start: int32 [2048], P('ctx'), may hold values from 0 to 1920, as said below
- ssm_grad: bfloat16 [2048, 8192], P('ctx', 'head'), may hold values from -6 to 6
- att_queries: bfloat16 [2048, 4096], P('ctx', 'head'), may hold values from -32 to 32
- att_keys: bfloat16 [2048, 4096], P('ctx', 'head'), may hold values from -20 to 20
- att_values: bfloat16 [2048, 4096], P('ctx', 'head'), may hold values from -6 to 6
- att_grad: bfloat16 [2048, 4096], P('ctx', 'head'), may hold values from -6 to 6
Outputs:
- mixer_out: bfloat16 [2048, 8192], P('ctx', 'head')
- window_out: bfloat16 [2048, 4096], P('ctx', 'head')
- input_grad: bfloat16 [2048, 8192], P('ctx', 'head')
- gate_grad: bfloat16 [2048, 8192], P('ctx', 'head')
- write_grad: bfloat16 [2048, 128], P('ctx')
- read_grad: bfloat16 [2048, 128], P('ctx')
- query_grad: bfloat16 [2048, 4096], P('ctx', 'head')
- key_grad: bfloat16 [2048, 4096], P('ctx', 'head')
- value_grad: bfloat16 [2048, 4096], P('ctx', 'head')
The draws below stay inside these ranges and needn't reach their ends.
Inputs may be any that keep to these rules, and one draw needn't show every extreme that they name: doc_start[t] is the position of the first token of the document holding token t; the 8 documents are runs of consecutive positions, the first starts at 0 and the last at 1920; one document other than the first and the last is exactly 4608 tokens long.
All inputs are finite; a program needn't handle non-finite values.
Results may differ from the reference program's by a relative error of at most 0.007.
Values may be sent and summed in bfloat16 or wider, within the bound.
No kernel may reach another device: no remote copies, remote signals or barrier semaphores. Data moves between devices by JAX's collectives and lax.ppermute only.
A program may use at most 128 MiB of HBM per device.

```python
import math
import jax
import jax.numpy as jnp
from jax import lax

SSM_HEADS = 64
HEAD_DIM = 128
STATE = 128
ATT_HEADS = 32
ATT_DIM = 128
WINDOW = 4096
BLOCK = 128
TOK_DEV = 256
DOCS = 8
TOKENS = 2048


def draw_ssm_input(key, part):
    width_all = SSM_HEADS * HEAD_DIM
    first_key, second_key = jax.random.split(key, 2)
    column_head = (jnp.arange(width_all) // HEAD_DIM).astype(jnp.float32)
    ramp = jnp.exp(math.log(3.0) * column_head / (SSM_HEADS - 1))
    jitter = jnp.exp(jax.random.uniform(second_key, (width_all,), minval=-0.4, maxval=0.4))
    base = jnp.clip(jax.random.normal(first_key, (TOKENS, width_all)), -3.5, 3.5)
    return (base * ramp[None, :] * jitter[None, :]).astype(jnp.bfloat16)


def draw_log_decay(key, part):
    subkeys = jax.random.split(key, 6)
    share = 0.5
    slow = jax.random.uniform(subkeys[0], (SSM_HEADS,)) < share
    slow_rate = jax.random.uniform(subkeys[1], (SSM_HEADS,), minval=0.2, maxval=0.6) / TOKENS
    fast_rate = 1.0 / jax.random.uniform(subkeys[2], (SSM_HEADS,), minval=30.0, maxval=50.0)
    base_rate = jnp.where(slow, slow_rate, fast_rate)
    factor = jnp.exp(jax.random.uniform(subkeys[3], (TOKENS, SSM_HEADS), minval=-0.69, maxval=0.69))
    spot_locations = jax.random.randint(subkeys[4], (3, SSM_HEADS), 0, TOKENS)
    dropped_rows = jax.random.uniform(subkeys[5], (3, SSM_HEADS), minval=math.log(0.5), maxval=math.log(0.8))
    token_position = jnp.arange(TOKENS)[:, None]
    final_result = -base_rate[None, :] * factor
    for spike_value in range(3):
        final_result = final_result + jnp.where(token_position == spot_locations[spike_value][None, :], dropped_rows[spike_value][None, :], 0.0)
    return final_result.astype(jnp.float32)


def draw_doc_start(key, part):
    last_start = TOKENS - TOK_DEV // 2
    span_len = min(WINDOW + 2 * TOK_DEV, last_start - DOCS - 2)
    place_key, rest_key = jax.random.split(key)
    span_first = jax.random.randint(place_key, (), 1, last_start - span_len).astype(jnp.int32)
    free_count = last_start - span_len - 2
    chosen = jax.random.permutation(rest_key, free_count)[:DOCS - 4].astype(jnp.int32)
    others = jnp.where(chosen + 1 < span_first, chosen + 1, chosen + span_len + 2).astype(jnp.int32)
    cuts = jnp.concatenate([others, span_first.reshape(1), (span_first + span_len).reshape(1), jnp.full((1,), last_start, jnp.int32)])
    token_position = jnp.arange(TOKENS)[:, None]
    return jnp.max(jnp.where(cuts[None, :] <= token_position, cuts[None, :], 0), axis=1).astype(jnp.int32)


def attention_pair(key):
    base_key = jax.random.fold_in(key, 17)
    first_key, second_key = jax.random.split(base_key, 2)
    width_all = ATT_HEADS * ATT_DIM
    queries = jnp.clip(jax.random.normal(first_key, (TOKENS, width_all)), -6.0, 6.0)
    keys_out = 3.0 * jnp.clip(jax.random.normal(second_key, (TOKENS, width_all)), -6.0, 6.0)
    return (queries, keys_out)


def draw_att_queries(key, part):
    return attention_pair(key)[0].astype(jnp.bfloat16)


def draw_att_keys(key, part):
    return attention_pair(key)[1].astype(jnp.bfloat16)


def block_levels(rng, extent, cuts, low, largest):
    factor_of = 1.0
    for position, blocks in cuts:
        heights = jax.random.uniform(jax.random.fold_in(jax.random.fold_in(rng, 6), position), (blocks,), jnp.float32, low / len(cuts), largest / len(cuts))
        factor_of = factor_of * jnp.repeat(jnp.exp(heights), extent[position] // blocks).reshape((-1,) + (1,) * (len(extent) - 1 - position))
    return factor_of


def noise(key, extent, scale, bound, pieces=(), kind=jnp.bfloat16):
    values = scale * jax.random.normal(key, extent, jnp.float32)
    if pieces:
        values = values * block_levels(key, extent, pieces, -0.22, 0.18)
    return jnp.clip(values, -bound, bound).astype(kind)


def setup_inputs(seed: int = 0) -> dict:
    key_of = jax.random.split(jax.random.key(seed), 12)
    return {
        "ssm_input": draw_ssm_input(jax.random.fold_in(key_of[11], 71), 0),
        "gate_input": noise(key_of[1], (TOKENS, SSM_HEADS * HEAD_DIM), 1.0, 6.0, ((0, 8), (1, 4))),
        "write_map": noise(key_of[2], (TOKENS, STATE), STATE ** -0.5, 0.5, ((0, 8),)),
        "read_map": noise(key_of[3], (TOKENS, STATE), STATE ** -0.5, 0.5, ((0, 8),)),
        "log_decay": draw_log_decay(jax.random.fold_in(key_of[11], 71), 0),
        "doc_start": draw_doc_start(jax.random.fold_in(key_of[11], 71), 0),
        "ssm_grad": noise(key_of[6], (TOKENS, SSM_HEADS * HEAD_DIM), 1.0, 6.0, ((0, 8), (1, 4))),
        "att_queries": draw_att_queries(jax.random.fold_in(key_of[11], 71), 0),
        "att_keys": draw_att_keys(jax.random.fold_in(key_of[11], 71), 0),
        "att_values": noise(key_of[9], (TOKENS, ATT_HEADS * ATT_DIM), 1.0, 6.0, ((0, 8), (1, 4))),
        "att_grad": noise(key_of[10], (TOKENS, ATT_HEADS * ATT_DIM), 1.0, 6.0, ((0, 8), (1, 4))),
    }


PRECISE = lax.Precision.HIGHEST
EPSILON = 1e-05

def run_scan(keys_in, values_in, log_rates, doc_marks, query_shared, query_heads):
    total_len = keys_in.shape[0]
    block_count = total_len // BLOCK

    def split(array):
        return array.reshape((block_count, BLOCK) + array.shape[1:])
    piece_list = (split(keys_in), split(values_in), split(log_rates), split(doc_marks), split(query_shared))
    if query_heads is not None:
        piece_list = piece_list + (split(query_heads),)
    lower = jnp.arange(BLOCK)[:, None] >= jnp.arange(BLOCK)[None, :]
    head_count = values_in.shape[1]
    start_state = jnp.zeros((head_count, keys_in.shape[1], values_in.shape[2]), jnp.float32)

    def step(running, piece):
        state, prev_mark = running
        key_blk, value_blk, rate_blk, mark_blk, query_blk = piece[:5]
        cumulative = jnp.cumsum(rate_blk, axis=0)
        joined = (mark_blk[:, None] == mark_blk[None, :]) & lower
        spread = cumulative[:, None, :] - cumulative[None, :, :]
        decay = jnp.where(joined[:, :, None], jnp.exp(jnp.minimum(spread, 0.0)), 0.0)
        enter = jnp.where((mark_blk == prev_mark)[:, None], jnp.exp(cumulative), 0.0)
        scores = jnp.dot(query_blk, key_blk.T, precision=PRECISE)
        mixed = jnp.einsum('tsh,shp->thp', decay * scores[:, :, None], value_blk, precision=PRECISE)
        mixed = mixed + enter[:, :, None] * jnp.einsum('tn,hnp->thp', query_blk, state, precision=PRECISE)
        results = (mixed,)
        if len(piece) > 5:
            head_query = piece[5]
            inner = jnp.einsum('thp,shp->tsh', head_query, value_blk, precision=PRECISE)
            shared = jnp.einsum('tsh,sn->tn', decay * inner, key_blk, precision=PRECISE)
            shared = shared + jnp.einsum('th,thp,hnp->tn', enter, head_query, state, precision=PRECISE)
            results = results + (shared,)
        to_end = jnp.where((mark_blk == mark_blk[-1])[:, None], jnp.exp(cumulative[-1:] - cumulative), 0.0)
        keep = jnp.where(mark_blk[-1] == prev_mark, jnp.exp(cumulative[-1]), 0.0)
        new_state = keep[:, None, None] * state + jnp.einsum('sh,sn,shp->hnp', to_end, key_blk, value_blk, precision=PRECISE)
        return ((new_state, mark_blk[-1]), results)
    start = (start_state, jnp.array(-1.0, jnp.float32))
    _, results = lax.scan(step, start, piece_list)
    mixed = results[0].reshape((total_len,) + values_in.shape[1:])
    if query_heads is not None:
        return (mixed, results[1].reshape(total_len, keys_in.shape[1]))
    return (mixed, None)

def attend(head_index, queries, keys_in, values_in, grads_in, doc_start):
    query_head = lax.dynamic_slice_in_dim(queries, head_index * ATT_DIM, ATT_DIM, 1)
    key_head = lax.dynamic_slice_in_dim(keys_in, head_index * ATT_DIM, ATT_DIM, 1)
    value_head = lax.dynamic_slice_in_dim(values_in, head_index * ATT_DIM, ATT_DIM, 1)
    grad_head = lax.dynamic_slice_in_dim(grads_in, head_index * ATT_DIM, ATT_DIM, 1)
    pad_rows = jnp.zeros((WINDOW, ATT_DIM), key_head.dtype)
    key_pad = jnp.concatenate([pad_rows, key_head], axis=0)
    value_pad = jnp.concatenate([pad_rows, value_head], axis=0)
    width_span = WINDOW + TOK_DEV
    score_scale = ATT_DIM ** (-0.5)
    block_count = TOKENS // TOK_DEV

    def step(running, block_index):
        key_acc, value_acc = running
        first = block_index * TOK_DEV
        query_blk = lax.dynamic_slice_in_dim(query_head, first, TOK_DEV, 0)
        grad_blk = lax.dynamic_slice_in_dim(grad_head, first, TOK_DEV, 0)
        start_blk = lax.dynamic_slice_in_dim(doc_start, first, TOK_DEV, 0)
        key_blk = lax.dynamic_slice_in_dim(key_pad, first, width_span, 0)
        value_blk = lax.dynamic_slice_in_dim(value_pad, first, width_span, 0)
        query_pos = first + jnp.arange(TOK_DEV, dtype=jnp.int32)
        key_pos = first - WINDOW + jnp.arange(width_span, dtype=jnp.int32)
        visible = (key_pos[None, :] <= query_pos[:, None]) & (query_pos[:, None] - key_pos[None, :] < WINDOW) & (key_pos[None, :] >= start_blk[:, None])
        score = jnp.dot(query_blk, key_blk.T, preferred_element_type=jnp.float32) * score_scale
        row_max = lax.optimization_barrier(jnp.max(jnp.where(visible, score, -jnp.inf), axis=1))
        expo = jnp.where(visible, jnp.exp(score - row_max[:, None]), 0.0)
        row_total = lax.optimization_barrier(jnp.sum(expo, axis=1))
        probs = expo / row_total[:, None]
        weights = probs.astype(jnp.bfloat16)
        attended = jnp.dot(weights, value_blk, preferred_element_type=jnp.float32)
        delta = lax.optimization_barrier(jnp.sum(grad_blk.astype(jnp.float32) * attended, axis=1))
        dprobs = jnp.dot(grad_blk, value_blk.T, preferred_element_type=jnp.float32)
        dscore = (probs * (dprobs - delta[:, None]) * score_scale).astype(jnp.bfloat16)
        query_grad = jnp.dot(dscore, key_blk, preferred_element_type=jnp.float32)
        key_part = jnp.dot(dscore.T, query_blk, preferred_element_type=jnp.float32)
        value_part = jnp.dot(weights.T, grad_blk, preferred_element_type=jnp.float32)
        key_acc = lax.dynamic_update_slice_in_dim(key_acc, lax.dynamic_slice_in_dim(key_acc, first, width_span, 0) + key_part, first, 0)
        value_acc = lax.dynamic_update_slice_in_dim(value_acc, lax.dynamic_slice_in_dim(value_acc, first, width_span, 0) + value_part, first, 0)
        return ((key_acc, value_acc), (attended.astype(jnp.bfloat16), query_grad.astype(jnp.bfloat16)))
    zeros_acc = jnp.zeros((WINDOW + TOKENS, ATT_DIM), jnp.float32)
    (key_acc, value_acc), (outputs, query_grads) = lax.scan(step, (zeros_acc, zeros_acc), jnp.arange(block_count, dtype=jnp.int32))
    return (outputs.reshape(TOKENS, ATT_DIM), query_grads.reshape(TOKENS, ATT_DIM), key_acc[WINDOW:].astype(jnp.bfloat16), value_acc[WINDOW:].astype(jnp.bfloat16))

def merge_heads(stacked):
    return jnp.transpose(stacked, (1, 0, 2)).reshape(TOKENS, -1)

def reference(ssm_input, gate_input, write_map, read_map, log_decay, doc_start, ssm_grad, att_queries, att_keys, att_values, att_grad):
    inputs_full = ssm_input.astype(jnp.float32).reshape(TOKENS, SSM_HEADS, HEAD_DIM)
    writes = write_map.astype(jnp.float32)
    reads = read_map.astype(jnp.float32)
    doc_marks = doc_start.astype(jnp.float32)
    mixed, _ = run_scan(writes, inputs_full, log_decay, doc_marks, reads, None)
    mixed = mixed.reshape(TOKENS, SSM_HEADS * HEAD_DIM)
    gate_full = gate_input.astype(jnp.float32)
    sigma = jax.nn.sigmoid(gate_full)
    swish = gate_full * sigma
    gated = mixed * swish
    width_all = SSM_HEADS * HEAD_DIM
    row_scale = lax.rsqrt(lax.optimization_barrier(jnp.sum(gated * gated, axis=1)) / width_all + EPSILON)
    mixer_out = (gated * row_scale[:, None]).astype(jnp.bfloat16)
    grad_full = ssm_grad.astype(jnp.float32)
    inner = lax.optimization_barrier(jnp.sum(grad_full * gated, axis=1))
    dgated = row_scale[:, None] * grad_full - (row_scale ** 3 * inner / width_all)[:, None] * gated
    dmixed = dgated * swish
    gate_grad = (dgated * mixed * sigma * (1.0 + gate_full * (1.0 - sigma))).astype(jnp.bfloat16)
    dmixed_heads = dmixed.reshape(TOKENS, SSM_HEADS, HEAD_DIM)
    _, read_sum = run_scan(writes, inputs_full, log_decay, doc_marks, reads, dmixed_heads)
    rev_rates = jnp.concatenate([jnp.zeros((1, SSM_HEADS), jnp.float32), log_decay[::-1][:-1]], axis=0)
    back, write_sum = run_scan(reads[::-1], dmixed_heads[::-1], rev_rates, doc_marks[::-1], writes[::-1], inputs_full[::-1])
    input_grad = back[::-1].reshape(TOKENS, SSM_HEADS * HEAD_DIM).astype(jnp.bfloat16)
    write_grad = write_sum[::-1].astype(jnp.bfloat16)
    read_grad = read_sum.astype(jnp.bfloat16)

    def one_head(head_index):
        return attend(head_index, att_queries, att_keys, att_values, att_grad, doc_start)
    outs, query_grads, key_grads, value_grads = lax.map(one_head, jnp.arange(ATT_HEADS, dtype=jnp.int32))
    return (mixer_out, merge_heads(outs), input_grad, gate_grad, write_grad, read_grad, merge_heads(query_grads), merge_heads(key_grads), merge_heads(value_grads))
```

```python
import jax
import jax.numpy as jnp
from jax import lax
from jax.experimental import pallas as pl
from jax.experimental.pallas import tpu as pltpu
from jax.sharding import PartitionSpec as P

HEAD_DIM = 128
ATT_DIM = 128
WINDOW = 4096
EPSILON = 1e-05
LOG2E = 1.4426950408889634
TAIL = 16
MASKED = -1e30
HIGH = lax.Precision.HIGHEST
F32 = jnp.float32
BF16 = jnp.bfloat16
VMEM_BYTES = 56 * 1024 * 1024


def call(kernel, out_shape, *operands, scratch=(), flops=0, name=None):
    moved = sum(a.size * a.dtype.itemsize for a in jax.tree.leaves((operands, out_shape)))
    return pl.pallas_call(
        kernel,
        out_shape=out_shape,
        in_specs=[pl.BlockSpec(memory_space=pltpu.VMEM)] * len(operands),
        out_specs=jax.tree.map(lambda _: pl.BlockSpec(memory_space=pltpu.VMEM), out_shape),
        scratch_shapes=scratch,
        compiler_params=pltpu.CompilerParams(vmem_limit_bytes=VMEM_BYTES),
        cost_estimate=pl.CostEstimate(flops=flops, bytes_accessed=moved, transcendentals=0),
        name=name,
    )(*operands)


def shape(dims, dtype):
    return jax.ShapeDtypeStruct(dims, dtype)


def dot(a, b):
    return jnp.dot(a, b, preferred_element_type=F32)


def dot_nt(a, b, precision=None):
    return lax.dot_general(
        a, b, (((1,), (1,)), ((), ())), preferred_element_type=F32, precision=precision
    )


def iota(dims, axis):
    return lax.broadcasted_iota(jnp.int32, dims, axis)


def flip(a):
    return a.astype(F32).T.astype(BF16)


def column(row):
    return jnp.broadcast_to(row, (128, row.shape[1])).T


def cols(h):
    return slice(h * HEAD_DIM, (h + 1) * HEAD_DIM)


def first_kernel(ld_ref, rel_ref, w_ref, x_ref, out_ref, lcol_ref, lrow_ref):
    length, heads = ld_ref.shape
    parts, rows = out_ref.shape[0], out_ref.shape[1] - TAIL
    rates = ld_ref[...] * LOG2E
    lower = jnp.where(iota((length, length), 0) >= iota((length, length), 1), 1.0, 0.0)
    upper = jnp.where(iota((length, length), 0) <= iota((length, length), 1), 1.0, 0.0)
    lcol_ref[...] = jnp.dot(lower, rates, preferred_element_type=F32, precision=HIGH)
    lrow = lax.dot_general(
        rates, upper, (((0,), (0,)), ((), ())), preferred_element_type=F32, precision=HIGH
    )
    lrow_ref[...] = lrow
    rel_last = rel_ref[:, length - 1 :]
    last_doc = iota((1, length), 1) >= rel_last
    keeps = rel_last < 0
    writes = w_ref[...].astype(F32).T
    tail_row = iota((TAIL, 128), 0)
    for h in range(heads):
        line = lrow[h : h + 1, :]
        total = line[:, length - 1 :]
        to_end = jnp.where(last_doc, jnp.exp2(total - line), 0.0)
        state = dot((writes * to_end).astype(BF16), x_ref[:, cols(h)]).astype(BF16)
        factor = jnp.where(keeps, jnp.exp2(total), 0.0)
        high = factor.astype(BF16).astype(F32)
        low = factor - high
        first = h * HEAD_DIM
        for part in range(first // rows, (first + HEAD_DIM - 1) // rows + 1):
            begin = max(first, part * rows)
            end = min(first + HEAD_DIM, (part + 1) * rows)
            out_ref[part, begin - part * rows : end - part * rows, :] = state[
                begin - first : end - first, :
            ]
            place = 2 * (begin - part * rows) // HEAD_DIM
            tail = jnp.where(tail_row == place, high, jnp.where(tail_row == place + 1, low, 0.0))
            if place:
                tail = tail + out_ref[part, rows:, :].astype(F32)
            out_ref[part, rows:, :] = tail.astype(BF16)


def carry_kernel(backward, tail_ref, in_ref, out_ref):
    parts, rows = out_ref.shape[0], out_ref.shape[1]
    step = min(rows, HEAD_DIM)
    for k in range(rows // step):
        here = slice(k * step, (k + 1) * step)
        state = jnp.zeros((step, 128), F32)
        for c in range(parts)[:: -1 if backward else 1]:
            out_ref[c, here, :] = state.astype(BF16)
            tail = tail_ref[c].astype(F32)
            factor = tail[2 * k : 2 * k + 1, :] + tail[2 * k + 1 : 2 * k + 2, :]
            state = factor * state + in_ref[c, here, :].astype(F32)


def mix_kernel(
    x_ref, gate_ref, grad_ref, w_ref, r_ref, rel_ref, lcol_ref, lrow_ref, s_ref, mixed_ref, sums_ref
):
    length, heads = lcol_ref.shape
    reads = r_ref[...]
    rel = column(rel_ref[...].astype(F32))
    wide = jnp.concatenate([rel] * (length // 128), axis=1)
    seen = (iota((length, length), 1).astype(F32) >= wide) & (
        iota((length, length), 1) <= iota((length, length), 0)
    )
    scores = jnp.where(seen, dot_nt(reads, w_ref[...]), 0.0)
    squares = jnp.zeros((length, 128), F32)
    inners = jnp.zeros((length, 128), F32)
    for h in range(heads):
        lc = lcol_ref[:, h : h + 1]
        decay = jnp.exp2(jnp.minimum(lc - lrow_ref[h : h + 1, :], 0.0))
        enter = jnp.where(rel < 0, jnp.exp2(jnp.broadcast_to(lc, rel.shape)), 0.0)
        mixed = dot((scores * decay).astype(BF16), x_ref[:, cols(h)]) + enter * dot(
            reads, s_ref[cols(h), :]
        )
        mixed_ref[:, cols(h)] = mixed
        gate = gate_ref[:, cols(h)].astype(F32)
        gated = mixed * (gate / (1.0 + jnp.exp(-gate)))
        squares = squares + gated * gated
        inners = inners + grad_ref[:, cols(h)].astype(F32) * gated
    ones = jnp.ones((8, 128), F32)
    square_row = dot_nt(ones, squares, HIGH)
    inner_row = dot_nt(ones, inners, HIGH)
    sums_ref[...] = jnp.where(iota((8, length), 0) == 0, square_row, inner_row)


def gate_kernel(
    width, sums_ref, mixed_ref, gate_ref, grad_ref, r_ref, rel_ref, lrow_ref,
    mixer_ref, ggrad_ref, dmixed_ref, out_ref,
):
    length = mixed_ref.shape[0]
    heads = lrow_ref.shape[0]
    rows = out_ref.shape[1]
    scale = lax.rsqrt(sums_ref[0:1, :] / width + EPSILON)
    rms = column(scale)
    pull = column(scale * scale * scale * sums_ref[1:2, :] / width)
    reads = r_ref[...].astype(F32).T
    enters = rel_ref[...] < 0
    for h in range(heads):
        mixed = mixed_ref[:, cols(h)]
        gate = gate_ref[:, cols(h)].astype(F32)
        sigma = 1.0 / (1.0 + jnp.exp(-gate))
        swish = gate * sigma
        gated = mixed * swish
        mixer_ref[:, cols(h)] = (gated * rms).astype(BF16)
        dgated = rms * grad_ref[:, cols(h)].astype(F32) - pull * gated
        dmixed = (dgated * swish).astype(BF16)
        dmixed_ref[:, cols(h)] = dmixed
        ggrad_ref[:, cols(h)] = (
            dgated * mixed * sigma * (1.0 + gate * (1.0 - sigma))
        ).astype(BF16)
        enter = jnp.where(enters, jnp.exp2(lrow_ref[h : h + 1, :]), 0.0)
        state = dot((reads * enter).astype(BF16), dmixed).astype(BF16)
        first = h * HEAD_DIM
        for part in range(first // rows, (first + HEAD_DIM - 1) // rows + 1):
            begin = max(first, part * rows)
            end = min(first + HEAD_DIM, (part + 1) * rows)
            out_ref[part, begin - part * rows : end - part * rows, :] = state[
                begin - first : end - first, :
            ]


def inner_kernel(
    dmixed_ref, x_ref, w_ref, r_ref, rel_ref, lcol_ref, lrow_ref, s_ref, gin_ref, read_ref, write_ref
):
    length, heads = lcol_ref.shape
    rel_row = rel_ref[...]
    rel = column(rel_row.astype(F32))
    seen = (iota((length, length), 0) >= rel_row) & (
        iota((length, length), 0) <= iota((length, length), 1)
    )
    scores = jnp.where(seen, dot_nt(w_ref[...], r_ref[...]), 0.0)
    total = jnp.zeros((length, length), F32)
    read = jnp.zeros((length, 128), F32)
    for h in range(heads):
        lc = lcol_ref[:, h : h + 1]
        decay = jnp.exp2(jnp.minimum(lrow_ref[h : h + 1, :] - lc, 0.0))
        dmixed = dmixed_ref[:, cols(h)]
        gin_ref[:, cols(h)] = dot((scores * decay).astype(BF16), dmixed)
        total = total + decay * dot_nt(x_ref[:, cols(h)], dmixed)
        enter = jnp.where(rel < 0, jnp.exp2(jnp.broadcast_to(lc, rel.shape)), 0.0)
        read = read + enter * dot_nt(dmixed, s_ref[cols(h), :])
    total = jnp.where(seen, total, 0.0)
    write_ref[...] = dot(total.astype(BF16), r_ref[...])
    read_ref[...] = read + dot(total.T.astype(BF16), w_ref[...])


def last_kernel(gin_ref, x_ref, w_ref, rel_ref, lcol_ref, back_ref, part_ref, out_ref, write_ref):
    length, heads = lcol_ref.shape
    rel_last = rel_ref[:, length - 1 :]
    last_doc = iota((length, 128), 0) >= rel_last
    writes = w_ref[...]
    write = part_ref[...]
    for h in range(heads):
        lc = lcol_ref[:, h : h + 1]
        line = jnp.broadcast_to(lc[length - 1 :, :] - lc, (length, 128))
        to_end = jnp.where(last_doc, jnp.exp2(line), 0.0)
        back = back_ref[cols(h), :]
        out_ref[:, cols(h)] = (gin_ref[:, cols(h)] + to_end * dot(writes, back)).astype(BF16)
        write = write + to_end * dot_nt(x_ref[:, cols(h)], back)
    write_ref[...] = write


def exchange(blocks):
    return lax.all_to_all(blocks, "ctx", 0, 0)


def mixer(ssm_input, gate_input, write_map, read_map, log_decay, rel, ssm_grad):
    length, width = ssm_input.shape
    heads = width // HEAD_DIM
    parts = lax.axis_size("ctx")
    rows = width // parts
    full_width = width * lax.axis_size("head")
    work = 2 * length * length * width
    sent, lcol, lrow = call(
        first_kernel,
        (
            shape((parts, rows + TAIL, 128), BF16),
            shape((length, heads), F32),
            shape((heads, length), F32),
        ),
        log_decay, rel, write_map, ssm_input, flops=work // 2, name="ssm_first",
    )
    got = exchange(sent)
    tail = got[:, rows:, :]
    carried = call(
        lambda *refs: carry_kernel(False, *refs), shape((parts, rows, 128), BF16), tail, got,
        name="ssm_carry",
    )
    state = exchange(carried).reshape(width, 128)
    mixed, sums = call(
        mix_kernel,
        (shape((length, width), F32), shape((8, length), F32)),
        ssm_input, gate_input, ssm_grad, write_map, read_map, rel, lcol, lrow, state,
        flops=work * 3 // 2, name="ssm_mix",
    )
    sums = lax.psum(sums, "head")
    mixer_out, gate_grad, dmixed, sent = call(
        lambda *refs: gate_kernel(full_width, *refs),
        (
            shape((length, width), BF16),
            shape((length, width), BF16),
            shape((length, width), BF16),
            shape((parts, rows, 128), BF16),
        ),
        sums, mixed, gate_input, ssm_grad, read_map, rel, lrow, flops=work // 2, name="ssm_gate",
    )
    got = exchange(sent)
    carried = call(
        lambda *refs: carry_kernel(True, *refs), shape((parts, rows, 128), BF16), tail, got,
        name="ssm_carry_back",
    )
    back = exchange(carried).reshape(width, 128)
    gin, read_part, write_part = call(
        inner_kernel,
        (shape((length, width), F32), shape((length, 128), F32), shape((length, 128), F32)),
        dmixed, ssm_input, write_map, read_map, rel, lcol, lrow, state,
        flops=work * 5 // 2, name="ssm_inner",
    )
    input_grad, write_part = call(
        last_kernel,
        (shape((length, width), BF16), shape((length, 128), F32)),
        gin, ssm_input, write_map, rel, lcol, back, write_part, flops=work, name="ssm_last",
    )
    write_sum, read_sum = lax.psum((write_part, read_part), "head")
    return mixer_out, input_grad, gate_grad, write_sum.astype(BF16), read_sum.astype(BF16)


def pack_kernel(marks_ref, q_ref, k_ref, v_ref, g_ref, out_ref):
    parts, per = out_ref.shape[:2]
    length = q_ref.shape[0]
    for part in range(parts):
        for a in range(per):
            here = cols(part * per + a)
            for place, ref in enumerate((q_ref, k_ref, v_ref, g_ref)):
                out_ref[part, a, place * length : (place + 1) * length, :] = ref[:, here]
            out_ref[part, a, 4 * length :, :] = marks_ref[...]


def unpack_kernel(in_ref, *out_refs):
    parts, per = in_ref.shape[:2]
    length = in_ref.shape[2] // 4
    for part in range(parts):
        for a in range(per):
            here = cols(part * per + a)
            for place, ref in enumerate(out_refs):
                ref[:, here] = in_ref[part, a, place * length : (place + 1) * length, :]


def attend_kernel(length, in_ref, out_ref, expo_ref, top_ref, kt_ref, vt_ref, dk_ref, dv_ref):
    parts = in_ref.shape[0]
    scale = ATT_DIM ** (-0.5)
    rate = scale * LOG2E
    for a in range(in_ref.shape[1]):

        def piece(block, place):
            return in_ref[block, a, place * length : (place + 1) * length, :]

        def turn(j, _):
            kt_ref[j] = flip(piece(j, 1))
            vt_ref[j] = flip(piece(j, 2))
            dk_ref[j] = jnp.zeros((length, ATT_DIM), F32)
            dv_ref[j] = jnp.zeros((length, ATT_DIM), F32)
            return 0

        lax.fori_loop(0, parts, turn, 0)

        def rows_of(i, _):
            queries, grads = piece(i, 0), piece(i, 3)
            marks = in_ref[i, a, 4 * length :, :].astype(F32)
            groups = length // 128
            starts = jnp.concatenate(
                [marks[2 * n : 2 * n + 1] * 128.0 + marks[2 * n + 1 : 2 * n + 2] for n in range(groups)],
                axis=1,
            ).astype(jnp.int32)
            query_at = i * length + iota((1, length), 1)

            def score(j, running):
                top, total = running
                key_at = j * length + iota((length, length), 0)
                seen = (key_at <= query_at) & (key_at >= starts)
                if parts * length > WINDOW:
                    seen = seen & (query_at - key_at < WINDOW)
                raw = jnp.where(seen, dot_nt(piece(j, 1), queries), MASKED)
                new = jnp.maximum(top, jnp.max(raw, axis=0, keepdims=True))
                expo = jnp.exp2((raw - new) * rate)
                expo_ref[j] = expo
                top_ref[j] = new
                total = total * jnp.exp2((top - new) * rate) + jnp.sum(expo, axis=0, keepdims=True)
                return new, total

            top, total = lax.fori_loop(
                0, i + 1, score,
                (jnp.full((1, length), MASKED, F32), jnp.zeros((1, length), F32)),
            )

            def weigh(j, out):
                factor = jnp.exp2((top_ref[j] - top) * rate) / total
                probs = expo_ref[j] * factor
                expo_ref[j] = probs
                weights = probs.astype(BF16)
                dv_ref[j] += dot(weights, grads)
                return out + dot(vt_ref[j], weights)

            out = lax.fori_loop(0, i + 1, weigh, jnp.zeros((ATT_DIM, length), F32))
            delta = jnp.sum(out * grads.astype(F32).T, axis=0, keepdims=True)

            def push(j, dquery):
                dprobs = dot_nt(piece(j, 2), grads)
                dscore = (expo_ref[j] * ((dprobs - delta) * scale)).astype(BF16)
                dk_ref[j] += dot(dscore, queries)
                return dquery + dot(kt_ref[j], dscore)

            dquery = lax.fori_loop(0, i + 1, push, jnp.zeros((ATT_DIM, length), F32))
            out_ref[i, a, 0:length, :] = out.T.astype(BF16)
            out_ref[i, a, length : 2 * length, :] = dquery.T.astype(BF16)
            return 0

        lax.fori_loop(0, parts, rows_of, 0)

        def finish(j, _):
            out_ref[j, a, 2 * length : 3 * length, :] = dk_ref[j].astype(BF16)
            out_ref[j, a, 3 * length :, :] = dv_ref[j].astype(BF16)
            return 0

        lax.fori_loop(0, parts, finish, 0)


def attention(att_queries, att_keys, att_values, att_grad, doc_start):
    length, width = att_queries.shape
    parts = lax.axis_size("ctx")
    per = width // ATT_DIM // parts
    marks = doc_start.reshape(length // 128, 128)
    marks = jnp.stack([marks // 128, marks % 128], axis=1).reshape(length // 64, 128)
    marks = jnp.pad(marks, ((0, TAIL - length // 64), (0, 0))).astype(BF16)
    sent = call(
        pack_kernel, shape((parts, per, 4 * length + TAIL, 128), BF16),
        marks, att_queries, att_keys, att_values, att_grad, name="att_pack",
    )
    got = exchange(sent)
    done = call(
        lambda *refs: attend_kernel(length, *refs),
        shape((parts, per, 4 * length, 128), BF16),
        got,
        scratch=[
            pltpu.VMEM((parts, length, length), F32),
            pltpu.VMEM((parts, 1, length), F32),
            pltpu.VMEM((parts, ATT_DIM, length), BF16),
            pltpu.VMEM((parts, ATT_DIM, length), BF16),
            pltpu.VMEM((parts, length, ATT_DIM), F32),
            pltpu.VMEM((parts, length, ATT_DIM), F32),
        ],
        flops=6 * per * (parts * length) ** 2 * ATT_DIM, name="att_attend",
    )
    got = exchange(done)
    return call(
        unpack_kernel, (shape((length, width), BF16),) * 4, got, name="att_unpack"
    )


def shifted(shard, axis, by):
    devices = lax.axis_size(axis)
    pairs = [(i, i + by) for i in range(devices) if 0 <= i + by < devices]
    return lax.ppermute(shard, axis, pairs)


def head_cols(array, head_index):
    return lax.dynamic_slice_in_dim(array, head_index * ATT_DIM, ATT_DIM, 1)


def ring_attention(att_queries, att_keys, att_values, att_grad, doc_start):
    length = att_queries.shape[0]
    shard_index = lax.axis_index("ctx")
    halo_shards = WINDOW // length
    att_count = att_queries.shape[1] // ATT_DIM
    att_width = att_queries.shape[1]
    score_scale = ATT_DIM ** (-0.5)

    def pass_keys(running, unused):
        moved = shifted((running[0], running[1]), "ctx", 1)
        return (moved, moved)

    _, earlier = lax.scan(pass_keys, (att_keys, att_values), None, length=halo_shards)
    key_all = jnp.concatenate(
        [earlier[0][::-1].reshape(halo_shards * length, att_width), att_keys], axis=0
    )
    value_all = jnp.concatenate(
        [earlier[1][::-1].reshape(halo_shards * length, att_width), att_values], axis=0
    )
    spread_rows = (halo_shards + 1) * length
    query_pos = shard_index * length + jnp.arange(length, dtype=jnp.int32)
    key_pos = (shard_index - halo_shards) * length + jnp.arange(spread_rows, dtype=jnp.int32)
    visible = (
        (key_pos[None, :] <= query_pos[:, None])
        & (query_pos[:, None] - key_pos[None, :] < WINDOW)
        & (key_pos[None, :] >= doc_start[:, None])
    )

    def forward_head(head_index, running):
        out_buf, max_buf, total_buf, delta_buf = running
        query_head = head_cols(att_queries, head_index)
        key_head = head_cols(key_all, head_index)
        value_head = head_cols(value_all, head_index)
        score = (
            jnp.einsum("td,sd->ts", query_head, key_head, preferred_element_type=jnp.float32)
            * score_scale
        )
        row_max = jnp.max(jnp.where(visible, score, -jnp.inf), axis=1)
        expo = jnp.where(visible, jnp.exp(score - row_max[:, None]), 0.0)
        row_total = jnp.sum(expo, axis=1)
        weights = (expo / row_total[:, None]).astype(jnp.bfloat16)
        attended = jnp.dot(weights, value_head, preferred_element_type=jnp.float32)
        delta = jnp.sum(head_cols(att_grad, head_index).astype(jnp.float32) * attended, axis=1)
        out_buf = lax.dynamic_update_slice_in_dim(
            out_buf, attended.astype(jnp.bfloat16), head_index * ATT_DIM, 1
        )
        return (
            out_buf,
            max_buf.at[:, head_index].set(row_max),
            total_buf.at[:, head_index].set(row_total),
            delta_buf.at[:, head_index].set(delta),
        )

    stats_zero = jnp.zeros((length, att_count), jnp.float32)
    window_out, row_maxes, row_totals, row_deltas = lax.fori_loop(
        0,
        att_count,
        forward_head,
        (jnp.zeros((length, att_width), jnp.bfloat16), stats_zero, stats_zero, stats_zero),
    )

    def query_terms(head_index):
        query_head = head_cols(att_queries, head_index)
        key_head = head_cols(key_all, head_index)
        value_head = head_cols(value_all, head_index)
        grad_head = head_cols(att_grad, head_index)
        score = (
            jnp.einsum("td,sd->ts", query_head, key_head, preferred_element_type=jnp.float32)
            * score_scale
        )
        probs = (
            jnp.where(visible, jnp.exp(score - row_maxes[:, head_index][:, None]), 0.0)
            / row_totals[:, head_index][:, None]
        )
        weights = probs.astype(jnp.bfloat16)
        dprobs = jnp.einsum("td,sd->ts", grad_head, value_head, preferred_element_type=jnp.float32)
        dscore = (probs * (dprobs - row_deltas[:, head_index][:, None]) * score_scale).astype(
            jnp.bfloat16
        )
        query_part = jnp.dot(dscore, key_head, preferred_element_type=jnp.float32)
        return (query_head, grad_head, weights, dscore, query_part)

    def backward_head(head_index, running):
        query_buf, key_buf, value_buf = running
        query_head, grad_head, weights, dscore, query_part = query_terms(head_index)
        key_part = jnp.einsum("ts,td->sd", dscore, query_head, preferred_element_type=jnp.float32)
        value_part = jnp.einsum("ts,td->sd", weights, grad_head, preferred_element_type=jnp.float32)
        query_buf = lax.dynamic_update_slice_in_dim(query_buf, query_part, head_index * ATT_DIM, 1)
        key_buf = lax.dynamic_update_slice_in_dim(key_buf, key_part, head_index * ATT_DIM, 1)
        value_buf = lax.dynamic_update_slice_in_dim(value_buf, value_part, head_index * ATT_DIM, 1)
        return (query_buf, key_buf, value_buf)

    part_zero = jnp.zeros((spread_rows, att_width), jnp.float32)
    query_sum, key_parts, value_parts = lax.fori_loop(
        0,
        att_count,
        backward_head,
        (jnp.zeros((length, att_width), jnp.float32), part_zero, part_zero),
    )
    key_blocks = key_parts.reshape(halo_shards + 1, length, att_width)
    value_blocks = value_parts.reshape(halo_shards + 1, length, att_width)

    def send_back(running, block_index):
        moved = shifted((running[0], running[1]), "ctx", -1)
        return ((moved[0] + key_blocks[block_index], moved[1] + value_blocks[block_index]), None)

    (key_sum, value_sum), _ = lax.scan(
        send_back, (key_blocks[0], value_blocks[0]), jnp.arange(1, halo_shards + 1, dtype=jnp.int32)
    )
    return (
        window_out,
        query_sum.astype(jnp.bfloat16),
        key_sum.astype(jnp.bfloat16),
        value_sum.astype(jnp.bfloat16),
    )


def body(
    ssm_input,
    gate_input,
    write_map,
    read_map,
    log_decay,
    doc_start,
    ssm_grad,
    att_queries,
    att_keys,
    att_values,
    att_grad,
):
    length = ssm_input.shape[0]
    rel = (doc_start - lax.axis_index("ctx") * length).reshape(1, length)
    whole_heads = (att_queries.shape[1] // ATT_DIM) % lax.axis_size("ctx") == 0
    attend = attention if whole_heads else ring_attention
    window_out, query_grad, key_grad, value_grad = attend(
        att_queries, att_keys, att_values, att_grad, doc_start
    )
    mixer_out, input_grad, gate_grad, write_grad, read_grad = mixer(
        ssm_input, gate_input, write_map, read_map, log_decay, rel, ssm_grad
    )
    return (
        mixer_out,
        window_out,
        input_grad,
        gate_grad,
        write_grad,
        read_grad,
        query_grad,
        key_grad,
        value_grad,
    )


def solution(mesh):
    in_specs = (
        P("ctx", "head"),
        P("ctx", "head"),
        P("ctx", None),
        P("ctx", None),
        P("ctx", "head"),
        P("ctx"),
        P("ctx", "head"),
        P("ctx", "head"),
        P("ctx", "head"),
        P("ctx", "head"),
        P("ctx", "head"),
    )
    out_specs = (
        P("ctx", "head"),
        P("ctx", "head"),
        P("ctx", "head"),
        P("ctx", "head"),
        P("ctx", None),
        P("ctx", None),
        P("ctx", "head"),
        P("ctx", "head"),
        P("ctx", "head"),
    )
    return jax.shard_map(body, mesh=mesh, in_specs=in_specs, out_specs=out_specs, check_vma=False)
```

```python
import jax
import jax.numpy as jnp
from jax import lax
from jax.experimental import pallas as pl
from jax.experimental.pallas import tpu as pltpu
from jax.sharding import PartitionSpec as P

HEAD_DIM = 128
ATT_DIM = 128
WINDOW = 4096
EPSILON = 1e-05
LOG2E = 1.4426950408889634
TAIL = 16
MASKED = -1e30
HIGH = lax.Precision.HIGHEST
F32 = jnp.float32
BF16 = jnp.bfloat16
VMEM_BYTES = 56 * 1024 * 1024


def call(kernel, out_shape, *operands, scratch=(), flops=0, name=None):
    moved = sum(a.size * a.dtype.itemsize for a in jax.tree.leaves((operands, out_shape)))
    return pl.pallas_call(
        kernel,
        out_shape=out_shape,
        in_specs=[pl.BlockSpec(memory_space=pltpu.VMEM)] * len(operands),
        out_specs=jax.tree.map(lambda _: pl.BlockSpec(memory_space=pltpu.VMEM), out_shape),
        scratch_shapes=scratch,
        compiler_params=pltpu.CompilerParams(vmem_limit_bytes=VMEM_BYTES),
        cost_estimate=pl.CostEstimate(flops=flops, bytes_accessed=moved, transcendentals=0),
        name=name,
    )(*operands)


def shape(dims, dtype):
    return jax.ShapeDtypeStruct(dims, dtype)


def dot(a, b):
    return jnp.dot(a, b, preferred_element_type=F32)


def dot_nt(a, b, precision=None):
    return lax.dot_general(
        a, b, (((1,), (1,)), ((), ())), preferred_element_type=F32, precision=precision
    )


def iota(dims, axis):
    return lax.broadcasted_iota(jnp.int32, dims, axis)


def flip(a):
    return a.astype(F32).T.astype(BF16)


def column(row):
    return jnp.broadcast_to(row, (128, row.shape[1])).T


def cols(h):
    return slice(h * HEAD_DIM, (h + 1) * HEAD_DIM)


def first_kernel(ld_ref, rel_ref, w_ref, x_ref, out_ref, lcol_ref, lrow_ref):
    heads, length = ld_ref.shape
    parts, rows = out_ref.shape[0], out_ref.shape[1] - TAIL
    rates = ld_ref[...] * LOG2E
    lower = jnp.where(iota((length, length), 0) >= iota((length, length), 1), 1.0, 0.0)
    upper = jnp.where(iota((length, length), 0) <= iota((length, length), 1), 1.0, 0.0)
    lcol_ref[...] = dot_nt(lower, rates, HIGH)
    lrow = jnp.dot(rates, upper, preferred_element_type=F32, precision=HIGH)
    lrow_ref[...] = lrow
    rel_last = rel_ref[:, length - 1 :]
    last_doc = iota((1, length), 1) >= rel_last
    keeps = rel_last < 0
    writes = w_ref[...].astype(F32).T
    tail_row = iota((TAIL, 128), 0)
    for h in range(heads):
        line = lrow[h : h + 1, :]
        total = line[:, length - 1 :]
        to_end = jnp.where(last_doc, jnp.exp2(total - line), 0.0)
        state = dot((writes * to_end).astype(BF16), x_ref[:, cols(h)]).astype(BF16)
        factor = jnp.where(keeps, jnp.exp2(total), 0.0)
        high = factor.astype(BF16).astype(F32)
        low = factor - high
        first = h * HEAD_DIM
        for part in range(first // rows, (first + HEAD_DIM - 1) // rows + 1):
            begin = max(first, part * rows)
            end = min(first + HEAD_DIM, (part + 1) * rows)
            out_ref[part, begin - part * rows : end - part * rows, :] = state[
                begin - first : end - first, :
            ]
            place = 2 * (begin - part * rows) // HEAD_DIM
            tail = jnp.where(tail_row == place, high, jnp.where(tail_row == place + 1, low, 0.0))
            if place:
                tail = tail + out_ref[part, rows:, :].astype(F32)
            out_ref[part, rows:, :] = tail.astype(BF16)


def carry_kernel(backward, tail_ref, in_ref, out_ref):
    parts, rows = out_ref.shape[0], out_ref.shape[1]
    step = min(rows, HEAD_DIM)
    for k in range(rows // step):
        here = slice(k * step, (k + 1) * step)
        state = jnp.zeros((step, 128), F32)
        for c in range(parts)[:: -1 if backward else 1]:
            out_ref[c, here, :] = state.astype(BF16)
            tail = tail_ref[c].astype(F32)
            factor = tail[2 * k : 2 * k + 1, :] + tail[2 * k + 1 : 2 * k + 2, :]
            state = factor * state + in_ref[c, here, :].astype(F32)


def mix_kernel(
    x_ref, gate_ref, grad_ref, w_ref, r_ref, rel_ref, lcol_ref, lrow_ref, s_ref, mixed_ref, sums_ref
):
    length, heads = lcol_ref.shape
    reads = r_ref[...]
    rel = column(rel_ref[...].astype(F32))
    wide = jnp.concatenate([rel] * (length // 128), axis=1)
    seen = (iota((length, length), 1).astype(F32) >= wide) & (
        iota((length, length), 1) <= iota((length, length), 0)
    )
    scores = jnp.where(seen, dot_nt(reads, w_ref[...]), 0.0)
    squares = jnp.zeros((length, 128), F32)
    inners = jnp.zeros((length, 128), F32)
    for h in range(heads):
        lc = lcol_ref[:, h : h + 1]
        decay = jnp.exp2(jnp.minimum(lc - lrow_ref[h : h + 1, :], 0.0))
        enter = jnp.where(rel < 0, jnp.exp2(jnp.broadcast_to(lc, rel.shape)), 0.0)
        mixed = dot((scores * decay).astype(BF16), x_ref[:, cols(h)]) + enter * dot(
            reads, s_ref[cols(h), :]
        )
        mixed_ref[:, cols(h)] = mixed
        gate = gate_ref[:, cols(h)].astype(F32)
        gated = mixed * (gate / (1.0 + jnp.exp(-gate)))
        squares = squares + gated * gated
        inners = inners + grad_ref[:, cols(h)].astype(F32) * gated
    ones = jnp.ones((8, 128), F32)
    square_row = dot_nt(ones, squares, HIGH)
    inner_row = dot_nt(ones, inners, HIGH)
    sums_ref[...] = jnp.where(iota((8, length), 0) == 0, square_row, inner_row)


def gate_kernel(
    width, sums_ref, mixed_ref, gate_ref, grad_ref, r_ref, rel_ref, lrow_ref,
    mixer_ref, ggrad_ref, dmixed_ref, out_ref,
):
    length = mixed_ref.shape[0]
    heads = lrow_ref.shape[0]
    rows = out_ref.shape[1]
    scale = lax.rsqrt(sums_ref[0:1, :] / width + EPSILON)
    rms = column(scale)
    pull = column(scale * scale * scale * sums_ref[1:2, :] / width)
    reads = r_ref[...].astype(F32).T
    enters = rel_ref[...] < 0
    for h in range(heads):
        mixed = mixed_ref[:, cols(h)]
        gate = gate_ref[:, cols(h)].astype(F32)
        sigma = 1.0 / (1.0 + jnp.exp(-gate))
        swish = gate * sigma
        gated = mixed * swish
        mixer_ref[:, cols(h)] = (gated * rms).astype(BF16)
        dgated = rms * grad_ref[:, cols(h)].astype(F32) - pull * gated
        dmixed = (dgated * swish).astype(BF16)
        dmixed_ref[:, cols(h)] = dmixed
        ggrad_ref[:, cols(h)] = (
            dgated * mixed * sigma * (1.0 + gate * (1.0 - sigma))
        ).astype(BF16)
        enter = jnp.where(enters, jnp.exp2(lrow_ref[h : h + 1, :]), 0.0)
        state = dot((reads * enter).astype(BF16), dmixed).astype(BF16)
        first = h * HEAD_DIM
        for part in range(first // rows, (first + HEAD_DIM - 1) // rows + 1):
            begin = max(first, part * rows)
            end = min(first + HEAD_DIM, (part + 1) * rows)
            out_ref[part, begin - part * rows : end - part * rows, :] = state[
                begin - first : end - first, :
            ]


def inner_kernel(
    dmixed_ref, x_ref, w_ref, r_ref, rel_ref, lcol_ref, lrow_ref, s_ref, gin_ref, read_ref, write_ref
):
    length, heads = lcol_ref.shape
    rel_row = rel_ref[...]
    rel = column(rel_row.astype(F32))
    seen = (iota((length, length), 0) >= rel_row) & (
        iota((length, length), 0) <= iota((length, length), 1)
    )
    scores = jnp.where(seen, dot_nt(w_ref[...], r_ref[...]), 0.0)
    total = jnp.zeros((length, length), F32)
    read = jnp.zeros((length, 128), F32)
    for h in range(heads):
        lc = lcol_ref[:, h : h + 1]
        decay = jnp.exp2(jnp.minimum(lrow_ref[h : h + 1, :] - lc, 0.0))
        dmixed = dmixed_ref[:, cols(h)]
        gin_ref[:, cols(h)] = dot((scores * decay).astype(BF16), dmixed)
        total = total + decay * dot_nt(x_ref[:, cols(h)], dmixed)
        enter = jnp.where(rel < 0, jnp.exp2(jnp.broadcast_to(lc, rel.shape)), 0.0)
        read = read + enter * dot_nt(dmixed, s_ref[cols(h), :])
    total = jnp.where(seen, total, 0.0)
    write_ref[...] = dot(total.astype(BF16), r_ref[...])
    read_ref[...] = read + dot(total.T.astype(BF16), w_ref[...])


def last_kernel(gin_ref, x_ref, w_ref, rel_ref, lcol_ref, back_ref, part_ref, out_ref, write_ref):
    length, heads = lcol_ref.shape
    rel_last = rel_ref[:, length - 1 :]
    last_doc = iota((length, 128), 0) >= rel_last
    writes = w_ref[...]
    write = part_ref[...]
    for h in range(heads):
        lc = lcol_ref[:, h : h + 1]
        line = jnp.broadcast_to(lc[length - 1 :, :] - lc, (length, 128))
        to_end = jnp.where(last_doc, jnp.exp2(line), 0.0)
        back = back_ref[cols(h), :]
        out_ref[:, cols(h)] = (gin_ref[:, cols(h)] + to_end * dot(writes, back)).astype(BF16)
        write = write + to_end * dot_nt(x_ref[:, cols(h)], back)
    write_ref[...] = write


def exchange(blocks):
    return lax.all_to_all(blocks, "ctx", 0, 0)


def pack_kernel(marks_ref, q_ref, k_ref, v_ref, g_ref, out_ref):
    parts, per = out_ref.shape[:2]
    length = q_ref.shape[0]
    for part in range(parts):
        for a in range(per):
            here = cols(part * per + a)
            for place, ref in enumerate((q_ref, k_ref, v_ref, g_ref)):
                out_ref[part, a, place * length : (place + 1) * length, :] = ref[:, here]
            out_ref[part, a, 4 * length :, :] = marks_ref[...]


def unpack_kernel(in_ref, *out_refs):
    parts, per = in_ref.shape[:2]
    length = in_ref.shape[2] // 4
    for part in range(parts):
        for a in range(per):
            here = cols(part * per + a)
            for place, ref in enumerate(out_refs):
                ref[:, here] = in_ref[part, a, place * length : (place + 1) * length, :]


def attend_kernel(length, in_ref, out_ref, expo_ref, kt_ref, vt_ref, dk_ref, dv_ref):
    parts = in_ref.shape[0]
    scale = ATT_DIM ** (-0.5)
    rate = scale * LOG2E
    key_in = iota((length, length), 0)
    causal = key_in <= iota((length, length), 1)
    for a in range(in_ref.shape[1]):

        def piece(block, place):
            return in_ref[block, a, place * length : (place + 1) * length, :]

        for i in range(parts):
            kt_ref[i] = flip(piece(i, 1))
            vt_ref[i] = flip(piece(i, 2))
            queries, grads = piece(i, 0), piece(i, 3)
            marks = in_ref[i, a, 4 * length :, :].astype(F32)
            starts = jnp.concatenate(
                [
                    marks[2 * n : 2 * n + 1] * 128.0 + marks[2 * n + 1 : 2 * n + 2]
                    for n in range(length // 128)
                ],
                axis=1,
            ).astype(jnp.int32)
            query_at = i * length + iota((1, length), 1)
            if parts * length > WINDOW:
                starts = jnp.maximum(starts, query_at - (WINDOW - 1))
            top = jnp.full((1, length), MASKED, F32)
            total = jnp.zeros((1, length), F32)
            tops = []
            for j in range(i + 1):
                seen = key_in >= starts - j * length
                if j == i:
                    seen = seen & causal
                raw = jnp.where(seen, dot_nt(piece(j, 1), queries), MASKED)
                new = jnp.maximum(top, jnp.max(raw, axis=0, keepdims=True))
                expo = jnp.exp2((raw - new) * rate)
                expo_ref[j] = expo
                total = total * jnp.exp2((top - new) * rate) + jnp.sum(expo, axis=0, keepdims=True)
                top = new
                tops.append(new)
            out = jnp.zeros((ATT_DIM, length), F32)
            for j in range(i + 1):
                probs = expo_ref[j] * (jnp.exp2((tops[j] - top) * rate) / total)
                expo_ref[j] = probs
                weights = probs.astype(BF16)
                dvalue = dot(weights, grads)
                dv_ref[j] = dvalue if j == i else dv_ref[j] + dvalue
                out = out + dot(vt_ref[j], weights)
            delta = jnp.sum(out * grads.astype(F32).T, axis=0, keepdims=True)
            dquery = jnp.zeros((ATT_DIM, length), F32)
            for j in range(i + 1):
                dprobs = dot_nt(piece(j, 2), grads)
                dscore = (expo_ref[j] * ((dprobs - delta) * scale)).astype(BF16)
                dkey = dot(dscore, queries)
                dk_ref[j] = dkey if j == i else dk_ref[j] + dkey
                dquery = dquery + dot(kt_ref[j], dscore)
            out_ref[i, a, 0:length, :] = out.T.astype(BF16)
            out_ref[i, a, length : 2 * length, :] = dquery.T.astype(BF16)
        for j in range(parts):
            out_ref[j, a, 2 * length : 3 * length, :] = dk_ref[j].astype(BF16)
            out_ref[j, a, 3 * length :, :] = dv_ref[j].astype(BF16)


def shifted(shard, axis, by):
    devices = lax.axis_size(axis)
    pairs = [(i, i + by) for i in range(devices) if 0 <= i + by < devices]
    return lax.ppermute(shard, axis, pairs)


def head_cols(array, head_index):
    return lax.dynamic_slice_in_dim(array, head_index * ATT_DIM, ATT_DIM, 1)


def ring_attention(att_queries, att_keys, att_values, att_grad, doc_start):
    length = att_queries.shape[0]
    shard_index = lax.axis_index("ctx")
    halo_shards = WINDOW // length
    att_count = att_queries.shape[1] // ATT_DIM
    att_width = att_queries.shape[1]
    score_scale = ATT_DIM ** (-0.5)

    def pass_keys(running, unused):
        moved = shifted((running[0], running[1]), "ctx", 1)
        return (moved, moved)

    _, earlier = lax.scan(pass_keys, (att_keys, att_values), None, length=halo_shards)
    key_all = jnp.concatenate(
        [earlier[0][::-1].reshape(halo_shards * length, att_width), att_keys], axis=0
    )
    value_all = jnp.concatenate(
        [earlier[1][::-1].reshape(halo_shards * length, att_width), att_values], axis=0
    )
    spread_rows = (halo_shards + 1) * length
    query_pos = shard_index * length + jnp.arange(length, dtype=jnp.int32)
    key_pos = (shard_index - halo_shards) * length + jnp.arange(spread_rows, dtype=jnp.int32)
    visible = (
        (key_pos[None, :] <= query_pos[:, None])
        & (query_pos[:, None] - key_pos[None, :] < WINDOW)
        & (key_pos[None, :] >= doc_start[:, None])
    )

    def forward_head(head_index, running):
        out_buf, max_buf, total_buf, delta_buf = running
        query_head = head_cols(att_queries, head_index)
        key_head = head_cols(key_all, head_index)
        value_head = head_cols(value_all, head_index)
        score = (
            jnp.einsum("td,sd->ts", query_head, key_head, preferred_element_type=jnp.float32)
            * score_scale
        )
        row_max = jnp.max(jnp.where(visible, score, -jnp.inf), axis=1)
        expo = jnp.where(visible, jnp.exp(score - row_max[:, None]), 0.0)
        row_total = jnp.sum(expo, axis=1)
        weights = (expo / row_total[:, None]).astype(jnp.bfloat16)
        attended = jnp.dot(weights, value_head, preferred_element_type=jnp.float32)
        delta = jnp.sum(head_cols(att_grad, head_index).astype(jnp.float32) * attended, axis=1)
        out_buf = lax.dynamic_update_slice_in_dim(
            out_buf, attended.astype(jnp.bfloat16), head_index * ATT_DIM, 1
        )
        return (
            out_buf,
            max_buf.at[:, head_index].set(row_max),
            total_buf.at[:, head_index].set(row_total),
            delta_buf.at[:, head_index].set(delta),
        )

    stats_zero = jnp.zeros((length, att_count), jnp.float32)
    window_out, row_maxes, row_totals, row_deltas = lax.fori_loop(
        0,
        att_count,
        forward_head,
        (jnp.zeros((length, att_width), jnp.bfloat16), stats_zero, stats_zero, stats_zero),
    )

    def query_terms(head_index):
        query_head = head_cols(att_queries, head_index)
        key_head = head_cols(key_all, head_index)
        value_head = head_cols(value_all, head_index)
        grad_head = head_cols(att_grad, head_index)
        score = (
            jnp.einsum("td,sd->ts", query_head, key_head, preferred_element_type=jnp.float32)
            * score_scale
        )
        probs = (
            jnp.where(visible, jnp.exp(score - row_maxes[:, head_index][:, None]), 0.0)
            / row_totals[:, head_index][:, None]
        )
        weights = probs.astype(jnp.bfloat16)
        dprobs = jnp.einsum("td,sd->ts", grad_head, value_head, preferred_element_type=jnp.float32)
        dscore = (probs * (dprobs - row_deltas[:, head_index][:, None]) * score_scale).astype(
            jnp.bfloat16
        )
        query_part = jnp.dot(dscore, key_head, preferred_element_type=jnp.float32)
        return (query_head, grad_head, weights, dscore, query_part)

    def backward_head(head_index, running):
        query_buf, key_buf, value_buf = running
        query_head, grad_head, weights, dscore, query_part = query_terms(head_index)
        key_part = jnp.einsum("ts,td->sd", dscore, query_head, preferred_element_type=jnp.float32)
        value_part = jnp.einsum("ts,td->sd", weights, grad_head, preferred_element_type=jnp.float32)
        query_buf = lax.dynamic_update_slice_in_dim(query_buf, query_part, head_index * ATT_DIM, 1)
        key_buf = lax.dynamic_update_slice_in_dim(key_buf, key_part, head_index * ATT_DIM, 1)
        value_buf = lax.dynamic_update_slice_in_dim(value_buf, value_part, head_index * ATT_DIM, 1)
        return (query_buf, key_buf, value_buf)

    part_zero = jnp.zeros((spread_rows, att_width), jnp.float32)
    query_sum, key_parts, value_parts = lax.fori_loop(
        0,
        att_count,
        backward_head,
        (jnp.zeros((length, att_width), jnp.float32), part_zero, part_zero),
    )
    key_blocks = key_parts.reshape(halo_shards + 1, length, att_width)
    value_blocks = value_parts.reshape(halo_shards + 1, length, att_width)

    def send_back(running, block_index):
        moved = shifted((running[0], running[1]), "ctx", -1)
        return ((moved[0] + key_blocks[block_index], moved[1] + value_blocks[block_index]), None)

    (key_sum, value_sum), _ = lax.scan(
        send_back, (key_blocks[0], value_blocks[0]), jnp.arange(1, halo_shards + 1, dtype=jnp.int32)
    )
    return (
        window_out,
        query_sum.astype(jnp.bfloat16),
        key_sum.astype(jnp.bfloat16),
        value_sum.astype(jnp.bfloat16),
    )


def body(
    ssm_input,
    gate_input,
    write_map,
    read_map,
    log_decay,
    doc_start,
    ssm_grad,
    att_queries,
    att_keys,
    att_values,
    att_grad,
):
    length, width = ssm_input.shape
    heads = width // HEAD_DIM
    parts = lax.axis_size("ctx")
    rows = width // parts
    full_width = width * lax.axis_size("head")
    work = 2 * length * length * width
    att_width = att_queries.shape[1]
    per = att_width // ATT_DIM // parts
    dealt = att_width // ATT_DIM % parts == 0
    rel = (doc_start - lax.axis_index("ctx") * length).reshape(1, length)

    sent, lcol, lrow = call(
        first_kernel,
        (
            shape((parts, rows + TAIL, 128), BF16),
            shape((length, heads), F32),
            shape((heads, length), F32),
        ),
        log_decay.T, rel, write_map, ssm_input, flops=work // 2, name="ssm_first",
    )
    got = exchange(sent)
    tail = got[:, rows:, :]
    carried = call(
        lambda *refs: carry_kernel(False, *refs), shape((parts, rows, 128), BF16), tail, got,
        name="ssm_carry",
    )
    state = exchange(carried).reshape(width, 128)

    if dealt:
        marks = doc_start.reshape(length // 128, 128)
        marks = jnp.stack([marks // 128, marks % 128], axis=1).reshape(length // 64, 128)
        marks = jnp.pad(marks, ((0, TAIL - length // 64), (0, 0))).astype(BF16)
        packed = call(
            pack_kernel, shape((parts, per, 4 * length + TAIL, 128), BF16),
            marks, att_queries, att_keys, att_values, att_grad, name="att_pack",
        )
        packed, state = lax.optimization_barrier((packed, state))
        att_got = exchange(packed)
    else:
        att_out = ring_attention(att_queries, att_keys, att_values, att_grad, doc_start)

    mixed, sums = call(
        mix_kernel,
        (shape((length, width), F32), shape((8, length), F32)),
        ssm_input, gate_input, ssm_grad, write_map, read_map, rel, lcol, lrow, state,
        flops=work * 3 // 2, name="ssm_mix",
    )
    sums = lax.psum(sums, "head")
    mixer_out, gate_grad, dmixed, sent = call(
        lambda *refs: gate_kernel(full_width, *refs),
        (
            shape((length, width), BF16),
            shape((length, width), BF16),
            shape((length, width), BF16),
            shape((parts, rows, 128), BF16),
        ),
        sums, mixed, gate_input, ssm_grad, read_map, rel, lrow, flops=work // 2, name="ssm_gate",
    )

    if dealt:
        sent, att_got = lax.optimization_barrier((sent, att_got))
    got = exchange(sent)
    carried = call(
        lambda *refs: carry_kernel(True, *refs), shape((parts, rows, 128), BF16), tail, got,
        name="ssm_carry_back",
    )
    back = exchange(carried).reshape(width, 128)
    if dealt:
        att_done = call(
            lambda *refs: attend_kernel(length, *refs),
            shape((parts, per, 4 * length, 128), BF16),
            att_got,
            scratch=[
                pltpu.VMEM((parts, length, length), F32),
                pltpu.VMEM((parts, ATT_DIM, length), BF16),
                pltpu.VMEM((parts, ATT_DIM, length), BF16),
                pltpu.VMEM((parts, length, ATT_DIM), F32),
                pltpu.VMEM((parts, length, ATT_DIM), F32),
            ],
            flops=6 * per * (parts * length) ** 2 * ATT_DIM, name="att_attend",
        )
        att_done, back = lax.optimization_barrier((att_done, back))
        att_out = call(
            unpack_kernel, (shape((length, att_width), BF16),) * 4, exchange(att_done),
            name="att_unpack",
        )

    gin, read_part, write_part = call(
        inner_kernel,
        (shape((length, width), F32), shape((length, 128), F32), shape((length, 128), F32)),
        dmixed, ssm_input, write_map, read_map, rel, lcol, lrow, state,
        flops=work * 5 // 2, name="ssm_inner",
    )
    input_grad, write_part = call(
        last_kernel,
        (shape((length, width), BF16), shape((length, 128), F32)),
        gin, ssm_input, write_map, rel, lcol, back, write_part, flops=work, name="ssm_last",
    )
    write_sum, read_sum = lax.psum((write_part, read_part), "head")
    window_out, query_grad, key_grad, value_grad = att_out
    return (
        mixer_out,
        window_out,
        input_grad,
        gate_grad,
        write_sum.astype(BF16),
        read_sum.astype(BF16),
        query_grad,
        key_grad,
        value_grad,
    )


def solution(mesh):
    in_specs = (
        P("ctx", "head"),
        P("ctx", "head"),
        P("ctx", None),
        P("ctx", None),
        P("ctx", "head"),
        P("ctx"),
        P("ctx", "head"),
        P("ctx", "head"),
        P("ctx", "head"),
        P("ctx", "head"),
        P("ctx", "head"),
    )
    out_specs = (
        P("ctx", "head"),
        P("ctx", "head"),
        P("ctx", "head"),
        P("ctx", "head"),
        P("ctx", None),
        P("ctx", None),
        P("ctx", "head"),
        P("ctx", "head"),
        P("ctx", "head"),
    )
    return jax.shard_map(body, mesh=mesh, in_specs=in_specs, out_specs=out_specs, check_vma=False)
```

```python
import jax
import jax.numpy as jnp
from jax import lax
from jax.experimental import pallas as pl
from jax.experimental.pallas import tpu as pltpu
from jax.sharding import PartitionSpec as P

HEAD_DIM = 128
ATT_DIM = 128
WINDOW = 4096
EPSILON = 1e-05
LOG2E = 1.4426950408889634
TAIL = 16
MASKED = -1e30
HIGH = lax.Precision.HIGHEST
F32 = jnp.float32
BF16 = jnp.bfloat16
VMEM_BYTES = 56 * 1024 * 1024


VMEM = pl.BlockSpec(memory_space=pltpu.VMEM)
SMEM = pl.BlockSpec(memory_space=pltpu.SMEM)
WHERE = pl.BlockSpec(memory_space=pl.ANY)


def call(kernel, out_shape, *operands, specs=None, out_spec=VMEM, scratch=(), flops=0, name=None):
    moved = sum(a.size * a.dtype.itemsize for a in jax.tree.leaves((operands, out_shape)))
    return pl.pallas_call(
        kernel,
        out_shape=out_shape,
        in_specs=specs or [VMEM] * len(operands),
        out_specs=jax.tree.map(lambda _: out_spec, out_shape),
        scratch_shapes=scratch,
        compiler_params=pltpu.CompilerParams(vmem_limit_bytes=VMEM_BYTES),
        cost_estimate=pl.CostEstimate(flops=flops, bytes_accessed=moved, transcendentals=0),
        name=name,
    )(*operands)


def shape(dims, dtype):
    return jax.ShapeDtypeStruct(dims, dtype)


def dot(a, b):
    return jnp.dot(a, b, preferred_element_type=F32)


def dot_nt(a, b, precision=None):
    return lax.dot_general(
        a, b, (((1,), (1,)), ((), ())), preferred_element_type=F32, precision=precision
    )


def iota(dims, axis):
    return lax.broadcasted_iota(jnp.int32, dims, axis)


def flip(a):
    return a.astype(F32).T.astype(BF16)


def column(row):
    return jnp.broadcast_to(row, (128, row.shape[1])).T


def cols(h):
    return slice(h * HEAD_DIM, (h + 1) * HEAD_DIM)


def first_kernel(ld_ref, rel_ref, w_ref, x_ref, out_ref, lcol_ref, lrow_ref):
    heads, length = ld_ref.shape
    parts, rows = out_ref.shape[0], out_ref.shape[1] - TAIL
    rates = ld_ref[...] * LOG2E
    lower = jnp.where(iota((length, length), 0) >= iota((length, length), 1), 1.0, 0.0)
    upper = jnp.where(iota((length, length), 0) <= iota((length, length), 1), 1.0, 0.0)
    lcol_ref[...] = dot_nt(lower, rates, HIGH)
    lrow = jnp.dot(rates, upper, preferred_element_type=F32, precision=HIGH)
    lrow_ref[...] = lrow
    rel_last = rel_ref[:, length - 1 :]
    last_doc = iota((1, length), 1) >= rel_last
    keeps = rel_last < 0
    writes = w_ref[...].astype(F32).T
    tail_row = iota((TAIL, 128), 0)
    totals = lcol_ref[length - 1 :, :]
    lanes = jnp.concatenate([totals, jnp.zeros((1, 128 - heads), F32)], axis=1)
    every = jnp.where(keeps, jnp.exp2(lanes), 0.0)
    every_high = every.astype(BF16).astype(F32)
    every_low = every - every_high
    base = jnp.where(
        tail_row == TAIL - 2, every_high, jnp.where(tail_row == TAIL - 1, every_low, 0.0)
    )
    for h in range(heads):
        line = lrow[h : h + 1, :]
        total = line[:, length - 1 :]
        to_end = jnp.where(last_doc, jnp.exp2(total - line), 0.0)
        state = dot((writes * to_end).astype(BF16), x_ref[:, cols(h)]).astype(BF16)
        factor = jnp.where(keeps, jnp.exp2(total), 0.0)
        high = factor.astype(BF16).astype(F32)
        low = factor - high
        first = h * HEAD_DIM
        for part in range(first // rows, (first + HEAD_DIM - 1) // rows + 1):
            begin = max(first, part * rows)
            end = min(first + HEAD_DIM, (part + 1) * rows)
            out_ref[part, begin - part * rows : end - part * rows, :] = state[
                begin - first : end - first, :
            ]
            place = 2 * (begin - part * rows) // HEAD_DIM
            tail = jnp.where(tail_row == place, high, jnp.where(tail_row == place + 1, low, base))
            if place:
                tail = jnp.where(tail_row < place, out_ref[part, rows:, :].astype(F32), tail)
            out_ref[part, rows:, :] = tail.astype(BF16)


def carry_kernel(backward, tail_ref, in_ref, out_ref):
    parts, rows = out_ref.shape[0], out_ref.shape[1]
    step = min(rows, HEAD_DIM)
    for k in range(rows // step):
        here = slice(k * step, (k + 1) * step)
        state = jnp.zeros((step, 128), F32)
        for c in range(parts)[:: -1 if backward else 1]:
            out_ref[c, here, :] = state.astype(BF16)
            tail = tail_ref[c, rows:, :].astype(F32)
            factor = tail[2 * k : 2 * k + 1, :] + tail[2 * k + 1 : 2 * k + 2, :]
            state = factor * state + in_ref[c, here, :].astype(F32)


def level_kernel(backward, at_ref, factor_ref, own_ref, got_ref, out_ref):
    half = out_ref.shape[0]
    z, x = at_ref[0], at_ref[1]
    far = 0 if backward else 1
    count = half // HEAD_DIM
    for k in range(count):
        mine = own_ref[pl.ds(pl.multiple_of(x * half + k * HEAD_DIM, HEAD_DIM), HEAD_DIM), :]
        mine, other = mine.astype(F32), got_ref[cols(k), :].astype(F32)
        factor = factor_ref[2 * z + far, x * count + k]
        out_ref[cols(k), :] = jnp.where(
            x == far, mine + factor * other, other + factor * mine
        ).astype(BF16)


def reach_kernel(backward, levels, at_ref, factor_ref, own_ref, got_ref, *refs):
    steps, (mine_ref, message_ref) = refs[: levels - 1], refs[levels - 1 :]
    half = got_ref.shape[0]
    z, x = at_ref[0], at_ref[1]
    far = 0 if backward else 1
    count = half // HEAD_DIM
    for k in range(count):
        head = x * count + k
        sum_in = steps[0][cols(k), :].astype(F32)
        factor = 1.0
        for n in range(1, levels - 1):
            level = jnp.clip(z + n if backward else z - n, 0, levels - 1)
            factor = factor * factor_ref[2 * level, head] * factor_ref[2 * level + 1, head]
            sum_in = sum_in + factor * steps[n][cols(k), :].astype(F32)
        mine = own_ref[pl.ds(pl.multiple_of(x * half + k * HEAD_DIM, HEAD_DIM), HEAD_DIM), :]
        mine, other = mine.astype(F32), got_ref[cols(k), :].astype(F32)
        near_state = jnp.where(x == far, other, mine)
        passed = near_state + factor_ref[2 * z + 1 - far, head] * sum_in
        mine_ref[cols(k), :] = jnp.where(x == far, passed, sum_in).astype(BF16)
        message_ref[cols(k), :] = jnp.where(x == far, sum_in, passed).astype(BF16)


def carry_by_levels(backward, at, factors, own):
    parts = lax.axis_size("ctx")
    levels = parts // 2
    rows = own.shape[0]
    half = rows // 2
    swap = [(i, i ^ 1) for i in range(parts)]
    other = lax.dynamic_slice_in_dim(own, (1 - at[1]) * half, half, 0)
    got = lax.ppermute(other, "ctx", swap)
    level = call(
        lambda *refs: level_kernel(backward, *refs), shape((half, 128), BF16),
        at, factors, own, got, specs=[SMEM, SMEM, VMEM, VMEM], name="ssm_level",
    )
    steps = []
    for n in range(1, levels):
        by = -2 * n if backward else 2 * n
        pairs = [(i, i + by) for i in range(parts) if 0 <= i + by < parts]
        steps.append(lax.ppermute(level, "ctx", pairs))
    mine, message = call(
        lambda *refs: reach_kernel(backward, levels, *refs),
        (shape((half, 128), BF16), shape((half, 128), BF16)),
        at, factors, own, got, *steps,
        specs=[SMEM, SMEM] + [VMEM] * (2 + len(steps)), name="ssm_reach",
    )
    return mine, lax.ppermute(message, "ctx", swap)


def mix_kernel(
    x_ref, gate_ref, grad_ref, w_ref, r_ref, rel_ref, lcol_ref, lrow_ref, s_ref, mixed_ref, sums_ref
):
    length, heads = lcol_ref.shape
    reads = r_ref[...]
    rel = column(rel_ref[...].astype(F32))
    wide = jnp.concatenate([rel] * (length // 128), axis=1)
    seen = (iota((length, length), 1).astype(F32) >= wide) & (
        iota((length, length), 1) <= iota((length, length), 0)
    )
    scores = jnp.where(seen, dot_nt(reads, w_ref[...]), 0.0)
    squares = jnp.zeros((length, 128), F32)
    inners = jnp.zeros((length, 128), F32)
    for h in range(heads):
        lc = lcol_ref[:, h : h + 1]
        decay = jnp.exp2(jnp.minimum(lc - lrow_ref[h : h + 1, :], 0.0))
        enter = jnp.where(rel < 0, jnp.exp2(jnp.broadcast_to(lc, rel.shape)), 0.0)
        mixed = dot((scores * decay).astype(BF16), x_ref[:, cols(h)]) + enter * dot(
            reads, s_ref[cols(h), :]
        )
        mixed_ref[:, cols(h)] = mixed
        gate = gate_ref[:, cols(h)].astype(F32)
        gated = mixed * (gate / (1.0 + jnp.exp(-gate)))
        squares = squares + gated * gated
        inners = inners + grad_ref[:, cols(h)].astype(F32) * gated
    ones = jnp.ones((8, 128), F32)
    square_row = dot_nt(ones, squares, HIGH)
    inner_row = dot_nt(ones, inners, HIGH)
    sums_ref[...] = jnp.where(iota((8, length), 0) == 0, square_row, inner_row)


def gate_kernel(
    width, sums_ref, mixed_ref, gate_ref, grad_ref, r_ref, rel_ref, lrow_ref,
    mixer_ref, ggrad_ref, dmixed_ref, out_ref,
):
    length = mixed_ref.shape[0]
    heads = lrow_ref.shape[0]
    rows = out_ref.shape[1]
    scale = lax.rsqrt(sums_ref[0:1, :] / width + EPSILON)
    rms = column(scale)
    pull = column(scale * scale * scale * sums_ref[1:2, :] / width)
    reads = r_ref[...].astype(F32).T
    enters = rel_ref[...] < 0
    for h in range(heads):
        mixed = mixed_ref[:, cols(h)]
        gate = gate_ref[:, cols(h)].astype(F32)
        sigma = 1.0 / (1.0 + jnp.exp(-gate))
        swish = gate * sigma
        gated = mixed * swish
        mixer_ref[:, cols(h)] = (gated * rms).astype(BF16)
        dgated = rms * grad_ref[:, cols(h)].astype(F32) - pull * gated
        dmixed = (dgated * swish).astype(BF16)
        dmixed_ref[:, cols(h)] = dmixed
        ggrad_ref[:, cols(h)] = (
            dgated * mixed * sigma * (1.0 + gate * (1.0 - sigma))
        ).astype(BF16)
        enter = jnp.where(enters, jnp.exp2(lrow_ref[h : h + 1, :]), 0.0)
        state = dot((reads * enter).astype(BF16), dmixed).astype(BF16)
        first = h * HEAD_DIM
        for part in range(first // rows, (first + HEAD_DIM - 1) // rows + 1):
            begin = max(first, part * rows)
            end = min(first + HEAD_DIM, (part + 1) * rows)
            out_ref[part, begin - part * rows : end - part * rows, :] = state[
                begin - first : end - first, :
            ]


def inner_kernel(
    dmixed_ref, x_ref, w_ref, r_ref, rel_ref, lcol_ref, lrow_ref, s_ref, gin_ref, read_ref, write_ref
):
    length, heads = lcol_ref.shape
    rel_row = rel_ref[...]
    rel = column(rel_row.astype(F32))
    seen = (iota((length, length), 0) >= rel_row) & (
        iota((length, length), 0) <= iota((length, length), 1)
    )
    scores = jnp.where(seen, dot_nt(w_ref[...], r_ref[...]), 0.0)
    total = jnp.zeros((length, length), F32)
    read = jnp.zeros((length, 128), F32)
    for h in range(heads):
        lc = lcol_ref[:, h : h + 1]
        decay = jnp.exp2(jnp.minimum(lrow_ref[h : h + 1, :] - lc, 0.0))
        dmixed = dmixed_ref[:, cols(h)]
        gin_ref[:, cols(h)] = dot((scores * decay).astype(BF16), dmixed)
        total = total + decay * dot_nt(x_ref[:, cols(h)], dmixed)
        enter = jnp.where(rel < 0, jnp.exp2(jnp.broadcast_to(lc, rel.shape)), 0.0)
        read = read + enter * dot_nt(dmixed, s_ref[cols(h), :])
    total = jnp.where(seen, total, 0.0)
    write_ref[...] = dot(total.astype(BF16), r_ref[...])
    read_ref[...] = read + dot(total.T.astype(BF16), w_ref[...])


def last_kernel(
    at_ref, gin_ref, x_ref, w_ref, rel_ref, lcol_ref, mine_ref, theirs_ref, part_ref, out_ref, write_ref
):
    length, heads = lcol_ref.shape
    half = heads // 2
    rel_last = rel_ref[:, length - 1 :]
    last_doc = iota((length, 128), 0) >= rel_last
    writes = w_ref[...]
    write = part_ref[...]
    for h in range(heads):
        lc = lcol_ref[:, h : h + 1]
        line = jnp.broadcast_to(lc[length - 1 :, :] - lc, (length, 128))
        to_end = jnp.where(last_doc, jnp.exp2(line), 0.0)
        here = cols(h % half)
        mine, theirs = mine_ref[here, :].astype(F32), theirs_ref[here, :].astype(F32)
        back = jnp.where(at_ref[1] == h // half, mine, theirs).astype(BF16)
        out_ref[:, cols(h)] = (gin_ref[:, cols(h)] + to_end * dot(writes, back)).astype(BF16)
        write = write + to_end * dot_nt(x_ref[:, cols(h)], back)
    write_ref[...] = write


def exchange(blocks):
    return lax.all_to_all(blocks, "ctx", 0, 0)


def pack_kernel(marks_ref, q_ref, k_ref, v_ref, g_ref, out_ref):
    parts, per = out_ref.shape[:2]
    length = q_ref.shape[0]
    for part in range(parts):
        for a in range(per):
            here = cols(part * per + a)
            for place, ref in enumerate((q_ref, k_ref, v_ref, g_ref)):
                out_ref[part, a, place * length : (place + 1) * length, :] = ref[:, here]
            out_ref[part, a, 4 * length :, :] = marks_ref[...]


def unpack_kernel(in_ref, *refs):
    out_refs, done = refs[:4], refs[4]
    parts, per = in_ref.shape[:2]
    length = in_ref.shape[2] // 4
    copies = []
    for part in range(parts):
        for a in range(per):
            for place, ref in enumerate(out_refs):
                copies.append(
                    pltpu.make_async_copy(
                        in_ref.at[part, a, pl.ds(place * length, length), :],
                        ref.at[:, pl.ds((part * per + a) * ATT_DIM, ATT_DIM)],
                        done.at[len(copies)],
                    )
                )
    for copy in copies:
        copy.start()
    for copy in copies:
        copy.wait()


def attend_kernel(length, in_ref, out_ref, expo_ref, kt_ref, vt_ref, dk_ref, dv_ref):
    parts = in_ref.shape[0]
    scale = ATT_DIM ** (-0.5)
    rate = scale * LOG2E
    key_in = iota((length, length), 0)
    causal = key_in <= iota((length, length), 1)
    for a in range(in_ref.shape[1]):

        def piece(block, place):
            return in_ref[block, a, place * length : (place + 1) * length, :]

        for i in range(parts):
            kt_ref[i] = flip(piece(i, 1))
            vt_ref[i] = flip(piece(i, 2))
            queries, grads = piece(i, 0), piece(i, 3)
            marks = in_ref[i, a, 4 * length :, :].astype(F32)
            starts = jnp.concatenate(
                [
                    marks[2 * n : 2 * n + 1] * 128.0 + marks[2 * n + 1 : 2 * n + 2]
                    for n in range(length // 128)
                ],
                axis=1,
            ).astype(jnp.int32)
            query_at = i * length + iota((1, length), 1)
            if parts * length > WINDOW:
                starts = jnp.maximum(starts, query_at - (WINDOW - 1))
            top = jnp.full((1, length), MASKED, F32)
            total = jnp.zeros((1, length), F32)
            tops = []
            for j in range(i + 1):
                seen = key_in >= starts - j * length
                if j == i:
                    seen = seen & causal
                raw = jnp.where(seen, dot_nt(piece(j, 1), queries), MASKED)
                new = jnp.maximum(top, jnp.max(raw, axis=0, keepdims=True))
                expo = jnp.exp2((raw - new) * rate)
                expo_ref[j] = expo
                total = total * jnp.exp2((top - new) * rate) + jnp.sum(expo, axis=0, keepdims=True)
                top = new
                tops.append(new)
            out = jnp.zeros((ATT_DIM, length), F32)
            for j in range(i + 1):
                probs = expo_ref[j] * (jnp.exp2((tops[j] - top) * rate) / total)
                expo_ref[j] = probs
                weights = probs.astype(BF16)
                dvalue = dot(weights, grads)
                dv_ref[j] = dvalue if j == i else dv_ref[j] + dvalue
                out = out + dot(vt_ref[j], weights)
            delta = jnp.sum(out * grads.astype(F32).T, axis=0, keepdims=True)
            dquery = jnp.zeros((ATT_DIM, length), F32)
            for j in range(i + 1):
                dprobs = dot_nt(piece(j, 2), grads)
                dscore = (expo_ref[j] * ((dprobs - delta) * scale)).astype(BF16)
                dkey = dot(dscore, queries)
                dk_ref[j] = dkey if j == i else dk_ref[j] + dkey
                dquery = dquery + dot(kt_ref[j], dscore)
            out_ref[i, a, 0:length, :] = out.T.astype(BF16)
            out_ref[i, a, length : 2 * length, :] = dquery.T.astype(BF16)
        for j in range(parts):
            out_ref[j, a, 2 * length : 3 * length, :] = dk_ref[j].astype(BF16)
            out_ref[j, a, 3 * length :, :] = dv_ref[j].astype(BF16)


def shifted(shard, axis, by):
    devices = lax.axis_size(axis)
    pairs = [(i, i + by) for i in range(devices) if 0 <= i + by < devices]
    return lax.ppermute(shard, axis, pairs)


def head_cols(array, head_index):
    return lax.dynamic_slice_in_dim(array, head_index * ATT_DIM, ATT_DIM, 1)


def ring_attention(att_queries, att_keys, att_values, att_grad, doc_start):
    length = att_queries.shape[0]
    shard_index = lax.axis_index("ctx")
    halo_shards = WINDOW // length
    att_count = att_queries.shape[1] // ATT_DIM
    att_width = att_queries.shape[1]
    score_scale = ATT_DIM ** (-0.5)

    def pass_keys(running, unused):
        moved = shifted((running[0], running[1]), "ctx", 1)
        return (moved, moved)

    _, earlier = lax.scan(pass_keys, (att_keys, att_values), None, length=halo_shards)
    key_all = jnp.concatenate(
        [earlier[0][::-1].reshape(halo_shards * length, att_width), att_keys], axis=0
    )
    value_all = jnp.concatenate(
        [earlier[1][::-1].reshape(halo_shards * length, att_width), att_values], axis=0
    )
    spread_rows = (halo_shards + 1) * length
    query_pos = shard_index * length + jnp.arange(length, dtype=jnp.int32)
    key_pos = (shard_index - halo_shards) * length + jnp.arange(spread_rows, dtype=jnp.int32)
    visible = (
        (key_pos[None, :] <= query_pos[:, None])
        & (query_pos[:, None] - key_pos[None, :] < WINDOW)
        & (key_pos[None, :] >= doc_start[:, None])
    )

    def forward_head(head_index, running):
        out_buf, max_buf, total_buf, delta_buf = running
        query_head = head_cols(att_queries, head_index)
        key_head = head_cols(key_all, head_index)
        value_head = head_cols(value_all, head_index)
        score = (
            jnp.einsum("td,sd->ts", query_head, key_head, preferred_element_type=jnp.float32)
            * score_scale
        )
        row_max = jnp.max(jnp.where(visible, score, -jnp.inf), axis=1)
        expo = jnp.where(visible, jnp.exp(score - row_max[:, None]), 0.0)
        row_total = jnp.sum(expo, axis=1)
        weights = (expo / row_total[:, None]).astype(jnp.bfloat16)
        attended = jnp.dot(weights, value_head, preferred_element_type=jnp.float32)
        delta = jnp.sum(head_cols(att_grad, head_index).astype(jnp.float32) * attended, axis=1)
        out_buf = lax.dynamic_update_slice_in_dim(
            out_buf, attended.astype(jnp.bfloat16), head_index * ATT_DIM, 1
        )
        return (
            out_buf,
            max_buf.at[:, head_index].set(row_max),
            total_buf.at[:, head_index].set(row_total),
            delta_buf.at[:, head_index].set(delta),
        )

    stats_zero = jnp.zeros((length, att_count), jnp.float32)
    window_out, row_maxes, row_totals, row_deltas = lax.fori_loop(
        0,
        att_count,
        forward_head,
        (jnp.zeros((length, att_width), jnp.bfloat16), stats_zero, stats_zero, stats_zero),
    )

    def query_terms(head_index):
        query_head = head_cols(att_queries, head_index)
        key_head = head_cols(key_all, head_index)
        value_head = head_cols(value_all, head_index)
        grad_head = head_cols(att_grad, head_index)
        score = (
            jnp.einsum("td,sd->ts", query_head, key_head, preferred_element_type=jnp.float32)
            * score_scale
        )
        probs = (
            jnp.where(visible, jnp.exp(score - row_maxes[:, head_index][:, None]), 0.0)
            / row_totals[:, head_index][:, None]
        )
        weights = probs.astype(jnp.bfloat16)
        dprobs = jnp.einsum("td,sd->ts", grad_head, value_head, preferred_element_type=jnp.float32)
        dscore = (probs * (dprobs - row_deltas[:, head_index][:, None]) * score_scale).astype(
            jnp.bfloat16
        )
        query_part = jnp.dot(dscore, key_head, preferred_element_type=jnp.float32)
        return (query_head, grad_head, weights, dscore, query_part)

    def backward_head(head_index, running):
        query_buf, key_buf, value_buf = running
        query_head, grad_head, weights, dscore, query_part = query_terms(head_index)
        key_part = jnp.einsum("ts,td->sd", dscore, query_head, preferred_element_type=jnp.float32)
        value_part = jnp.einsum("ts,td->sd", weights, grad_head, preferred_element_type=jnp.float32)
        query_buf = lax.dynamic_update_slice_in_dim(query_buf, query_part, head_index * ATT_DIM, 1)
        key_buf = lax.dynamic_update_slice_in_dim(key_buf, key_part, head_index * ATT_DIM, 1)
        value_buf = lax.dynamic_update_slice_in_dim(value_buf, value_part, head_index * ATT_DIM, 1)
        return (query_buf, key_buf, value_buf)

    part_zero = jnp.zeros((spread_rows, att_width), jnp.float32)
    query_sum, key_parts, value_parts = lax.fori_loop(
        0,
        att_count,
        backward_head,
        (jnp.zeros((length, att_width), jnp.float32), part_zero, part_zero),
    )
    key_blocks = key_parts.reshape(halo_shards + 1, length, att_width)
    value_blocks = value_parts.reshape(halo_shards + 1, length, att_width)

    def send_back(running, block_index):
        moved = shifted((running[0], running[1]), "ctx", -1)
        return ((moved[0] + key_blocks[block_index], moved[1] + value_blocks[block_index]), None)

    (key_sum, value_sum), _ = lax.scan(
        send_back, (key_blocks[0], value_blocks[0]), jnp.arange(1, halo_shards + 1, dtype=jnp.int32)
    )
    return (
        window_out,
        query_sum.astype(jnp.bfloat16),
        key_sum.astype(jnp.bfloat16),
        value_sum.astype(jnp.bfloat16),
    )


def body(
    ssm_input,
    gate_input,
    write_map,
    read_map,
    log_decay,
    doc_start,
    ssm_grad,
    att_queries,
    att_keys,
    att_values,
    att_grad,
):
    length, width = ssm_input.shape
    heads = width // HEAD_DIM
    parts = lax.axis_size("ctx")
    rows = width // parts
    full_width = width * lax.axis_size("head")
    work = 2 * length * length * width
    att_width = att_queries.shape[1]
    per = att_width // ATT_DIM // parts
    dealt = att_width // ATT_DIM % parts == 0
    rel = (doc_start - lax.axis_index("ctx") * length).reshape(1, length)

    sent, lcol, lrow = call(
        first_kernel,
        (
            shape((parts, rows + TAIL, 128), BF16),
            shape((length, heads), F32),
            shape((heads, length), F32),
        ),
        log_decay.T, rel, write_map, ssm_input, flops=work // 2, name="ssm_first",
    )
    got = exchange(sent)
    first_got = got
    carried = call(
        lambda in_ref, out_ref: carry_kernel(False, in_ref, in_ref, out_ref),
        shape((parts, rows, 128), BF16), got, name="ssm_carry",
    )
    state = exchange(carried).reshape(width, 128)

    if dealt:
        marks = doc_start.reshape(length // 128, 128)
        marks = jnp.stack([marks // 128, marks % 128], axis=1).reshape(length // 64, 128)
        marks = jnp.pad(marks, ((0, TAIL - length // 64), (0, 0))).astype(BF16)
        packed = call(
            pack_kernel, shape((parts, per, 4 * length + TAIL, 128), BF16),
            marks, att_queries, att_keys, att_values, att_grad, name="att_pack",
        )
        packed, state = lax.optimization_barrier((packed, state))
        att_got = exchange(packed)
    else:
        att_out = ring_attention(att_queries, att_keys, att_values, att_grad, doc_start)

    mixed, sums = call(
        mix_kernel,
        (shape((length, width), F32), shape((8, length), F32)),
        ssm_input, gate_input, ssm_grad, write_map, read_map, rel, lcol, lrow, state,
        flops=work * 3 // 2, name="ssm_mix",
    )
    sums = lax.psum(sums, "head")
    mixer_out, gate_grad, dmixed, sent = call(
        lambda *refs: gate_kernel(full_width, *refs),
        (
            shape((length, width), BF16),
            shape((length, width), BF16),
            shape((length, width), BF16),
            shape((parts, rows, 128), BF16),
        ),
        sums, mixed, gate_input, ssm_grad, read_map, rel, lrow, flops=work // 2, name="ssm_gate",
    )

    place = lax.axis_index("ctx")
    at = jnp.stack([place // 2, place % 2]).astype(jnp.int32)
    if parts <= 8:
        factors = got[:, rows + TAIL - 2 :, :heads].astype(F32)
        factors = factors[:, 0, :] + factors[:, 1, :]
        mine, theirs = carry_by_levels(True, at, factors, sent.reshape(width, 128))
    else:
        got = exchange(sent)
        carried = call(
            lambda *refs: carry_kernel(True, *refs), shape((parts, rows, 128), BF16),
            first_got, got, name="ssm_carry_back",
        )
        back = exchange(carried).reshape(width, 128)
        mine = lax.dynamic_slice_in_dim(back, at[1] * (width // 2), width // 2, 0)
        theirs = lax.dynamic_slice_in_dim(back, (1 - at[1]) * (width // 2), width // 2, 0)
    if dealt:
        att_done = call(
            lambda *refs: attend_kernel(length, *refs),
            shape((parts, per, 4 * length, 128), BF16),
            att_got,
            scratch=[
                pltpu.VMEM((parts, length, length), F32),
                pltpu.VMEM((parts, ATT_DIM, length), BF16),
                pltpu.VMEM((parts, ATT_DIM, length), BF16),
                pltpu.VMEM((parts, length, ATT_DIM), F32),
                pltpu.VMEM((parts, length, ATT_DIM), F32),
            ],
            flops=6 * per * (parts * length) ** 2 * ATT_DIM, name="att_attend",
        )
        att_out = call(
            unpack_kernel, (shape((length, att_width), BF16),) * 4, exchange(att_done),
            specs=[WHERE], out_spec=WHERE,
            scratch=[pltpu.SemaphoreType.DMA((4 * per * parts,))], name="att_unpack",
        )

    gin, read_part, write_part = call(
        inner_kernel,
        (shape((length, width), F32), shape((length, 128), F32), shape((length, 128), F32)),
        dmixed, ssm_input, write_map, read_map, rel, lcol, lrow, state,
        flops=work * 5 // 2, name="ssm_inner",
    )
    input_grad, write_part = call(
        last_kernel,
        (shape((length, width), BF16), shape((length, 128), F32)),
        at, gin, ssm_input, write_map, rel, lcol, mine, theirs, write_part,
        specs=[SMEM] + [VMEM] * 8, flops=work, name="ssm_last",
    )
    write_sum, read_sum = lax.psum((write_part, read_part), "head")
    window_out, query_grad, key_grad, value_grad = att_out
    return (
        mixer_out,
        window_out,
        input_grad,
        gate_grad,
        write_sum.astype(BF16),
        read_sum.astype(BF16),
        query_grad,
        key_grad,
        value_grad,
    )


def solution(mesh):
    in_specs = (
        P("ctx", "head"),
        P("ctx", "head"),
        P("ctx", None),
        P("ctx", None),
        P("ctx", "head"),
        P("ctx"),
        P("ctx", "head"),
        P("ctx", "head"),
        P("ctx", "head"),
        P("ctx", "head"),
        P("ctx", "head"),
    )
    out_specs = (
        P("ctx", "head"),
        P("ctx", "head"),
        P("ctx", "head"),
        P("ctx", "head"),
        P("ctx", None),
        P("ctx", None),
        P("ctx", "head"),
        P("ctx", "head"),
        P("ctx", "head"),
    )
    return jax.shard_map(body, mesh=mesh, in_specs=in_specs, out_specs=out_specs, check_vma=False)
```

```python
import jax
import jax.numpy as jnp
from jax import lax
from jax.experimental import pallas as pl
from jax.experimental.pallas import tpu as pltpu
from jax.sharding import PartitionSpec as P

HEAD_DIM = 128
ATT_DIM = 128
WINDOW = 4096
EPSILON = 1e-05
LOG2E = 1.4426950408889634
TAIL = 16
MASKED = -1e30
HIGH = lax.Precision.HIGHEST
F32 = jnp.float32
BF16 = jnp.bfloat16
VMEM_BYTES = 56 * 1024 * 1024


VMEM = pl.BlockSpec(memory_space=pltpu.VMEM)
SMEM = pl.BlockSpec(memory_space=pltpu.SMEM)
SMALL = 16 * 1024 * 1024


def call(kernel, out_shape, *operands, specs=None, scratch=(), flops=0, vmem=VMEM_BYTES, name=None):
    moved = sum(a.size * a.dtype.itemsize for a in jax.tree.leaves((operands, out_shape)))
    return pl.pallas_call(
        kernel,
        out_shape=out_shape,
        in_specs=specs or [VMEM] * len(operands),
        out_specs=jax.tree.map(lambda _: VMEM, out_shape),
        scratch_shapes=scratch,
        compiler_params=pltpu.CompilerParams(vmem_limit_bytes=vmem),
        cost_estimate=pl.CostEstimate(flops=flops, bytes_accessed=moved, transcendentals=0),
        name=name,
    )(*operands)


def shape(dims, dtype):
    return jax.ShapeDtypeStruct(dims, dtype)


def dot(a, b):
    return jnp.dot(a, b, preferred_element_type=F32)


def dot_nt(a, b, precision=None):
    return lax.dot_general(
        a, b, (((1,), (1,)), ((), ())), preferred_element_type=F32, precision=precision
    )


def iota(dims, axis):
    return lax.broadcasted_iota(jnp.int32, dims, axis)


def flip(a):
    return a.astype(F32).T.astype(BF16)


def column(row):
    return jnp.broadcast_to(row, (128, row.shape[1])).T


def cols(h):
    return slice(h * HEAD_DIM, (h + 1) * HEAD_DIM)


def put_state(x, h, heads, state, mine_ref, other_ref):
    half = heads // 2

    @pl.when(x == h // half)
    def _():
        mine_ref[cols(h % half), :] = state

    @pl.when(x != h // half)
    def _():
        other_ref[cols(h % half), :] = state


def put_tails(x, factors, mine_ref, other_ref):
    half = len(factors) // 2
    row = iota((TAIL, 128), 0)
    tails = []
    for part in range(2):
        tail = jnp.zeros((TAIL, 128), F32)
        for k in range(half):
            factor = factors[part * half + k]
            high = factor.astype(BF16).astype(F32)
            tail = jnp.where(row == 2 * k, high, jnp.where(row == 2 * k + 1, factor - high, tail))
        tails.append(tail)
    mine_ref[half * HEAD_DIM :, :] = jnp.where(x == 0, tails[0], tails[1]).astype(BF16)
    other_ref[half * HEAD_DIM :, :] = jnp.where(x == 0, tails[1], tails[0]).astype(BF16)


def factor_of(tail, k):
    return tail[2 * k : 2 * k + 1, :] + tail[2 * k + 1 : 2 * k + 2, :]


def first_kernel(x_ref, ld_ref, rel_ref, w_ref, in_ref, mine_ref, other_ref, lcol_ref, lrow_ref):
    heads, length = ld_ref.shape
    x = x_ref[0]
    rates = ld_ref[...] * LOG2E
    lower = jnp.where(iota((length, length), 0) >= iota((length, length), 1), 1.0, 0.0)
    upper = jnp.where(iota((length, length), 0) <= iota((length, length), 1), 1.0, 0.0)
    lcol_ref[...] = dot_nt(lower, rates, HIGH)
    lrow = jnp.dot(rates, upper, preferred_element_type=F32, precision=HIGH)
    lrow_ref[...] = lrow
    rel_last = rel_ref[:, length - 1 :]
    last_doc = iota((1, length), 1) >= rel_last
    writes = w_ref[...].astype(F32).T
    factors = []
    for h in range(heads):
        line = lrow[h : h + 1, :]
        total = line[:, length - 1 :]
        to_end = jnp.where(last_doc, jnp.exp2(total - line), 0.0)
        state = dot((writes * to_end).astype(BF16), in_ref[:, cols(h)]).astype(BF16)
        put_state(x, h, heads, state, mine_ref, other_ref)
        factors.append(jnp.where(rel_last < 0, jnp.exp2(total), 0.0))
    put_tails(x, factors, mine_ref, other_ref)


def level_kernel(backward, x_ref, mine_ref, got_ref, out_ref):
    half = out_ref.shape[0] - TAIL
    is_far = x_ref[0] == (0 if backward else 1)
    mine_tail, got_tail = mine_ref[half:, :].astype(F32), got_ref[half:, :].astype(F32)
    row = iota((TAIL, 128), 0)
    tail = jnp.zeros((TAIL, 128), F32)
    for k in range(half // HEAD_DIM):
        mine, got = mine_ref[cols(k), :].astype(F32), got_ref[cols(k), :].astype(F32)
        mine_factor, got_factor = factor_of(mine_tail, k), factor_of(got_tail, k)
        out_ref[cols(k), :] = jnp.where(
            is_far, mine + mine_factor * got, got + got_factor * mine
        ).astype(BF16)
        factor = mine_factor * got_factor
        high = factor.astype(BF16).astype(F32)
        tail = jnp.where(row == 2 * k, high, jnp.where(row == 2 * k + 1, factor - high, tail))
    out_ref[half:, :] = tail.astype(BF16)


def reach_kernel(backward, x_ref, mine_ref, got_ref, *refs):
    steps, (keep_ref, message_ref) = refs[:-2], refs[-2:]
    half = keep_ref.shape[0]
    is_far = x_ref[0] == (0 if backward else 1)
    mine_tail, got_tail = mine_ref[half:, :].astype(F32), got_ref[half:, :].astype(F32)
    tails = [step[half:, :].astype(F32) for step in steps]
    for k in range(half // HEAD_DIM):
        entering = steps[0][cols(k), :].astype(F32)
        factor = 1.0
        for n in range(1, len(steps)):
            factor = factor * factor_of(tails[n - 1], k)
            entering = entering + factor * steps[n][cols(k), :].astype(F32)
        near = jnp.where(is_far, got_ref[cols(k), :].astype(F32), mine_ref[cols(k), :].astype(F32))
        near_factor = jnp.where(is_far, factor_of(got_tail, k), factor_of(mine_tail, k))
        passed = near + near_factor * entering
        keep_ref[cols(k), :] = jnp.where(is_far, passed, entering).astype(BF16)
        message_ref[cols(k), :] = jnp.where(is_far, entering, passed).astype(BF16)


def carry_start(other):
    swap = [(i, i ^ 1) for i in range(lax.axis_size("ctx"))]
    return lax.ppermute(other, "ctx", swap)


def carry_rest(backward, x, mine, got):
    parts = lax.axis_size("ctx")
    half = mine.shape[0] - TAIL
    level = call(
        lambda *refs: level_kernel(backward, *refs), shape(mine.shape, BF16),
        x, mine, got, specs=[SMEM, VMEM, VMEM], vmem=SMALL, name="ssm_level",
    )
    steps = []
    for n in range(1, parts // 2):
        by = -2 * n if backward else 2 * n
        pairs = [(i, i + by) for i in range(parts) if 0 <= i + by < parts]
        steps.append(lax.ppermute(level, "ctx", pairs))
    keep, message = call(
        lambda *refs: reach_kernel(backward, *refs),
        (shape((half, 128), BF16), shape((half, 128), BF16)),
        x, mine, got, *steps,
        specs=[SMEM] + [VMEM] * (2 + len(steps)), vmem=SMALL, name="ssm_reach",
    )
    return keep, carry_start(message)


def state_of(x, h, heads, keep_ref, theirs_ref):
    half = heads // 2
    here = cols(h % half)
    keep, theirs = keep_ref[here, :].astype(F32), theirs_ref[here, :].astype(F32)
    return jnp.where(x == h // half, keep, theirs).astype(BF16)


def mix_kernel(
    at_ref, x_ref, gate_ref, grad_ref, w_ref, r_ref, rel_ref, lcol_ref, lrow_ref, keep_ref, theirs_ref,
    mixed_ref, sums_ref, state_ref,
):
    length, heads = lcol_ref.shape
    x = at_ref[0]
    reads = r_ref[...]
    rel = column(rel_ref[...].astype(F32))
    wide = jnp.concatenate([rel] * (length // 128), axis=1)
    seen = (iota((length, length), 1).astype(F32) >= wide) & (
        iota((length, length), 1) <= iota((length, length), 0)
    )
    scores = jnp.where(seen, dot_nt(reads, w_ref[...]), 0.0)
    squares = jnp.zeros((length, 128), F32)
    inners = jnp.zeros((length, 128), F32)
    for h in range(heads):
        lc = lcol_ref[:, h : h + 1]
        decay = jnp.exp2(jnp.minimum(lc - lrow_ref[h : h + 1, :], 0.0))
        enter = jnp.where(rel < 0, jnp.exp2(jnp.broadcast_to(lc, rel.shape)), 0.0)
        state = state_of(x, h, heads, keep_ref, theirs_ref)
        state_ref[cols(h), :] = state
        mixed = dot((scores * decay).astype(BF16), x_ref[:, cols(h)]) + enter * dot(reads, state)
        mixed_ref[:, cols(h)] = mixed
        gate = gate_ref[:, cols(h)].astype(F32)
        gated = mixed * (gate / (1.0 + jnp.exp(-gate)))
        squares = squares + gated * gated
        inners = inners + grad_ref[:, cols(h)].astype(F32) * gated
    ones = jnp.ones((8, 128), F32)
    square_row = dot_nt(ones, squares, HIGH)
    inner_row = dot_nt(ones, inners, HIGH)
    sums_ref[...] = jnp.where(iota((8, length), 0) == 0, square_row, inner_row)


def gate_kernel(
    width, x_ref, sums_ref, mixed_ref, gate_ref, grad_ref, r_ref, rel_ref, lrow_ref,
    mixer_ref, ggrad_ref, dmixed_ref, mine_ref, other_ref,
):
    length = mixed_ref.shape[0]
    heads = lrow_ref.shape[0]
    x = x_ref[0]
    rel_last = rel_ref[:, length - 1 :]
    factors = []
    scale = lax.rsqrt(sums_ref[0:1, :] / width + EPSILON)
    rms = column(scale)
    pull = column(scale * scale * scale * sums_ref[1:2, :] / width)
    reads = r_ref[...].astype(F32).T
    enters = rel_ref[...] < 0
    for h in range(heads):
        mixed = mixed_ref[:, cols(h)]
        gate = gate_ref[:, cols(h)].astype(F32)
        sigma = 1.0 / (1.0 + jnp.exp(-gate))
        swish = gate * sigma
        gated = mixed * swish
        mixer_ref[:, cols(h)] = (gated * rms).astype(BF16)
        dgated = rms * grad_ref[:, cols(h)].astype(F32) - pull * gated
        dmixed = (dgated * swish).astype(BF16)
        dmixed_ref[:, cols(h)] = dmixed
        ggrad_ref[:, cols(h)] = (
            dgated * mixed * sigma * (1.0 + gate * (1.0 - sigma))
        ).astype(BF16)
        enter = jnp.where(enters, jnp.exp2(lrow_ref[h : h + 1, :]), 0.0)
        state = dot((reads * enter).astype(BF16), dmixed).astype(BF16)
        put_state(x, h, heads, state, mine_ref, other_ref)
        total = lrow_ref[h : h + 1, length - 1 :]
        factors.append(jnp.where(rel_last < 0, jnp.exp2(total), 0.0))
    put_tails(x, factors, mine_ref, other_ref)


def inner_kernel(
    dmixed_ref, x_ref, w_ref, r_ref, rel_ref, lcol_ref, lrow_ref, s_ref, gin_ref, read_ref, write_ref
):
    length, heads = lcol_ref.shape
    rel_row = rel_ref[...]
    rel = column(rel_row.astype(F32))
    seen = (iota((length, length), 0) >= rel_row) & (
        iota((length, length), 0) <= iota((length, length), 1)
    )
    scores = jnp.where(seen, dot_nt(w_ref[...], r_ref[...]), 0.0)
    total = jnp.zeros((length, length), F32)
    read = jnp.zeros((length, 128), F32)
    for h in range(heads):
        lc = lcol_ref[:, h : h + 1]
        decay = jnp.exp2(jnp.minimum(lrow_ref[h : h + 1, :] - lc, 0.0))
        dmixed = dmixed_ref[:, cols(h)]
        gin_ref[:, cols(h)] = dot((scores * decay).astype(BF16), dmixed)
        total = total + decay * dot_nt(x_ref[:, cols(h)], dmixed)
        enter = jnp.where(rel < 0, jnp.exp2(jnp.broadcast_to(lc, rel.shape)), 0.0)
        read = read + enter * dot_nt(dmixed, s_ref[cols(h), :])
    total = jnp.where(seen, total, 0.0)
    write_ref[...] = dot(total.astype(BF16), r_ref[...])
    read_ref[...] = read + dot(total.T.astype(BF16), w_ref[...])


def last_kernel(
    at_ref, gin_ref, x_ref, w_ref, rel_ref, lcol_ref, keep_ref, theirs_ref, part_ref, out_ref, write_ref
):
    length, heads = lcol_ref.shape
    x = at_ref[0]
    rel_last = rel_ref[:, length - 1 :]
    last_doc = iota((length, 128), 0) >= rel_last
    writes = w_ref[...]
    write = part_ref[...]
    for h in range(heads):
        lc = lcol_ref[:, h : h + 1]
        line = jnp.broadcast_to(lc[length - 1 :, :] - lc, (length, 128))
        to_end = jnp.where(last_doc, jnp.exp2(line), 0.0)
        back = state_of(x, h, heads, keep_ref, theirs_ref)
        out_ref[:, cols(h)] = (gin_ref[:, cols(h)] + to_end * dot(writes, back)).astype(BF16)
        write = write + to_end * dot_nt(x_ref[:, cols(h)], back)
    write_ref[...] = write


def sum_heads(part):
    count = lax.axis_size("head")
    total = part
    for by in range(1, count):
        total = total + lax.ppermute(part, "head", [(i, (i + by) % count) for i in range(count)])
    return total


def exchange(blocks):
    return lax.all_to_all(blocks, "ctx", 0, 0)


def pack_kernel(marks_ref, q_ref, k_ref, v_ref, g_ref, out_ref):
    parts, per = out_ref.shape[:2]
    length = q_ref.shape[0]
    for part in range(parts):
        for a in range(per):
            here = cols(part * per + a)
            for place, ref in enumerate((q_ref, k_ref, v_ref, g_ref)):
                out_ref[part, a, place * length : (place + 1) * length, :] = ref[:, here]
            out_ref[part, a, 4 * length :, :] = marks_ref[...]


def unpack_kernel(in_ref, *out_refs):
    parts, per = in_ref.shape[:2]
    length = in_ref.shape[2] // 4
    for part in range(parts):
        for a in range(per):
            here = cols(part * per + a)
            for place, ref in enumerate(out_refs):
                ref[:, here] = in_ref[part, a, place * length : (place + 1) * length, :]


def attend_kernel(length, in_ref, out_ref, expo_ref, kt_ref, vt_ref, dk_ref, dv_ref):
    parts = in_ref.shape[0]
    scale = ATT_DIM ** (-0.5)
    rate = scale * LOG2E
    key_in = iota((length, length), 0)
    causal = key_in <= iota((length, length), 1)
    for a in range(in_ref.shape[1]):

        def piece(block, place):
            return in_ref[block, a, place * length : (place + 1) * length, :]

        for i in range(parts):
            kt_ref[i] = flip(piece(i, 1))
            vt_ref[i] = flip(piece(i, 2))
            queries, grads = piece(i, 0), piece(i, 3)
            marks = in_ref[i, a, 4 * length :, :].astype(F32)
            starts = jnp.concatenate(
                [
                    marks[2 * n : 2 * n + 1] * 128.0 + marks[2 * n + 1 : 2 * n + 2]
                    for n in range(length // 128)
                ],
                axis=1,
            ).astype(jnp.int32)
            query_at = i * length + iota((1, length), 1)
            if parts * length > WINDOW:
                starts = jnp.maximum(starts, query_at - (WINDOW - 1))
            top = jnp.full((1, length), MASKED, F32)
            total = jnp.zeros((1, length), F32)
            tops = []
            for j in range(i + 1):
                seen = key_in >= starts - j * length
                if j == i:
                    seen = seen & causal
                raw = jnp.where(seen, dot_nt(piece(j, 1), queries), MASKED)
                new = jnp.maximum(top, jnp.max(raw, axis=0, keepdims=True))
                expo = jnp.exp2((raw - new) * rate)
                expo_ref[j] = expo
                total = total * jnp.exp2((top - new) * rate) + jnp.sum(expo, axis=0, keepdims=True)
                top = new
                tops.append(new)
            out = jnp.zeros((ATT_DIM, length), F32)
            for j in range(i + 1):
                probs = expo_ref[j] * (jnp.exp2((tops[j] - top) * rate) / total)
                expo_ref[j] = probs
                weights = probs.astype(BF16)
                dvalue = dot(weights, grads)
                dv_ref[j] = dvalue if j == i else dv_ref[j] + dvalue
                out = out + dot(vt_ref[j], weights)
            delta = jnp.sum(out * grads.astype(F32).T, axis=0, keepdims=True)
            dquery = jnp.zeros((ATT_DIM, length), F32)
            for j in range(i + 1):
                dprobs = dot_nt(piece(j, 2), grads)
                dscore = (expo_ref[j] * ((dprobs - delta) * scale)).astype(BF16)
                dkey = dot(dscore, queries)
                dk_ref[j] = dkey if j == i else dk_ref[j] + dkey
                dquery = dquery + dot(kt_ref[j], dscore)
            out_ref[i, a, 0:length, :] = out.T.astype(BF16)
            out_ref[i, a, length : 2 * length, :] = dquery.T.astype(BF16)
        for j in range(parts):
            out_ref[j, a, 2 * length : 3 * length, :] = dk_ref[j].astype(BF16)
            out_ref[j, a, 3 * length :, :] = dv_ref[j].astype(BF16)


def shifted(shard, axis, by):
    devices = lax.axis_size(axis)
    pairs = [(i, i + by) for i in range(devices) if 0 <= i + by < devices]
    return lax.ppermute(shard, axis, pairs)


def head_cols(array, head_index):
    return lax.dynamic_slice_in_dim(array, head_index * ATT_DIM, ATT_DIM, 1)


def ring_attention(att_queries, att_keys, att_values, att_grad, doc_start):
    length = att_queries.shape[0]
    shard_index = lax.axis_index("ctx")
    halo_shards = WINDOW // length
    att_count = att_queries.shape[1] // ATT_DIM
    att_width = att_queries.shape[1]
    score_scale = ATT_DIM ** (-0.5)

    def pass_keys(running, unused):
        moved = shifted((running[0], running[1]), "ctx", 1)
        return (moved, moved)

    _, earlier = lax.scan(pass_keys, (att_keys, att_values), None, length=halo_shards)
    key_all = jnp.concatenate(
        [earlier[0][::-1].reshape(halo_shards * length, att_width), att_keys], axis=0
    )
    value_all = jnp.concatenate(
        [earlier[1][::-1].reshape(halo_shards * length, att_width), att_values], axis=0
    )
    spread_rows = (halo_shards + 1) * length
    query_pos = shard_index * length + jnp.arange(length, dtype=jnp.int32)
    key_pos = (shard_index - halo_shards) * length + jnp.arange(spread_rows, dtype=jnp.int32)
    visible = (
        (key_pos[None, :] <= query_pos[:, None])
        & (query_pos[:, None] - key_pos[None, :] < WINDOW)
        & (key_pos[None, :] >= doc_start[:, None])
    )

    def forward_head(head_index, running):
        out_buf, max_buf, total_buf, delta_buf = running
        query_head = head_cols(att_queries, head_index)
        key_head = head_cols(key_all, head_index)
        value_head = head_cols(value_all, head_index)
        score = (
            jnp.einsum("td,sd->ts", query_head, key_head, preferred_element_type=jnp.float32)
            * score_scale
        )
        row_max = jnp.max(jnp.where(visible, score, -jnp.inf), axis=1)
        expo = jnp.where(visible, jnp.exp(score - row_max[:, None]), 0.0)
        row_total = jnp.sum(expo, axis=1)
        weights = (expo / row_total[:, None]).astype(jnp.bfloat16)
        attended = jnp.dot(weights, value_head, preferred_element_type=jnp.float32)
        delta = jnp.sum(head_cols(att_grad, head_index).astype(jnp.float32) * attended, axis=1)
        out_buf = lax.dynamic_update_slice_in_dim(
            out_buf, attended.astype(jnp.bfloat16), head_index * ATT_DIM, 1
        )
        return (
            out_buf,
            max_buf.at[:, head_index].set(row_max),
            total_buf.at[:, head_index].set(row_total),
            delta_buf.at[:, head_index].set(delta),
        )

    stats_zero = jnp.zeros((length, att_count), jnp.float32)
    window_out, row_maxes, row_totals, row_deltas = lax.fori_loop(
        0,
        att_count,
        forward_head,
        (jnp.zeros((length, att_width), jnp.bfloat16), stats_zero, stats_zero, stats_zero),
    )

    def query_terms(head_index):
        query_head = head_cols(att_queries, head_index)
        key_head = head_cols(key_all, head_index)
        value_head = head_cols(value_all, head_index)
        grad_head = head_cols(att_grad, head_index)
        score = (
            jnp.einsum("td,sd->ts", query_head, key_head, preferred_element_type=jnp.float32)
            * score_scale
        )
        probs = (
            jnp.where(visible, jnp.exp(score - row_maxes[:, head_index][:, None]), 0.0)
            / row_totals[:, head_index][:, None]
        )
        weights = probs.astype(jnp.bfloat16)
        dprobs = jnp.einsum("td,sd->ts", grad_head, value_head, preferred_element_type=jnp.float32)
        dscore = (probs * (dprobs - row_deltas[:, head_index][:, None]) * score_scale).astype(
            jnp.bfloat16
        )
        query_part = jnp.dot(dscore, key_head, preferred_element_type=jnp.float32)
        return (query_head, grad_head, weights, dscore, query_part)

    def backward_head(head_index, running):
        query_buf, key_buf, value_buf = running
        query_head, grad_head, weights, dscore, query_part = query_terms(head_index)
        key_part = jnp.einsum("ts,td->sd", dscore, query_head, preferred_element_type=jnp.float32)
        value_part = jnp.einsum("ts,td->sd", weights, grad_head, preferred_element_type=jnp.float32)
        query_buf = lax.dynamic_update_slice_in_dim(query_buf, query_part, head_index * ATT_DIM, 1)
        key_buf = lax.dynamic_update_slice_in_dim(key_buf, key_part, head_index * ATT_DIM, 1)
        value_buf = lax.dynamic_update_slice_in_dim(value_buf, value_part, head_index * ATT_DIM, 1)
        return (query_buf, key_buf, value_buf)

    part_zero = jnp.zeros((spread_rows, att_width), jnp.float32)
    query_sum, key_parts, value_parts = lax.fori_loop(
        0,
        att_count,
        backward_head,
        (jnp.zeros((length, att_width), jnp.float32), part_zero, part_zero),
    )
    key_blocks = key_parts.reshape(halo_shards + 1, length, att_width)
    value_blocks = value_parts.reshape(halo_shards + 1, length, att_width)

    def send_back(running, block_index):
        moved = shifted((running[0], running[1]), "ctx", -1)
        return ((moved[0] + key_blocks[block_index], moved[1] + value_blocks[block_index]), None)

    (key_sum, value_sum), _ = lax.scan(
        send_back, (key_blocks[0], value_blocks[0]), jnp.arange(1, halo_shards + 1, dtype=jnp.int32)
    )
    return (
        window_out,
        query_sum.astype(jnp.bfloat16),
        key_sum.astype(jnp.bfloat16),
        value_sum.astype(jnp.bfloat16),
    )


def body(
    ssm_input,
    gate_input,
    write_map,
    read_map,
    log_decay,
    doc_start,
    ssm_grad,
    att_queries,
    att_keys,
    att_values,
    att_grad,
):
    length, width = ssm_input.shape
    heads = width // HEAD_DIM
    parts = lax.axis_size("ctx")
    full_width = width * lax.axis_size("head")
    att_width = att_queries.shape[1]
    per = att_width // ATT_DIM // parts
    dealt = att_width // ATT_DIM % parts == 0
    place = lax.axis_index("ctx")
    rel = (doc_start - place * length).reshape(1, length)
    x = (place % 2).reshape(1)
    half = shape((width // 2 + TAIL, 128), BF16)

    mine, other, lcol, lrow = call(
        first_kernel,
        (half, half, shape((length, heads), F32), shape((heads, length), F32)),
        x, log_decay.T, rel, write_map, ssm_input, specs=[SMEM] + [VMEM] * 4, name="ssm_first",
    )
    if dealt:
        marks = doc_start.reshape(length // 128, 128)
        marks = jnp.stack([marks // 128, marks % 128], axis=1).reshape(length // 64, 128)
        marks = jnp.pad(marks, ((0, TAIL - length // 64), (0, 0))).astype(BF16)
        marks, other = lax.optimization_barrier((marks, other))
        packed = call(
            pack_kernel, shape((parts, per, 4 * length + TAIL, 128), BF16),
            marks, att_queries, att_keys, att_values, att_grad, vmem=SMALL, name="att_pack",
        )
        att_got = exchange(packed)
        got = carry_start(other)
        got, packed = lax.optimization_barrier((got, packed))
    else:
        att_out = ring_attention(att_queries, att_keys, att_values, att_grad, doc_start)
        got = carry_start(other)
    keep, theirs = carry_rest(False, x, mine, got)
    mixed, sums, state = call(
        mix_kernel,
        (shape((length, width), F32), shape((8, length), F32), shape((width, 128), BF16)),
        x, ssm_input, gate_input, ssm_grad, write_map, read_map, rel, lcol, lrow, keep, theirs,
        specs=[SMEM] + [VMEM] * 10, name="ssm_mix",
    )
    sums = lax.psum(sums, "head")
    mixer_out, gate_grad, dmixed, mine, other = call(
        lambda *refs: gate_kernel(full_width, *refs),
        (
            shape((length, width), BF16),
            shape((length, width), BF16),
            shape((length, width), BF16),
            half,
            half,
        ),
        x, sums, mixed, gate_input, ssm_grad, read_map, rel, lrow,
        specs=[SMEM] + [VMEM] * 7, name="ssm_gate",
    )
    got = carry_start(other)
    if dealt:
        att_got, other = lax.optimization_barrier((att_got, other))
        att_done = call(
            lambda *refs: attend_kernel(length, *refs),
            shape((parts, per, 4 * length, 128), BF16),
            att_got,
            scratch=[
                pltpu.VMEM((parts, length, length), F32),
                pltpu.VMEM((parts, ATT_DIM, length), BF16),
                pltpu.VMEM((parts, ATT_DIM, length), BF16),
                pltpu.VMEM((parts, length, ATT_DIM), F32),
                pltpu.VMEM((parts, length, ATT_DIM), F32),
            ],
            flops=6 * per * (parts * length) ** 2 * ATT_DIM, name="att_attend",
        )
        att_out = call(
            unpack_kernel, (shape((length, att_width), BF16),) * 4, exchange(att_done),
            vmem=SMALL, name="att_unpack",
        )
        got, att_done = lax.optimization_barrier((got, att_done))
    keep, theirs = carry_rest(True, x, mine, got)

    gin, read_part, write_part = call(
        inner_kernel,
        (shape((length, width), F32), shape((length, 128), F32), shape((length, 128), F32)),
        dmixed, ssm_input, write_map, read_map, rel, lcol, lrow, state, name="ssm_inner",
    )
    input_grad, write_part = call(
        last_kernel,
        (shape((length, width), BF16), shape((length, 128), F32)),
        x, gin, ssm_input, write_map, rel, lcol, keep, theirs, write_part,
        specs=[SMEM] + [VMEM] * 8, name="ssm_last",
    )
    read_sum = sum_heads(read_part)
    write_sum = sum_heads(write_part)
    window_out, query_grad, key_grad, value_grad = att_out
    return (
        mixer_out,
        window_out,
        input_grad,
        gate_grad,
        write_sum.astype(BF16),
        read_sum.astype(BF16),
        query_grad,
        key_grad,
        value_grad,
    )


def solution(mesh):
    in_specs = (
        P("ctx", "head"),
        P("ctx", "head"),
        P("ctx", None),
        P("ctx", None),
        P("ctx", "head"),
        P("ctx"),
        P("ctx", "head"),
        P("ctx", "head"),
        P("ctx", "head"),
        P("ctx", "head"),
        P("ctx", "head"),
    )
    out_specs = (
        P("ctx", "head"),
        P("ctx", "head"),
        P("ctx", "head"),
        P("ctx", "head"),
        P("ctx", None),
        P("ctx", None),
        P("ctx", "head"),
        P("ctx", "head"),
        P("ctx", "head"),
    )
    return jax.shard_map(body, mesh=mesh, in_specs=in_specs, out_specs=out_specs, check_vma=False)
```

```python
import jax
import jax.numpy as jnp
from jax import lax
from jax.experimental import pallas as pl
from jax.experimental.pallas import tpu as pltpu
from jax.sharding import PartitionSpec as P

HEAD_DIM = 128
ATT_DIM = 128
WINDOW = 4096
EPSILON = 1e-05
LOG2E = 1.4426950408889634
TAIL = 16
MASKED = -1e30
HIGH = lax.Precision.HIGHEST
F32 = jnp.float32
BF16 = jnp.bfloat16
VMEM_BYTES = 56 * 1024 * 1024


VMEM = pl.BlockSpec(memory_space=pltpu.VMEM)
SMEM = pl.BlockSpec(memory_space=pltpu.SMEM)
SMALL = 16 * 1024 * 1024


def call(kernel, out_shape, *operands, specs=None, scratch=(), flops=0, vmem=VMEM_BYTES, name=None):
    moved = sum(a.size * a.dtype.itemsize for a in jax.tree.leaves((operands, out_shape)))
    return pl.pallas_call(
        kernel,
        out_shape=out_shape,
        in_specs=specs or [VMEM] * len(operands),
        out_specs=jax.tree.map(lambda _: VMEM, out_shape),
        scratch_shapes=scratch,
        compiler_params=pltpu.CompilerParams(vmem_limit_bytes=vmem),
        cost_estimate=pl.CostEstimate(flops=flops, bytes_accessed=moved, transcendentals=0),
        name=name,
    )(*operands)


def shape(dims, dtype):
    return jax.ShapeDtypeStruct(dims, dtype)


def dot(a, b):
    return jnp.dot(a, b, preferred_element_type=F32)


def dot_nt(a, b, precision=None):
    return lax.dot_general(
        a, b, (((1,), (1,)), ((), ())), preferred_element_type=F32, precision=precision
    )


def iota(dims, axis):
    return lax.broadcasted_iota(jnp.int32, dims, axis)


def flip(a):
    return a.astype(F32).T.astype(BF16)


def column(row):
    return jnp.broadcast_to(row, (128, row.shape[1])).T


def cols(h):
    return slice(h * HEAD_DIM, (h + 1) * HEAD_DIM)


def first_kernel(ld_ref, rel_ref, w_ref, x_ref, out_ref, lcol_ref, lrow_ref):
    heads, length = ld_ref.shape
    parts, rows = out_ref.shape[0], out_ref.shape[1] - TAIL
    rates = ld_ref[...] * LOG2E
    lower = jnp.where(iota((length, length), 0) >= iota((length, length), 1), 1.0, 0.0)
    upper = jnp.where(iota((length, length), 0) <= iota((length, length), 1), 1.0, 0.0)
    lcol_ref[...] = dot_nt(lower, rates, HIGH)
    lrow = jnp.dot(rates, upper, preferred_element_type=F32, precision=HIGH)
    lrow_ref[...] = lrow
    rel_last = rel_ref[:, length - 1 :]
    last_doc = iota((1, length), 1) >= rel_last
    keeps = rel_last < 0
    writes = w_ref[...].astype(F32).T
    tail_row = iota((TAIL, 128), 0)
    for h in range(heads):
        line = lrow[h : h + 1, :]
        total = line[:, length - 1 :]
        to_end = jnp.where(last_doc, jnp.exp2(total - line), 0.0)
        state = dot((writes * to_end).astype(BF16), x_ref[:, cols(h)]).astype(BF16)
        factor = jnp.where(keeps, jnp.exp2(total), 0.0)
        high = factor.astype(BF16).astype(F32)
        low = factor - high
        first = h * HEAD_DIM
        for part in range(first // rows, (first + HEAD_DIM - 1) // rows + 1):
            begin = max(first, part * rows)
            end = min(first + HEAD_DIM, (part + 1) * rows)
            out_ref[part, begin - part * rows : end - part * rows, :] = state[
                begin - first : end - first, :
            ]
            place = 2 * (begin - part * rows) // HEAD_DIM
            tail = jnp.where(tail_row == place, high, jnp.where(tail_row == place + 1, low, 0.0))
            if place:
                tail = tail + out_ref[part, rows:, :].astype(F32)
            out_ref[part, rows:, :] = tail.astype(BF16)


def carry_kernel(backward, tail_ref, in_ref, out_ref):
    parts, rows = out_ref.shape[0], out_ref.shape[1]
    step = min(rows, HEAD_DIM)
    for k in range(rows // step):
        here = slice(k * step, (k + 1) * step)
        state = jnp.zeros((step, 128), F32)
        for c in range(parts)[:: -1 if backward else 1]:
            out_ref[c, here, :] = state.astype(BF16)
            tail = tail_ref[c, rows:, :].astype(F32)
            factor = tail[2 * k : 2 * k + 1, :] + tail[2 * k + 1 : 2 * k + 2, :]
            state = factor * state + in_ref[c, here, :].astype(F32)


def mix_kernel(
    x_ref, gate_ref, grad_ref, w_ref, r_ref, rel_ref, lcol_ref, lrow_ref, s_ref, mixed_ref, sums_ref
):
    length, heads = lcol_ref.shape
    reads = r_ref[...]
    rel = column(rel_ref[...].astype(F32))
    wide = jnp.concatenate([rel] * (length // 128), axis=1)
    seen = (iota((length, length), 1).astype(F32) >= wide) & (
        iota((length, length), 1) <= iota((length, length), 0)
    )
    scores = jnp.where(seen, dot_nt(reads, w_ref[...]), 0.0)
    squares = jnp.zeros((length, 128), F32)
    inners = jnp.zeros((length, 128), F32)
    for h in range(heads):
        lc = lcol_ref[:, h : h + 1]
        decay = jnp.exp2(jnp.minimum(lc - lrow_ref[h : h + 1, :], 0.0))
        enter = jnp.where(rel < 0, jnp.exp2(jnp.broadcast_to(lc, rel.shape)), 0.0)
        mixed = dot((scores * decay).astype(BF16), x_ref[:, cols(h)]) + enter * dot(
            reads, s_ref[cols(h), :]
        )
        mixed_ref[:, cols(h)] = mixed
        gate = gate_ref[:, cols(h)].astype(F32)
        gated = mixed * (gate / (1.0 + jnp.exp(-gate)))
        squares = squares + gated * gated
        inners = inners + grad_ref[:, cols(h)].astype(F32) * gated
    ones = jnp.ones((8, 128), F32)
    square_row = dot_nt(ones, squares, HIGH)
    inner_row = dot_nt(ones, inners, HIGH)
    sums_ref[...] = jnp.where(iota((8, length), 0) == 0, square_row, inner_row)


def gate_kernel(
    width, sums_ref, mixed_ref, gate_ref, grad_ref, r_ref, rel_ref, lrow_ref,
    mixer_ref, ggrad_ref, dmixed_ref, out_ref,
):
    length = mixed_ref.shape[0]
    heads = lrow_ref.shape[0]
    rows = out_ref.shape[1]
    scale = lax.rsqrt(sums_ref[0:1, :] / width + EPSILON)
    rms = column(scale)
    pull = column(scale * scale * scale * sums_ref[1:2, :] / width)
    reads = r_ref[...].astype(F32).T
    enters = rel_ref[...] < 0
    for h in range(heads):
        mixed = mixed_ref[:, cols(h)]
        gate = gate_ref[:, cols(h)].astype(F32)
        sigma = 1.0 / (1.0 + jnp.exp(-gate))
        swish = gate * sigma
        gated = mixed * swish
        mixer_ref[:, cols(h)] = (gated * rms).astype(BF16)
        dgated = rms * grad_ref[:, cols(h)].astype(F32) - pull * gated
        dmixed = (dgated * swish).astype(BF16)
        dmixed_ref[:, cols(h)] = dmixed
        ggrad_ref[:, cols(h)] = (
            dgated * mixed * sigma * (1.0 + gate * (1.0 - sigma))
        ).astype(BF16)
        enter = jnp.where(enters, jnp.exp2(lrow_ref[h : h + 1, :]), 0.0)
        state = dot((reads * enter).astype(BF16), dmixed).astype(BF16)
        first = h * HEAD_DIM
        for part in range(first // rows, (first + HEAD_DIM - 1) // rows + 1):
            begin = max(first, part * rows)
            end = min(first + HEAD_DIM, (part + 1) * rows)
            out_ref[part, begin - part * rows : end - part * rows, :] = state[
                begin - first : end - first, :
            ]


def inner_kernel(
    dmixed_ref, x_ref, w_ref, r_ref, rel_ref, lcol_ref, lrow_ref, s_ref, gin_ref, read_ref, write_ref
):
    length, heads = lcol_ref.shape
    rel_row = rel_ref[...]
    rel = column(rel_row.astype(F32))
    seen = (iota((length, length), 0) >= rel_row) & (
        iota((length, length), 0) <= iota((length, length), 1)
    )
    scores = jnp.where(seen, dot_nt(w_ref[...], r_ref[...]), 0.0)
    total = jnp.zeros((length, length), F32)
    read = jnp.zeros((length, 128), F32)
    for h in range(heads):
        lc = lcol_ref[:, h : h + 1]
        decay = jnp.exp2(jnp.minimum(lrow_ref[h : h + 1, :] - lc, 0.0))
        dmixed = dmixed_ref[:, cols(h)]
        gin_ref[:, cols(h)] = dot((scores * decay).astype(BF16), dmixed)
        total = total + decay * dot_nt(x_ref[:, cols(h)], dmixed)
        enter = jnp.where(rel < 0, jnp.exp2(jnp.broadcast_to(lc, rel.shape)), 0.0)
        read = read + enter * dot_nt(dmixed, s_ref[cols(h), :])
    total = jnp.where(seen, total, 0.0)
    write_ref[...] = dot(total.astype(BF16), r_ref[...])
    read_ref[...] = read + dot(total.T.astype(BF16), w_ref[...])


def last_kernel(gin_ref, x_ref, w_ref, rel_ref, lcol_ref, back_ref, part_ref, out_ref, write_ref):
    length, heads = lcol_ref.shape
    rel_last = rel_ref[:, length - 1 :]
    last_doc = iota((length, 128), 0) >= rel_last
    writes = w_ref[...]
    write = part_ref[...]
    for h in range(heads):
        lc = lcol_ref[:, h : h + 1]
        line = jnp.broadcast_to(lc[length - 1 :, :] - lc, (length, 128))
        to_end = jnp.where(last_doc, jnp.exp2(line), 0.0)
        back = back_ref[cols(h), :]
        out_ref[:, cols(h)] = (gin_ref[:, cols(h)] + to_end * dot(writes, back)).astype(BF16)
        write = write + to_end * dot_nt(x_ref[:, cols(h)], back)
    write_ref[...] = write


def pass_block(block, n):
    if n == 0:
        return block
    return lax.ppermute(block, "ctx", [(i, i ^ n) for i in range(lax.axis_size("ctx"))])


def exchange(blocks):
    return lax.all_to_all(blocks, "ctx", 0, 0)


def pack_kernel(me_ref, marks_ref, q_ref, k_ref, v_ref, g_ref, *out_refs):
    length = q_ref.shape[0]
    for n, out_ref in enumerate(out_refs):
        for a in range(out_ref.shape[0]):
            head = (me_ref[0] ^ n) * out_ref.shape[0] + a
            here = pl.ds(pl.multiple_of(head * ATT_DIM, ATT_DIM), ATT_DIM)
            for place, ref in enumerate((q_ref, k_ref, v_ref, g_ref)):
                out_ref[a, place * length : (place + 1) * length, :] = ref[:, here]
            out_ref[a, 4 * length :, :] = marks_ref[...]


def unpack_kernel(me_ref, *refs):
    in_refs, out_refs = refs[:-4], refs[-4:]
    length = out_refs[0].shape[0]
    for n, in_ref in enumerate(in_refs):
        for a in range(in_ref.shape[0]):
            head = (me_ref[0] ^ n) * in_ref.shape[0] + a
            here = pl.ds(pl.multiple_of(head * ATT_DIM, ATT_DIM), ATT_DIM)
            for place, ref in enumerate(out_refs):
                ref[:, here] = in_ref[a, place * length : (place + 1) * length, :]


def attend_blocks(length, parts, me_ref, *refs):
    in_refs, out_refs = refs[:parts], refs[parts : 2 * parts]
    all_in, all_out = refs[2 * parts : 2 * parts + 2]
    for n in range(parts):
        all_in[me_ref[0] ^ n] = in_refs[n][...]
    attend_kernel(length, all_in, all_out, *refs[2 * parts + 2 :])
    for n in range(parts):
        out_refs[n][...] = all_out[me_ref[0] ^ n]


def attend_kernel(length, in_ref, out_ref, expo_ref, kt_ref, vt_ref, dk_ref, dv_ref):
    parts = in_ref.shape[0]
    scale = ATT_DIM ** (-0.5)
    rate = scale * LOG2E
    key_in = iota((length, length), 0)
    causal = key_in <= iota((length, length), 1)
    for a in range(in_ref.shape[1]):

        def piece(block, place):
            return in_ref[block, a, place * length : (place + 1) * length, :]

        for i in range(parts):
            kt_ref[i] = flip(piece(i, 1))
            vt_ref[i] = flip(piece(i, 2))
            queries, grads = piece(i, 0), piece(i, 3)
            marks = in_ref[i, a, 4 * length :, :].astype(F32)
            starts = jnp.concatenate(
                [
                    marks[2 * n : 2 * n + 1] * 128.0 + marks[2 * n + 1 : 2 * n + 2]
                    for n in range(length // 128)
                ],
                axis=1,
            ).astype(jnp.int32)
            query_at = i * length + iota((1, length), 1)
            if parts * length > WINDOW:
                starts = jnp.maximum(starts, query_at - (WINDOW - 1))
            top = jnp.full((1, length), MASKED, F32)
            total = jnp.zeros((1, length), F32)
            tops = []
            for j in range(i + 1):
                seen = key_in >= starts - j * length
                if j == i:
                    seen = seen & causal
                raw = jnp.where(seen, dot_nt(piece(j, 1), queries), MASKED)
                new = jnp.maximum(top, jnp.max(raw, axis=0, keepdims=True))
                expo = jnp.exp2((raw - new) * rate)
                expo_ref[j] = expo
                total = total * jnp.exp2((top - new) * rate) + jnp.sum(expo, axis=0, keepdims=True)
                top = new
                tops.append(new)
            out = jnp.zeros((ATT_DIM, length), F32)
            for j in range(i + 1):
                probs = expo_ref[j] * (jnp.exp2((tops[j] - top) * rate) / total)
                expo_ref[j] = probs
                weights = probs.astype(BF16)
                dvalue = dot(weights, grads)
                dv_ref[j] = dvalue if j == i else dv_ref[j] + dvalue
                out = out + dot(vt_ref[j], weights)
            delta = jnp.sum(out * grads.astype(F32).T, axis=0, keepdims=True)
            dquery = jnp.zeros((ATT_DIM, length), F32)
            for j in range(i + 1):
                dprobs = dot_nt(piece(j, 2), grads)
                dscore = (expo_ref[j] * ((dprobs - delta) * scale)).astype(BF16)
                dkey = dot(dscore, queries)
                dk_ref[j] = dkey if j == i else dk_ref[j] + dkey
                dquery = dquery + dot(kt_ref[j], dscore)
            out_ref[i, a, 0:length, :] = out.T.astype(BF16)
            out_ref[i, a, length : 2 * length, :] = dquery.T.astype(BF16)
        for j in range(parts):
            out_ref[j, a, 2 * length : 3 * length, :] = dk_ref[j].astype(BF16)
            out_ref[j, a, 3 * length :, :] = dv_ref[j].astype(BF16)


def shifted(shard, axis, by):
    devices = lax.axis_size(axis)
    pairs = [(i, i + by) for i in range(devices) if 0 <= i + by < devices]
    return lax.ppermute(shard, axis, pairs)


def head_cols(array, head_index):
    return lax.dynamic_slice_in_dim(array, head_index * ATT_DIM, ATT_DIM, 1)


def ring_attention(att_queries, att_keys, att_values, att_grad, doc_start):
    length = att_queries.shape[0]
    shard_index = lax.axis_index("ctx")
    halo_shards = WINDOW // length
    att_count = att_queries.shape[1] // ATT_DIM
    att_width = att_queries.shape[1]
    score_scale = ATT_DIM ** (-0.5)

    def pass_keys(running, unused):
        moved = shifted((running[0], running[1]), "ctx", 1)
        return (moved, moved)

    _, earlier = lax.scan(pass_keys, (att_keys, att_values), None, length=halo_shards)
    key_all = jnp.concatenate(
        [earlier[0][::-1].reshape(halo_shards * length, att_width), att_keys], axis=0
    )
    value_all = jnp.concatenate(
        [earlier[1][::-1].reshape(halo_shards * length, att_width), att_values], axis=0
    )
    spread_rows = (halo_shards + 1) * length
    query_pos = shard_index * length + jnp.arange(length, dtype=jnp.int32)
    key_pos = (shard_index - halo_shards) * length + jnp.arange(spread_rows, dtype=jnp.int32)
    visible = (
        (key_pos[None, :] <= query_pos[:, None])
        & (query_pos[:, None] - key_pos[None, :] < WINDOW)
        & (key_pos[None, :] >= doc_start[:, None])
    )

    def forward_head(head_index, running):
        out_buf, max_buf, total_buf, delta_buf = running
        query_head = head_cols(att_queries, head_index)
        key_head = head_cols(key_all, head_index)
        value_head = head_cols(value_all, head_index)
        score = (
            jnp.einsum("td,sd->ts", query_head, key_head, preferred_element_type=jnp.float32)
            * score_scale
        )
        row_max = jnp.max(jnp.where(visible, score, -jnp.inf), axis=1)
        expo = jnp.where(visible, jnp.exp(score - row_max[:, None]), 0.0)
        row_total = jnp.sum(expo, axis=1)
        weights = (expo / row_total[:, None]).astype(jnp.bfloat16)
        attended = jnp.dot(weights, value_head, preferred_element_type=jnp.float32)
        delta = jnp.sum(head_cols(att_grad, head_index).astype(jnp.float32) * attended, axis=1)
        out_buf = lax.dynamic_update_slice_in_dim(
            out_buf, attended.astype(jnp.bfloat16), head_index * ATT_DIM, 1
        )
        return (
            out_buf,
            max_buf.at[:, head_index].set(row_max),
            total_buf.at[:, head_index].set(row_total),
            delta_buf.at[:, head_index].set(delta),
        )

    stats_zero = jnp.zeros((length, att_count), jnp.float32)
    window_out, row_maxes, row_totals, row_deltas = lax.fori_loop(
        0,
        att_count,
        forward_head,
        (jnp.zeros((length, att_width), jnp.bfloat16), stats_zero, stats_zero, stats_zero),
    )

    def query_terms(head_index):
        query_head = head_cols(att_queries, head_index)
        key_head = head_cols(key_all, head_index)
        value_head = head_cols(value_all, head_index)
        grad_head = head_cols(att_grad, head_index)
        score = (
            jnp.einsum("td,sd->ts", query_head, key_head, preferred_element_type=jnp.float32)
            * score_scale
        )
        probs = (
            jnp.where(visible, jnp.exp(score - row_maxes[:, head_index][:, None]), 0.0)
            / row_totals[:, head_index][:, None]
        )
        weights = probs.astype(jnp.bfloat16)
        dprobs = jnp.einsum("td,sd->ts", grad_head, value_head, preferred_element_type=jnp.float32)
        dscore = (probs * (dprobs - row_deltas[:, head_index][:, None]) * score_scale).astype(
            jnp.bfloat16
        )
        query_part = jnp.dot(dscore, key_head, preferred_element_type=jnp.float32)
        return (query_head, grad_head, weights, dscore, query_part)

    def backward_head(head_index, running):
        query_buf, key_buf, value_buf = running
        query_head, grad_head, weights, dscore, query_part = query_terms(head_index)
        key_part = jnp.einsum("ts,td->sd", dscore, query_head, preferred_element_type=jnp.float32)
        value_part = jnp.einsum("ts,td->sd", weights, grad_head, preferred_element_type=jnp.float32)
        query_buf = lax.dynamic_update_slice_in_dim(query_buf, query_part, head_index * ATT_DIM, 1)
        key_buf = lax.dynamic_update_slice_in_dim(key_buf, key_part, head_index * ATT_DIM, 1)
        value_buf = lax.dynamic_update_slice_in_dim(value_buf, value_part, head_index * ATT_DIM, 1)
        return (query_buf, key_buf, value_buf)

    part_zero = jnp.zeros((spread_rows, att_width), jnp.float32)
    query_sum, key_parts, value_parts = lax.fori_loop(
        0,
        att_count,
        backward_head,
        (jnp.zeros((length, att_width), jnp.float32), part_zero, part_zero),
    )
    key_blocks = key_parts.reshape(halo_shards + 1, length, att_width)
    value_blocks = value_parts.reshape(halo_shards + 1, length, att_width)

    def send_back(running, block_index):
        moved = shifted((running[0], running[1]), "ctx", -1)
        return ((moved[0] + key_blocks[block_index], moved[1] + value_blocks[block_index]), None)

    (key_sum, value_sum), _ = lax.scan(
        send_back, (key_blocks[0], value_blocks[0]), jnp.arange(1, halo_shards + 1, dtype=jnp.int32)
    )
    return (
        window_out,
        query_sum.astype(jnp.bfloat16),
        key_sum.astype(jnp.bfloat16),
        value_sum.astype(jnp.bfloat16),
    )


def body(
    ssm_input,
    gate_input,
    write_map,
    read_map,
    log_decay,
    doc_start,
    ssm_grad,
    att_queries,
    att_keys,
    att_values,
    att_grad,
):
    length, width = ssm_input.shape
    heads = width // HEAD_DIM
    parts = lax.axis_size("ctx")
    rows = width // parts
    full_width = width * lax.axis_size("head")
    work = 2 * length * length * width
    att_width = att_queries.shape[1]
    per = att_width // ATT_DIM // parts
    dealt = att_width // ATT_DIM % parts == 0
    place = lax.axis_index("ctx")
    rel = (doc_start - place * length).reshape(1, length)
    me = place.reshape(1).astype(jnp.int32)

    sent, lcol, lrow = call(
        first_kernel,
        (
            shape((parts, rows + TAIL, 128), BF16),
            shape((length, heads), F32),
            shape((heads, length), F32),
        ),
        log_decay.T, rel, write_map, ssm_input, flops=work // 2, name="ssm_first",
    )
    if dealt:
        marks = doc_start.reshape(length // 128, 128)
        marks = jnp.stack([marks // 128, marks % 128], axis=1).reshape(length // 64, 128)
        marks = jnp.pad(marks, ((0, TAIL - length // 64), (0, 0))).astype(BF16)
        marks, sent = lax.optimization_barrier((marks, sent))
        packed = call(
            pack_kernel, [shape((per, 4 * length + TAIL, 128), BF16)] * parts,
            me, marks, att_queries, att_keys, att_values, att_grad,
            specs=[SMEM] + [VMEM] * 5, vmem=SMALL, name="att_pack",
        )
        half = parts // 2
        order = [half] + list(range(1, half)) + list(range(half + 1, parts))
        early, middle, late = order[:half], order[half:-1], order[-1:]
        att_got = {0: packed[0]}
        for n in early:
            att_got[n] = pass_block(packed[n], n)
    else:
        att_out = ring_attention(att_queries, att_keys, att_values, att_grad, doc_start)
    got = exchange(sent)
    first_got = got
    carried = call(
        lambda in_ref, out_ref: carry_kernel(False, in_ref, in_ref, out_ref),
        shape((parts, rows, 128), BF16), got, vmem=SMALL, name="ssm_carry",
    )
    state = exchange(carried).reshape(width, 128)

    if dealt:
        held, done, state = lax.optimization_barrier(
            ([packed[n] for n in middle], [att_got[n] for n in early], state)
        )
        att_got.update(zip(early, done))
        for n, block in zip(middle, held):
            att_got[n] = pass_block(block, n)

    mixed, sums = call(
        mix_kernel,
        (shape((length, width), F32), shape((8, length), F32)),
        ssm_input, gate_input, ssm_grad, write_map, read_map, rel, lcol, lrow, state,
        flops=work * 3 // 2, name="ssm_mix",
    )
    sums = lax.psum(sums, "head")
    mixer_out, gate_grad, dmixed, sent = call(
        lambda *refs: gate_kernel(full_width, *refs),
        (
            shape((length, width), BF16),
            shape((length, width), BF16),
            shape((length, width), BF16),
            shape((parts, rows, 128), BF16),
        ),
        sums, mixed, gate_input, ssm_grad, read_map, rel, lrow, flops=work // 2, name="ssm_gate",
    )

    if dealt:
        held, done, sent = lax.optimization_barrier(
            ([packed[n] for n in late], [att_got[n] for n in middle], sent)
        )
        att_got.update(zip(middle, done))
        for n, block in zip(late, held):
            att_got[n] = pass_block(block, n)
    got = exchange(sent)
    carried = call(
        lambda *refs: carry_kernel(True, *refs), shape((parts, rows, 128), BF16), first_got, got,
        vmem=SMALL, name="ssm_carry_back",
    )
    back = exchange(carried).reshape(width, 128)
    if dealt:
        last_got, carried = lax.optimization_barrier((att_got[parts - 1], carried))
        att_got[parts - 1] = last_got
        att_done = call(
            lambda *refs: attend_blocks(length, parts, *refs),
            [shape((per, 4 * length, 128), BF16)] * parts,
            me, *[att_got[n] for n in range(parts)],
            specs=[SMEM] + [VMEM] * parts,
            scratch=[
                pltpu.VMEM((parts, per, 4 * length + TAIL, 128), BF16),
                pltpu.VMEM((parts, per, 4 * length, 128), BF16),
                pltpu.VMEM((parts, length, length), F32),
                pltpu.VMEM((parts, ATT_DIM, length), BF16),
                pltpu.VMEM((parts, ATT_DIM, length), BF16),
                pltpu.VMEM((parts, length, ATT_DIM), F32),
                pltpu.VMEM((parts, length, ATT_DIM), F32),
            ],
            flops=6 * per * (parts * length) ** 2 * ATT_DIM, name="att_attend",
        )
        att_done, back = lax.optimization_barrier((att_done, back))
        att_out = call(
            unpack_kernel, (shape((length, att_width), BF16),) * 4,
            me, *[pass_block(block, n) for n, block in enumerate(att_done)],
            specs=[SMEM] + [VMEM] * parts, vmem=SMALL, name="att_unpack",
        )

    gin, read_part, write_part = call(
        inner_kernel,
        (shape((length, width), F32), shape((length, 128), F32), shape((length, 128), F32)),
        dmixed, ssm_input, write_map, read_map, rel, lcol, lrow, state,
        flops=work * 5 // 2, name="ssm_inner",
    )
    input_grad, write_part = call(
        last_kernel,
        (shape((length, width), BF16), shape((length, 128), F32)),
        gin, ssm_input, write_map, rel, lcol, back, write_part, flops=work, name="ssm_last",
    )
    write_sum, read_sum = lax.psum((write_part, read_part), "head")
    window_out, query_grad, key_grad, value_grad = att_out
    return (
        mixer_out,
        window_out,
        input_grad,
        gate_grad,
        write_sum.astype(BF16),
        read_sum.astype(BF16),
        query_grad,
        key_grad,
        value_grad,
    )


def solution(mesh):
    in_specs = (
        P("ctx", "head"),
        P("ctx", "head"),
        P("ctx", None),
        P("ctx", None),
        P("ctx", "head"),
        P("ctx"),
        P("ctx", "head"),
        P("ctx", "head"),
        P("ctx", "head"),
        P("ctx", "head"),
        P("ctx", "head"),
    )
    out_specs = (
        P("ctx", "head"),
        P("ctx", "head"),
        P("ctx", "head"),
        P("ctx", "head"),
        P("ctx", None),
        P("ctx", None),
        P("ctx", "head"),
        P("ctx", "head"),
        P("ctx", "head"),
    )
    return jax.shard_map(body, mesh=mesh, in_specs=in_specs, out_specs=out_specs, check_vma=False)
```

```python
import jax
import jax.numpy as jnp
from jax import lax
from jax.experimental import pallas as pl
from jax.experimental.pallas import tpu as pltpu
from jax.sharding import PartitionSpec as P

HEAD_DIM = 128
ATT_DIM = 128
WINDOW = 4096
EPSILON = 1e-05
LOG2E = 1.4426950408889634
TAIL = 16
MASKED = -1e30
HIGH = lax.Precision.HIGHEST
F32 = jnp.float32
BF16 = jnp.bfloat16
VMEM_BYTES = 56 * 1024 * 1024


VMEM = pl.BlockSpec(memory_space=pltpu.VMEM)
SMEM = pl.BlockSpec(memory_space=pltpu.SMEM)
SMALL = 16 * 1024 * 1024


def call(kernel, out_shape, *operands, specs=None, scratch=(), flops=0, vmem=VMEM_BYTES, name=None):
    moved = sum(a.size * a.dtype.itemsize for a in jax.tree.leaves((operands, out_shape)))
    return pl.pallas_call(
        kernel,
        out_shape=out_shape,
        in_specs=specs or [VMEM] * len(operands),
        out_specs=jax.tree.map(lambda _: VMEM, out_shape),
        scratch_shapes=scratch,
        compiler_params=pltpu.CompilerParams(vmem_limit_bytes=vmem),
        cost_estimate=pl.CostEstimate(flops=flops, bytes_accessed=moved, transcendentals=0),
        name=name,
    )(*operands)


def shape(dims, dtype):
    return jax.ShapeDtypeStruct(dims, dtype)


def dot(a, b):
    return jnp.dot(a, b, preferred_element_type=F32)


def dot_nt(a, b, precision=None):
    return lax.dot_general(
        a, b, (((1,), (1,)), ((), ())), preferred_element_type=F32, precision=precision
    )


def iota(dims, axis):
    return lax.broadcasted_iota(jnp.int32, dims, axis)


def flip(a):
    return a.astype(F32).T.astype(BF16)


def column(row):
    return jnp.broadcast_to(row, (128, row.shape[1])).T


def cols(h):
    return slice(h * HEAD_DIM, (h + 1) * HEAD_DIM)


def deal(me_ref, held, out_refs):
    for n, out_ref in enumerate(out_refs):
        out_ref[...] = held[me_ref[0] ^ n]


def collect(me_ref, in_refs, held):
    for n, in_ref in enumerate(in_refs):
        held[me_ref[0] ^ n] = in_ref[...]


def gather_state(me_ref, in_refs, state_ref):
    rows = in_refs[0].shape[0]
    for n, in_ref in enumerate(in_refs):
        here = pl.ds(pl.multiple_of((me_ref[0] ^ n) * rows, rows), rows)
        state_ref[here, :] = in_ref[...]


def first_kernel(shares, me_ref, ld_ref, rel_ref, w_ref, x_ref, lcol_ref, lrow_ref, *refs):
    out_refs, out_ref = refs[:shares], refs[shares]
    heads, length = ld_ref.shape
    parts, rows = out_ref.shape[0], out_ref.shape[1] - TAIL
    rates = ld_ref[...] * LOG2E
    lower = jnp.where(iota((length, length), 0) >= iota((length, length), 1), 1.0, 0.0)
    upper = jnp.where(iota((length, length), 0) <= iota((length, length), 1), 1.0, 0.0)
    lcol_ref[...] = dot_nt(lower, rates, HIGH)
    lrow = jnp.dot(rates, upper, preferred_element_type=F32, precision=HIGH)
    lrow_ref[...] = lrow
    rel_last = rel_ref[:, length - 1 :]
    last_doc = iota((1, length), 1) >= rel_last
    keeps = rel_last < 0
    writes = w_ref[...].astype(F32).T
    tail_row = iota((TAIL, 128), 0)
    for h in range(heads):
        line = lrow[h : h + 1, :]
        total = line[:, length - 1 :]
        to_end = jnp.where(last_doc, jnp.exp2(total - line), 0.0)
        state = dot((writes * to_end).astype(BF16), x_ref[:, cols(h)]).astype(BF16)
        factor = jnp.where(keeps, jnp.exp2(total), 0.0)
        high = factor.astype(BF16).astype(F32)
        low = factor - high
        first = h * HEAD_DIM
        for part in range(first // rows, (first + HEAD_DIM - 1) // rows + 1):
            begin = max(first, part * rows)
            end = min(first + HEAD_DIM, (part + 1) * rows)
            out_ref[part, begin - part * rows : end - part * rows, :] = state[
                begin - first : end - first, :
            ]
            place = 2 * (begin - part * rows) // HEAD_DIM
            tail = jnp.where(tail_row == place, high, jnp.where(tail_row == place + 1, low, 0.0))
            if place:
                tail = tail + out_ref[part, rows:, :].astype(F32)
            out_ref[part, rows:, :] = tail.astype(BF16)
    deal(me_ref, out_ref, out_refs)


def carry(backward, start_ref, tails, held, total_ref, out):
    shares, rows = tails.shape[0], tails.shape[1] - TAIL
    step = min(rows, HEAD_DIM)
    for k in range(rows // step):
        here = slice(k * step, (k + 1) * step)
        state = jnp.zeros((step, 128), F32) if start_ref is None else start_ref[here, :].astype(F32)
        for c in range(shares)[:: -1 if backward else 1]:
            if out is not None:
                out[c, here, :] = state.astype(BF16)
            tail = tails[c, rows:, :].astype(F32)
            factor = tail[2 * k : 2 * k + 1, :] + tail[2 * k + 1 : 2 * k + 2, :]
            state = factor * state + held[c, here, :].astype(F32)
        if total_ref is not None:
            total_ref[here, :] = state.astype(BF16)


def total_kernel(backward, shares, me_ref, *refs):
    count = 2 if backward else 1
    in_refs, (total_ref, *held) = refs[: count * shares], refs[count * shares :]
    for n in range(count):
        collect(me_ref, in_refs[n * shares : (n + 1) * shares], held[n])
    carry(backward, None, held[0], held[-1], total_ref, None)


def carry_kernel(backward, shares, me_ref, start_ref, *refs):
    count = 2 if backward else 1
    in_refs, out_refs = refs[: count * shares], refs[count * shares : (count + 1) * shares]
    *held, out = refs[(count + 1) * shares :]
    for n in range(count):
        collect(me_ref, in_refs[n * shares : (n + 1) * shares], held[n])
    carry(backward, start_ref, held[0], held[-1], None, out)
    deal(me_ref, out, out_refs)


def mix_kernel(
    shares, me_ref, x_ref, gate_ref, grad_ref, w_ref, r_ref, rel_ref, lcol_ref, lrow_ref, *refs
):
    state_refs, (mixed_ref, sums_ref, s_ref) = refs[:shares], refs[shares:]
    gather_state(me_ref, state_refs, s_ref)
    length, heads = lcol_ref.shape
    reads = r_ref[...]
    rel = column(rel_ref[...].astype(F32))
    wide = jnp.concatenate([rel] * (length // 128), axis=1)
    seen = (iota((length, length), 1).astype(F32) >= wide) & (
        iota((length, length), 1) <= iota((length, length), 0)
    )
    scores = jnp.where(seen, dot_nt(reads, w_ref[...]), 0.0)
    squares = jnp.zeros((length, 128), F32)
    inners = jnp.zeros((length, 128), F32)
    for h in range(heads):
        lc = lcol_ref[:, h : h + 1]
        decay = jnp.exp2(jnp.minimum(lc - lrow_ref[h : h + 1, :], 0.0))
        enter = jnp.where(rel < 0, jnp.exp2(jnp.broadcast_to(lc, rel.shape)), 0.0)
        mixed = dot((scores * decay).astype(BF16), x_ref[:, cols(h)]) + enter * dot(
            reads, s_ref[cols(h), :]
        )
        mixed_ref[:, cols(h)] = mixed
        gate = gate_ref[:, cols(h)].astype(F32)
        gated = mixed * (gate / (1.0 + jnp.exp(-gate)))
        squares = squares + gated * gated
        inners = inners + grad_ref[:, cols(h)].astype(F32) * gated
    ones = jnp.ones((8, 128), F32)
    square_row = dot_nt(ones, squares, HIGH)
    inner_row = dot_nt(ones, inners, HIGH)
    sums_ref[...] = jnp.where(iota((8, length), 0) == 0, square_row, inner_row)


def gate_kernel(
    width, shares, me_ref, sums_ref, mixed_ref, gate_ref, grad_ref, r_ref, rel_ref, lrow_ref,
    mixer_ref, ggrad_ref, dmixed_ref, *refs,
):
    out_refs, out_ref = refs[:shares], refs[shares]
    length = mixed_ref.shape[0]
    heads = lrow_ref.shape[0]
    rows = out_ref.shape[1]
    scale = lax.rsqrt(sums_ref[0:1, :] / width + EPSILON)
    rms = column(scale)
    pull = column(scale * scale * scale * sums_ref[1:2, :] / width)
    reads = r_ref[...].astype(F32).T
    enters = rel_ref[...] < 0
    for h in range(heads):
        mixed = mixed_ref[:, cols(h)]
        gate = gate_ref[:, cols(h)].astype(F32)
        sigma = 1.0 / (1.0 + jnp.exp(-gate))
        swish = gate * sigma
        gated = mixed * swish
        mixer_ref[:, cols(h)] = (gated * rms).astype(BF16)
        dgated = rms * grad_ref[:, cols(h)].astype(F32) - pull * gated
        dmixed = (dgated * swish).astype(BF16)
        dmixed_ref[:, cols(h)] = dmixed
        ggrad_ref[:, cols(h)] = (
            dgated * mixed * sigma * (1.0 + gate * (1.0 - sigma))
        ).astype(BF16)
        enter = jnp.where(enters, jnp.exp2(lrow_ref[h : h + 1, :]), 0.0)
        state = dot((reads * enter).astype(BF16), dmixed).astype(BF16)
        first = h * HEAD_DIM
        for part in range(first // rows, (first + HEAD_DIM - 1) // rows + 1):
            begin = max(first, part * rows)
            end = min(first + HEAD_DIM, (part + 1) * rows)
            out_ref[part, begin - part * rows : end - part * rows, :] = state[
                begin - first : end - first, :
            ]
    deal(me_ref, out_ref, out_refs)


def inner_kernel(
    dmixed_ref, x_ref, w_ref, r_ref, rel_ref, lcol_ref, lrow_ref, s_ref, gin_ref, read_ref, write_ref
):
    length, heads = lcol_ref.shape
    rel_row = rel_ref[...]
    rel = column(rel_row.astype(F32))
    seen = (iota((length, length), 0) >= rel_row) & (
        iota((length, length), 0) <= iota((length, length), 1)
    )
    scores = jnp.where(seen, dot_nt(w_ref[...], r_ref[...]), 0.0)
    total = jnp.zeros((length, length), F32)
    read = jnp.zeros((length, 128), F32)
    for h in range(heads):
        lc = lcol_ref[:, h : h + 1]
        decay = jnp.exp2(jnp.minimum(lrow_ref[h : h + 1, :] - lc, 0.0))
        dmixed = dmixed_ref[:, cols(h)]
        gin_ref[:, cols(h)] = dot((scores * decay).astype(BF16), dmixed)
        total = total + decay * dot_nt(x_ref[:, cols(h)], dmixed)
        enter = jnp.where(rel < 0, jnp.exp2(jnp.broadcast_to(lc, rel.shape)), 0.0)
        read = read + enter * dot_nt(dmixed, s_ref[cols(h), :])
    total = jnp.where(seen, total, 0.0)
    write_ref[...] = dot(total.astype(BF16), r_ref[...])
    read_ref[...] = read + dot(total.T.astype(BF16), w_ref[...])


def last_kernel(shares, me_ref, gin_ref, x_ref, w_ref, rel_ref, lcol_ref, part_ref, *refs):
    state_refs, (out_ref, write_ref, back_ref) = refs[:shares], refs[shares:]
    gather_state(me_ref, state_refs, back_ref)
    length, heads = lcol_ref.shape
    rel_last = rel_ref[:, length - 1 :]
    last_doc = iota((length, 128), 0) >= rel_last
    writes = w_ref[...]
    write = part_ref[...]
    for h in range(heads):
        lc = lcol_ref[:, h : h + 1]
        line = jnp.broadcast_to(lc[length - 1 :, :] - lc, (length, 128))
        to_end = jnp.where(last_doc, jnp.exp2(line), 0.0)
        back = back_ref[cols(h), :]
        out_ref[:, cols(h)] = (gin_ref[:, cols(h)] + to_end * dot(writes, back)).astype(BF16)
        write = write + to_end * dot_nt(x_ref[:, cols(h)], back)
    write_ref[...] = write


def pass_block(block, n):
    if n == 0:
        return block
    return lax.ppermute(block, "ctx", [(i, i ^ n) for i in range(lax.axis_size("ctx"))])


def cross(total, backward):
    count = lax.axis_size("ctx")
    half = count // 2
    pairs = [(i + half, i) if backward else (i, i + half) for i in range(half)]
    return lax.ppermute(total, "ctx", pairs)


def pack_kernel(me_ref, marks_ref, q_ref, k_ref, v_ref, g_ref, *out_refs):
    length = q_ref.shape[0]
    for n, out_ref in enumerate(out_refs):
        for a in range(out_ref.shape[0]):
            head = (me_ref[0] ^ n) * out_ref.shape[0] + a
            here = pl.ds(pl.multiple_of(head * ATT_DIM, ATT_DIM), ATT_DIM)
            for place, ref in enumerate((q_ref, k_ref, v_ref, g_ref)):
                out_ref[a, place * length : (place + 1) * length, :] = ref[:, here]
            out_ref[a, 4 * length :, :] = marks_ref[...]


def unpack_kernel(me_ref, *refs):
    in_refs, out_refs = refs[:-4], refs[-4:]
    length = out_refs[0].shape[0]
    for n, in_ref in enumerate(in_refs):
        for a in range(in_ref.shape[0]):
            head = (me_ref[0] ^ n) * in_ref.shape[0] + a
            here = pl.ds(pl.multiple_of(head * ATT_DIM, ATT_DIM), ATT_DIM)
            for place, ref in enumerate(out_refs):
                ref[:, here] = in_ref[a, place * length : (place + 1) * length, :]


def attend_blocks(length, parts, me_ref, *refs):
    in_refs, out_refs = refs[:parts], refs[parts : 2 * parts]
    all_in, all_out = refs[2 * parts : 2 * parts + 2]
    for n in range(parts):
        all_in[me_ref[0] ^ n] = in_refs[n][...]
    attend_kernel(length, all_in, all_out, *refs[2 * parts + 2 :])
    for n in range(parts):
        out_refs[n][...] = all_out[me_ref[0] ^ n]


def attend_kernel(length, in_ref, out_ref, expo_ref, kt_ref, vt_ref, dk_ref, dv_ref):
    parts = in_ref.shape[0]
    scale = ATT_DIM ** (-0.5)
    rate = scale * LOG2E
    key_in = iota((length, length), 0)
    causal = key_in <= iota((length, length), 1)
    for a in range(in_ref.shape[1]):

        def piece(block, place):
            return in_ref[block, a, place * length : (place + 1) * length, :]

        for i in range(parts):
            kt_ref[i] = flip(piece(i, 1))
            vt_ref[i] = flip(piece(i, 2))
            queries, grads = piece(i, 0), piece(i, 3)
            marks = in_ref[i, a, 4 * length :, :].astype(F32)
            starts = jnp.concatenate(
                [
                    marks[2 * n : 2 * n + 1] * 128.0 + marks[2 * n + 1 : 2 * n + 2]
                    for n in range(length // 128)
                ],
                axis=1,
            ).astype(jnp.int32)
            query_at = i * length + iota((1, length), 1)
            if parts * length > WINDOW:
                starts = jnp.maximum(starts, query_at - (WINDOW - 1))
            top = jnp.full((1, length), MASKED, F32)
            total = jnp.zeros((1, length), F32)
            tops = []
            for j in range(i + 1):
                seen = key_in >= starts - j * length
                if j == i:
                    seen = seen & causal
                raw = jnp.where(seen, dot_nt(piece(j, 1), queries), MASKED)
                new = jnp.maximum(top, jnp.max(raw, axis=0, keepdims=True))
                expo = jnp.exp2((raw - new) * rate)
                expo_ref[j] = expo
                total = total * jnp.exp2((top - new) * rate) + jnp.sum(expo, axis=0, keepdims=True)
                top = new
                tops.append(new)
            out = jnp.zeros((ATT_DIM, length), F32)
            for j in range(i + 1):
                probs = expo_ref[j] * (jnp.exp2((tops[j] - top) * rate) / total)
                expo_ref[j] = probs
                weights = probs.astype(BF16)
                dvalue = dot(weights, grads)
                dv_ref[j] = dvalue if j == i else dv_ref[j] + dvalue
                out = out + dot(vt_ref[j], weights)
            delta = jnp.sum(out * grads.astype(F32).T, axis=0, keepdims=True)
            dquery = jnp.zeros((ATT_DIM, length), F32)
            for j in range(i + 1):
                dprobs = dot_nt(piece(j, 2), grads)
                dscore = (expo_ref[j] * ((dprobs - delta) * scale)).astype(BF16)
                dkey = dot(dscore, queries)
                dk_ref[j] = dkey if j == i else dk_ref[j] + dkey
                dquery = dquery + dot(kt_ref[j], dscore)
            out_ref[i, a, 0:length, :] = out.T.astype(BF16)
            out_ref[i, a, length : 2 * length, :] = dquery.T.astype(BF16)
        for j in range(parts):
            out_ref[j, a, 2 * length : 3 * length, :] = dk_ref[j].astype(BF16)
            out_ref[j, a, 3 * length :, :] = dv_ref[j].astype(BF16)


def shifted(shard, axis, by):
    devices = lax.axis_size(axis)
    pairs = [(i, i + by) for i in range(devices) if 0 <= i + by < devices]
    return lax.ppermute(shard, axis, pairs)


def head_cols(array, head_index):
    return lax.dynamic_slice_in_dim(array, head_index * ATT_DIM, ATT_DIM, 1)


def ring_attention(att_queries, att_keys, att_values, att_grad, doc_start):
    length = att_queries.shape[0]
    shard_index = lax.axis_index("ctx")
    halo_shards = WINDOW // length
    att_count = att_queries.shape[1] // ATT_DIM
    att_width = att_queries.shape[1]
    score_scale = ATT_DIM ** (-0.5)

    def pass_keys(running, unused):
        moved = shifted((running[0], running[1]), "ctx", 1)
        return (moved, moved)

    _, earlier = lax.scan(pass_keys, (att_keys, att_values), None, length=halo_shards)
    key_all = jnp.concatenate(
        [earlier[0][::-1].reshape(halo_shards * length, att_width), att_keys], axis=0
    )
    value_all = jnp.concatenate(
        [earlier[1][::-1].reshape(halo_shards * length, att_width), att_values], axis=0
    )
    spread_rows = (halo_shards + 1) * length
    query_pos = shard_index * length + jnp.arange(length, dtype=jnp.int32)
    key_pos = (shard_index - halo_shards) * length + jnp.arange(spread_rows, dtype=jnp.int32)
    visible = (
        (key_pos[None, :] <= query_pos[:, None])
        & (query_pos[:, None] - key_pos[None, :] < WINDOW)
        & (key_pos[None, :] >= doc_start[:, None])
    )

    def forward_head(head_index, running):
        out_buf, max_buf, total_buf, delta_buf = running
        query_head = head_cols(att_queries, head_index)
        key_head = head_cols(key_all, head_index)
        value_head = head_cols(value_all, head_index)
        score = (
            jnp.einsum("td,sd->ts", query_head, key_head, preferred_element_type=jnp.float32)
            * score_scale
        )
        row_max = jnp.max(jnp.where(visible, score, -jnp.inf), axis=1)
        expo = jnp.where(visible, jnp.exp(score - row_max[:, None]), 0.0)
        row_total = jnp.sum(expo, axis=1)
        weights = (expo / row_total[:, None]).astype(jnp.bfloat16)
        attended = jnp.dot(weights, value_head, preferred_element_type=jnp.float32)
        delta = jnp.sum(head_cols(att_grad, head_index).astype(jnp.float32) * attended, axis=1)
        out_buf = lax.dynamic_update_slice_in_dim(
            out_buf, attended.astype(jnp.bfloat16), head_index * ATT_DIM, 1
        )
        return (
            out_buf,
            max_buf.at[:, head_index].set(row_max),
            total_buf.at[:, head_index].set(row_total),
            delta_buf.at[:, head_index].set(delta),
        )

    stats_zero = jnp.zeros((length, att_count), jnp.float32)
    window_out, row_maxes, row_totals, row_deltas = lax.fori_loop(
        0,
        att_count,
        forward_head,
        (jnp.zeros((length, att_width), jnp.bfloat16), stats_zero, stats_zero, stats_zero),
    )

    def query_terms(head_index):
        query_head = head_cols(att_queries, head_index)
        key_head = head_cols(key_all, head_index)
        value_head = head_cols(value_all, head_index)
        grad_head = head_cols(att_grad, head_index)
        score = (
            jnp.einsum("td,sd->ts", query_head, key_head, preferred_element_type=jnp.float32)
            * score_scale
        )
        probs = (
            jnp.where(visible, jnp.exp(score - row_maxes[:, head_index][:, None]), 0.0)
            / row_totals[:, head_index][:, None]
        )
        weights = probs.astype(jnp.bfloat16)
        dprobs = jnp.einsum("td,sd->ts", grad_head, value_head, preferred_element_type=jnp.float32)
        dscore = (probs * (dprobs - row_deltas[:, head_index][:, None]) * score_scale).astype(
            jnp.bfloat16
        )
        query_part = jnp.dot(dscore, key_head, preferred_element_type=jnp.float32)
        return (query_head, grad_head, weights, dscore, query_part)

    def backward_head(head_index, running):
        query_buf, key_buf, value_buf = running
        query_head, grad_head, weights, dscore, query_part = query_terms(head_index)
        key_part = jnp.einsum("ts,td->sd", dscore, query_head, preferred_element_type=jnp.float32)
        value_part = jnp.einsum("ts,td->sd", weights, grad_head, preferred_element_type=jnp.float32)
        query_buf = lax.dynamic_update_slice_in_dim(query_buf, query_part, head_index * ATT_DIM, 1)
        key_buf = lax.dynamic_update_slice_in_dim(key_buf, key_part, head_index * ATT_DIM, 1)
        value_buf = lax.dynamic_update_slice_in_dim(value_buf, value_part, head_index * ATT_DIM, 1)
        return (query_buf, key_buf, value_buf)

    part_zero = jnp.zeros((spread_rows, att_width), jnp.float32)
    query_sum, key_parts, value_parts = lax.fori_loop(
        0,
        att_count,
        backward_head,
        (jnp.zeros((length, att_width), jnp.float32), part_zero, part_zero),
    )
    key_blocks = key_parts.reshape(halo_shards + 1, length, att_width)
    value_blocks = value_parts.reshape(halo_shards + 1, length, att_width)

    def send_back(running, block_index):
        moved = shifted((running[0], running[1]), "ctx", -1)
        return ((moved[0] + key_blocks[block_index], moved[1] + value_blocks[block_index]), None)

    (key_sum, value_sum), _ = lax.scan(
        send_back, (key_blocks[0], value_blocks[0]), jnp.arange(1, halo_shards + 1, dtype=jnp.int32)
    )
    return (
        window_out,
        query_sum.astype(jnp.bfloat16),
        key_sum.astype(jnp.bfloat16),
        value_sum.astype(jnp.bfloat16),
    )


def body(
    ssm_input,
    gate_input,
    write_map,
    read_map,
    log_decay,
    doc_start,
    ssm_grad,
    att_queries,
    att_keys,
    att_values,
    att_grad,
):
    length, width = ssm_input.shape
    heads = width // HEAD_DIM
    parts = lax.axis_size("ctx")
    shares = parts // 2
    rows = width // shares
    full_width = width * lax.axis_size("head")
    att_width = att_queries.shape[1]
    per = att_width // ATT_DIM // parts
    dealt = att_width // ATT_DIM % parts == 0
    place = lax.axis_index("ctx")
    rel = (doc_start - place * length).reshape(1, length)
    me = place.reshape(1).astype(jnp.int32)
    share = (place % shares).reshape(1).astype(jnp.int32)
    tailed = [shape((rows + TAIL, 128), BF16)] * shares
    plain = [shape((rows, 128), BF16)] * shares
    held_tails = pltpu.VMEM((shares, rows + TAIL, 128), BF16)
    held_plain = pltpu.VMEM((shares, rows, 128), BF16)

    def carry_total(backward, *blocks):
        return call(
            lambda *refs: total_kernel(backward, shares, *refs),
            shape((rows, 128), BF16), share, *blocks,
            specs=[SMEM] + [VMEM] * len(blocks),
            scratch=[held_tails, held_plain] if backward else [held_tails],
            vmem=SMALL, name="ssm_total",
        )

    def carry_states(backward, start, *blocks):
        return call(
            lambda *refs: carry_kernel(backward, shares, *refs),
            plain, share, start, *blocks,
            specs=[SMEM] + [VMEM] * (1 + len(blocks)),
            scratch=[held_tails, held_plain, held_plain] if backward else [held_tails, held_plain],
            vmem=SMALL, name="ssm_carry",
        )

    lcol, lrow, *sent = call(
        lambda *refs: first_kernel(shares, *refs),
        [shape((length, heads), F32), shape((heads, length), F32)] + tailed,
        share, log_decay.T, rel, write_map, ssm_input,
        specs=[SMEM] + [VMEM] * 4, scratch=[held_tails], name="ssm_first",
    )
    tails = [pass_block(block, n) for n, block in enumerate(sent)]
    if dealt:
        marks = doc_start.reshape(length // 128, 128)
        marks = jnp.stack([marks // 128, marks % 128], axis=1).reshape(length // 64, 128)
        marks = jnp.pad(marks, ((0, TAIL - length // 64), (0, 0))).astype(BF16)
        marks, sent = lax.optimization_barrier((marks, sent))
        packed = call(
            pack_kernel, [shape((per, 4 * length + TAIL, 128), BF16)] * parts,
            me, marks, att_queries, att_keys, att_values, att_grad,
            specs=[SMEM] + [VMEM] * 5, vmem=SMALL, name="att_pack",
        )
        packed = list(packed)
        att_got = {0: packed[0]}
        att_got[shares] = pass_block(packed[shares], shares)
    else:
        att_out = ring_attention(att_queries, att_keys, att_values, att_grad, doc_start)
    total = carry_total(False, *tails)
    if dealt:
        total, att_got[shares] = lax.optimization_barrier((total, att_got[shares]))
    start = cross(total, False)
    if dealt:
        start, packed[shares + 1] = lax.optimization_barrier((start, packed[shares + 1]))
        att_got[shares + 1] = pass_block(packed[shares + 1], shares + 1)
    state = [
        pass_block(block, n) for n, block in enumerate(carry_states(False, start, *tails))
    ]
    if dealt:
        rest = [n for n in range(1, parts) if n not in att_got]
        rest = [n for n in rest if n > shares] + [n for n in rest if n < shares]
        held, att_got[shares + 1], state = lax.optimization_barrier(
            ([packed[n] for n in rest], att_got[shares + 1], state)
        )
        for n, block in zip(rest, held):
            att_got[n] = pass_block(block, n)
    mixed, sums, state = call(
        lambda *refs: mix_kernel(shares, *refs),
        (shape((length, width), F32), shape((8, length), F32), shape((width, 128), BF16)),
        share, ssm_input, gate_input, ssm_grad, write_map, read_map, rel, lcol, lrow, *state,
        specs=[SMEM] + [VMEM] * (8 + shares), name="ssm_mix",
    )
    sums = lax.psum(sums, "head")
    mixer_out, gate_grad, dmixed, *sent = call(
        lambda *refs: gate_kernel(full_width, shares, *refs),
        [shape((length, width), BF16)] * 3 + plain,
        share, sums, mixed, gate_input, ssm_grad, read_map, rel, lrow,
        specs=[SMEM] + [VMEM] * 7, scratch=[held_plain], name="ssm_gate",
    )

    blocks = [pass_block(block, n) for n, block in enumerate(sent)]
    total = carry_total(True, *tails, *blocks)
    start = cross(total, True)
    if dealt:
        att_in, total = lax.optimization_barrier(([att_got[n] for n in range(parts)], total))
        att_done = call(
            lambda *refs: attend_blocks(length, parts, *refs),
            [shape((per, 4 * length, 128), BF16)] * parts, me, *att_in,
            specs=[SMEM] + [VMEM] * parts,
            scratch=[
                pltpu.VMEM((parts, per, 4 * length + TAIL, 128), BF16),
                pltpu.VMEM((parts, per, 4 * length, 128), BF16),
                pltpu.VMEM((parts, length, length), F32),
                pltpu.VMEM((parts, ATT_DIM, length), BF16),
                pltpu.VMEM((parts, ATT_DIM, length), BF16),
                pltpu.VMEM((parts, length, ATT_DIM), F32),
                pltpu.VMEM((parts, length, ATT_DIM), F32),
            ],
            flops=6 * per * (parts * length) ** 2 * ATT_DIM, name="att_attend",
        )
        start, att_done = lax.optimization_barrier((start, att_done))
    back = [
        pass_block(block, n) for n, block in enumerate(carry_states(True, start, *tails, *blocks))
    ]
    if dealt:
        att_back = {shares: pass_block(att_done[shares], shares)}
        held, back = lax.optimization_barrier((att_done, back))
        for n in [n for n in range(parts)[::-1] if n != shares]:
            att_back[n] = pass_block(held[n], n)
        att_out = call(
            unpack_kernel, (shape((length, att_width), BF16),) * 4,
            me, *[att_back[n] for n in range(parts)],
            specs=[SMEM] + [VMEM] * parts, vmem=SMALL, name="att_unpack",
        )

    gin, read_part, write_part = call(
        inner_kernel,
        (shape((length, width), F32), shape((length, 128), F32), shape((length, 128), F32)),
        dmixed, ssm_input, write_map, read_map, rel, lcol, lrow, state, name="ssm_inner",
    )
    input_grad, write_part = call(
        lambda *refs: last_kernel(shares, *refs),
        (shape((length, width), BF16), shape((length, 128), F32)),
        share, gin, ssm_input, write_map, rel, lcol, write_part, *back,
        specs=[SMEM] + [VMEM] * (6 + shares),
        scratch=[pltpu.VMEM((width, 128), BF16)], name="ssm_last",
    )
    write_sum, read_sum = lax.psum((write_part, read_part), "head")
    window_out, query_grad, key_grad, value_grad = att_out
    return (
        mixer_out,
        window_out,
        input_grad,
        gate_grad,
        write_sum.astype(BF16),
        read_sum.astype(BF16),
        query_grad,
        key_grad,
        value_grad,
    )


def solution(mesh):
    in_specs = (
        P("ctx", "head"),
        P("ctx", "head"),
        P("ctx", None),
        P("ctx", None),
        P("ctx", "head"),
        P("ctx"),
        P("ctx", "head"),
        P("ctx", "head"),
        P("ctx", "head"),
        P("ctx", "head"),
        P("ctx", "head"),
    )
    out_specs = (
        P("ctx", "head"),
        P("ctx", "head"),
        P("ctx", "head"),
        P("ctx", "head"),
        P("ctx", None),
        P("ctx", None),
        P("ctx", "head"),
        P("ctx", "head"),
        P("ctx", "head"),
    )
    return jax.shard_map(body, mesh=mesh, in_specs=in_specs, out_specs=out_specs, check_vma=False)
```

```python
import jax
import jax.numpy as jnp
from jax import lax
from jax.experimental import pallas as pl
from jax.experimental.pallas import tpu as pltpu
from jax.sharding import PartitionSpec as P

HEAD_DIM = 128
ATT_DIM = 128
WINDOW = 4096
EPSILON = 1e-05
LOG2E = 1.4426950408889634
TAIL = 16
MASKED = -1e30
HIGH = lax.Precision.HIGHEST
F32 = jnp.float32
BF16 = jnp.bfloat16
VMEM_BYTES = 56 * 1024 * 1024


VMEM = pl.BlockSpec(memory_space=pltpu.VMEM)
SMEM = pl.BlockSpec(memory_space=pltpu.SMEM)
SMALL = 16 * 1024 * 1024


def call(kernel, out_shape, *operands, specs=None, scratch=(), flops=0, vmem=VMEM_BYTES, name=None):
    moved = sum(a.size * a.dtype.itemsize for a in jax.tree.leaves((operands, out_shape)))
    return pl.pallas_call(
        kernel,
        out_shape=out_shape,
        in_specs=specs or [VMEM] * len(operands),
        out_specs=jax.tree.map(lambda _: VMEM, out_shape),
        scratch_shapes=scratch,
        compiler_params=pltpu.CompilerParams(vmem_limit_bytes=vmem),
        cost_estimate=pl.CostEstimate(flops=flops, bytes_accessed=moved, transcendentals=0),
        name=name,
    )(*operands)


def shape(dims, dtype):
    return jax.ShapeDtypeStruct(dims, dtype)


def dot(a, b):
    return jnp.dot(a, b, preferred_element_type=F32)


def dot_nt(a, b, precision=None):
    return lax.dot_general(
        a, b, (((1,), (1,)), ((), ())), preferred_element_type=F32, precision=precision
    )


def iota(dims, axis):
    return lax.broadcasted_iota(jnp.int32, dims, axis)


def flip(a):
    return a.astype(F32).T.astype(BF16)


def column(row):
    return jnp.broadcast_to(row, (128, row.shape[1])).T


def cols(h):
    return slice(h * HEAD_DIM, (h + 1) * HEAD_DIM)


def shifted_starts(me_ref, starts_ref):
    return starts_ref[...] - me_ref[0] * starts_ref.shape[1]


def deal(me_ref, held, out_refs):
    share = me_ref[0] & (len(out_refs) - 1)
    for n, out_ref in enumerate(out_refs):
        out_ref[...] = held[share ^ n]


def collect(me_ref, in_refs, held):
    share = me_ref[0] & (len(in_refs) - 1)
    for n, in_ref in enumerate(in_refs):
        held[share ^ n] = in_ref[...]


def gather_state(me_ref, in_refs, state_ref):
    rows = in_refs[0].shape[0]
    share = me_ref[0] & (len(in_refs) - 1)
    for n, in_ref in enumerate(in_refs):
        here = pl.ds(pl.multiple_of((share ^ n) * rows, rows), rows)
        state_ref[here, :] = in_ref[...]


def first_kernel(shares, me_ref, ld_ref, rel_ref, w_ref, x_ref, lcol_ref, lrow_ref, *refs):
    out_refs, out_ref = refs[:shares], refs[shares]
    heads, length = ld_ref.shape
    rel_row = shifted_starts(me_ref, rel_ref)
    parts, rows = out_ref.shape[0], out_ref.shape[1] - TAIL
    rates = ld_ref[...] * LOG2E
    lower = jnp.where(iota((length, length), 0) >= iota((length, length), 1), 1.0, 0.0)
    upper = jnp.where(iota((length, length), 0) <= iota((length, length), 1), 1.0, 0.0)
    lcol_ref[...] = dot_nt(lower, rates, HIGH)
    lrow = jnp.dot(rates, upper, preferred_element_type=F32, precision=HIGH)
    lrow_ref[...] = lrow
    rel_last = rel_row[:, length - 1 :]
    last_doc = iota((1, length), 1) >= rel_last
    keeps = rel_last < 0
    writes = w_ref[...].astype(F32).T
    tail_row = iota((TAIL, 128), 0)
    for h in range(heads):
        line = lrow[h : h + 1, :]
        total = line[:, length - 1 :]
        to_end = jnp.where(last_doc, jnp.exp2(total - line), 0.0)
        state = dot((writes * to_end).astype(BF16), x_ref[:, cols(h)]).astype(BF16)
        factor = jnp.where(keeps, jnp.exp2(total), 0.0)
        high = factor.astype(BF16).astype(F32)
        low = factor - high
        first = h * HEAD_DIM
        for part in range(first // rows, (first + HEAD_DIM - 1) // rows + 1):
            begin = max(first, part * rows)
            end = min(first + HEAD_DIM, (part + 1) * rows)
            out_ref[part, begin - part * rows : end - part * rows, :] = state[
                begin - first : end - first, :
            ]
            place = 2 * (begin - part * rows) // HEAD_DIM
            tail = jnp.where(tail_row == place, high, jnp.where(tail_row == place + 1, low, 0.0))
            if place:
                tail = tail + out_ref[part, rows:, :].astype(F32)
            out_ref[part, rows:, :] = tail.astype(BF16)
    deal(me_ref, out_ref, out_refs)


def carry(backward, start_ref, tails, held, total_ref, out):
    shares, rows = tails.shape[0], tails.shape[1] - TAIL
    step = min(rows, HEAD_DIM)
    for k in range(rows // step):
        here = slice(k * step, (k + 1) * step)
        state = jnp.zeros((step, 128), F32) if start_ref is None else start_ref[here, :].astype(F32)
        for c in range(shares)[:: -1 if backward else 1]:
            if out is not None:
                out[c, here, :] = state.astype(BF16)
            tail = tails[c, rows:, :].astype(F32)
            factor = tail[2 * k : 2 * k + 1, :] + tail[2 * k + 1 : 2 * k + 2, :]
            state = factor * state + held[c, here, :].astype(F32)
        if total_ref is not None:
            total_ref[here, :] = state.astype(BF16)


def total_kernel(backward, shares, me_ref, *refs):
    count = 2 if backward else 1
    in_refs, (total_ref, *held) = refs[: count * shares], refs[count * shares :]
    for n in range(count):
        collect(me_ref, in_refs[n * shares : (n + 1) * shares], held[n])
    carry(backward, None, held[0], held[-1], total_ref, None)


def carry_kernel(backward, shares, me_ref, start_ref, *refs):
    count = 2 if backward else 1
    in_refs, out_refs = refs[: count * shares], refs[count * shares : (count + 1) * shares]
    *held, out = refs[(count + 1) * shares :]
    for n in range(count):
        collect(me_ref, in_refs[n * shares : (n + 1) * shares], held[n])
    carry(backward, start_ref, held[0], held[-1], None, out)
    deal(me_ref, out, out_refs)


def mix_kernel(
    shares, me_ref, x_ref, gate_ref, grad_ref, w_ref, r_ref, rel_ref, lcol_ref, lrow_ref, *refs
):
    state_refs, (mixed_ref, sums_ref, s_ref) = refs[:shares], refs[shares:]
    gather_state(me_ref, state_refs, s_ref)
    length, heads = lcol_ref.shape
    reads = r_ref[...]
    rel = column(shifted_starts(me_ref, rel_ref).astype(F32))
    wide = jnp.concatenate([rel] * (length // 128), axis=1)
    seen = (iota((length, length), 1).astype(F32) >= wide) & (
        iota((length, length), 1) <= iota((length, length), 0)
    )
    scores = jnp.where(seen, dot_nt(reads, w_ref[...]), 0.0)
    squares = jnp.zeros((length, 128), F32)
    inners = jnp.zeros((length, 128), F32)
    for h in range(heads):
        lc = lcol_ref[:, h : h + 1]
        decay = jnp.exp2(jnp.minimum(lc - lrow_ref[h : h + 1, :], 0.0))
        enter = jnp.where(rel < 0, jnp.exp2(jnp.broadcast_to(lc, rel.shape)), 0.0)
        mixed = dot((scores * decay).astype(BF16), x_ref[:, cols(h)]) + enter * dot(
            reads, s_ref[cols(h), :]
        )
        mixed_ref[:, cols(h)] = mixed
        gate = gate_ref[:, cols(h)].astype(F32)
        gated = mixed * (gate / (1.0 + jnp.exp(-gate)))
        squares = squares + gated * gated
        inners = inners + grad_ref[:, cols(h)].astype(F32) * gated
    ones = jnp.ones((8, 128), F32)
    square_row = dot_nt(ones, squares, HIGH)
    inner_row = dot_nt(ones, inners, HIGH)
    sums_ref[...] = jnp.where(iota((8, length), 0) == 0, square_row, inner_row)


def gate_kernel(
    width, shares, me_ref, sums_ref, mixed_ref, gate_ref, grad_ref, r_ref, rel_ref, lrow_ref,
    mixer_ref, ggrad_ref, dmixed_ref, *refs,
):
    out_refs, out_ref = refs[:shares], refs[shares]
    length = mixed_ref.shape[0]
    heads = lrow_ref.shape[0]
    rows = out_ref.shape[1]
    scale = lax.rsqrt(sums_ref[0:1, :] / width + EPSILON)
    rms = column(scale)
    pull = column(scale * scale * scale * sums_ref[1:2, :] / width)
    reads = r_ref[...].astype(F32).T
    enters = shifted_starts(me_ref, rel_ref) < 0
    for h in range(heads):
        mixed = mixed_ref[:, cols(h)]
        gate = gate_ref[:, cols(h)].astype(F32)
        sigma = 1.0 / (1.0 + jnp.exp(-gate))
        swish = gate * sigma
        gated = mixed * swish
        mixer_ref[:, cols(h)] = (gated * rms).astype(BF16)
        dgated = rms * grad_ref[:, cols(h)].astype(F32) - pull * gated
        dmixed = (dgated * swish).astype(BF16)
        dmixed_ref[:, cols(h)] = dmixed
        ggrad_ref[:, cols(h)] = (
            dgated * mixed * sigma * (1.0 + gate * (1.0 - sigma))
        ).astype(BF16)
        enter = jnp.where(enters, jnp.exp2(lrow_ref[h : h + 1, :]), 0.0)
        state = dot((reads * enter).astype(BF16), dmixed).astype(BF16)
        first = h * HEAD_DIM
        for part in range(first // rows, (first + HEAD_DIM - 1) // rows + 1):
            begin = max(first, part * rows)
            end = min(first + HEAD_DIM, (part + 1) * rows)
            out_ref[part, begin - part * rows : end - part * rows, :] = state[
                begin - first : end - first, :
            ]
    deal(me_ref, out_ref, out_refs)


def inner_kernel(
    me_ref, dmixed_ref, x_ref, w_ref, r_ref, rel_ref, lcol_ref, lrow_ref, s_ref, gin_ref, read_ref, write_ref
):
    length, heads = lcol_ref.shape
    rel_row = shifted_starts(me_ref, rel_ref)
    rel = column(rel_row.astype(F32))
    seen = (iota((length, length), 0) >= rel_row) & (
        iota((length, length), 0) <= iota((length, length), 1)
    )
    scores = jnp.where(seen, dot_nt(w_ref[...], r_ref[...]), 0.0)
    total = jnp.zeros((length, length), F32)
    read = jnp.zeros((length, 128), F32)
    for h in range(heads):
        lc = lcol_ref[:, h : h + 1]
        decay = jnp.exp2(jnp.minimum(lrow_ref[h : h + 1, :] - lc, 0.0))
        dmixed = dmixed_ref[:, cols(h)]
        gin_ref[:, cols(h)] = dot((scores * decay).astype(BF16), dmixed)
        total = total + decay * dot_nt(x_ref[:, cols(h)], dmixed)
        enter = jnp.where(rel < 0, jnp.exp2(jnp.broadcast_to(lc, rel.shape)), 0.0)
        read = read + enter * dot_nt(dmixed, s_ref[cols(h), :])
    total = jnp.where(seen, total, 0.0)
    write_ref[...] = dot(total.astype(BF16), r_ref[...])
    read_ref[...] = read + dot(total.T.astype(BF16), w_ref[...])


def last_kernel(shares, me_ref, gin_ref, x_ref, w_ref, rel_ref, lcol_ref, part_ref, *refs):
    state_refs, (out_ref, write_ref, back_ref) = refs[:shares], refs[shares:]
    gather_state(me_ref, state_refs, back_ref)
    length, heads = lcol_ref.shape
    rel_last = shifted_starts(me_ref, rel_ref)[:, length - 1 :]
    last_doc = iota((length, 128), 0) >= rel_last
    writes = w_ref[...]
    write = part_ref[...]
    for h in range(heads):
        lc = lcol_ref[:, h : h + 1]
        line = jnp.broadcast_to(lc[length - 1 :, :] - lc, (length, 128))
        to_end = jnp.where(last_doc, jnp.exp2(line), 0.0)
        back = back_ref[cols(h), :]
        out_ref[:, cols(h)] = (gin_ref[:, cols(h)] + to_end * dot(writes, back)).astype(BF16)
        write = write + to_end * dot_nt(x_ref[:, cols(h)], back)
    write_ref[...] = write


def pass_block(block, n):
    if n == 0:
        return block
    return lax.ppermute(block, "ctx", [(i, i ^ n) for i in range(lax.axis_size("ctx"))])


def cross(total, backward):
    count = lax.axis_size("ctx")
    half = count // 2
    pairs = [(i + half, i) if backward else (i, i + half) for i in range(half)]
    return lax.ppermute(total, "ctx", pairs)


def pack_kernel(me_ref, marks_ref, q_ref, k_ref, v_ref, g_ref, *out_refs):
    length = q_ref.shape[0]
    for n, out_ref in enumerate(out_refs):
        for a in range(out_ref.shape[0]):
            head = (me_ref[0] ^ n) * out_ref.shape[0] + a
            here = pl.ds(pl.multiple_of(head * ATT_DIM, ATT_DIM), ATT_DIM)
            for place, ref in enumerate((q_ref, k_ref, v_ref, g_ref)):
                out_ref[a, place * length : (place + 1) * length, :] = ref[:, here]
            out_ref[a, 4 * length :, :] = marks_ref[...]


def unpack_kernel(me_ref, *refs):
    in_refs, out_refs = refs[:-4], refs[-4:]
    length = out_refs[0].shape[0]
    for n, in_ref in enumerate(in_refs):
        for a in range(in_ref.shape[0]):
            head = (me_ref[0] ^ n) * in_ref.shape[0] + a
            here = pl.ds(pl.multiple_of(head * ATT_DIM, ATT_DIM), ATT_DIM)
            for place, ref in enumerate(out_refs):
                ref[:, here] = in_ref[a, place * length : (place + 1) * length, :]


def attend_blocks(length, parts, me_ref, *refs):
    in_refs, out_refs = refs[:parts], refs[parts : 2 * parts]
    all_in, all_out = refs[2 * parts : 2 * parts + 2]
    for n in range(parts):
        all_in[me_ref[0] ^ n] = in_refs[n][...]
    attend_kernel(length, all_in, all_out, *refs[2 * parts + 2 :])
    for n in range(parts):
        out_refs[n][...] = all_out[me_ref[0] ^ n]


def attend_kernel(length, in_ref, out_ref, expo_ref, kt_ref, vt_ref, dk_ref, dv_ref):
    parts = in_ref.shape[0]
    scale = ATT_DIM ** (-0.5)
    rate = scale * LOG2E
    key_in = iota((length, length), 0)
    causal = key_in <= iota((length, length), 1)
    for a in range(in_ref.shape[1]):

        def piece(block, place):
            return in_ref[block, a, place * length : (place + 1) * length, :]

        for i in range(parts):
            kt_ref[i] = flip(piece(i, 1))
            vt_ref[i] = flip(piece(i, 2))
            queries, grads = piece(i, 0), piece(i, 3)
            marks = in_ref[i, a, 4 * length :, :].astype(F32)
            starts = jnp.concatenate(
                [
                    marks[2 * n : 2 * n + 1] * 128.0 + marks[2 * n + 1 : 2 * n + 2]
                    for n in range(length // 128)
                ],
                axis=1,
            ).astype(jnp.int32)
            query_at = i * length + iota((1, length), 1)
            if parts * length > WINDOW:
                starts = jnp.maximum(starts, query_at - (WINDOW - 1))
            top = jnp.full((1, length), MASKED, F32)
            total = jnp.zeros((1, length), F32)
            tops = []
            for j in range(i + 1):
                seen = key_in >= starts - j * length
                if j == i:
                    seen = seen & causal
                raw = jnp.where(seen, dot_nt(piece(j, 1), queries), MASKED)
                new = jnp.maximum(top, jnp.max(raw, axis=0, keepdims=True))
                expo = jnp.exp2((raw - new) * rate)
                expo_ref[j] = expo
                total = total * jnp.exp2((top - new) * rate) + jnp.sum(expo, axis=0, keepdims=True)
                top = new
                tops.append(new)
            out = jnp.zeros((ATT_DIM, length), F32)
            for j in range(i + 1):
                probs = expo_ref[j] * (jnp.exp2((tops[j] - top) * rate) / total)
                expo_ref[j] = probs
                weights = probs.astype(BF16)
                dvalue = dot(weights, grads)
                dv_ref[j] = dvalue if j == i else dv_ref[j] + dvalue
                out = out + dot(vt_ref[j], weights)
            delta = jnp.sum(out * grads.astype(F32).T, axis=0, keepdims=True)
            dquery = jnp.zeros((ATT_DIM, length), F32)
            for j in range(i + 1):
                dprobs = dot_nt(piece(j, 2), grads)
                dscore = (expo_ref[j] * ((dprobs - delta) * scale)).astype(BF16)
                dkey = dot(dscore, queries)
                dk_ref[j] = dkey if j == i else dk_ref[j] + dkey
                dquery = dquery + dot(kt_ref[j], dscore)
            out_ref[i, a, 0:length, :] = out.T.astype(BF16)
            out_ref[i, a, length : 2 * length, :] = dquery.T.astype(BF16)
        for j in range(parts):
            out_ref[j, a, 2 * length : 3 * length, :] = dk_ref[j].astype(BF16)
            out_ref[j, a, 3 * length :, :] = dv_ref[j].astype(BF16)


def shifted(shard, axis, by):
    devices = lax.axis_size(axis)
    pairs = [(i, i + by) for i in range(devices) if 0 <= i + by < devices]
    return lax.ppermute(shard, axis, pairs)


def head_cols(array, head_index):
    return lax.dynamic_slice_in_dim(array, head_index * ATT_DIM, ATT_DIM, 1)


def ring_attention(att_queries, att_keys, att_values, att_grad, doc_start):
    length = att_queries.shape[0]
    shard_index = lax.axis_index("ctx")
    halo_shards = WINDOW // length
    att_count = att_queries.shape[1] // ATT_DIM
    att_width = att_queries.shape[1]
    score_scale = ATT_DIM ** (-0.5)

    def pass_keys(running, unused):
        moved = shifted((running[0], running[1]), "ctx", 1)
        return (moved, moved)

    _, earlier = lax.scan(pass_keys, (att_keys, att_values), None, length=halo_shards)
    key_all = jnp.concatenate(
        [earlier[0][::-1].reshape(halo_shards * length, att_width), att_keys], axis=0
    )
    value_all = jnp.concatenate(
        [earlier[1][::-1].reshape(halo_shards * length, att_width), att_values], axis=0
    )
    spread_rows = (halo_shards + 1) * length
    query_pos = shard_index * length + jnp.arange(length, dtype=jnp.int32)
    key_pos = (shard_index - halo_shards) * length + jnp.arange(spread_rows, dtype=jnp.int32)
    visible = (
        (key_pos[None, :] <= query_pos[:, None])
        & (query_pos[:, None] - key_pos[None, :] < WINDOW)
        & (key_pos[None, :] >= doc_start[:, None])
    )

    def forward_head(head_index, running):
        out_buf, max_buf, total_buf, delta_buf = running
        query_head = head_cols(att_queries, head_index)
        key_head = head_cols(key_all, head_index)
        value_head = head_cols(value_all, head_index)
        score = (
            jnp.einsum("td,sd->ts", query_head, key_head, preferred_element_type=jnp.float32)
            * score_scale
        )
        row_max = jnp.max(jnp.where(visible, score, -jnp.inf), axis=1)
        expo = jnp.where(visible, jnp.exp(score - row_max[:, None]), 0.0)
        row_total = jnp.sum(expo, axis=1)
        weights = (expo / row_total[:, None]).astype(jnp.bfloat16)
        attended = jnp.dot(weights, value_head, preferred_element_type=jnp.float32)
        delta = jnp.sum(head_cols(att_grad, head_index).astype(jnp.float32) * attended, axis=1)
        out_buf = lax.dynamic_update_slice_in_dim(
            out_buf, attended.astype(jnp.bfloat16), head_index * ATT_DIM, 1
        )
        return (
            out_buf,
            max_buf.at[:, head_index].set(row_max),
            total_buf.at[:, head_index].set(row_total),
            delta_buf.at[:, head_index].set(delta),
        )

    stats_zero = jnp.zeros((length, att_count), jnp.float32)
    window_out, row_maxes, row_totals, row_deltas = lax.fori_loop(
        0,
        att_count,
        forward_head,
        (jnp.zeros((length, att_width), jnp.bfloat16), stats_zero, stats_zero, stats_zero),
    )

    def query_terms(head_index):
        query_head = head_cols(att_queries, head_index)
        key_head = head_cols(key_all, head_index)
        value_head = head_cols(value_all, head_index)
        grad_head = head_cols(att_grad, head_index)
        score = (
            jnp.einsum("td,sd->ts", query_head, key_head, preferred_element_type=jnp.float32)
            * score_scale
        )
        probs = (
            jnp.where(visible, jnp.exp(score - row_maxes[:, head_index][:, None]), 0.0)
            / row_totals[:, head_index][:, None]
        )
        weights = probs.astype(jnp.bfloat16)
        dprobs = jnp.einsum("td,sd->ts", grad_head, value_head, preferred_element_type=jnp.float32)
        dscore = (probs * (dprobs - row_deltas[:, head_index][:, None]) * score_scale).astype(
            jnp.bfloat16
        )
        query_part = jnp.dot(dscore, key_head, preferred_element_type=jnp.float32)
        return (query_head, grad_head, weights, dscore, query_part)

    def backward_head(head_index, running):
        query_buf, key_buf, value_buf = running
        query_head, grad_head, weights, dscore, query_part = query_terms(head_index)
        key_part = jnp.einsum("ts,td->sd", dscore, query_head, preferred_element_type=jnp.float32)
        value_part = jnp.einsum("ts,td->sd", weights, grad_head, preferred_element_type=jnp.float32)
        query_buf = lax.dynamic_update_slice_in_dim(query_buf, query_part, head_index * ATT_DIM, 1)
        key_buf = lax.dynamic_update_slice_in_dim(key_buf, key_part, head_index * ATT_DIM, 1)
        value_buf = lax.dynamic_update_slice_in_dim(value_buf, value_part, head_index * ATT_DIM, 1)
        return (query_buf, key_buf, value_buf)

    part_zero = jnp.zeros((spread_rows, att_width), jnp.float32)
    query_sum, key_parts, value_parts = lax.fori_loop(
        0,
        att_count,
        backward_head,
        (jnp.zeros((length, att_width), jnp.float32), part_zero, part_zero),
    )
    key_blocks = key_parts.reshape(halo_shards + 1, length, att_width)
    value_blocks = value_parts.reshape(halo_shards + 1, length, att_width)

    def send_back(running, block_index):
        moved = shifted((running[0], running[1]), "ctx", -1)
        return ((moved[0] + key_blocks[block_index], moved[1] + value_blocks[block_index]), None)

    (key_sum, value_sum), _ = lax.scan(
        send_back, (key_blocks[0], value_blocks[0]), jnp.arange(1, halo_shards + 1, dtype=jnp.int32)
    )
    return (
        window_out,
        query_sum.astype(jnp.bfloat16),
        key_sum.astype(jnp.bfloat16),
        value_sum.astype(jnp.bfloat16),
    )


def body(
    ssm_input,
    gate_input,
    write_map,
    read_map,
    log_decay,
    doc_start,
    ssm_grad,
    att_queries,
    att_keys,
    att_values,
    att_grad,
):
    length, width = ssm_input.shape
    heads = width // HEAD_DIM
    parts = lax.axis_size("ctx")
    shares = parts // 2
    rows = width // shares
    full_width = width * lax.axis_size("head")
    att_width = att_queries.shape[1]
    per = att_width // ATT_DIM // parts
    dealt = att_width // ATT_DIM % parts == 0
    place = lax.axis_index("ctx")
    starts = doc_start.reshape(1, length)
    me = place.reshape(1).astype(jnp.int32)
    tailed = [shape((rows + TAIL, 128), BF16)] * shares
    plain = [shape((rows, 128), BF16)] * shares
    held_tails = pltpu.VMEM((shares, rows + TAIL, 128), BF16)
    held_plain = pltpu.VMEM((shares, rows, 128), BF16)

    def carry_total(backward, *blocks):
        return call(
            lambda *refs: total_kernel(backward, shares, *refs),
            shape((rows, 128), BF16), me, *blocks,
            specs=[SMEM] + [VMEM] * len(blocks),
            scratch=[held_tails, held_plain] if backward else [held_tails],
            vmem=SMALL, name="ssm_total",
        )

    def carry_states(backward, start, *blocks):
        return call(
            lambda *refs: carry_kernel(backward, shares, *refs),
            plain, me, start, *blocks,
            specs=[SMEM] + [VMEM] * (1 + len(blocks)),
            scratch=[held_tails, held_plain, held_plain] if backward else [held_tails, held_plain],
            vmem=SMALL, name="ssm_carry",
        )

    lcol, lrow, *sent = call(
        lambda *refs: first_kernel(shares, *refs),
        [shape((length, heads), F32), shape((heads, length), F32)] + tailed,
        me, log_decay.T, starts, write_map, ssm_input,
        specs=[SMEM] + [VMEM] * 4, scratch=[held_tails], name="ssm_first",
    )
    tails = [pass_block(block, n) for n, block in enumerate(sent)]
    if dealt:
        marks = doc_start.reshape(length // 128, 128)
        marks = jnp.stack([marks // 128, marks % 128], axis=1).reshape(length // 64, 128)
        marks = jnp.pad(marks, ((0, TAIL - length // 64), (0, 0))).astype(BF16)
        marks, tails[1] = lax.optimization_barrier((marks, tails[1]))
        packed = call(
            pack_kernel, [shape((per, 4 * length + TAIL, 128), BF16)] * parts,
            me, marks, att_queries, att_keys, att_values, att_grad,
            specs=[SMEM] + [VMEM] * 5, vmem=SMALL, name="att_pack",
        )
        packed = list(packed)
        att_got = {0: packed[0]}
        att_got[shares] = pass_block(packed[shares], shares)
    else:
        att_out = ring_attention(att_queries, att_keys, att_values, att_grad, doc_start)
    total = carry_total(False, *tails)
    if dealt:
        total, att_got[shares] = lax.optimization_barrier((total, att_got[shares]))
    start = cross(total, False)
    if dealt:
        start, packed[shares + 1] = lax.optimization_barrier((start, packed[shares + 1]))
        att_got[shares + 1] = pass_block(packed[shares + 1], shares + 1)
    state = [
        pass_block(block, n) for n, block in enumerate(carry_states(False, start, *tails))
    ]
    if dealt:
        rest = [n for n in range(1, parts) if n not in att_got]
        rest = [n for n in rest if n > shares] + [n for n in rest if n < shares]
        held, att_got[shares + 1], state = lax.optimization_barrier(
            ([packed[n] for n in rest], att_got[shares + 1], state)
        )
        for n, block in zip(rest, held):
            att_got[n] = pass_block(block, n)
    mixed, sums, state = call(
        lambda *refs: mix_kernel(shares, *refs),
        (shape((length, width), F32), shape((8, length), F32), shape((width, 128), BF16)),
        me, ssm_input, gate_input, ssm_grad, write_map, read_map, starts, lcol, lrow, *state,
        specs=[SMEM] + [VMEM] * (8 + shares), name="ssm_mix",
    )
    sums = lax.psum(sums, "head")
    mixer_out, gate_grad, dmixed, *sent = call(
        lambda *refs: gate_kernel(full_width, shares, *refs),
        [shape((length, width), BF16)] * 3 + plain,
        me, sums, mixed, gate_input, ssm_grad, read_map, starts, lrow,
        specs=[SMEM] + [VMEM] * 7, scratch=[held_plain], name="ssm_gate",
    )

    if dealt:
        done, sent = lax.optimization_barrier(([att_got[n] for n in rest], sent))
        att_got.update(zip(rest, done))
    blocks = [pass_block(block, n) for n, block in enumerate(sent)]
    total = carry_total(True, *tails, *blocks)
    start = cross(total, True)
    if dealt:
        att_in, total = lax.optimization_barrier(([att_got[n] for n in range(parts)], total))
        att_done = call(
            lambda *refs: attend_blocks(length, parts, *refs),
            [shape((per, 4 * length, 128), BF16)] * parts, me, *att_in,
            specs=[SMEM] + [VMEM] * parts,
            scratch=[
                pltpu.VMEM((parts, per, 4 * length + TAIL, 128), BF16),
                pltpu.VMEM((parts, per, 4 * length, 128), BF16),
                pltpu.VMEM((parts, length, length), F32),
                pltpu.VMEM((parts, ATT_DIM, length), BF16),
                pltpu.VMEM((parts, ATT_DIM, length), BF16),
                pltpu.VMEM((parts, length, ATT_DIM), F32),
                pltpu.VMEM((parts, length, ATT_DIM), F32),
            ],
            flops=6 * per * (parts * length) ** 2 * ATT_DIM, name="att_attend",
        )
        start, att_done = lax.optimization_barrier((start, att_done))
    back = [
        pass_block(block, n) for n, block in enumerate(carry_states(True, start, *tails, *blocks))
    ]
    if dealt:
        att_back = {shares: pass_block(att_done[shares], shares)}
        held, back = lax.optimization_barrier((att_done, back))
        for n in [n for n in range(parts)[::-1] if n != shares]:
            att_back[n] = pass_block(held[n], n)
        att_out = call(
            unpack_kernel, (shape((length, att_width), BF16),) * 4,
            me, *[att_back[n] for n in range(parts)],
            specs=[SMEM] + [VMEM] * parts, vmem=SMALL, name="att_unpack",
        )

    gin, read_part, write_part = call(
        inner_kernel,
        (shape((length, width), F32), shape((length, 128), F32), shape((length, 128), F32)),
        me, dmixed, ssm_input, write_map, read_map, starts, lcol, lrow, state,
        specs=[SMEM] + [VMEM] * 8, name="ssm_inner",
    )
    input_grad, write_part = call(
        lambda *refs: last_kernel(shares, *refs),
        (shape((length, width), BF16), shape((length, 128), F32)),
        me, gin, ssm_input, write_map, starts, lcol, write_part, *back,
        specs=[SMEM] + [VMEM] * (6 + shares),
        scratch=[pltpu.VMEM((width, 128), BF16)], name="ssm_last",
    )
    write_sum, read_sum = lax.psum((write_part, read_part), "head")
    window_out, query_grad, key_grad, value_grad = att_out
    return (
        mixer_out,
        window_out,
        input_grad,
        gate_grad,
        write_sum.astype(BF16),
        read_sum.astype(BF16),
        query_grad,
        key_grad,
        value_grad,
    )


def solution(mesh):
    in_specs = (
        P("ctx", "head"),
        P("ctx", "head"),
        P("ctx", None),
        P("ctx", None),
        P("ctx", "head"),
        P("ctx"),
        P("ctx", "head"),
        P("ctx", "head"),
        P("ctx", "head"),
        P("ctx", "head"),
        P("ctx", "head"),
    )
    out_specs = (
        P("ctx", "head"),
        P("ctx", "head"),
        P("ctx", "head"),
        P("ctx", "head"),
        P("ctx", None),
        P("ctx", None),
        P("ctx", "head"),
        P("ctx", "head"),
        P("ctx", "head"),
    )
    return jax.shard_map(body, mesh=mesh, in_specs=in_specs, out_specs=out_specs, check_vma=False)
```

```python
import jax
import jax.numpy as jnp
from jax import lax
from jax.experimental import pallas as pl
from jax.experimental.pallas import tpu as pltpu
from jax.sharding import PartitionSpec as P

HEAD_DIM = 128
ATT_DIM = 128
WINDOW = 4096
EPSILON = 1e-05
LOG2E = 1.4426950408889634
TAIL = 16
MASKED = -1e30
HIGH = lax.Precision.HIGHEST
F32 = jnp.float32
BF16 = jnp.bfloat16
VMEM_BYTES = 56 * 1024 * 1024


VMEM = pl.BlockSpec(memory_space=pltpu.VMEM)
SMEM = pl.BlockSpec(memory_space=pltpu.SMEM)
SMALL = 16 * 1024 * 1024


def call(kernel, out_shape, *operands, specs=None, scratch=(), flops=0, vmem=VMEM_BYTES, name=None):
    moved = sum(a.size * a.dtype.itemsize for a in jax.tree.leaves((operands, out_shape)))
    return pl.pallas_call(
        kernel,
        out_shape=out_shape,
        in_specs=specs or [VMEM] * len(operands),
        out_specs=jax.tree.map(lambda _: VMEM, out_shape),
        scratch_shapes=scratch,
        compiler_params=pltpu.CompilerParams(vmem_limit_bytes=vmem),
        cost_estimate=pl.CostEstimate(flops=flops, bytes_accessed=moved, transcendentals=0),
        name=name,
    )(*operands)


def shape(dims, dtype):
    return jax.ShapeDtypeStruct(dims, dtype)


def dot(a, b):
    return jnp.dot(a, b, preferred_element_type=F32)


def dot_nt(a, b, precision=None):
    return lax.dot_general(
        a, b, (((1,), (1,)), ((), ())), preferred_element_type=F32, precision=precision
    )


def iota(dims, axis):
    return lax.broadcasted_iota(jnp.int32, dims, axis)


def flip(a):
    return a.astype(F32).T.astype(BF16)


def column(row):
    return jnp.broadcast_to(row, (128, row.shape[1])).T


def cols(h):
    return slice(h * HEAD_DIM, (h + 1) * HEAD_DIM)


def shifted_starts(me_ref, starts_ref):
    return starts_ref[...] - me_ref[0] * starts_ref.shape[1]


def deal(me_ref, held, out_refs):
    share = me_ref[0] & (len(out_refs) - 1)
    for n, out_ref in enumerate(out_refs):
        out_ref[...] = held[share ^ n]


def collect(me_ref, in_refs, held):
    share = me_ref[0] & (len(in_refs) - 1)
    for n, in_ref in enumerate(in_refs):
        held[share ^ n] = in_ref[...]


def gather_state(me_ref, in_refs, state_ref):
    rows = in_refs[0].shape[0]
    share = me_ref[0] & (len(in_refs) - 1)
    for n, in_ref in enumerate(in_refs):
        here = pl.ds(pl.multiple_of((share ^ n) * rows, rows), rows)
        state_ref[here, :] = in_ref[...]


def first_kernel(shares, me_ref, ld_ref, rel_ref, w_ref, x_ref, lcol_ref, lrow_ref, *refs):
    out_refs, out_ref = refs[:shares], refs[shares]
    heads, length = ld_ref.shape
    rel_row = shifted_starts(me_ref, rel_ref)
    parts, rows = out_ref.shape[0], out_ref.shape[1] - TAIL
    rates = ld_ref[...] * LOG2E
    lower = jnp.where(iota((length, length), 0) >= iota((length, length), 1), 1.0, 0.0)
    upper = jnp.where(iota((length, length), 0) <= iota((length, length), 1), 1.0, 0.0)
    lcol_ref[...] = dot_nt(lower, rates, HIGH)
    lrow = jnp.dot(rates, upper, preferred_element_type=F32, precision=HIGH)
    lrow_ref[...] = lrow
    rel_last = rel_row[:, length - 1 :]
    last_doc = iota((1, length), 1) >= rel_last
    keeps = rel_last < 0
    writes = w_ref[...].astype(F32).T
    tail_row = iota((TAIL, 128), 0)
    for h in range(heads):
        line = lrow[h : h + 1, :]
        total = line[:, length - 1 :]
        to_end = jnp.where(last_doc, jnp.exp2(total - line), 0.0)
        state = dot((writes * to_end).astype(BF16), x_ref[:, cols(h)]).astype(BF16)
        factor = jnp.where(keeps, jnp.exp2(total), 0.0)
        high = factor.astype(BF16).astype(F32)
        low = factor - high
        first = h * HEAD_DIM
        for part in range(first // rows, (first + HEAD_DIM - 1) // rows + 1):
            begin = max(first, part * rows)
            end = min(first + HEAD_DIM, (part + 1) * rows)
            out_ref[part, begin - part * rows : end - part * rows, :] = state[
                begin - first : end - first, :
            ]
            place = 2 * (begin - part * rows) // HEAD_DIM
            tail = jnp.where(tail_row == place, high, jnp.where(tail_row == place + 1, low, 0.0))
            if place:
                tail = tail + out_ref[part, rows:, :].astype(F32)
            out_ref[part, rows:, :] = tail.astype(BF16)
    deal(me_ref, out_ref, out_refs)


def carry(backward, start_ref, tails, held, total_ref, out):
    shares, rows = tails.shape[0], tails.shape[1] - TAIL
    step = min(rows, HEAD_DIM)
    for k in range(rows // step):
        here = slice(k * step, (k + 1) * step)
        state = jnp.zeros((step, 128), F32) if start_ref is None else start_ref[here, :].astype(F32)
        for c in range(shares)[:: -1 if backward else 1]:
            if out is not None:
                out[c, here, :] = state.astype(BF16)
            tail = tails[c, rows:, :].astype(F32)
            factor = tail[2 * k : 2 * k + 1, :] + tail[2 * k + 1 : 2 * k + 2, :]
            state = factor * state + held[c, here, :].astype(F32)
        if total_ref is not None:
            total_ref[here, :] = state.astype(BF16)


def total_kernel(backward, shares, me_ref, *refs):
    count = 2 if backward else 1
    in_refs, (total_ref, *held) = refs[: count * shares], refs[count * shares :]
    for n in range(count):
        collect(me_ref, in_refs[n * shares : (n + 1) * shares], held[n])
    carry(backward, None, held[0], held[-1], total_ref, None)


def carry_kernel(backward, shares, me_ref, start_ref, *refs):
    count = 2 if backward else 1
    in_refs, out_refs = refs[: count * shares], refs[count * shares : (count + 1) * shares]
    *held, out = refs[(count + 1) * shares :]
    for n in range(count):
        collect(me_ref, in_refs[n * shares : (n + 1) * shares], held[n])
    carry(backward, start_ref, held[0], held[-1], None, out)
    deal(me_ref, out, out_refs)


def mix_kernel(
    shares, me_ref, x_ref, gate_ref, grad_ref, w_ref, r_ref, rel_ref, lcol_ref, lrow_ref, *refs
):
    state_refs, (mixed_ref, sums_ref, s_ref) = refs[:shares], refs[shares:]
    gather_state(me_ref, state_refs, s_ref)
    length, heads = lcol_ref.shape
    reads = r_ref[...]
    rel = column(shifted_starts(me_ref, rel_ref).astype(F32))
    wide = jnp.concatenate([rel] * (length // 128), axis=1)
    seen = (iota((length, length), 1).astype(F32) >= wide) & (
        iota((length, length), 1) <= iota((length, length), 0)
    )
    scores = jnp.where(seen, dot_nt(reads, w_ref[...]), 0.0)
    squares = jnp.zeros((length, 128), F32)
    inners = jnp.zeros((length, 128), F32)
    for h in range(heads):
        lc = lcol_ref[:, h : h + 1]
        decay = jnp.exp2(jnp.minimum(lc - lrow_ref[h : h + 1, :], 0.0))
        enter = jnp.where(rel < 0, jnp.exp2(jnp.broadcast_to(lc, rel.shape)), 0.0)
        mixed = dot((scores * decay).astype(BF16), x_ref[:, cols(h)]) + enter * dot(
            reads, s_ref[cols(h), :]
        )
        mixed_ref[:, cols(h)] = mixed
        gate = gate_ref[:, cols(h)].astype(F32)
        gated = mixed * (gate / (1.0 + jnp.exp(-gate)))
        squares = squares + gated * gated
        inners = inners + grad_ref[:, cols(h)].astype(F32) * gated
    ones = jnp.ones((8, 128), F32)
    square_row = dot_nt(ones, squares, HIGH)
    inner_row = dot_nt(ones, inners, HIGH)
    sums_ref[...] = jnp.where(iota((8, length), 0) == 0, square_row, inner_row)


def gate_kernel(
    width, shares, me_ref, sums_ref, mixed_ref, gate_ref, grad_ref, r_ref, rel_ref, lrow_ref,
    mixer_ref, ggrad_ref, dmixed_ref, *refs,
):
    out_refs, out_ref = refs[:shares], refs[shares]
    length = mixed_ref.shape[0]
    heads = lrow_ref.shape[0]
    rows = out_ref.shape[1]
    scale = lax.rsqrt(sums_ref[0:1, :] / width + EPSILON)
    rms = column(scale)
    pull = column(scale * scale * scale * sums_ref[1:2, :] / width)
    reads = r_ref[...].astype(F32).T
    enters = shifted_starts(me_ref, rel_ref) < 0
    for h in range(heads):
        mixed = mixed_ref[:, cols(h)]
        gate = gate_ref[:, cols(h)].astype(F32)
        sigma = 1.0 / (1.0 + jnp.exp(-gate))
        swish = gate * sigma
        gated = mixed * swish
        mixer_ref[:, cols(h)] = (gated * rms).astype(BF16)
        dgated = rms * grad_ref[:, cols(h)].astype(F32) - pull * gated
        dmixed = (dgated * swish).astype(BF16)
        dmixed_ref[:, cols(h)] = dmixed
        ggrad_ref[:, cols(h)] = (
            dgated * mixed * sigma * (1.0 + gate * (1.0 - sigma))
        ).astype(BF16)
        enter = jnp.where(enters, jnp.exp2(lrow_ref[h : h + 1, :]), 0.0)
        state = dot((reads * enter).astype(BF16), dmixed).astype(BF16)
        first = h * HEAD_DIM
        for part in range(first // rows, (first + HEAD_DIM - 1) // rows + 1):
            begin = max(first, part * rows)
            end = min(first + HEAD_DIM, (part + 1) * rows)
            out_ref[part, begin - part * rows : end - part * rows, :] = state[
                begin - first : end - first, :
            ]
    deal(me_ref, out_ref, out_refs)


def inner_kernel(
    me_ref, dmixed_ref, x_ref, w_ref, r_ref, rel_ref, lcol_ref, lrow_ref, s_ref, gin_ref, read_ref, write_ref
):
    length, heads = lcol_ref.shape
    rel_row = shifted_starts(me_ref, rel_ref)
    rel = column(rel_row.astype(F32))
    seen = (iota((length, length), 0) >= rel_row) & (
        iota((length, length), 0) <= iota((length, length), 1)
    )
    scores = jnp.where(seen, dot_nt(w_ref[...], r_ref[...]), 0.0)
    total = jnp.zeros((length, length), F32)
    read = jnp.zeros((length, 128), F32)
    for h in range(heads):
        lc = lcol_ref[:, h : h + 1]
        decay = jnp.exp2(jnp.minimum(lrow_ref[h : h + 1, :] - lc, 0.0))
        dmixed = dmixed_ref[:, cols(h)]
        gin_ref[:, cols(h)] = dot((scores * decay).astype(BF16), dmixed)
        total = total + decay * dot_nt(x_ref[:, cols(h)], dmixed)
        enter = jnp.where(rel < 0, jnp.exp2(jnp.broadcast_to(lc, rel.shape)), 0.0)
        read = read + enter * dot_nt(dmixed, s_ref[cols(h), :])
    total = jnp.where(seen, total, 0.0)
    write_ref[...] = dot(total.astype(BF16), r_ref[...])
    read_ref[...] = read + dot(total.T.astype(BF16), w_ref[...])


def last_kernel(shares, me_ref, gin_ref, x_ref, w_ref, rel_ref, lcol_ref, part_ref, *refs):
    state_refs, (out_ref, write_ref, back_ref) = refs[:shares], refs[shares:]
    gather_state(me_ref, state_refs, back_ref)
    length, heads = lcol_ref.shape
    rel_last = shifted_starts(me_ref, rel_ref)[:, length - 1 :]
    last_doc = iota((length, 128), 0) >= rel_last
    writes = w_ref[...]
    write = part_ref[...]
    for h in range(heads):
        lc = lcol_ref[:, h : h + 1]
        line = jnp.broadcast_to(lc[length - 1 :, :] - lc, (length, 128))
        to_end = jnp.where(last_doc, jnp.exp2(line), 0.0)
        back = back_ref[cols(h), :]
        out_ref[:, cols(h)] = (gin_ref[:, cols(h)] + to_end * dot(writes, back)).astype(BF16)
        write = write + to_end * dot_nt(x_ref[:, cols(h)], back)
    write_ref[...] = write


def pass_block(block, n):
    if n == 0:
        return block
    return lax.ppermute(block, "ctx", [(i, i ^ n) for i in range(lax.axis_size("ctx"))])


def cross(total, backward):
    count = lax.axis_size("ctx")
    half = count // 2
    pairs = [(i + half, i) if backward else (i, i + half) for i in range(half)]
    return lax.ppermute(total, "ctx", pairs)


def pack_kernel(me_ref, marks_ref, q_ref, k_ref, v_ref, g_ref, *out_refs):
    length = q_ref.shape[0]
    for n, out_ref in enumerate(out_refs):
        for a in range(out_ref.shape[0]):
            head = (me_ref[0] ^ n) * out_ref.shape[0] + a
            here = pl.ds(pl.multiple_of(head * ATT_DIM, ATT_DIM), ATT_DIM)
            for place, ref in enumerate((q_ref, k_ref, v_ref, g_ref)):
                out_ref[a, place * length : (place + 1) * length, :] = ref[:, here]
            out_ref[a, 4 * length :, :] = marks_ref[...]


def unpack_kernel(me_ref, *refs):
    in_refs, out_refs = refs[:-4], refs[-4:]
    length = out_refs[0].shape[0]
    for n, in_ref in enumerate(in_refs):
        for a in range(in_ref.shape[0]):
            head = (me_ref[0] ^ n) * in_ref.shape[0] + a
            here = pl.ds(pl.multiple_of(head * ATT_DIM, ATT_DIM), ATT_DIM)
            for place, ref in enumerate(out_refs):
                ref[:, here] = in_ref[a, place * length : (place + 1) * length, :]


def attend_blocks(length, parts, me_ref, *refs):
    in_refs, out_refs = refs[:parts], refs[parts : 2 * parts]
    all_in, all_out = refs[2 * parts : 2 * parts + 2]
    for n in range(parts):
        all_in[me_ref[0] ^ n] = in_refs[n][...]
    attend_kernel(length, all_in, all_out, *refs[2 * parts + 2 :])
    for n in range(parts):
        out_refs[n][...] = all_out[me_ref[0] ^ n]


def attend_kernel(length, in_ref, out_ref, expo_ref, kt_ref, vt_ref, dk_ref, dv_ref):
    parts = in_ref.shape[0]
    scale = ATT_DIM ** (-0.5)
    rate = scale * LOG2E
    key_in = iota((length, length), 0)
    causal = key_in <= iota((length, length), 1)
    for a in range(in_ref.shape[1]):

        def piece(block, place):
            return in_ref[block, a, place * length : (place + 1) * length, :]

        for i in range(parts):
            kt_ref[i] = flip(piece(i, 1))
            vt_ref[i] = flip(piece(i, 2))
            queries, grads = piece(i, 0), piece(i, 3)
            marks = in_ref[i, a, 4 * length :, :].astype(F32)
            starts = jnp.concatenate(
                [
                    marks[2 * n : 2 * n + 1] * 128.0 + marks[2 * n + 1 : 2 * n + 2]
                    for n in range(length // 128)
                ],
                axis=1,
            ).astype(jnp.int32)
            query_at = i * length + iota((1, length), 1)
            if parts * length > WINDOW:
                starts = jnp.maximum(starts, query_at - (WINDOW - 1))
            top = jnp.full((1, length), MASKED, F32)
            total = jnp.zeros((1, length), F32)
            tops = []
            for j in range(i + 1):
                seen = key_in >= starts - j * length
                if j == i:
                    seen = seen & causal
                raw = jnp.where(seen, dot_nt(piece(j, 1), queries), MASKED)
                new = jnp.maximum(top, jnp.max(raw, axis=0, keepdims=True))
                expo = jnp.exp2((raw - new) * rate)
                expo_ref[j] = expo
                total = total * jnp.exp2((top - new) * rate) + jnp.sum(expo, axis=0, keepdims=True)
                top = new
                tops.append(new)
            out = jnp.zeros((ATT_DIM, length), F32)
            for j in range(i + 1):
                probs = expo_ref[j] * (jnp.exp2((tops[j] - top) * rate) / total)
                expo_ref[j] = probs
                weights = probs.astype(BF16)
                dvalue = dot(weights, grads)
                dv_ref[j] = dvalue if j == i else dv_ref[j] + dvalue
                out = out + dot(vt_ref[j], weights)
            delta = jnp.sum(out * grads.astype(F32).T, axis=0, keepdims=True)
            dquery = jnp.zeros((ATT_DIM, length), F32)
            for j in range(i + 1):
                dprobs = dot_nt(piece(j, 2), grads)
                dscore = (expo_ref[j] * ((dprobs - delta) * scale)).astype(BF16)
                dkey = dot(dscore, queries)
                dk_ref[j] = dkey if j == i else dk_ref[j] + dkey
                dquery = dquery + dot(kt_ref[j], dscore)
            out_ref[i, a, 0:length, :] = out.T.astype(BF16)
            out_ref[i, a, length : 2 * length, :] = dquery.T.astype(BF16)
        for j in range(parts):
            out_ref[j, a, 2 * length : 3 * length, :] = dk_ref[j].astype(BF16)
            out_ref[j, a, 3 * length :, :] = dv_ref[j].astype(BF16)


def shifted(shard, axis, by):
    devices = lax.axis_size(axis)
    pairs = [(i, i + by) for i in range(devices) if 0 <= i + by < devices]
    return lax.ppermute(shard, axis, pairs)


def head_cols(array, head_index):
    return lax.dynamic_slice_in_dim(array, head_index * ATT_DIM, ATT_DIM, 1)


def ring_attention(att_queries, att_keys, att_values, att_grad, doc_start):
    length = att_queries.shape[0]
    shard_index = lax.axis_index("ctx")
    halo_shards = WINDOW // length
    att_count = att_queries.shape[1] // ATT_DIM
    att_width = att_queries.shape[1]
    score_scale = ATT_DIM ** (-0.5)

    def pass_keys(running, unused):
        moved = shifted((running[0], running[1]), "ctx", 1)
        return (moved, moved)

    _, earlier = lax.scan(pass_keys, (att_keys, att_values), None, length=halo_shards)
    key_all = jnp.concatenate(
        [earlier[0][::-1].reshape(halo_shards * length, att_width), att_keys], axis=0
    )
    value_all = jnp.concatenate(
        [earlier[1][::-1].reshape(halo_shards * length, att_width), att_values], axis=0
    )
    spread_rows = (halo_shards + 1) * length
    query_pos = shard_index * length + jnp.arange(length, dtype=jnp.int32)
    key_pos = (shard_index - halo_shards) * length + jnp.arange(spread_rows, dtype=jnp.int32)
    visible = (
        (key_pos[None, :] <= query_pos[:, None])
        & (query_pos[:, None] - key_pos[None, :] < WINDOW)
        & (key_pos[None, :] >= doc_start[:, None])
    )

    def forward_head(head_index, running):
        out_buf, max_buf, total_buf, delta_buf = running
        query_head = head_cols(att_queries, head_index)
        key_head = head_cols(key_all, head_index)
        value_head = head_cols(value_all, head_index)
        score = (
            jnp.einsum("td,sd->ts", query_head, key_head, preferred_element_type=jnp.float32)
            * score_scale
        )
        row_max = jnp.max(jnp.where(visible, score, -jnp.inf), axis=1)
        expo = jnp.where(visible, jnp.exp(score - row_max[:, None]), 0.0)
        row_total = jnp.sum(expo, axis=1)
        weights = (expo / row_total[:, None]).astype(jnp.bfloat16)
        attended = jnp.dot(weights, value_head, preferred_element_type=jnp.float32)
        delta = jnp.sum(head_cols(att_grad, head_index).astype(jnp.float32) * attended, axis=1)
        out_buf = lax.dynamic_update_slice_in_dim(
            out_buf, attended.astype(jnp.bfloat16), head_index * ATT_DIM, 1
        )
        return (
            out_buf,
            max_buf.at[:, head_index].set(row_max),
            total_buf.at[:, head_index].set(row_total),
            delta_buf.at[:, head_index].set(delta),
        )

    stats_zero = jnp.zeros((length, att_count), jnp.float32)
    window_out, row_maxes, row_totals, row_deltas = lax.fori_loop(
        0,
        att_count,
        forward_head,
        (jnp.zeros((length, att_width), jnp.bfloat16), stats_zero, stats_zero, stats_zero),
    )

    def query_terms(head_index):
        query_head = head_cols(att_queries, head_index)
        key_head = head_cols(key_all, head_index)
        value_head = head_cols(value_all, head_index)
        grad_head = head_cols(att_grad, head_index)
        score = (
            jnp.einsum("td,sd->ts", query_head, key_head, preferred_element_type=jnp.float32)
            * score_scale
        )
        probs = (
            jnp.where(visible, jnp.exp(score - row_maxes[:, head_index][:, None]), 0.0)
            / row_totals[:, head_index][:, None]
        )
        weights = probs.astype(jnp.bfloat16)
        dprobs = jnp.einsum("td,sd->ts", grad_head, value_head, preferred_element_type=jnp.float32)
        dscore = (probs * (dprobs - row_deltas[:, head_index][:, None]) * score_scale).astype(
            jnp.bfloat16
        )
        query_part = jnp.dot(dscore, key_head, preferred_element_type=jnp.float32)
        return (query_head, grad_head, weights, dscore, query_part)

    def backward_head(head_index, running):
        query_buf, key_buf, value_buf = running
        query_head, grad_head, weights, dscore, query_part = query_terms(head_index)
        key_part = jnp.einsum("ts,td->sd", dscore, query_head, preferred_element_type=jnp.float32)
        value_part = jnp.einsum("ts,td->sd", weights, grad_head, preferred_element_type=jnp.float32)
        query_buf = lax.dynamic_update_slice_in_dim(query_buf, query_part, head_index * ATT_DIM, 1)
        key_buf = lax.dynamic_update_slice_in_dim(key_buf, key_part, head_index * ATT_DIM, 1)
        value_buf = lax.dynamic_update_slice_in_dim(value_buf, value_part, head_index * ATT_DIM, 1)
        return (query_buf, key_buf, value_buf)

    part_zero = jnp.zeros((spread_rows, att_width), jnp.float32)
    query_sum, key_parts, value_parts = lax.fori_loop(
        0,
        att_count,
        backward_head,
        (jnp.zeros((length, att_width), jnp.float32), part_zero, part_zero),
    )
    key_blocks = key_parts.reshape(halo_shards + 1, length, att_width)
    value_blocks = value_parts.reshape(halo_shards + 1, length, att_width)

    def send_back(running, block_index):
        moved = shifted((running[0], running[1]), "ctx", -1)
        return ((moved[0] + key_blocks[block_index], moved[1] + value_blocks[block_index]), None)

    (key_sum, value_sum), _ = lax.scan(
        send_back, (key_blocks[0], value_blocks[0]), jnp.arange(1, halo_shards + 1, dtype=jnp.int32)
    )
    return (
        window_out,
        query_sum.astype(jnp.bfloat16),
        key_sum.astype(jnp.bfloat16),
        value_sum.astype(jnp.bfloat16),
    )


def body(
    ssm_input,
    gate_input,
    write_map,
    read_map,
    log_decay,
    doc_start,
    ssm_grad,
    att_queries,
    att_keys,
    att_values,
    att_grad,
):
    length, width = ssm_input.shape
    heads = width // HEAD_DIM
    parts = lax.axis_size("ctx")
    shares = parts // 2
    rows = width // shares
    full_width = width * lax.axis_size("head")
    att_width = att_queries.shape[1]
    per = att_width // ATT_DIM // parts
    dealt = att_width // ATT_DIM % parts == 0
    place = lax.axis_index("ctx")
    starts = doc_start.reshape(1, length)
    me = place.reshape(1).astype(jnp.int32)
    tailed = [shape((rows + TAIL, 128), BF16)] * shares
    plain = [shape((rows, 128), BF16)] * shares
    held_tails = pltpu.VMEM((shares, rows + TAIL, 128), BF16)
    held_plain = pltpu.VMEM((shares, rows, 128), BF16)

    def carry_total(backward, *blocks):
        return call(
            lambda *refs: total_kernel(backward, shares, *refs),
            shape((rows, 128), BF16), me, *blocks,
            specs=[SMEM] + [VMEM] * len(blocks),
            scratch=[held_tails, held_plain] if backward else [held_tails],
            vmem=SMALL, name="ssm_total",
        )

    def carry_states(backward, start, *blocks):
        return call(
            lambda *refs: carry_kernel(backward, shares, *refs),
            plain, me, start, *blocks,
            specs=[SMEM] + [VMEM] * (1 + len(blocks)),
            scratch=[held_tails, held_plain, held_plain] if backward else [held_tails, held_plain],
            vmem=SMALL, name="ssm_carry",
        )

    lcol, lrow, *sent = call(
        lambda *refs: first_kernel(shares, *refs),
        [shape((length, heads), F32), shape((heads, length), F32)] + tailed,
        me, log_decay.T, starts, write_map, ssm_input,
        specs=[SMEM] + [VMEM] * 4, scratch=[held_tails], name="ssm_first",
    )
    tails = [pass_block(block, n) for n, block in enumerate(sent)]
    if dealt:
        marks = doc_start.reshape(length // 128, 128)
        marks = jnp.stack([marks // 128, marks % 128], axis=1).reshape(length // 64, 128)
        marks = jnp.pad(marks, ((0, TAIL - length // 64), (0, 0))).astype(BF16)
        marks, tails = lax.optimization_barrier((marks, tails))
        packed = call(
            pack_kernel, [shape((per, 4 * length + TAIL, 128), BF16)] * parts,
            me, marks, att_queries, att_keys, att_values, att_grad,
            specs=[SMEM] + [VMEM] * 5, vmem=SMALL, name="att_pack",
        )
        att_got = {n: pass_block(block, n) for n, block in enumerate(packed)}
    else:
        att_out = ring_attention(att_queries, att_keys, att_values, att_grad, doc_start)
    total = carry_total(False, *tails)
    start = cross(total, False)
    state = [
        pass_block(block, n) for n, block in enumerate(carry_states(False, start, *tails))
    ]
    if dealt:
        att_got[shares], state = lax.optimization_barrier((att_got[shares], state))
    mixed, sums, state = call(
        lambda *refs: mix_kernel(shares, *refs),
        (shape((length, width), F32), shape((8, length), F32), shape((width, 128), BF16)),
        me, ssm_input, gate_input, ssm_grad, write_map, read_map, starts, lcol, lrow, *state,
        specs=[SMEM] + [VMEM] * (8 + shares), name="ssm_mix",
    )
    sums = lax.psum(sums, "head")
    mixer_out, gate_grad, dmixed, *sent = call(
        lambda *refs: gate_kernel(full_width, shares, *refs),
        [shape((length, width), BF16)] * 3 + plain,
        me, sums, mixed, gate_input, ssm_grad, read_map, starts, lrow,
        specs=[SMEM] + [VMEM] * 7, scratch=[held_plain], name="ssm_gate",
    )

    if dealt:
        rest = [n for n in range(1, parts - 1) if n != shares]
        done, sent = lax.optimization_barrier(([att_got[n] for n in rest], sent))
        att_got.update(zip(rest, done))
    blocks = [pass_block(block, n) for n, block in enumerate(sent)]
    total = carry_total(True, *tails, *blocks)
    start = cross(total, True)
    if dealt:
        att_in, total = lax.optimization_barrier(([att_got[n] for n in range(parts)], total))
        att_done = call(
            lambda *refs: attend_blocks(length, parts, *refs),
            [shape((per, 4 * length, 128), BF16)] * parts, me, *att_in,
            specs=[SMEM] + [VMEM] * parts,
            scratch=[
                pltpu.VMEM((parts, per, 4 * length + TAIL, 128), BF16),
                pltpu.VMEM((parts, per, 4 * length, 128), BF16),
                pltpu.VMEM((parts, length, length), F32),
                pltpu.VMEM((parts, ATT_DIM, length), BF16),
                pltpu.VMEM((parts, ATT_DIM, length), BF16),
                pltpu.VMEM((parts, length, ATT_DIM), F32),
                pltpu.VMEM((parts, length, ATT_DIM), F32),
            ],
            flops=6 * per * (parts * length) ** 2 * ATT_DIM, name="att_attend",
        )
        start, att_done = lax.optimization_barrier((start, att_done))
    back = [
        pass_block(block, n) for n, block in enumerate(carry_states(True, start, *tails, *blocks))
    ]
    gin, read_part, write_part = call(
        inner_kernel,
        (shape((length, width), F32), shape((length, 128), F32), shape((length, 128), F32)),
        me, dmixed, ssm_input, write_map, read_map, starts, lcol, lrow, state,
        specs=[SMEM] + [VMEM] * 8, name="ssm_inner",
    )
    if dealt:
        att_back = {shares: pass_block(att_done[shares], shares)}
        held, back, gin = lax.optimization_barrier((att_done, back, gin))
        for n in [n for n in range(parts)[::-1] if n != shares]:
            att_back[n] = pass_block(held[n], n)
        att_out = call(
            unpack_kernel, (shape((length, att_width), BF16),) * 4,
            me, *[att_back[n] for n in range(parts)],
            specs=[SMEM] + [VMEM] * parts, vmem=SMALL, name="att_unpack",
        )

    input_grad, write_part = call(
        lambda *refs: last_kernel(shares, *refs),
        (shape((length, width), BF16), shape((length, 128), F32)),
        me, gin, ssm_input, write_map, starts, lcol, write_part, *back,
        specs=[SMEM] + [VMEM] * (6 + shares),
        scratch=[pltpu.VMEM((width, 128), BF16)], name="ssm_last",
    )
    write_sum, read_sum = lax.psum((write_part, read_part), "head")
    window_out, query_grad, key_grad, value_grad = att_out
    return (
        mixer_out,
        window_out,
        input_grad,
        gate_grad,
        write_sum.astype(BF16),
        read_sum.astype(BF16),
        query_grad,
        key_grad,
        value_grad,
    )


def solution(mesh):
    in_specs = (
        P("ctx", "head"),
        P("ctx", "head"),
        P("ctx", None),
        P("ctx", None),
        P("ctx", "head"),
        P("ctx"),
        P("ctx", "head"),
        P("ctx", "head"),
        P("ctx", "head"),
        P("ctx", "head"),
        P("ctx", "head"),
    )
    out_specs = (
        P("ctx", "head"),
        P("ctx", "head"),
        P("ctx", "head"),
        P("ctx", "head"),
        P("ctx", None),
        P("ctx", None),
        P("ctx", "head"),
        P("ctx", "head"),
        P("ctx", "head"),
    )
    return jax.shard_map(body, mesh=mesh, in_specs=in_specs, out_specs=out_specs, check_vma=False)
```

```python
import jax
import jax.numpy as jnp
from jax import lax
from jax.experimental import pallas as pl
from jax.experimental.pallas import tpu as pltpu
from jax.sharding import PartitionSpec as P

HEAD_DIM = 128
ATT_DIM = 128
WINDOW = 4096
EPSILON = 1e-05
LOG2E = 1.4426950408889634
TAIL = 16
MASKED = -1e30
HIGH = lax.Precision.HIGHEST
F32 = jnp.float32
BF16 = jnp.bfloat16
VMEM_BYTES = 56 * 1024 * 1024


VMEM = pl.BlockSpec(memory_space=pltpu.VMEM)
SMEM = pl.BlockSpec(memory_space=pltpu.SMEM)
SMALL = 16 * 1024 * 1024


def call(kernel, out_shape, *operands, specs=None, scratch=(), flops=0, vmem=VMEM_BYTES, name=None):
    moved = sum(a.size * a.dtype.itemsize for a in jax.tree.leaves((operands, out_shape)))
    return pl.pallas_call(
        kernel,
        out_shape=out_shape,
        in_specs=specs or [VMEM] * len(operands),
        out_specs=jax.tree.map(lambda _: VMEM, out_shape),
        scratch_shapes=scratch,
        compiler_params=pltpu.CompilerParams(vmem_limit_bytes=vmem),
        cost_estimate=pl.CostEstimate(flops=flops, bytes_accessed=moved, transcendentals=0),
        name=name,
    )(*operands)


def shape(dims, dtype):
    return jax.ShapeDtypeStruct(dims, dtype)


def dot(a, b):
    return jnp.dot(a, b, preferred_element_type=F32)


def dot_nt(a, b, precision=None):
    return lax.dot_general(
        a, b, (((1,), (1,)), ((), ())), preferred_element_type=F32, precision=precision
    )


def iota(dims, axis):
    return lax.broadcasted_iota(jnp.int32, dims, axis)


def flip(a):
    return a.astype(F32).T.astype(BF16)


def column(row):
    return jnp.broadcast_to(row, (128, row.shape[1])).T


def cols(h):
    return slice(h * HEAD_DIM, (h + 1) * HEAD_DIM)


def shifted_starts(me_ref, starts_ref):
    return starts_ref[...] - me_ref[0] * starts_ref.shape[1]


def deal(me_ref, held, out_refs):
    share = me_ref[0] & (len(out_refs) - 1)
    for n, out_ref in enumerate(out_refs):
        out_ref[...] = held[share ^ n]


def collect(me_ref, in_refs, held):
    share = me_ref[0] & (len(in_refs) - 1)
    for n, in_ref in enumerate(in_refs):
        held[share ^ n] = in_ref[...]


def gather_state(me_ref, in_refs, state_ref):
    rows = in_refs[0].shape[0]
    share = me_ref[0] & (len(in_refs) - 1)
    for n, in_ref in enumerate(in_refs):
        here = pl.ds(pl.multiple_of((share ^ n) * rows, rows), rows)
        state_ref[here, :] = in_ref[...]


def first_kernel(shares, me_ref, ld_ref, rel_ref, w_ref, x_ref, lcol_ref, lrow_ref, *refs):
    out_refs, out_ref = refs[:shares], refs[shares]
    heads, length = ld_ref.shape
    rel_row = shifted_starts(me_ref, rel_ref)
    parts, rows = out_ref.shape[0], out_ref.shape[1] - TAIL
    rates = ld_ref[...] * LOG2E
    lower = jnp.where(iota((length, length), 0) >= iota((length, length), 1), 1.0, 0.0)
    upper = jnp.where(iota((length, length), 0) <= iota((length, length), 1), 1.0, 0.0)
    lcol_ref[...] = dot_nt(lower, rates, HIGH)
    lrow = jnp.dot(rates, upper, preferred_element_type=F32, precision=HIGH)
    lrow_ref[...] = lrow
    rel_last = rel_row[:, length - 1 :]
    last_doc = iota((1, length), 1) >= rel_last
    keeps = rel_last < 0
    writes = w_ref[...].astype(F32).T
    tail_row = iota((TAIL, 128), 0)
    for h in range(heads):
        line = lrow[h : h + 1, :]
        total = line[:, length - 1 :]
        to_end = jnp.where(last_doc, jnp.exp2(total - line), 0.0)
        state = dot((writes * to_end).astype(BF16), x_ref[:, cols(h)]).astype(BF16)
        factor = jnp.where(keeps, jnp.exp2(total), 0.0)
        high = factor.astype(BF16).astype(F32)
        low = factor - high
        first = h * HEAD_DIM
        for part in range(first // rows, (first + HEAD_DIM - 1) // rows + 1):
            begin = max(first, part * rows)
            end = min(first + HEAD_DIM, (part + 1) * rows)
            out_ref[part, begin - part * rows : end - part * rows, :] = state[
                begin - first : end - first, :
            ]
            place = 2 * (begin - part * rows) // HEAD_DIM
            tail = jnp.where(tail_row == place, high, jnp.where(tail_row == place + 1, low, 0.0))
            if place:
                tail = tail + out_ref[part, rows:, :].astype(F32)
            out_ref[part, rows:, :] = tail.astype(BF16)
    deal(me_ref, out_ref, out_refs)


def carry(backward, start_ref, tails, held, total_ref, out):
    shares, rows = tails.shape[0], tails.shape[1] - TAIL
    step = min(rows, HEAD_DIM)
    for k in range(rows // step):
        here = slice(k * step, (k + 1) * step)
        state = jnp.zeros((step, 128), F32) if start_ref is None else start_ref[here, :].astype(F32)
        for c in range(shares)[:: -1 if backward else 1]:
            if out is not None:
                out[c, here, :] = state.astype(BF16)
            tail = tails[c, rows:, :].astype(F32)
            factor = tail[2 * k : 2 * k + 1, :] + tail[2 * k + 1 : 2 * k + 2, :]
            state = factor * state + held[c, here, :].astype(F32)
        if total_ref is not None:
            total_ref[here, :] = state.astype(BF16)


def total_kernel(backward, shares, me_ref, *refs):
    count = 2 if backward else 1
    in_refs, (total_ref, *held) = refs[: count * shares], refs[count * shares :]
    for n in range(count):
        collect(me_ref, in_refs[n * shares : (n + 1) * shares], held[n])
    carry(backward, None, held[0], held[-1], total_ref, None)


def carry_kernel(backward, shares, me_ref, start_ref, *refs):
    count = 2 if backward else 1
    in_refs, out_refs = refs[: count * shares], refs[count * shares : (count + 1) * shares]
    *held, out = refs[(count + 1) * shares :]
    for n in range(count):
        collect(me_ref, in_refs[n * shares : (n + 1) * shares], held[n])
    carry(backward, start_ref, held[0], held[-1], None, out)
    deal(me_ref, out, out_refs)


def mix_kernel(
    shares, me_ref, x_ref, gate_ref, grad_ref, w_ref, r_ref, rel_ref, lcol_ref, lrow_ref, *refs
):
    state_refs, (mixed_ref, sums_ref, s_ref) = refs[:shares], refs[shares:]
    gather_state(me_ref, state_refs, s_ref)
    length, heads = lcol_ref.shape
    reads = r_ref[...]
    rel = column(shifted_starts(me_ref, rel_ref).astype(F32))
    wide = jnp.concatenate([rel] * (length // 128), axis=1)
    seen = (iota((length, length), 1).astype(F32) >= wide) & (
        iota((length, length), 1) <= iota((length, length), 0)
    )
    scores = jnp.where(seen, dot_nt(reads, w_ref[...]), 0.0)
    squares = jnp.zeros((length, 128), F32)
    inners = jnp.zeros((length, 128), F32)
    for h in range(heads):
        lc = lcol_ref[:, h : h + 1]
        decay = jnp.exp2(jnp.minimum(lc - lrow_ref[h : h + 1, :], 0.0))
        enter = jnp.where(rel < 0, jnp.exp2(jnp.broadcast_to(lc, rel.shape)), 0.0)
        mixed = dot((scores * decay).astype(BF16), x_ref[:, cols(h)]) + enter * dot(
            reads, s_ref[cols(h), :]
        )
        mixed_ref[:, cols(h)] = mixed
        gate = gate_ref[:, cols(h)].astype(F32)
        gated = mixed * (gate / (1.0 + jnp.exp(-gate)))
        squares = squares + gated * gated
        inners = inners + grad_ref[:, cols(h)].astype(F32) * gated
    ones = jnp.ones((8, 128), F32)
    square_row = dot_nt(ones, squares, HIGH)
    inner_row = dot_nt(ones, inners, HIGH)
    sums_ref[...] = jnp.where(iota((8, length), 0) == 0, square_row, inner_row)


def gate_kernel(
    width, shares, me_ref, sums_ref, mixed_ref, gate_ref, grad_ref, r_ref, rel_ref, lrow_ref,
    mixer_ref, ggrad_ref, dmixed_ref, *refs,
):
    out_refs, out_ref = refs[:shares], refs[shares]
    length = mixed_ref.shape[0]
    heads = lrow_ref.shape[0]
    rows = out_ref.shape[1]
    scale = lax.rsqrt(sums_ref[0:1, :] / width + EPSILON)
    rms = column(scale)
    pull = column(scale * scale * scale * sums_ref[1:2, :] / width)
    reads = r_ref[...].astype(F32).T
    enters = shifted_starts(me_ref, rel_ref) < 0
    for h in range(heads):
        mixed = mixed_ref[:, cols(h)]
        gate = gate_ref[:, cols(h)].astype(F32)
        sigma = 1.0 / (1.0 + jnp.exp(-gate))
        swish = gate * sigma
        gated = mixed * swish
        mixer_ref[:, cols(h)] = (gated * rms).astype(BF16)
        dgated = rms * grad_ref[:, cols(h)].astype(F32) - pull * gated
        dmixed = (dgated * swish).astype(BF16)
        dmixed_ref[:, cols(h)] = dmixed
        ggrad_ref[:, cols(h)] = (
            dgated * mixed * sigma * (1.0 + gate * (1.0 - sigma))
        ).astype(BF16)
        enter = jnp.where(enters, jnp.exp2(lrow_ref[h : h + 1, :]), 0.0)
        state = dot((reads * enter).astype(BF16), dmixed).astype(BF16)
        first = h * HEAD_DIM
        for part in range(first // rows, (first + HEAD_DIM - 1) // rows + 1):
            begin = max(first, part * rows)
            end = min(first + HEAD_DIM, (part + 1) * rows)
            out_ref[part, begin - part * rows : end - part * rows, :] = state[
                begin - first : end - first, :
            ]
    deal(me_ref, out_ref, out_refs)


def inner_kernel(
    me_ref, dmixed_ref, x_ref, w_ref, r_ref, rel_ref, lcol_ref, lrow_ref, s_ref, gin_ref, read_ref, write_ref
):
    length, heads = lcol_ref.shape
    rel_row = shifted_starts(me_ref, rel_ref)
    rel = column(rel_row.astype(F32))
    seen = (iota((length, length), 0) >= rel_row) & (
        iota((length, length), 0) <= iota((length, length), 1)
    )
    scores = jnp.where(seen, dot_nt(w_ref[...], r_ref[...]), 0.0)
    total = jnp.zeros((length, length), F32)
    read = jnp.zeros((length, 128), F32)
    for h in range(heads):
        lc = lcol_ref[:, h : h + 1]
        decay = jnp.exp2(jnp.minimum(lrow_ref[h : h + 1, :] - lc, 0.0))
        dmixed = dmixed_ref[:, cols(h)]
        gin_ref[:, cols(h)] = dot((scores * decay).astype(BF16), dmixed)
        total = total + decay * dot_nt(x_ref[:, cols(h)], dmixed)
        enter = jnp.where(rel < 0, jnp.exp2(jnp.broadcast_to(lc, rel.shape)), 0.0)
        read = read + enter * dot_nt(dmixed, s_ref[cols(h), :])
    total = jnp.where(seen, total, 0.0)
    write_ref[...] = dot(total.astype(BF16), r_ref[...])
    read_ref[...] = read + dot(total.T.astype(BF16), w_ref[...])


def last_kernel(shares, me_ref, gin_ref, x_ref, w_ref, rel_ref, lcol_ref, part_ref, *refs):
    state_refs, (out_ref, write_ref, back_ref) = refs[:shares], refs[shares:]
    gather_state(me_ref, state_refs, back_ref)
    length, heads = lcol_ref.shape
    rel_last = shifted_starts(me_ref, rel_ref)[:, length - 1 :]
    last_doc = iota((length, 128), 0) >= rel_last
    writes = w_ref[...]
    write = part_ref[...]
    for h in range(heads):
        lc = lcol_ref[:, h : h + 1]
        line = jnp.broadcast_to(lc[length - 1 :, :] - lc, (length, 128))
        to_end = jnp.where(last_doc, jnp.exp2(line), 0.0)
        back = back_ref[cols(h), :]
        out_ref[:, cols(h)] = (gin_ref[:, cols(h)] + to_end * dot(writes, back)).astype(BF16)
        write = write + to_end * dot_nt(x_ref[:, cols(h)], back)
    write_ref[...] = write


def pass_block(block, n):
    if n == 0:
        return block
    return lax.ppermute(block, "ctx", [(i, i ^ n) for i in range(lax.axis_size("ctx"))])


def cross(total, backward):
    count = lax.axis_size("ctx")
    half = count // 2
    pairs = [(i + half, i) if backward else (i, i + half) for i in range(half)]
    return lax.ppermute(total, "ctx", pairs)


def pack_kernel(me_ref, marks_ref, q_ref, k_ref, v_ref, g_ref, *out_refs):
    length = q_ref.shape[0]
    for n, out_ref in enumerate(out_refs):
        for a in range(out_ref.shape[0]):
            head = (me_ref[0] ^ n) * out_ref.shape[0] + a
            here = pl.ds(pl.multiple_of(head * ATT_DIM, ATT_DIM), ATT_DIM)
            for place, ref in enumerate((q_ref, k_ref, v_ref, g_ref)):
                out_ref[a, place * length : (place + 1) * length, :] = ref[:, here]
            out_ref[a, 4 * length :, :] = marks_ref[...]


def unpack_kernel(me_ref, *refs):
    in_refs, out_refs = refs[:-4], refs[-4:]
    length = out_refs[0].shape[0]
    for n, in_ref in enumerate(in_refs):
        for a in range(in_ref.shape[0]):
            head = (me_ref[0] ^ n) * in_ref.shape[0] + a
            here = pl.ds(pl.multiple_of(head * ATT_DIM, ATT_DIM), ATT_DIM)
            for place, ref in enumerate(out_refs):
                ref[:, here] = in_ref[a, place * length : (place + 1) * length, :]


def attend_blocks(length, parts, me_ref, *refs):
    in_refs, out_refs = refs[:parts], refs[parts : 2 * parts]
    all_in, all_out = refs[2 * parts : 2 * parts + 2]
    for n in range(parts):
        all_in[me_ref[0] ^ n] = in_refs[n][...]
    attend_kernel(length, all_in, all_out, *refs[2 * parts + 2 :])
    for n in range(parts):
        out_refs[n][...] = all_out[me_ref[0] ^ n]


def attend_kernel(length, in_ref, out_ref, expo_ref, kt_ref, vt_ref, dk_ref, dv_ref):
    parts = in_ref.shape[0]
    scale = ATT_DIM ** (-0.5)
    rate = scale * LOG2E
    key_in = iota((length, length), 0)
    causal = key_in <= iota((length, length), 1)
    for a in range(in_ref.shape[1]):

        def piece(block, place):
            return in_ref[block, a, place * length : (place + 1) * length, :]

        for i in range(parts):
            kt_ref[i] = flip(piece(i, 1))
            vt_ref[i] = flip(piece(i, 2))
            queries, grads = piece(i, 0), piece(i, 3)
            marks = in_ref[i, a, 4 * length :, :].astype(F32)
            starts = jnp.concatenate(
                [
                    marks[2 * n : 2 * n + 1] * 128.0 + marks[2 * n + 1 : 2 * n + 2]
                    for n in range(length // 128)
                ],
                axis=1,
            ).astype(jnp.int32)
            query_at = i * length + iota((1, length), 1)
            if parts * length > WINDOW:
                starts = jnp.maximum(starts, query_at - (WINDOW - 1))
            top = jnp.full((1, length), MASKED, F32)
            total = jnp.zeros((1, length), F32)
            tops = []
            for j in range(i + 1):
                seen = key_in >= starts - j * length
                if j == i:
                    seen = seen & causal
                raw = jnp.where(seen, dot_nt(piece(j, 1), queries), MASKED)
                new = jnp.maximum(top, jnp.max(raw, axis=0, keepdims=True))
                expo = jnp.exp2((raw - new) * rate)
                expo_ref[j] = expo
                total = total * jnp.exp2((top - new) * rate) + jnp.sum(expo, axis=0, keepdims=True)
                top = new
                tops.append(new)
            out = jnp.zeros((ATT_DIM, length), F32)
            for j in range(i + 1):
                probs = expo_ref[j] * (jnp.exp2((tops[j] - top) * rate) / total)
                expo_ref[j] = probs
                weights = probs.astype(BF16)
                dvalue = dot(weights, grads)
                dv_ref[j] = dvalue if j == i else dv_ref[j] + dvalue
                out = out + dot(vt_ref[j], weights)
            delta = jnp.sum(out * grads.astype(F32).T, axis=0, keepdims=True)
            dquery = jnp.zeros((ATT_DIM, length), F32)
            for j in range(i + 1):
                dprobs = dot_nt(piece(j, 2), grads)
                dscore = (expo_ref[j] * ((dprobs - delta) * scale)).astype(BF16)
                dkey = dot(dscore, queries)
                dk_ref[j] = dkey if j == i else dk_ref[j] + dkey
                dquery = dquery + dot(kt_ref[j], dscore)
            out_ref[i, a, 0:length, :] = out.T.astype(BF16)
            out_ref[i, a, length : 2 * length, :] = dquery.T.astype(BF16)
        for j in range(parts):
            out_ref[j, a, 2 * length : 3 * length, :] = dk_ref[j].astype(BF16)
            out_ref[j, a, 3 * length :, :] = dv_ref[j].astype(BF16)


def shifted(shard, axis, by):
    devices = lax.axis_size(axis)
    pairs = [(i, i + by) for i in range(devices) if 0 <= i + by < devices]
    return lax.ppermute(shard, axis, pairs)


def head_cols(array, head_index):
    return lax.dynamic_slice_in_dim(array, head_index * ATT_DIM, ATT_DIM, 1)


def ring_attention(att_queries, att_keys, att_values, att_grad, doc_start):
    length = att_queries.shape[0]
    shard_index = lax.axis_index("ctx")
    halo_shards = WINDOW // length
    att_count = att_queries.shape[1] // ATT_DIM
    att_width = att_queries.shape[1]
    score_scale = ATT_DIM ** (-0.5)

    def pass_keys(running, unused):
        moved = shifted((running[0], running[1]), "ctx", 1)
        return (moved, moved)

    _, earlier = lax.scan(pass_keys, (att_keys, att_values), None, length=halo_shards)
    key_all = jnp.concatenate(
        [earlier[0][::-1].reshape(halo_shards * length, att_width), att_keys], axis=0
    )
    value_all = jnp.concatenate(
        [earlier[1][::-1].reshape(halo_shards * length, att_width), att_values], axis=0
    )
    spread_rows = (halo_shards + 1) * length
    query_pos = shard_index * length + jnp.arange(length, dtype=jnp.int32)
    key_pos = (shard_index - halo_shards) * length + jnp.arange(spread_rows, dtype=jnp.int32)
    visible = (
        (key_pos[None, :] <= query_pos[:, None])
        & (query_pos[:, None] - key_pos[None, :] < WINDOW)
        & (key_pos[None, :] >= doc_start[:, None])
    )

    def forward_head(head_index, running):
        out_buf, max_buf, total_buf, delta_buf = running
        query_head = head_cols(att_queries, head_index)
        key_head = head_cols(key_all, head_index)
        value_head = head_cols(value_all, head_index)
        score = (
            jnp.einsum("td,sd->ts", query_head, key_head, preferred_element_type=jnp.float32)
            * score_scale
        )
        row_max = jnp.max(jnp.where(visible, score, -jnp.inf), axis=1)
        expo = jnp.where(visible, jnp.exp(score - row_max[:, None]), 0.0)
        row_total = jnp.sum(expo, axis=1)
        weights = (expo / row_total[:, None]).astype(jnp.bfloat16)
        attended = jnp.dot(weights, value_head, preferred_element_type=jnp.float32)
        delta = jnp.sum(head_cols(att_grad, head_index).astype(jnp.float32) * attended, axis=1)
        out_buf = lax.dynamic_update_slice_in_dim(
            out_buf, attended.astype(jnp.bfloat16), head_index * ATT_DIM, 1
        )
        return (
            out_buf,
            max_buf.at[:, head_index].set(row_max),
            total_buf.at[:, head_index].set(row_total),
            delta_buf.at[:, head_index].set(delta),
        )

    stats_zero = jnp.zeros((length, att_count), jnp.float32)
    window_out, row_maxes, row_totals, row_deltas = lax.fori_loop(
        0,
        att_count,
        forward_head,
        (jnp.zeros((length, att_width), jnp.bfloat16), stats_zero, stats_zero, stats_zero),
    )

    def query_terms(head_index):
        query_head = head_cols(att_queries, head_index)
        key_head = head_cols(key_all, head_index)
        value_head = head_cols(value_all, head_index)
        grad_head = head_cols(att_grad, head_index)
        score = (
            jnp.einsum("td,sd->ts", query_head, key_head, preferred_element_type=jnp.float32)
            * score_scale
        )
        probs = (
            jnp.where(visible, jnp.exp(score - row_maxes[:, head_index][:, None]), 0.0)
            / row_totals[:, head_index][:, None]
        )
        weights = probs.astype(jnp.bfloat16)
        dprobs = jnp.einsum("td,sd->ts", grad_head, value_head, preferred_element_type=jnp.float32)
        dscore = (probs * (dprobs - row_deltas[:, head_index][:, None]) * score_scale).astype(
            jnp.bfloat16
        )
        query_part = jnp.dot(dscore, key_head, preferred_element_type=jnp.float32)
        return (query_head, grad_head, weights, dscore, query_part)

    def backward_head(head_index, running):
        query_buf, key_buf, value_buf = running
        query_head, grad_head, weights, dscore, query_part = query_terms(head_index)
        key_part = jnp.einsum("ts,td->sd", dscore, query_head, preferred_element_type=jnp.float32)
        value_part = jnp.einsum("ts,td->sd", weights, grad_head, preferred_element_type=jnp.float32)
        query_buf = lax.dynamic_update_slice_in_dim(query_buf, query_part, head_index * ATT_DIM, 1)
        key_buf = lax.dynamic_update_slice_in_dim(key_buf, key_part, head_index * ATT_DIM, 1)
        value_buf = lax.dynamic_update_slice_in_dim(value_buf, value_part, head_index * ATT_DIM, 1)
        return (query_buf, key_buf, value_buf)

    part_zero = jnp.zeros((spread_rows, att_width), jnp.float32)
    query_sum, key_parts, value_parts = lax.fori_loop(
        0,
        att_count,
        backward_head,
        (jnp.zeros((length, att_width), jnp.float32), part_zero, part_zero),
    )
    key_blocks = key_parts.reshape(halo_shards + 1, length, att_width)
    value_blocks = value_parts.reshape(halo_shards + 1, length, att_width)

    def send_back(running, block_index):
        moved = shifted((running[0], running[1]), "ctx", -1)
        return ((moved[0] + key_blocks[block_index], moved[1] + value_blocks[block_index]), None)

    (key_sum, value_sum), _ = lax.scan(
        send_back, (key_blocks[0], value_blocks[0]), jnp.arange(1, halo_shards + 1, dtype=jnp.int32)
    )
    return (
        window_out,
        query_sum.astype(jnp.bfloat16),
        key_sum.astype(jnp.bfloat16),
        value_sum.astype(jnp.bfloat16),
    )


def body(
    ssm_input,
    gate_input,
    write_map,
    read_map,
    log_decay,
    doc_start,
    ssm_grad,
    att_queries,
    att_keys,
    att_values,
    att_grad,
):
    length, width = ssm_input.shape
    heads = width // HEAD_DIM
    parts = lax.axis_size("ctx")
    shares = parts // 2
    rows = width // shares
    full_width = width * lax.axis_size("head")
    att_width = att_queries.shape[1]
    per = att_width // ATT_DIM // parts
    dealt = att_width // ATT_DIM % parts == 0
    place = lax.axis_index("ctx")
    starts = doc_start.reshape(1, length)
    me = place.reshape(1).astype(jnp.int32)
    tailed = [shape((rows + TAIL, 128), BF16)] * shares
    plain = [shape((rows, 128), BF16)] * shares
    held_tails = pltpu.VMEM((shares, rows + TAIL, 128), BF16)
    held_plain = pltpu.VMEM((shares, rows, 128), BF16)

    def carry_total(backward, *blocks):
        return call(
            lambda *refs: total_kernel(backward, shares, *refs),
            shape((rows, 128), BF16), me, *blocks,
            specs=[SMEM] + [VMEM] * len(blocks),
            scratch=[held_tails, held_plain] if backward else [held_tails],
            vmem=SMALL, name="ssm_total",
        )

    def carry_states(backward, start, *blocks):
        return call(
            lambda *refs: carry_kernel(backward, shares, *refs),
            plain, me, start, *blocks,
            specs=[SMEM] + [VMEM] * (1 + len(blocks)),
            scratch=[held_tails, held_plain, held_plain] if backward else [held_tails, held_plain],
            vmem=SMALL, name="ssm_carry",
        )

    lcol, lrow, *sent = call(
        lambda *refs: first_kernel(shares, *refs),
        [shape((length, heads), F32), shape((heads, length), F32)] + tailed,
        me, log_decay.T, starts, write_map, ssm_input,
        specs=[SMEM] + [VMEM] * 4, scratch=[held_tails], name="ssm_first",
    )
    tails = [pass_block(block, n) for n, block in enumerate(sent)]
    total = carry_total(False, *tails)
    start = cross(total, False)
    if dealt:
        marks = doc_start.reshape(length // 128, 128)
        marks = jnp.stack([marks // 128, marks % 128], axis=1).reshape(length // 64, 128)
        marks = jnp.pad(marks, ((0, TAIL - length // 64), (0, 0))).astype(BF16)
        marks, total = lax.optimization_barrier((marks, total))
        packed = call(
            pack_kernel, [shape((per, 4 * length + TAIL, 128), BF16)] * parts,
            me, marks, att_queries, att_keys, att_values, att_grad,
            specs=[SMEM] + [VMEM] * 5, vmem=SMALL, name="att_pack",
        )
        packed, start = lax.optimization_barrier((packed, start))
        att_got = {n: pass_block(block, n) for n, block in enumerate(packed)}
    else:
        att_out = ring_attention(att_queries, att_keys, att_values, att_grad, doc_start)
    state = [
        pass_block(block, n) for n, block in enumerate(carry_states(False, start, *tails))
    ]
    if dealt:
        att_got[shares], state = lax.optimization_barrier((att_got[shares], state))
    mixed, sums, state = call(
        lambda *refs: mix_kernel(shares, *refs),
        (shape((length, width), F32), shape((8, length), F32), shape((width, 128), BF16)),
        me, ssm_input, gate_input, ssm_grad, write_map, read_map, starts, lcol, lrow, *state,
        specs=[SMEM] + [VMEM] * (8 + shares), name="ssm_mix",
    )
    sums = lax.psum(sums, "head")
    mixer_out, gate_grad, dmixed, *sent = call(
        lambda *refs: gate_kernel(full_width, shares, *refs),
        [shape((length, width), BF16)] * 3 + plain,
        me, sums, mixed, gate_input, ssm_grad, read_map, starts, lrow,
        specs=[SMEM] + [VMEM] * 7, scratch=[held_plain], name="ssm_gate",
    )

    if dealt:
        rest = [n for n in range(1, parts - 1) if n != shares]
        done, sent = lax.optimization_barrier(([att_got[n] for n in rest], sent))
        att_got.update(zip(rest, done))
    blocks = [pass_block(block, n) for n, block in enumerate(sent)]
    if dealt:
        att_in, sent = lax.optimization_barrier(([att_got[n] for n in range(parts)], sent))
        att_done = call(
            lambda *refs: attend_blocks(length, parts, *refs),
            [shape((per, 4 * length, 128), BF16)] * parts, me, *att_in,
            specs=[SMEM] + [VMEM] * parts,
            scratch=[
                pltpu.VMEM((parts, per, 4 * length + TAIL, 128), BF16),
                pltpu.VMEM((parts, per, 4 * length, 128), BF16),
                pltpu.VMEM((parts, length, length), F32),
                pltpu.VMEM((parts, ATT_DIM, length), BF16),
                pltpu.VMEM((parts, ATT_DIM, length), BF16),
                pltpu.VMEM((parts, length, ATT_DIM), F32),
                pltpu.VMEM((parts, length, ATT_DIM), F32),
            ],
            flops=6 * per * (parts * length) ** 2 * ATT_DIM, name="att_attend",
        )
        blocks, att_done = lax.optimization_barrier((blocks, att_done))
    total = carry_total(True, *tails, *blocks)
    start = cross(total, True)
    back = [
        pass_block(block, n) for n, block in enumerate(carry_states(True, start, *tails, *blocks))
    ]
    gin, read_part, write_part = call(
        inner_kernel,
        (shape((length, width), F32), shape((length, 128), F32), shape((length, 128), F32)),
        me, dmixed, ssm_input, write_map, read_map, starts, lcol, lrow, state,
        specs=[SMEM] + [VMEM] * 8, name="ssm_inner",
    )
    if dealt:
        early = [shares, shares + 1]
        late = [*range(shares + 2, parts), *range(1, shares)]
        att_back = {0: att_done[0]}
        held, total = lax.optimization_barrier((att_done, total))
        att_back[early[0]] = pass_block(held[early[0]], early[0])
        held, start = lax.optimization_barrier((att_done, start))
        att_back[early[1]] = pass_block(held[early[1]], early[1])
        held, back, gin = lax.optimization_barrier((att_done, back, gin))
        att_back.update((n, pass_block(held[n], n)) for n in late)
        done, back = lax.optimization_barrier(([att_back[n] for n in early], back))
        att_back.update(zip(early, done))
        att_out = call(
            unpack_kernel, (shape((length, att_width), BF16),) * 4,
            me, *[att_back[n] for n in range(parts)],
            specs=[SMEM] + [VMEM] * parts, vmem=SMALL, name="att_unpack",
        )

    input_grad, write_part = call(
        lambda *refs: last_kernel(shares, *refs),
        (shape((length, width), BF16), shape((length, 128), F32)),
        me, gin, ssm_input, write_map, starts, lcol, write_part, *back,
        specs=[SMEM] + [VMEM] * (6 + shares),
        scratch=[pltpu.VMEM((width, 128), BF16)], name="ssm_last",
    )
    write_sum, read_sum = lax.psum((write_part, read_part), "head")
    window_out, query_grad, key_grad, value_grad = att_out
    return (
        mixer_out,
        window_out,
        input_grad,
        gate_grad,
        write_sum.astype(BF16),
        read_sum.astype(BF16),
        query_grad,
        key_grad,
        value_grad,
    )


def solution(mesh):
    in_specs = (
        P("ctx", "head"),
        P("ctx", "head"),
        P("ctx", None),
        P("ctx", None),
        P("ctx", "head"),
        P("ctx"),
        P("ctx", "head"),
        P("ctx", "head"),
        P("ctx", "head"),
        P("ctx", "head"),
        P("ctx", "head"),
    )
    out_specs = (
        P("ctx", "head"),
        P("ctx", "head"),
        P("ctx", "head"),
        P("ctx", "head"),
        P("ctx", None),
        P("ctx", None),
        P("ctx", "head"),
        P("ctx", "head"),
        P("ctx", "head"),
    )
    return jax.shard_map(body, mesh=mesh, in_specs=in_specs, out_specs=out_specs, check_vma=False)
```

```python
import jax
import jax.numpy as jnp
from jax import lax
from jax.experimental import pallas as pl
from jax.experimental.pallas import tpu as pltpu
from jax.sharding import PartitionSpec as P

HEAD_DIM = 128
ATT_DIM = 128
WINDOW = 4096
EPSILON = 1e-05
LOG2E = 1.4426950408889634
TAIL = 16
MASKED = -1e30
HIGH = lax.Precision.HIGHEST
F32 = jnp.float32
BF16 = jnp.bfloat16
VMEM_BYTES = 56 * 1024 * 1024


VMEM = pl.BlockSpec(memory_space=pltpu.VMEM)
SMEM = pl.BlockSpec(memory_space=pltpu.SMEM)
SMALL = 16 * 1024 * 1024


def call(kernel, out_shape, *operands, specs=None, scratch=(), flops=0, vmem=VMEM_BYTES, name=None):
    moved = sum(a.size * a.dtype.itemsize for a in jax.tree.leaves((operands, out_shape)))
    return pl.pallas_call(
        kernel,
        out_shape=out_shape,
        in_specs=specs or [VMEM] * len(operands),
        out_specs=jax.tree.map(lambda _: VMEM, out_shape),
        scratch_shapes=scratch,
        compiler_params=pltpu.CompilerParams(vmem_limit_bytes=vmem),
        cost_estimate=pl.CostEstimate(flops=flops, bytes_accessed=moved, transcendentals=0),
        name=name,
    )(*operands)


def shape(dims, dtype):
    return jax.ShapeDtypeStruct(dims, dtype)


def dot(a, b):
    return jnp.dot(a, b, preferred_element_type=F32)


def dot_nt(a, b, precision=None):
    return lax.dot_general(
        a, b, (((1,), (1,)), ((), ())), preferred_element_type=F32, precision=precision
    )


def iota(dims, axis):
    return lax.broadcasted_iota(jnp.int32, dims, axis)


def flip(a):
    return a.astype(F32).T.astype(BF16)


def column(row):
    return jnp.broadcast_to(row, (128, row.shape[1])).T


def cols(h):
    return slice(h * HEAD_DIM, (h + 1) * HEAD_DIM)


def shifted_starts(me_ref, starts_ref):
    return starts_ref[...] - me_ref[0] * starts_ref.shape[1]


def deal(me_ref, held, out_refs):
    share = me_ref[0] & (len(out_refs) - 1)
    for n, out_ref in enumerate(out_refs):
        out_ref[...] = held[share ^ n]


def collect(me_ref, in_refs, held):
    share = me_ref[0] & (len(in_refs) - 1)
    for n, in_ref in enumerate(in_refs):
        held[share ^ n] = in_ref[...]


def gather_state(me_ref, in_refs, state_ref):
    rows = in_refs[0].shape[0]
    share = me_ref[0] & (len(in_refs) - 1)
    for n, in_ref in enumerate(in_refs):
        here = pl.ds(pl.multiple_of((share ^ n) * rows, rows), rows)
        state_ref[here, :] = in_ref[...]


def first_kernel(shares, me_ref, ld_ref, rel_ref, w_ref, x_ref, lcol_ref, lrow_ref, *refs):
    out_refs, out_ref = refs[:shares], refs[shares]
    heads, length = ld_ref.shape
    rel_row = shifted_starts(me_ref, rel_ref)
    parts, rows = out_ref.shape[0], out_ref.shape[1] - TAIL
    rates = ld_ref[...] * LOG2E
    lower = jnp.where(iota((length, length), 0) >= iota((length, length), 1), 1.0, 0.0)
    upper = jnp.where(iota((length, length), 0) <= iota((length, length), 1), 1.0, 0.0)
    lcol_ref[...] = dot_nt(lower, rates, HIGH)
    lrow = jnp.dot(rates, upper, preferred_element_type=F32, precision=HIGH)
    lrow_ref[...] = lrow
    rel_last = rel_row[:, length - 1 :]
    last_doc = iota((1, length), 1) >= rel_last
    keeps = rel_last < 0
    writes = w_ref[...].astype(F32).T
    tail_row = iota((TAIL, 128), 0)
    for h in range(heads):
        line = lrow[h : h + 1, :]
        total = line[:, length - 1 :]
        to_end = jnp.where(last_doc, jnp.exp2(total - line), 0.0)
        state = dot((writes * to_end).astype(BF16), x_ref[:, cols(h)]).astype(BF16)
        factor = jnp.where(keeps, jnp.exp2(total), 0.0)
        high = factor.astype(BF16).astype(F32)
        low = factor - high
        first = h * HEAD_DIM
        for part in range(first // rows, (first + HEAD_DIM - 1) // rows + 1):
            begin = max(first, part * rows)
            end = min(first + HEAD_DIM, (part + 1) * rows)
            out_ref[part, begin - part * rows : end - part * rows, :] = state[
                begin - first : end - first, :
            ]
            place = 2 * (begin - part * rows) // HEAD_DIM
            tail = jnp.where(tail_row == place, high, jnp.where(tail_row == place + 1, low, 0.0))
            if place:
                tail = tail + out_ref[part, rows:, :].astype(F32)
            out_ref[part, rows:, :] = tail.astype(BF16)
    deal(me_ref, out_ref, out_refs)


def carry(backward, start_ref, tails, held, total_ref, out):
    shares, rows = tails.shape[0], tails.shape[1] - TAIL
    step = min(rows, HEAD_DIM)
    for k in range(rows // step):
        here = slice(k * step, (k + 1) * step)
        state = jnp.zeros((step, 128), F32) if start_ref is None else start_ref[here, :].astype(F32)
        for c in range(shares)[:: -1 if backward else 1]:
            if out is not None:
                out[c, here, :] = state.astype(BF16)
            tail = tails[c, rows:, :].astype(F32)
            factor = tail[2 * k : 2 * k + 1, :] + tail[2 * k + 1 : 2 * k + 2, :]
            state = factor * state + held[c, here, :].astype(F32)
        if total_ref is not None:
            total_ref[here, :] = state.astype(BF16)


def total_kernel(backward, shares, me_ref, *refs):
    count = 2 if backward else 1
    in_refs, (total_ref, *held) = refs[: count * shares], refs[count * shares :]
    for n in range(count):
        collect(me_ref, in_refs[n * shares : (n + 1) * shares], held[n])
    carry(backward, None, held[0], held[-1], total_ref, None)


def carry_kernel(backward, shares, me_ref, start_ref, *refs):
    count = 2 if backward else 1
    in_refs, out_refs = refs[: count * shares], refs[count * shares : (count + 1) * shares]
    *held, out = refs[(count + 1) * shares :]
    for n in range(count):
        collect(me_ref, in_refs[n * shares : (n + 1) * shares], held[n])
    carry(backward, start_ref, held[0], held[-1], None, out)
    deal(me_ref, out, out_refs)


def mix_kernel(
    shares, me_ref, x_ref, gate_ref, grad_ref, w_ref, r_ref, rel_ref, lcol_ref, lrow_ref, *refs
):
    state_refs, (mixed_ref, sums_ref, s_ref) = refs[:shares], refs[shares:]
    gather_state(me_ref, state_refs, s_ref)
    length, heads = lcol_ref.shape
    reads = r_ref[...]
    rel = column(shifted_starts(me_ref, rel_ref).astype(F32))
    wide = jnp.concatenate([rel] * (length // 128), axis=1)
    seen = (iota((length, length), 1).astype(F32) >= wide) & (
        iota((length, length), 1) <= iota((length, length), 0)
    )
    scores = jnp.where(seen, dot_nt(reads, w_ref[...]), 0.0)
    squares = jnp.zeros((length, 128), F32)
    inners = jnp.zeros((length, 128), F32)
    for h in range(heads):
        lc = lcol_ref[:, h : h + 1]
        decay = jnp.exp2(jnp.minimum(lc - lrow_ref[h : h + 1, :], 0.0))
        enter = jnp.where(rel < 0, jnp.exp2(jnp.broadcast_to(lc, rel.shape)), 0.0)
        mixed = dot((scores * decay).astype(BF16), x_ref[:, cols(h)]) + enter * dot(
            reads, s_ref[cols(h), :]
        )
        mixed_ref[:, cols(h)] = mixed
        gate = gate_ref[:, cols(h)].astype(F32)
        gated = mixed * (gate / (1.0 + jnp.exp(-gate)))
        squares = squares + gated * gated
        inners = inners + grad_ref[:, cols(h)].astype(F32) * gated
    ones = jnp.ones((8, 128), F32)
    square_row = dot_nt(ones, squares, HIGH)
    inner_row = dot_nt(ones, inners, HIGH)
    sums_ref[...] = jnp.where(iota((8, length), 0) == 0, square_row, inner_row)


def gate_kernel(
    width, shares, me_ref, sums_ref, mixed_ref, gate_ref, grad_ref, r_ref, rel_ref, lrow_ref,
    mixer_ref, ggrad_ref, dmixed_ref, *refs,
):
    out_refs, out_ref = refs[:shares], refs[shares]
    length = mixed_ref.shape[0]
    heads = lrow_ref.shape[0]
    rows = out_ref.shape[1]
    scale = lax.rsqrt(sums_ref[0:1, :] / width + EPSILON)
    rms = column(scale)
    pull = column(scale * scale * scale * sums_ref[1:2, :] / width)
    reads = r_ref[...].astype(F32).T
    enters = shifted_starts(me_ref, rel_ref) < 0
    for h in range(heads):
        mixed = mixed_ref[:, cols(h)]
        gate = gate_ref[:, cols(h)].astype(F32)
        sigma = 1.0 / (1.0 + jnp.exp(-gate))
        swish = gate * sigma
        gated = mixed * swish
        mixer_ref[:, cols(h)] = (gated * rms).astype(BF16)
        dgated = rms * grad_ref[:, cols(h)].astype(F32) - pull * gated
        dmixed = (dgated * swish).astype(BF16)
        dmixed_ref[:, cols(h)] = dmixed
        ggrad_ref[:, cols(h)] = (
            dgated * mixed * sigma * (1.0 + gate * (1.0 - sigma))
        ).astype(BF16)
        enter = jnp.where(enters, jnp.exp2(lrow_ref[h : h + 1, :]), 0.0)
        state = dot((reads * enter).astype(BF16), dmixed).astype(BF16)
        first = h * HEAD_DIM
        for part in range(first // rows, (first + HEAD_DIM - 1) // rows + 1):
            begin = max(first, part * rows)
            end = min(first + HEAD_DIM, (part + 1) * rows)
            out_ref[part, begin - part * rows : end - part * rows, :] = state[
                begin - first : end - first, :
            ]
    deal(me_ref, out_ref, out_refs)


def inner_kernel(
    me_ref, dmixed_ref, x_ref, w_ref, r_ref, rel_ref, lcol_ref, lrow_ref, s_ref, gin_ref, read_ref, write_ref
):
    length, heads = lcol_ref.shape
    rel_row = shifted_starts(me_ref, rel_ref)
    rel = column(rel_row.astype(F32))
    seen = (iota((length, length), 0) >= rel_row) & (
        iota((length, length), 0) <= iota((length, length), 1)
    )
    scores = jnp.where(seen, dot_nt(w_ref[...], r_ref[...]), 0.0)
    total = jnp.zeros((length, length), F32)
    read = jnp.zeros((length, 128), F32)
    for h in range(heads):
        lc = lcol_ref[:, h : h + 1]
        decay = jnp.exp2(jnp.minimum(lrow_ref[h : h + 1, :] - lc, 0.0))
        dmixed = dmixed_ref[:, cols(h)]
        gin_ref[:, cols(h)] = dot((scores * decay).astype(BF16), dmixed)
        total = total + decay * dot_nt(x_ref[:, cols(h)], dmixed)
        enter = jnp.where(rel < 0, jnp.exp2(jnp.broadcast_to(lc, rel.shape)), 0.0)
        read = read + enter * dot_nt(dmixed, s_ref[cols(h), :])
    total = jnp.where(seen, total, 0.0)
    write_ref[...] = dot(total.astype(BF16), r_ref[...])
    read_ref[...] = read + dot(total.T.astype(BF16), w_ref[...])


def last_kernel(shares, me_ref, gin_ref, x_ref, w_ref, rel_ref, lcol_ref, part_ref, *refs):
    state_refs, (out_ref, write_ref, back_ref) = refs[:shares], refs[shares:]
    gather_state(me_ref, state_refs, back_ref)
    length, heads = lcol_ref.shape
    rel_last = shifted_starts(me_ref, rel_ref)[:, length - 1 :]
    last_doc = iota((length, 128), 0) >= rel_last
    writes = w_ref[...]
    write = part_ref[...]
    for h in range(heads):
        lc = lcol_ref[:, h : h + 1]
        line = jnp.broadcast_to(lc[length - 1 :, :] - lc, (length, 128))
        to_end = jnp.where(last_doc, jnp.exp2(line), 0.0)
        back = back_ref[cols(h), :]
        out_ref[:, cols(h)] = (gin_ref[:, cols(h)] + to_end * dot(writes, back)).astype(BF16)
        write = write + to_end * dot_nt(x_ref[:, cols(h)], back)
    write_ref[...] = write


def pass_block(block, n):
    if n == 0:
        return block
    return lax.ppermute(block, "ctx", [(i, i ^ n) for i in range(lax.axis_size("ctx"))])


def cross(total, backward):
    count = lax.axis_size("ctx")
    half = count // 2
    pairs = [(i + half, i) if backward else (i, i + half) for i in range(half)]
    return lax.ppermute(total, "ctx", pairs)


def pack_kernel(me_ref, marks_ref, q_ref, k_ref, v_ref, g_ref, *out_refs):
    length = q_ref.shape[0]
    for n, out_ref in enumerate(out_refs):
        for a in range(out_ref.shape[0]):
            head = (me_ref[0] ^ n) * out_ref.shape[0] + a
            here = pl.ds(pl.multiple_of(head * ATT_DIM, ATT_DIM), ATT_DIM)
            for place, ref in enumerate((q_ref, k_ref, v_ref, g_ref)):
                out_ref[a, place * length : (place + 1) * length, :] = ref[:, here]
            out_ref[a, 4 * length :, :] = marks_ref[...]


def unpack_kernel(me_ref, *refs):
    in_refs, out_refs = refs[:-4], refs[-4:]
    length = out_refs[0].shape[0]
    for n, in_ref in enumerate(in_refs):
        for a in range(in_ref.shape[0]):
            head = (me_ref[0] ^ n) * in_ref.shape[0] + a
            here = pl.ds(pl.multiple_of(head * ATT_DIM, ATT_DIM), ATT_DIM)
            for place, ref in enumerate(out_refs):
                ref[:, here] = in_ref[a, place * length : (place + 1) * length, :]


def attend_blocks(length, parts, me_ref, *refs):
    in_refs, out_refs = refs[:parts], refs[parts : 2 * parts]
    all_in, all_out = refs[2 * parts : 2 * parts + 2]
    for n in range(parts):
        all_in[me_ref[0] ^ n] = in_refs[n][...]
    attend_kernel(length, all_in, all_out, *refs[2 * parts + 2 :])
    for n in range(parts):
        out_refs[n][...] = all_out[me_ref[0] ^ n]


def attend_kernel(length, in_ref, out_ref, expo_ref, kt_ref, vt_ref, dk_ref, dv_ref):
    parts = in_ref.shape[0]
    scale = ATT_DIM ** (-0.5)
    rate = scale * LOG2E
    key_in = iota((length, length), 0)
    causal = key_in <= iota((length, length), 1)
    for a in range(in_ref.shape[1]):

        def piece(block, place):
            return in_ref[block, a, place * length : (place + 1) * length, :]

        for i in range(parts):
            kt_ref[i] = flip(piece(i, 1))
            vt_ref[i] = flip(piece(i, 2))
            queries, grads = piece(i, 0), piece(i, 3)
            marks = in_ref[i, a, 4 * length :, :].astype(F32)
            starts = jnp.concatenate(
                [
                    marks[2 * n : 2 * n + 1] * 128.0 + marks[2 * n + 1 : 2 * n + 2]
                    for n in range(length // 128)
                ],
                axis=1,
            ).astype(jnp.int32)
            query_at = i * length + iota((1, length), 1)
            if parts * length > WINDOW:
                starts = jnp.maximum(starts, query_at - (WINDOW - 1))
            top = jnp.full((1, length), MASKED, F32)
            total = jnp.zeros((1, length), F32)
            tops = []
            for j in range(i + 1):
                seen = key_in >= starts - j * length
                if j == i:
                    seen = seen & causal
                raw = jnp.where(seen, dot_nt(piece(j, 1), queries), MASKED)
                new = jnp.maximum(top, jnp.max(raw, axis=0, keepdims=True))
                expo = jnp.exp2((raw - new) * rate)
                expo_ref[j] = expo
                total = total * jnp.exp2((top - new) * rate) + jnp.sum(expo, axis=0, keepdims=True)
                top = new
                tops.append(new)
            out = jnp.zeros((ATT_DIM, length), F32)
            for j in range(i + 1):
                probs = expo_ref[j] * (jnp.exp2((tops[j] - top) * rate) / total)
                expo_ref[j] = probs
                weights = probs.astype(BF16)
                dvalue = dot(weights, grads)
                dv_ref[j] = dvalue if j == i else dv_ref[j] + dvalue
                out = out + dot(vt_ref[j], weights)
            delta = jnp.sum(out * grads.astype(F32).T, axis=0, keepdims=True)
            dquery = jnp.zeros((ATT_DIM, length), F32)
            for j in range(i + 1):
                dprobs = dot_nt(piece(j, 2), grads)
                dscore = (expo_ref[j] * ((dprobs - delta) * scale)).astype(BF16)
                dkey = dot(dscore, queries)
                dk_ref[j] = dkey if j == i else dk_ref[j] + dkey
                dquery = dquery + dot(kt_ref[j], dscore)
            out_ref[i, a, 0:length, :] = out.T.astype(BF16)
            out_ref[i, a, length : 2 * length, :] = dquery.T.astype(BF16)
        for j in range(parts):
            out_ref[j, a, 2 * length : 3 * length, :] = dk_ref[j].astype(BF16)
            out_ref[j, a, 3 * length :, :] = dv_ref[j].astype(BF16)


def shifted(shard, axis, by):
    devices = lax.axis_size(axis)
    pairs = [(i, i + by) for i in range(devices) if 0 <= i + by < devices]
    return lax.ppermute(shard, axis, pairs)


def head_cols(array, head_index):
    return lax.dynamic_slice_in_dim(array, head_index * ATT_DIM, ATT_DIM, 1)


def ring_attention(att_queries, att_keys, att_values, att_grad, doc_start):
    length = att_queries.shape[0]
    shard_index = lax.axis_index("ctx")
    halo_shards = WINDOW // length
    att_count = att_queries.shape[1] // ATT_DIM
    att_width = att_queries.shape[1]
    score_scale = ATT_DIM ** (-0.5)

    def pass_keys(running, unused):
        moved = shifted((running[0], running[1]), "ctx", 1)
        return (moved, moved)

    _, earlier = lax.scan(pass_keys, (att_keys, att_values), None, length=halo_shards)
    key_all = jnp.concatenate(
        [earlier[0][::-1].reshape(halo_shards * length, att_width), att_keys], axis=0
    )
    value_all = jnp.concatenate(
        [earlier[1][::-1].reshape(halo_shards * length, att_width), att_values], axis=0
    )
    spread_rows = (halo_shards + 1) * length
    query_pos = shard_index * length + jnp.arange(length, dtype=jnp.int32)
    key_pos = (shard_index - halo_shards) * length + jnp.arange(spread_rows, dtype=jnp.int32)
    visible = (
        (key_pos[None, :] <= query_pos[:, None])
        & (query_pos[:, None] - key_pos[None, :] < WINDOW)
        & (key_pos[None, :] >= doc_start[:, None])
    )

    def forward_head(head_index, running):
        out_buf, max_buf, total_buf, delta_buf = running
        query_head = head_cols(att_queries, head_index)
        key_head = head_cols(key_all, head_index)
        value_head = head_cols(value_all, head_index)
        score = (
            jnp.einsum("td,sd->ts", query_head, key_head, preferred_element_type=jnp.float32)
            * score_scale
        )
        row_max = jnp.max(jnp.where(visible, score, -jnp.inf), axis=1)
        expo = jnp.where(visible, jnp.exp(score - row_max[:, None]), 0.0)
        row_total = jnp.sum(expo, axis=1)
        weights = (expo / row_total[:, None]).astype(jnp.bfloat16)
        attended = jnp.dot(weights, value_head, preferred_element_type=jnp.float32)
        delta = jnp.sum(head_cols(att_grad, head_index).astype(jnp.float32) * attended, axis=1)
        out_buf = lax.dynamic_update_slice_in_dim(
            out_buf, attended.astype(jnp.bfloat16), head_index * ATT_DIM, 1
        )
        return (
            out_buf,
            max_buf.at[:, head_index].set(row_max),
            total_buf.at[:, head_index].set(row_total),
            delta_buf.at[:, head_index].set(delta),
        )

    stats_zero = jnp.zeros((length, att_count), jnp.float32)
    window_out, row_maxes, row_totals, row_deltas = lax.fori_loop(
        0,
        att_count,
        forward_head,
        (jnp.zeros((length, att_width), jnp.bfloat16), stats_zero, stats_zero, stats_zero),
    )

    def query_terms(head_index):
        query_head = head_cols(att_queries, head_index)
        key_head = head_cols(key_all, head_index)
        value_head = head_cols(value_all, head_index)
        grad_head = head_cols(att_grad, head_index)
        score = (
            jnp.einsum("td,sd->ts", query_head, key_head, preferred_element_type=jnp.float32)
            * score_scale
        )
        probs = (
            jnp.where(visible, jnp.exp(score - row_maxes[:, head_index][:, None]), 0.0)
            / row_totals[:, head_index][:, None]
        )
        weights = probs.astype(jnp.bfloat16)
        dprobs = jnp.einsum("td,sd->ts", grad_head, value_head, preferred_element_type=jnp.float32)
        dscore = (probs * (dprobs - row_deltas[:, head_index][:, None]) * score_scale).astype(
            jnp.bfloat16
        )
        query_part = jnp.dot(dscore, key_head, preferred_element_type=jnp.float32)
        return (query_head, grad_head, weights, dscore, query_part)

    def backward_head(head_index, running):
        query_buf, key_buf, value_buf = running
        query_head, grad_head, weights, dscore, query_part = query_terms(head_index)
        key_part = jnp.einsum("ts,td->sd", dscore, query_head, preferred_element_type=jnp.float32)
        value_part = jnp.einsum("ts,td->sd", weights, grad_head, preferred_element_type=jnp.float32)
        query_buf = lax.dynamic_update_slice_in_dim(query_buf, query_part, head_index * ATT_DIM, 1)
        key_buf = lax.dynamic_update_slice_in_dim(key_buf, key_part, head_index * ATT_DIM, 1)
        value_buf = lax.dynamic_update_slice_in_dim(value_buf, value_part, head_index * ATT_DIM, 1)
        return (query_buf, key_buf, value_buf)

    part_zero = jnp.zeros((spread_rows, att_width), jnp.float32)
    query_sum, key_parts, value_parts = lax.fori_loop(
        0,
        att_count,
        backward_head,
        (jnp.zeros((length, att_width), jnp.float32), part_zero, part_zero),
    )
    key_blocks = key_parts.reshape(halo_shards + 1, length, att_width)
    value_blocks = value_parts.reshape(halo_shards + 1, length, att_width)

    def send_back(running, block_index):
        moved = shifted((running[0], running[1]), "ctx", -1)
        return ((moved[0] + key_blocks[block_index], moved[1] + value_blocks[block_index]), None)

    (key_sum, value_sum), _ = lax.scan(
        send_back, (key_blocks[0], value_blocks[0]), jnp.arange(1, halo_shards + 1, dtype=jnp.int32)
    )
    return (
        window_out,
        query_sum.astype(jnp.bfloat16),
        key_sum.astype(jnp.bfloat16),
        value_sum.astype(jnp.bfloat16),
    )


def body(
    ssm_input,
    gate_input,
    write_map,
    read_map,
    log_decay,
    doc_start,
    ssm_grad,
    att_queries,
    att_keys,
    att_values,
    att_grad,
):
    length, width = ssm_input.shape
    heads = width // HEAD_DIM
    parts = lax.axis_size("ctx")
    shares = parts // 2
    rows = width // shares
    full_width = width * lax.axis_size("head")
    att_width = att_queries.shape[1]
    per = att_width // ATT_DIM // parts
    dealt = att_width // ATT_DIM % parts == 0
    place = lax.axis_index("ctx")
    starts = doc_start.reshape(1, length)
    me = place.reshape(1).astype(jnp.int32)
    tailed = [shape((rows + TAIL, 128), BF16)] * shares
    plain = [shape((rows, 128), BF16)] * shares
    held_tails = pltpu.VMEM((shares, rows + TAIL, 128), BF16)
    held_plain = pltpu.VMEM((shares, rows, 128), BF16)

    def carry_total(backward, *blocks):
        return call(
            lambda *refs: total_kernel(backward, shares, *refs),
            shape((rows, 128), BF16), me, *blocks,
            specs=[SMEM] + [VMEM] * len(blocks),
            scratch=[held_tails, held_plain] if backward else [held_tails],
            vmem=SMALL, name="ssm_total",
        )

    def carry_states(backward, start, *blocks):
        return call(
            lambda *refs: carry_kernel(backward, shares, *refs),
            plain, me, start, *blocks,
            specs=[SMEM] + [VMEM] * (1 + len(blocks)),
            scratch=[held_tails, held_plain, held_plain] if backward else [held_tails, held_plain],
            vmem=SMALL, name="ssm_carry",
        )

    lcol, lrow, *sent = call(
        lambda *refs: first_kernel(shares, *refs),
        [shape((length, heads), F32), shape((heads, length), F32)] + tailed,
        me, log_decay.T, starts, write_map, ssm_input,
        specs=[SMEM] + [VMEM] * 4, scratch=[held_tails], name="ssm_first",
    )
    tails = [pass_block(block, n) for n, block in enumerate(sent)]
    total = carry_total(False, *tails)
    if dealt:
        marks = doc_start.reshape(length // 128, 128)
        marks = jnp.stack([marks // 128, marks % 128], axis=1).reshape(length // 64, 128)
        marks = jnp.pad(marks, ((0, TAIL - length // 64), (0, 0))).astype(BF16)
        packed = call(
            pack_kernel, [shape((per, 4 * length + TAIL, 128), BF16)] * parts,
            me, marks, att_queries, att_keys, att_values, att_grad,
            specs=[SMEM] + [VMEM] * 5, vmem=SMALL, name="att_pack",
        )
        crossed, total = lax.optimization_barrier((pass_block(packed[shares], shares), total))
        start = cross(total, False)
        packed, start = lax.optimization_barrier((packed, start))
        att_got = {n: pass_block(block, n) for n, block in enumerate(packed) if n != shares}
        att_got[shares] = crossed
    else:
        att_out = ring_attention(att_queries, att_keys, att_values, att_grad, doc_start)
        start = cross(total, False)
    state = [
        pass_block(block, n) for n, block in enumerate(carry_states(False, start, *tails))
    ]
    mixed, sums, state = call(
        lambda *refs: mix_kernel(shares, *refs),
        (shape((length, width), F32), shape((8, length), F32), shape((width, 128), BF16)),
        me, ssm_input, gate_input, ssm_grad, write_map, read_map, starts, lcol, lrow, *state,
        specs=[SMEM] + [VMEM] * (8 + shares), name="ssm_mix",
    )
    sums = lax.psum(sums, "head")
    mixer_out, gate_grad, dmixed, *sent = call(
        lambda *refs: gate_kernel(full_width, shares, *refs),
        [shape((length, width), BF16)] * 3 + plain,
        me, sums, mixed, gate_input, ssm_grad, read_map, starts, lrow,
        specs=[SMEM] + [VMEM] * 7, scratch=[held_plain], name="ssm_gate",
    )

    if dealt:
        rest = [n for n in range(1, parts - 1) if n != shares]
        done, sent = lax.optimization_barrier(([att_got[n] for n in rest], sent))
        att_got.update(zip(rest, done))
    blocks = [pass_block(block, n) for n, block in enumerate(sent)]
    if dealt:
        att_in, sent = lax.optimization_barrier(([att_got[n] for n in range(parts)], sent))
        att_done = call(
            lambda *refs: attend_blocks(length, parts, *refs),
            [shape((per, 4 * length, 128), BF16)] * parts, me, *att_in,
            specs=[SMEM] + [VMEM] * parts,
            scratch=[
                pltpu.VMEM((parts, per, 4 * length + TAIL, 128), BF16),
                pltpu.VMEM((parts, per, 4 * length, 128), BF16),
                pltpu.VMEM((parts, length, length), F32),
                pltpu.VMEM((parts, ATT_DIM, length), BF16),
                pltpu.VMEM((parts, ATT_DIM, length), BF16),
                pltpu.VMEM((parts, length, ATT_DIM), F32),
                pltpu.VMEM((parts, length, ATT_DIM), F32),
            ],
            flops=6 * per * (parts * length) ** 2 * ATT_DIM, name="att_attend",
        )
        blocks, att_done = lax.optimization_barrier((blocks, att_done))
    total = carry_total(True, *tails, *blocks)
    start = cross(total, True)
    carried = carry_states(True, start, *tails, *blocks)
    back = [pass_block(block, n) for n, block in enumerate(carried)]
    gin, read_part, write_part = call(
        inner_kernel,
        (shape((length, width), F32), shape((length, 128), F32), shape((length, 128), F32)),
        me, dmixed, ssm_input, write_map, read_map, starts, lcol, lrow, state,
        specs=[SMEM] + [VMEM] * 8, name="ssm_inner",
    )
    if dealt:
        early = [shares, shares + 1]
        middle = [shares + 2]
        late = [*range(shares + 3, parts), *range(1, shares)]
        att_back = {0: att_done[0]}
        held, total = lax.optimization_barrier((att_done, total))
        att_back.update((n, pass_block(held[n], n)) for n in early)
        held, carried = lax.optimization_barrier((att_done, carried))
        att_back.update((n, pass_block(held[n], n)) for n in middle)
        held, back, gin = lax.optimization_barrier((att_done, back, gin))
        att_back.update((n, pass_block(held[n], n)) for n in late)
        done, back = lax.optimization_barrier(([att_back[n] for n in early], back))
        att_back.update(zip(early, done))
        att_out = call(
            unpack_kernel, (shape((length, att_width), BF16),) * 4,
            me, *[att_back[n] for n in range(parts)],
            specs=[SMEM] + [VMEM] * parts, vmem=SMALL, name="att_unpack",
        )

    input_grad, write_part = call(
        lambda *refs: last_kernel(shares, *refs),
        (shape((length, width), BF16), shape((length, 128), F32)),
        me, gin, ssm_input, write_map, starts, lcol, write_part, *back,
        specs=[SMEM] + [VMEM] * (6 + shares),
        scratch=[pltpu.VMEM((width, 128), BF16)], name="ssm_last",
    )
    write_sum, read_sum = lax.psum((write_part, read_part), "head")
    window_out, query_grad, key_grad, value_grad = att_out
    return (
        mixer_out,
        window_out,
        input_grad,
        gate_grad,
        write_sum.astype(BF16),
        read_sum.astype(BF16),
        query_grad,
        key_grad,
        value_grad,
    )


def solution(mesh):
    in_specs = (
        P("ctx", "head"),
        P("ctx", "head"),
        P("ctx", None),
        P("ctx", None),
        P("ctx", "head"),
        P("ctx"),
        P("ctx", "head"),
        P("ctx", "head"),
        P("ctx", "head"),
        P("ctx", "head"),
        P("ctx", "head"),
    )
    out_specs = (
        P("ctx", "head"),
        P("ctx", "head"),
        P("ctx", "head"),
        P("ctx", "head"),
        P("ctx", None),
        P("ctx", None),
        P("ctx", "head"),
        P("ctx", "head"),
        P("ctx", "head"),
    )
    return jax.shard_map(body, mesh=mesh, in_specs=in_specs, out_specs=out_specs, check_vma=False)
```

```python
import jax
import jax.numpy as jnp
from jax import lax
from jax.experimental import pallas as pl
from jax.experimental.pallas import tpu as pltpu
from jax.sharding import PartitionSpec as P

HEAD_DIM = 128
ATT_DIM = 128
WINDOW = 4096
EPSILON = 1e-05
LOG2E = 1.4426950408889634
TAIL = 16
MASKED = -1e30
HIGH = lax.Precision.HIGHEST
F32 = jnp.float32
BF16 = jnp.bfloat16
VMEM_BYTES = 56 * 1024 * 1024


VMEM = pl.BlockSpec(memory_space=pltpu.VMEM)
SMEM = pl.BlockSpec(memory_space=pltpu.SMEM)
SMALL = 16 * 1024 * 1024


def call(kernel, out_shape, *operands, specs=None, scratch=(), flops=0, vmem=VMEM_BYTES, name=None):
    moved = sum(a.size * a.dtype.itemsize for a in jax.tree.leaves((operands, out_shape)))
    return pl.pallas_call(
        kernel,
        out_shape=out_shape,
        in_specs=specs or [VMEM] * len(operands),
        out_specs=jax.tree.map(lambda _: VMEM, out_shape),
        scratch_shapes=scratch,
        compiler_params=pltpu.CompilerParams(vmem_limit_bytes=vmem),
        cost_estimate=pl.CostEstimate(flops=flops, bytes_accessed=moved, transcendentals=0),
        name=name,
    )(*operands)


def shape(dims, dtype):
    return jax.ShapeDtypeStruct(dims, dtype)


def dot(a, b):
    return jnp.dot(a, b, preferred_element_type=F32)


def dot_nt(a, b, precision=None):
    return lax.dot_general(
        a, b, (((1,), (1,)), ((), ())), preferred_element_type=F32, precision=precision
    )


def iota(dims, axis):
    return lax.broadcasted_iota(jnp.int32, dims, axis)


def flip(a):
    return a.astype(F32).T.astype(BF16)


def column(row):
    return jnp.broadcast_to(row, (128, row.shape[1])).T


def cols(h):
    return slice(h * HEAD_DIM, (h + 1) * HEAD_DIM)


def shifted_starts(me_ref, starts_ref):
    return starts_ref[...] - me_ref[0] * starts_ref.shape[1]


def deal(me_ref, held, out_refs):
    share = me_ref[0] & (len(out_refs) - 1)
    for n, out_ref in enumerate(out_refs):
        out_ref[...] = held[share ^ n]


def collect(me_ref, in_refs, held):
    share = me_ref[0] & (len(in_refs) - 1)
    for n, in_ref in enumerate(in_refs):
        held[share ^ n] = in_ref[...]


def gather_state(me_ref, in_refs, state_ref):
    rows = in_refs[0].shape[0]
    share = me_ref[0] & (len(in_refs) - 1)
    for n, in_ref in enumerate(in_refs):
        here = pl.ds(pl.multiple_of((share ^ n) * rows, rows), rows)
        state_ref[here, :] = in_ref[...]


def first_kernel(shares, me_ref, ld_ref, rel_ref, w_ref, x_ref, lcol_ref, lrow_ref, *refs):
    out_refs, out_ref = refs[:shares], refs[shares]
    heads, length = ld_ref.shape
    rel_row = shifted_starts(me_ref, rel_ref)
    parts, rows = out_ref.shape[0], out_ref.shape[1] - TAIL
    rates = ld_ref[...] * LOG2E
    lower = jnp.where(iota((length, length), 0) >= iota((length, length), 1), 1.0, 0.0)
    upper = jnp.where(iota((length, length), 0) <= iota((length, length), 1), 1.0, 0.0)
    lcol_ref[...] = dot_nt(lower, rates, HIGH)
    lrow = jnp.dot(rates, upper, preferred_element_type=F32, precision=HIGH)
    lrow_ref[...] = lrow
    rel_last = rel_row[:, length - 1 :]
    last_doc = iota((1, length), 1) >= rel_last
    keeps = rel_last < 0
    writes = w_ref[...].astype(F32).T
    tail_row = iota((TAIL, 128), 0)
    for h in range(heads):
        line = lrow[h : h + 1, :]
        total = line[:, length - 1 :]
        to_end = jnp.where(last_doc, jnp.exp2(total - line), 0.0)
        state = dot((writes * to_end).astype(BF16), x_ref[:, cols(h)]).astype(BF16)
        factor = jnp.where(keeps, jnp.exp2(total), 0.0)
        high = factor.astype(BF16).astype(F32)
        low = factor - high
        first = h * HEAD_DIM
        for part in range(first // rows, (first + HEAD_DIM - 1) // rows + 1):
            begin = max(first, part * rows)
            end = min(first + HEAD_DIM, (part + 1) * rows)
            out_ref[part, begin - part * rows : end - part * rows, :] = state[
                begin - first : end - first, :
            ]
            place = 2 * (begin - part * rows) // HEAD_DIM
            tail = jnp.where(tail_row == place, high, jnp.where(tail_row == place + 1, low, 0.0))
            if place:
                tail = tail + out_ref[part, rows:, :].astype(F32)
            out_ref[part, rows:, :] = tail.astype(BF16)
    deal(me_ref, out_ref, out_refs)


def carry(backward, start_ref, tails, held, total_ref, out):
    shares, rows = tails.shape[0], tails.shape[1] - TAIL
    step = min(rows, HEAD_DIM)
    for k in range(rows // step):
        here = slice(k * step, (k + 1) * step)
        state = jnp.zeros((step, 128), F32) if start_ref is None else start_ref[here, :].astype(F32)
        for c in range(shares)[:: -1 if backward else 1]:
            if out is not None:
                out[c, here, :] = state.astype(BF16)
            tail = tails[c, rows:, :].astype(F32)
            factor = tail[2 * k : 2 * k + 1, :] + tail[2 * k + 1 : 2 * k + 2, :]
            state = factor * state + held[c, here, :].astype(F32)
        if total_ref is not None:
            total_ref[here, :] = state.astype(BF16)


def total_kernel(backward, shares, me_ref, *refs):
    count = 2 if backward else 1
    in_refs, (total_ref, *held) = refs[: count * shares], refs[count * shares :]
    for n in range(count):
        collect(me_ref, in_refs[n * shares : (n + 1) * shares], held[n])
    carry(backward, None, held[0], held[-1], total_ref, None)


def carry_kernel(backward, shares, me_ref, start_ref, *refs):
    count = 2 if backward else 1
    in_refs, out_refs = refs[: count * shares], refs[count * shares : (count + 1) * shares]
    *held, out = refs[(count + 1) * shares :]
    for n in range(count):
        collect(me_ref, in_refs[n * shares : (n + 1) * shares], held[n])
    carry(backward, start_ref, held[0], held[-1], None, out)
    deal(me_ref, out, out_refs)


def mix_kernel(
    shares, me_ref, x_ref, gate_ref, grad_ref, w_ref, r_ref, rel_ref, lcol_ref, lrow_ref, *refs
):
    state_refs, (mixed_ref, sums_ref, s_ref) = refs[:shares], refs[shares:]
    gather_state(me_ref, state_refs, s_ref)
    length, heads = lcol_ref.shape
    reads = r_ref[...]
    rel = column(shifted_starts(me_ref, rel_ref).astype(F32))
    wide = jnp.concatenate([rel] * (length // 128), axis=1)
    seen = (iota((length, length), 1).astype(F32) >= wide) & (
        iota((length, length), 1) <= iota((length, length), 0)
    )
    scores = jnp.where(seen, dot_nt(reads, w_ref[...]), 0.0)
    squares = jnp.zeros((length, 128), F32)
    inners = jnp.zeros((length, 128), F32)
    for h in range(heads):
        lc = lcol_ref[:, h : h + 1]
        decay = jnp.exp2(jnp.minimum(lc - lrow_ref[h : h + 1, :], 0.0))
        enter = jnp.where(rel < 0, jnp.exp2(jnp.broadcast_to(lc, rel.shape)), 0.0)
        mixed = dot((scores * decay).astype(BF16), x_ref[:, cols(h)]) + enter * dot(
            reads, s_ref[cols(h), :]
        )
        mixed_ref[:, cols(h)] = mixed
        gate = gate_ref[:, cols(h)].astype(F32)
        gated = mixed * (gate / (1.0 + jnp.exp(-gate)))
        squares = squares + gated * gated
        inners = inners + grad_ref[:, cols(h)].astype(F32) * gated
    ones = jnp.ones((8, 128), F32)
    square_row = dot_nt(ones, squares, HIGH)
    inner_row = dot_nt(ones, inners, HIGH)
    sums_ref[...] = jnp.where(iota((8, length), 0) == 0, square_row, inner_row)


def gate_kernel(
    width, shares, me_ref, sums_ref, mixed_ref, gate_ref, grad_ref, r_ref, rel_ref, lrow_ref,
    mixer_ref, ggrad_ref, dmixed_ref, *refs,
):
    out_refs, out_ref = refs[:shares], refs[shares]
    length = mixed_ref.shape[0]
    heads = lrow_ref.shape[0]
    rows = out_ref.shape[1]
    scale = lax.rsqrt(sums_ref[0:1, :] / width + EPSILON)
    rms = column(scale)
    pull = column(scale * scale * scale * sums_ref[1:2, :] / width)
    reads = r_ref[...].astype(F32).T
    enters = shifted_starts(me_ref, rel_ref) < 0
    for h in range(heads):
        mixed = mixed_ref[:, cols(h)]
        gate = gate_ref[:, cols(h)].astype(F32)
        sigma = 1.0 / (1.0 + jnp.exp(-gate))
        swish = gate * sigma
        gated = mixed * swish
        mixer_ref[:, cols(h)] = (gated * rms).astype(BF16)
        dgated = rms * grad_ref[:, cols(h)].astype(F32) - pull * gated
        dmixed = (dgated * swish).astype(BF16)
        dmixed_ref[:, cols(h)] = dmixed
        ggrad_ref[:, cols(h)] = (
            dgated * mixed * sigma * (1.0 + gate * (1.0 - sigma))
        ).astype(BF16)
        enter = jnp.where(enters, jnp.exp2(lrow_ref[h : h + 1, :]), 0.0)
        state = dot((reads * enter).astype(BF16), dmixed).astype(BF16)
        first = h * HEAD_DIM
        for part in range(first // rows, (first + HEAD_DIM - 1) // rows + 1):
            begin = max(first, part * rows)
            end = min(first + HEAD_DIM, (part + 1) * rows)
            out_ref[part, begin - part * rows : end - part * rows, :] = state[
                begin - first : end - first, :
            ]
    deal(me_ref, out_ref, out_refs)


def inner_kernel(
    me_ref, dmixed_ref, x_ref, w_ref, r_ref, rel_ref, lcol_ref, lrow_ref, s_ref, gin_ref, read_ref, write_ref
):
    length, heads = lcol_ref.shape
    rel_row = shifted_starts(me_ref, rel_ref)
    rel = column(rel_row.astype(F32))
    seen = (iota((length, length), 0) >= rel_row) & (
        iota((length, length), 0) <= iota((length, length), 1)
    )
    scores = jnp.where(seen, dot_nt(w_ref[...], r_ref[...]), 0.0)
    total = jnp.zeros((length, length), F32)
    read = jnp.zeros((length, 128), F32)
    for h in range(heads):
        lc = lcol_ref[:, h : h + 1]
        decay = jnp.exp2(jnp.minimum(lrow_ref[h : h + 1, :] - lc, 0.0))
        dmixed = dmixed_ref[:, cols(h)]
        gin_ref[:, cols(h)] = dot((scores * decay).astype(BF16), dmixed)
        total = total + decay * dot_nt(x_ref[:, cols(h)], dmixed)
        enter = jnp.where(rel < 0, jnp.exp2(jnp.broadcast_to(lc, rel.shape)), 0.0)
        read = read + enter * dot_nt(dmixed, s_ref[cols(h), :])
    total = jnp.where(seen, total, 0.0)
    write_ref[...] = dot(total.astype(BF16), r_ref[...])
    read_ref[...] = read + dot(total.T.astype(BF16), w_ref[...])


def last_kernel(shares, me_ref, gin_ref, x_ref, w_ref, rel_ref, lcol_ref, part_ref, *refs):
    state_refs, (out_ref, write_ref, back_ref) = refs[:shares], refs[shares:]
    gather_state(me_ref, state_refs, back_ref)
    length, heads = lcol_ref.shape
    rel_last = shifted_starts(me_ref, rel_ref)[:, length - 1 :]
    last_doc = iota((length, 128), 0) >= rel_last
    writes = w_ref[...]
    write = part_ref[...]
    for h in range(heads):
        lc = lcol_ref[:, h : h + 1]
        line = jnp.broadcast_to(lc[length - 1 :, :] - lc, (length, 128))
        to_end = jnp.where(last_doc, jnp.exp2(line), 0.0)
        back = back_ref[cols(h), :]
        out_ref[:, cols(h)] = (gin_ref[:, cols(h)] + to_end * dot(writes, back)).astype(BF16)
        write = write + to_end * dot_nt(x_ref[:, cols(h)], back)
    write_ref[...] = write


def pass_block(block, n):
    if n == 0:
        return block
    return lax.ppermute(block, "ctx", [(i, i ^ n) for i in range(lax.axis_size("ctx"))])


def cross(total, backward):
    count = lax.axis_size("ctx")
    half = count // 2
    pairs = [(i + half, i) if backward else (i, i + half) for i in range(half)]
    return lax.ppermute(total, "ctx", pairs)


def pack_kernel(me_ref, marks_ref, q_ref, k_ref, v_ref, g_ref, *out_refs):
    length = q_ref.shape[0]
    for n, out_ref in enumerate(out_refs):
        for a in range(out_ref.shape[0]):
            head = (me_ref[0] ^ n) * out_ref.shape[0] + a
            here = pl.ds(pl.multiple_of(head * ATT_DIM, ATT_DIM), ATT_DIM)
            for place, ref in enumerate((q_ref, k_ref, v_ref, g_ref)):
                out_ref[a, place * length : (place + 1) * length, :] = ref[:, here]
            out_ref[a, 4 * length :, :] = marks_ref[...]


def unpack_kernel(me_ref, *refs):
    in_refs, out_refs = refs[:-4], refs[-4:]
    length = out_refs[0].shape[0]
    for n, in_ref in enumerate(in_refs):
        for a in range(in_ref.shape[0]):
            head = (me_ref[0] ^ n) * in_ref.shape[0] + a
            here = pl.ds(pl.multiple_of(head * ATT_DIM, ATT_DIM), ATT_DIM)
            for place, ref in enumerate(out_refs):
                ref[:, here] = in_ref[a, place * length : (place + 1) * length, :]


def attend_blocks(length, parts, me_ref, *refs):
    in_refs, out_refs = refs[:parts], refs[parts : 2 * parts]
    all_in, all_out = refs[2 * parts : 2 * parts + 2]
    for n in range(parts):
        all_in[me_ref[0] ^ n] = in_refs[n][...]
    attend_kernel(length, all_in, all_out, *refs[2 * parts + 2 :])
    for n in range(parts):
        out_refs[n][...] = all_out[me_ref[0] ^ n]


def attend_kernel(length, in_ref, out_ref, expo_ref, kt_ref, vt_ref, dk_ref, dv_ref):
    parts = in_ref.shape[0]
    scale = ATT_DIM ** (-0.5)
    rate = scale * LOG2E
    key_in = iota((length, length), 0)
    causal = key_in <= iota((length, length), 1)
    for a in range(in_ref.shape[1]):

        def piece(block, place):
            return in_ref[block, a, place * length : (place + 1) * length, :]

        for i in range(parts):
            kt_ref[i] = flip(piece(i, 1))
            vt_ref[i] = flip(piece(i, 2))
            queries, grads = piece(i, 0), piece(i, 3)
            marks = in_ref[i, a, 4 * length :, :].astype(F32)
            starts = jnp.concatenate(
                [
                    marks[2 * n : 2 * n + 1] * 128.0 + marks[2 * n + 1 : 2 * n + 2]
                    for n in range(length // 128)
                ],
                axis=1,
            ).astype(jnp.int32)
            query_at = i * length + iota((1, length), 1)
            if parts * length > WINDOW:
                starts = jnp.maximum(starts, query_at - (WINDOW - 1))
            top = jnp.full((1, length), MASKED, F32)
            total = jnp.zeros((1, length), F32)
            tops = []
            for j in range(i + 1):
                seen = key_in >= starts - j * length
                if j == i:
                    seen = seen & causal
                raw = jnp.where(seen, dot_nt(piece(j, 1), queries), MASKED)
                new = jnp.maximum(top, jnp.max(raw, axis=0, keepdims=True))
                expo = jnp.exp2((raw - new) * rate)
                expo_ref[j] = expo
                total = total * jnp.exp2((top - new) * rate) + jnp.sum(expo, axis=0, keepdims=True)
                top = new
                tops.append(new)
            out = jnp.zeros((ATT_DIM, length), F32)
            for j in range(i + 1):
                probs = expo_ref[j] * (jnp.exp2((tops[j] - top) * rate) / total)
                expo_ref[j] = probs
                weights = probs.astype(BF16)
                dvalue = dot(weights, grads)
                dv_ref[j] = dvalue if j == i else dv_ref[j] + dvalue
                out = out + dot(vt_ref[j], weights)
            delta = jnp.sum(out * grads.astype(F32).T, axis=0, keepdims=True)
            dquery = jnp.zeros((ATT_DIM, length), F32)
            for j in range(i + 1):
                dprobs = dot_nt(piece(j, 2), grads)
                dscore = (expo_ref[j] * ((dprobs - delta) * scale)).astype(BF16)
                dkey = dot(dscore, queries)
                dk_ref[j] = dkey if j == i else dk_ref[j] + dkey
                dquery = dquery + dot(kt_ref[j], dscore)
            out_ref[i, a, 0:length, :] = out.T.astype(BF16)
            out_ref[i, a, length : 2 * length, :] = dquery.T.astype(BF16)
        for j in range(parts):
            out_ref[j, a, 2 * length : 3 * length, :] = dk_ref[j].astype(BF16)
            out_ref[j, a, 3 * length :, :] = dv_ref[j].astype(BF16)


def shifted(shard, axis, by):
    devices = lax.axis_size(axis)
    pairs = [(i, i + by) for i in range(devices) if 0 <= i + by < devices]
    return lax.ppermute(shard, axis, pairs)


def head_cols(array, head_index):
    return lax.dynamic_slice_in_dim(array, head_index * ATT_DIM, ATT_DIM, 1)


def ring_attention(att_queries, att_keys, att_values, att_grad, doc_start):
    length = att_queries.shape[0]
    shard_index = lax.axis_index("ctx")
    halo_shards = WINDOW // length
    att_count = att_queries.shape[1] // ATT_DIM
    att_width = att_queries.shape[1]
    score_scale = ATT_DIM ** (-0.5)

    def pass_keys(running, unused):
        moved = shifted((running[0], running[1]), "ctx", 1)
        return (moved, moved)

    _, earlier = lax.scan(pass_keys, (att_keys, att_values), None, length=halo_shards)
    key_all = jnp.concatenate(
        [earlier[0][::-1].reshape(halo_shards * length, att_width), att_keys], axis=0
    )
    value_all = jnp.concatenate(
        [earlier[1][::-1].reshape(halo_shards * length, att_width), att_values], axis=0
    )
    spread_rows = (halo_shards + 1) * length
    query_pos = shard_index * length + jnp.arange(length, dtype=jnp.int32)
    key_pos = (shard_index - halo_shards) * length + jnp.arange(spread_rows, dtype=jnp.int32)
    visible = (
        (key_pos[None, :] <= query_pos[:, None])
        & (query_pos[:, None] - key_pos[None, :] < WINDOW)
        & (key_pos[None, :] >= doc_start[:, None])
    )

    def forward_head(head_index, running):
        out_buf, max_buf, total_buf, delta_buf = running
        query_head = head_cols(att_queries, head_index)
        key_head = head_cols(key_all, head_index)
        value_head = head_cols(value_all, head_index)
        score = (
            jnp.einsum("td,sd->ts", query_head, key_head, preferred_element_type=jnp.float32)
            * score_scale
        )
        row_max = jnp.max(jnp.where(visible, score, -jnp.inf), axis=1)
        expo = jnp.where(visible, jnp.exp(score - row_max[:, None]), 0.0)
        row_total = jnp.sum(expo, axis=1)
        weights = (expo / row_total[:, None]).astype(jnp.bfloat16)
        attended = jnp.dot(weights, value_head, preferred_element_type=jnp.float32)
        delta = jnp.sum(head_cols(att_grad, head_index).astype(jnp.float32) * attended, axis=1)
        out_buf = lax.dynamic_update_slice_in_dim(
            out_buf, attended.astype(jnp.bfloat16), head_index * ATT_DIM, 1
        )
        return (
            out_buf,
            max_buf.at[:, head_index].set(row_max),
            total_buf.at[:, head_index].set(row_total),
            delta_buf.at[:, head_index].set(delta),
        )

    stats_zero = jnp.zeros((length, att_count), jnp.float32)
    window_out, row_maxes, row_totals, row_deltas = lax.fori_loop(
        0,
        att_count,
        forward_head,
        (jnp.zeros((length, att_width), jnp.bfloat16), stats_zero, stats_zero, stats_zero),
    )

    def query_terms(head_index):
        query_head = head_cols(att_queries, head_index)
        key_head = head_cols(key_all, head_index)
        value_head = head_cols(value_all, head_index)
        grad_head = head_cols(att_grad, head_index)
        score = (
            jnp.einsum("td,sd->ts", query_head, key_head, preferred_element_type=jnp.float32)
            * score_scale
        )
        probs = (
            jnp.where(visible, jnp.exp(score - row_maxes[:, head_index][:, None]), 0.0)
            / row_totals[:, head_index][:, None]
        )
        weights = probs.astype(jnp.bfloat16)
        dprobs = jnp.einsum("td,sd->ts", grad_head, value_head, preferred_element_type=jnp.float32)
        dscore = (probs * (dprobs - row_deltas[:, head_index][:, None]) * score_scale).astype(
            jnp.bfloat16
        )
        query_part = jnp.dot(dscore, key_head, preferred_element_type=jnp.float32)
        return (query_head, grad_head, weights, dscore, query_part)

    def backward_head(head_index, running):
        query_buf, key_buf, value_buf = running
        query_head, grad_head, weights, dscore, query_part = query_terms(head_index)
        key_part = jnp.einsum("ts,td->sd", dscore, query_head, preferred_element_type=jnp.float32)
        value_part = jnp.einsum("ts,td->sd", weights, grad_head, preferred_element_type=jnp.float32)
        query_buf = lax.dynamic_update_slice_in_dim(query_buf, query_part, head_index * ATT_DIM, 1)
        key_buf = lax.dynamic_update_slice_in_dim(key_buf, key_part, head_index * ATT_DIM, 1)
        value_buf = lax.dynamic_update_slice_in_dim(value_buf, value_part, head_index * ATT_DIM, 1)
        return (query_buf, key_buf, value_buf)

    part_zero = jnp.zeros((spread_rows, att_width), jnp.float32)
    query_sum, key_parts, value_parts = lax.fori_loop(
        0,
        att_count,
        backward_head,
        (jnp.zeros((length, att_width), jnp.float32), part_zero, part_zero),
    )
    key_blocks = key_parts.reshape(halo_shards + 1, length, att_width)
    value_blocks = value_parts.reshape(halo_shards + 1, length, att_width)

    def send_back(running, block_index):
        moved = shifted((running[0], running[1]), "ctx", -1)
        return ((moved[0] + key_blocks[block_index], moved[1] + value_blocks[block_index]), None)

    (key_sum, value_sum), _ = lax.scan(
        send_back, (key_blocks[0], value_blocks[0]), jnp.arange(1, halo_shards + 1, dtype=jnp.int32)
    )
    return (
        window_out,
        query_sum.astype(jnp.bfloat16),
        key_sum.astype(jnp.bfloat16),
        value_sum.astype(jnp.bfloat16),
    )


def body(
    ssm_input,
    gate_input,
    write_map,
    read_map,
    log_decay,
    doc_start,
    ssm_grad,
    att_queries,
    att_keys,
    att_values,
    att_grad,
):
    length, width = ssm_input.shape
    heads = width // HEAD_DIM
    parts = lax.axis_size("ctx")
    shares = parts // 2
    rows = width // shares
    full_width = width * lax.axis_size("head")
    att_width = att_queries.shape[1]
    per = att_width // ATT_DIM // parts
    dealt = att_width // ATT_DIM % parts == 0
    place = lax.axis_index("ctx")
    starts = doc_start.reshape(1, length)
    me = place.reshape(1).astype(jnp.int32)
    tailed = [shape((rows + TAIL, 128), BF16)] * shares
    plain = [shape((rows, 128), BF16)] * shares
    held_tails = pltpu.VMEM((shares, rows + TAIL, 128), BF16)
    held_plain = pltpu.VMEM((shares, rows, 128), BF16)

    def carry_total(backward, *blocks):
        return call(
            lambda *refs: total_kernel(backward, shares, *refs),
            shape((rows, 128), BF16), me, *blocks,
            specs=[SMEM] + [VMEM] * len(blocks),
            scratch=[held_tails, held_plain] if backward else [held_tails],
            vmem=SMALL, name="ssm_total",
        )

    def carry_states(backward, start, *blocks):
        return call(
            lambda *refs: carry_kernel(backward, shares, *refs),
            plain, me, start, *blocks,
            specs=[SMEM] + [VMEM] * (1 + len(blocks)),
            scratch=[held_tails, held_plain, held_plain] if backward else [held_tails, held_plain],
            vmem=SMALL, name="ssm_carry",
        )

    lcol, lrow, *sent = call(
        lambda *refs: first_kernel(shares, *refs),
        [shape((length, heads), F32), shape((heads, length), F32)] + tailed,
        me, log_decay.T, starts, write_map, ssm_input,
        specs=[SMEM] + [VMEM] * 4, scratch=[held_tails], name="ssm_first",
    )
    tails = [pass_block(block, n) for n, block in enumerate(sent)]
    total = carry_total(False, *tails)
    start = cross(total, False)
    if dealt:
        marks = doc_start.reshape(length // 128, 128)
        marks = jnp.stack([marks // 128, marks % 128], axis=1).reshape(length // 64, 128)
        marks = jnp.pad(marks, ((0, TAIL - length // 64), (0, 0))).astype(BF16)
        marks, total = lax.optimization_barrier((marks, total))
        packed = call(
            pack_kernel, [shape((per, 4 * length + TAIL, 128), BF16)] * parts,
            me, marks, att_queries, att_keys, att_values, att_grad,
            specs=[SMEM] + [VMEM] * 5, vmem=SMALL, name="att_pack",
        )
        packed, start = lax.optimization_barrier((packed, start))
        att_got = {n: pass_block(block, n) for n, block in enumerate(packed)}
    else:
        att_out = ring_attention(att_queries, att_keys, att_values, att_grad, doc_start)
    state = [
        pass_block(block, n) for n, block in enumerate(carry_states(False, start, *tails))
    ]
    if dealt:
        att_got[shares], state = lax.optimization_barrier((att_got[shares], state))
    mixed, sums, state = call(
        lambda *refs: mix_kernel(shares, *refs),
        (shape((length, width), F32), shape((8, length), F32), shape((width, 128), BF16)),
        me, ssm_input, gate_input, ssm_grad, write_map, read_map, starts, lcol, lrow, *state,
        specs=[SMEM] + [VMEM] * (8 + shares), name="ssm_mix",
    )
    sums = lax.psum(sums, "head")
    mixer_out, gate_grad, dmixed, *sent = call(
        lambda *refs: gate_kernel(full_width, shares, *refs),
        [shape((length, width), BF16)] * 3 + plain,
        me, sums, mixed, gate_input, ssm_grad, read_map, starts, lrow,
        specs=[SMEM] + [VMEM] * 7, scratch=[held_plain], name="ssm_gate",
    )

    if dealt:
        rest = [n for n in range(1, parts - 1) if n != shares]
        done, sent = lax.optimization_barrier(([att_got[n] for n in rest], sent))
        att_got.update(zip(rest, done))
    blocks = [pass_block(block, n) for n, block in enumerate(sent)]
    gin, read_part, write_part = call(
        inner_kernel,
        (shape((length, width), F32), shape((length, 128), F32), shape((length, 128), F32)),
        me, dmixed, ssm_input, write_map, read_map, starts, lcol, lrow, state,
        specs=[SMEM] + [VMEM] * 8, name="ssm_inner",
    )
    blocks, gin = lax.optimization_barrier((blocks, gin))
    total = carry_total(True, *tails, *blocks)
    start = cross(total, True)
    if dealt:
        att_in, total = lax.optimization_barrier(([att_got[n] for n in range(parts)], total))
        att_done = call(
            lambda *refs: attend_blocks(length, parts, *refs),
            [shape((per, 4 * length, 128), BF16)] * parts, me, *att_in,
            specs=[SMEM] + [VMEM] * parts,
            scratch=[
                pltpu.VMEM((parts, per, 4 * length + TAIL, 128), BF16),
                pltpu.VMEM((parts, per, 4 * length, 128), BF16),
                pltpu.VMEM((parts, length, length), F32),
                pltpu.VMEM((parts, ATT_DIM, length), BF16),
                pltpu.VMEM((parts, ATT_DIM, length), BF16),
                pltpu.VMEM((parts, length, ATT_DIM), F32),
                pltpu.VMEM((parts, length, ATT_DIM), F32),
            ],
            flops=6 * per * (parts * length) ** 2 * ATT_DIM, name="att_attend",
        )
        start, att_done = lax.optimization_barrier((start, att_done))
    carried = carry_states(True, start, *tails, *blocks)
    back = [pass_block(block, n) for n, block in enumerate(carried)]
    if dealt:
        held, carried = lax.optimization_barrier((att_done, carried))
        att_back = {n: pass_block(held[n], n) for n in (0, shares)}
        held, back = lax.optimization_barrier((att_done, back))
        late = [*range(shares + 1, parts), *range(1, shares)]
        att_back.update((n, pass_block(held[n], n)) for n in late)
        att_out = call(
            unpack_kernel, (shape((length, att_width), BF16),) * 4,
            me, *[att_back[n] for n in range(parts)],
            specs=[SMEM] + [VMEM] * parts, vmem=SMALL, name="att_unpack",
        )

    input_grad, write_part = call(
        lambda *refs: last_kernel(shares, *refs),
        (shape((length, width), BF16), shape((length, 128), F32)),
        me, gin, ssm_input, write_map, starts, lcol, write_part, *back,
        specs=[SMEM] + [VMEM] * (6 + shares),
        scratch=[pltpu.VMEM((width, 128), BF16)], name="ssm_last",
    )
    write_sum, read_sum = lax.psum((write_part, read_part), "head")
    window_out, query_grad, key_grad, value_grad = att_out
    return (
        mixer_out,
        window_out,
        input_grad,
        gate_grad,
        write_sum.astype(BF16),
        read_sum.astype(BF16),
        query_grad,
        key_grad,
        value_grad,
    )


def solution(mesh):
    in_specs = (
        P("ctx", "head"),
        P("ctx", "head"),
        P("ctx", None),
        P("ctx", None),
        P("ctx", "head"),
        P("ctx"),
        P("ctx", "head"),
        P("ctx", "head"),
        P("ctx", "head"),
        P("ctx", "head"),
        P("ctx", "head"),
    )
    out_specs = (
        P("ctx", "head"),
        P("ctx", "head"),
        P("ctx", "head"),
        P("ctx", "head"),
        P("ctx", None),
        P("ctx", None),
        P("ctx", "head"),
        P("ctx", "head"),
        P("ctx", "head"),
    )
    return jax.shard_map(body, mesh=mesh, in_specs=in_specs, out_specs=out_specs, check_vma=False)
```

```python
import jax
import jax.numpy as jnp
from jax import lax
from jax.experimental import pallas as pl
from jax.experimental.pallas import tpu as pltpu
from jax.sharding import PartitionSpec as P

HEAD_DIM = 128
ATT_DIM = 128
WINDOW = 4096
EPSILON = 1e-05
LOG2E = 1.4426950408889634
TAIL = 16
MASKED = -1e30
HIGH = lax.Precision.HIGHEST
F32 = jnp.float32
BF16 = jnp.bfloat16
VMEM_BYTES = 56 * 1024 * 1024


VMEM = pl.BlockSpec(memory_space=pltpu.VMEM)
SMEM = pl.BlockSpec(memory_space=pltpu.SMEM)
SMALL = 16 * 1024 * 1024


def call(kernel, out_shape, *operands, specs=None, scratch=(), flops=0, vmem=VMEM_BYTES, name=None):
    moved = sum(a.size * a.dtype.itemsize for a in jax.tree.leaves((operands, out_shape)))
    return pl.pallas_call(
        kernel,
        out_shape=out_shape,
        in_specs=specs or [VMEM] * len(operands),
        out_specs=jax.tree.map(lambda _: VMEM, out_shape),
        scratch_shapes=scratch,
        compiler_params=pltpu.CompilerParams(vmem_limit_bytes=vmem),
        cost_estimate=pl.CostEstimate(flops=flops, bytes_accessed=moved, transcendentals=0),
        name=name,
    )(*operands)


def shape(dims, dtype):
    return jax.ShapeDtypeStruct(dims, dtype)


def dot(a, b):
    return jnp.dot(a, b, preferred_element_type=F32)


def dot_nt(a, b, precision=None):
    return lax.dot_general(
        a, b, (((1,), (1,)), ((), ())), preferred_element_type=F32, precision=precision
    )


def iota(dims, axis):
    return lax.broadcasted_iota(jnp.int32, dims, axis)


def flip(a):
    return a.astype(F32).T.astype(BF16)


def column(row):
    return jnp.broadcast_to(row, (128, row.shape[1])).T


def cols(h):
    return slice(h * HEAD_DIM, (h + 1) * HEAD_DIM)


def shifted_starts(me_ref, starts_ref):
    return starts_ref[...] - me_ref[0] * starts_ref.shape[1]


def deal(me_ref, held, out_refs):
    share = me_ref[0] & (len(out_refs) - 1)
    for n, out_ref in enumerate(out_refs):
        out_ref[...] = held[share ^ n]


def collect(me_ref, in_refs, held):
    share = me_ref[0] & (len(in_refs) - 1)
    for n, in_ref in enumerate(in_refs):
        held[share ^ n] = in_ref[...]


def gather_state(me_ref, in_refs, state_ref):
    rows = in_refs[0].shape[0]
    share = me_ref[0] & (len(in_refs) - 1)
    for n, in_ref in enumerate(in_refs):
        here = pl.ds(pl.multiple_of((share ^ n) * rows, rows), rows)
        state_ref[here, :] = in_ref[...]


def first_kernel(shares, me_ref, ld_ref, rel_ref, w_ref, x_ref, lcol_ref, lrow_ref, *refs):
    out_refs, out_ref = refs[:shares], refs[shares]
    heads, length = ld_ref.shape
    rel_row = shifted_starts(me_ref, rel_ref)
    parts, rows = out_ref.shape[0], out_ref.shape[1] - TAIL
    rates = ld_ref[...] * LOG2E
    lower = jnp.where(iota((length, length), 0) >= iota((length, length), 1), 1.0, 0.0)
    upper = jnp.where(iota((length, length), 0) <= iota((length, length), 1), 1.0, 0.0)
    lcol_ref[...] = dot_nt(lower, rates, HIGH)
    lrow = jnp.dot(rates, upper, preferred_element_type=F32, precision=HIGH)
    lrow_ref[...] = lrow
    rel_last = rel_row[:, length - 1 :]
    last_doc = iota((1, length), 1) >= rel_last
    keeps = rel_last < 0
    writes = w_ref[...].astype(F32).T
    tail_row = iota((TAIL, 128), 0)
    for h in range(heads):
        line = lrow[h : h + 1, :]
        total = line[:, length - 1 :]
        to_end = jnp.where(last_doc, jnp.exp2(total - line), 0.0)
        state = dot((writes * to_end).astype(BF16), x_ref[:, cols(h)]).astype(BF16)
        factor = jnp.where(keeps, jnp.exp2(total), 0.0)
        high = factor.astype(BF16).astype(F32)
        low = factor - high
        first = h * HEAD_DIM
        for part in range(first // rows, (first + HEAD_DIM - 1) // rows + 1):
            begin = max(first, part * rows)
            end = min(first + HEAD_DIM, (part + 1) * rows)
            out_ref[part, begin - part * rows : end - part * rows, :] = state[
                begin - first : end - first, :
            ]
            place = 2 * (begin - part * rows) // HEAD_DIM
            tail = jnp.where(tail_row == place, high, jnp.where(tail_row == place + 1, low, 0.0))
            if place:
                tail = tail + out_ref[part, rows:, :].astype(F32)
            out_ref[part, rows:, :] = tail.astype(BF16)
    deal(me_ref, out_ref, out_refs)


def carry(backward, start_ref, tails, held, total_ref, out):
    shares, rows = tails.shape[0], tails.shape[1] - TAIL
    step = min(rows, HEAD_DIM)
    for k in range(rows // step):
        here = slice(k * step, (k + 1) * step)
        state = jnp.zeros((step, 128), F32) if start_ref is None else start_ref[here, :].astype(F32)
        for c in range(shares)[:: -1 if backward else 1]:
            if out is not None:
                out[c, here, :] = state.astype(BF16)
            tail = tails[c, rows:, :].astype(F32)
            factor = tail[2 * k : 2 * k + 1, :] + tail[2 * k + 1 : 2 * k + 2, :]
            state = factor * state + held[c, here, :].astype(F32)
        if total_ref is not None:
            total_ref[here, :] = state.astype(BF16)


def total_kernel(backward, shares, me_ref, *refs):
    count = 2 if backward else 1
    in_refs, (total_ref, *held) = refs[: count * shares], refs[count * shares :]
    for n in range(count):
        collect(me_ref, in_refs[n * shares : (n + 1) * shares], held[n])
    carry(backward, None, held[0], held[-1], total_ref, None)


def carry_kernel(backward, shares, me_ref, start_ref, *refs):
    count = 2 if backward else 1
    in_refs, out_refs = refs[: count * shares], refs[count * shares : (count + 1) * shares]
    *held, out = refs[(count + 1) * shares :]
    for n in range(count):
        collect(me_ref, in_refs[n * shares : (n + 1) * shares], held[n])
    carry(backward, start_ref, held[0], held[-1], None, out)
    deal(me_ref, out, out_refs)


def mix_kernel(
    shares, me_ref, x_ref, gate_ref, grad_ref, w_ref, r_ref, rel_ref, lcol_ref, lrow_ref, *refs
):
    state_refs, (mixed_ref, sums_ref, s_ref) = refs[:shares], refs[shares:]
    gather_state(me_ref, state_refs, s_ref)
    length, heads = lcol_ref.shape
    reads = r_ref[...]
    rel = column(shifted_starts(me_ref, rel_ref).astype(F32))
    wide = jnp.concatenate([rel] * (length // 128), axis=1)
    seen = (iota((length, length), 1).astype(F32) >= wide) & (
        iota((length, length), 1) <= iota((length, length), 0)
    )
    scores = jnp.where(seen, dot_nt(reads, w_ref[...]), 0.0)
    squares = jnp.zeros((length, 128), F32)
    inners = jnp.zeros((length, 128), F32)
    for h in range(heads):
        lc = lcol_ref[:, h : h + 1]
        decay = jnp.exp2(jnp.minimum(lc - lrow_ref[h : h + 1, :], 0.0))
        enter = jnp.where(rel < 0, jnp.exp2(jnp.broadcast_to(lc, rel.shape)), 0.0)
        mixed = dot((scores * decay).astype(BF16), x_ref[:, cols(h)]) + enter * dot(
            reads, s_ref[cols(h), :]
        )
        mixed_ref[:, cols(h)] = mixed
        gate = gate_ref[:, cols(h)].astype(F32)
        gated = mixed * (gate / (1.0 + jnp.exp(-gate)))
        squares = squares + gated * gated
        inners = inners + grad_ref[:, cols(h)].astype(F32) * gated
    ones = jnp.ones((8, 128), F32)
    square_row = dot_nt(ones, squares, HIGH)
    inner_row = dot_nt(ones, inners, HIGH)
    sums_ref[...] = jnp.where(iota((8, length), 0) == 0, square_row, inner_row)


def gate_kernel(
    width, shares, me_ref, sums_ref, mixed_ref, gate_ref, grad_ref, r_ref, rel_ref, lrow_ref,
    mixer_ref, ggrad_ref, dmixed_ref, *refs,
):
    out_refs, out_ref = refs[:shares], refs[shares]
    length = mixed_ref.shape[0]
    heads = lrow_ref.shape[0]
    rows = out_ref.shape[1]
    scale = lax.rsqrt(sums_ref[0:1, :] / width + EPSILON)
    rms = column(scale)
    pull = column(scale * scale * scale * sums_ref[1:2, :] / width)
    reads = r_ref[...].astype(F32).T
    enters = shifted_starts(me_ref, rel_ref) < 0
    for h in range(heads):
        mixed = mixed_ref[:, cols(h)]
        gate = gate_ref[:, cols(h)].astype(F32)
        sigma = 1.0 / (1.0 + jnp.exp(-gate))
        swish = gate * sigma
        gated = mixed * swish
        mixer_ref[:, cols(h)] = (gated * rms).astype(BF16)
        dgated = rms * grad_ref[:, cols(h)].astype(F32) - pull * gated
        dmixed = (dgated * swish).astype(BF16)
        dmixed_ref[:, cols(h)] = dmixed
        ggrad_ref[:, cols(h)] = (
            dgated * mixed * sigma * (1.0 + gate * (1.0 - sigma))
        ).astype(BF16)
        enter = jnp.where(enters, jnp.exp2(lrow_ref[h : h + 1, :]), 0.0)
        state = dot((reads * enter).astype(BF16), dmixed).astype(BF16)
        first = h * HEAD_DIM
        for part in range(first // rows, (first + HEAD_DIM - 1) // rows + 1):
            begin = max(first, part * rows)
            end = min(first + HEAD_DIM, (part + 1) * rows)
            out_ref[part, begin - part * rows : end - part * rows, :] = state[
                begin - first : end - first, :
            ]
    deal(me_ref, out_ref, out_refs)


def inner_kernel(
    me_ref, dmixed_ref, x_ref, w_ref, r_ref, rel_ref, lcol_ref, lrow_ref, s_ref, gin_ref, read_ref, write_ref
):
    length, heads = lcol_ref.shape
    rel_row = shifted_starts(me_ref, rel_ref)
    rel = column(rel_row.astype(F32))
    seen = (iota((length, length), 0) >= rel_row) & (
        iota((length, length), 0) <= iota((length, length), 1)
    )
    scores = jnp.where(seen, dot_nt(w_ref[...], r_ref[...]), 0.0)
    total = jnp.zeros((length, length), F32)
    read = jnp.zeros((length, 128), F32)
    for h in range(heads):
        lc = lcol_ref[:, h : h + 1]
        decay = jnp.exp2(jnp.minimum(lrow_ref[h : h + 1, :] - lc, 0.0))
        dmixed = dmixed_ref[:, cols(h)]
        gin_ref[:, cols(h)] = dot((scores * decay).astype(BF16), dmixed)
        total = total + decay * dot_nt(x_ref[:, cols(h)], dmixed)
        enter = jnp.where(rel < 0, jnp.exp2(jnp.broadcast_to(lc, rel.shape)), 0.0)
        read = read + enter * dot_nt(dmixed, s_ref[cols(h), :])
    total = jnp.where(seen, total, 0.0)
    write_ref[...] = dot(total.astype(BF16), r_ref[...])
    read_ref[...] = read + dot(total.T.astype(BF16), w_ref[...])


def last_kernel(shares, me_ref, gin_ref, x_ref, w_ref, rel_ref, lcol_ref, part_ref, *refs):
    state_refs, (out_ref, write_ref, back_ref) = refs[:shares], refs[shares:]
    gather_state(me_ref, state_refs, back_ref)
    length, heads = lcol_ref.shape
    rel_last = shifted_starts(me_ref, rel_ref)[:, length - 1 :]
    last_doc = iota((length, 128), 0) >= rel_last
    writes = w_ref[...]
    write = part_ref[...]
    for h in range(heads):
        lc = lcol_ref[:, h : h + 1]
        line = jnp.broadcast_to(lc[length - 1 :, :] - lc, (length, 128))
        to_end = jnp.where(last_doc, jnp.exp2(line), 0.0)
        back = back_ref[cols(h), :]
        out_ref[:, cols(h)] = (gin_ref[:, cols(h)] + to_end * dot(writes, back)).astype(BF16)
        write = write + to_end * dot_nt(x_ref[:, cols(h)], back)
    write_ref[...] = write


def pass_block(block, n):
    if n == 0:
        return block
    return lax.ppermute(block, "ctx", [(i, i ^ n) for i in range(lax.axis_size("ctx"))])


def cross(total, backward):
    count = lax.axis_size("ctx")
    half = count // 2
    pairs = [(i + half, i) if backward else (i, i + half) for i in range(half)]
    return lax.ppermute(total, "ctx", pairs)


def pack_kernel(me_ref, marks_ref, q_ref, k_ref, v_ref, g_ref, *out_refs):
    length = q_ref.shape[0]
    for n, out_ref in enumerate(out_refs):
        for a in range(out_ref.shape[0]):
            head = (me_ref[0] ^ n) * out_ref.shape[0] + a
            here = pl.ds(pl.multiple_of(head * ATT_DIM, ATT_DIM), ATT_DIM)
            for place, ref in enumerate((q_ref, k_ref, v_ref, g_ref)):
                out_ref[a, place * length : (place + 1) * length, :] = ref[:, here]
            out_ref[a, 4 * length :, :] = marks_ref[...]


def unpack_kernel(me_ref, *refs):
    in_refs, out_refs = refs[:-4], refs[-4:]
    length = out_refs[0].shape[0]
    for n, in_ref in enumerate(in_refs):
        for a in range(in_ref.shape[0]):
            head = (me_ref[0] ^ n) * in_ref.shape[0] + a
            here = pl.ds(pl.multiple_of(head * ATT_DIM, ATT_DIM), ATT_DIM)
            for place, ref in enumerate(out_refs):
                ref[:, here] = in_ref[a, place * length : (place + 1) * length, :]


def attend_blocks(length, parts, me_ref, *refs):
    in_refs, out_refs = refs[:parts], refs[parts : 2 * parts]
    all_in, all_out = refs[2 * parts : 2 * parts + 2]
    for n in range(parts):
        all_in[me_ref[0] ^ n] = in_refs[n][...]
    attend_kernel(length, all_in, all_out, *refs[2 * parts + 2 :])
    for n in range(parts):
        out_refs[n][...] = all_out[me_ref[0] ^ n]


def attend_kernel(length, in_ref, out_ref, expo_ref, kt_ref, vt_ref, dk_ref, dv_ref):
    parts = in_ref.shape[0]
    scale = ATT_DIM ** (-0.5)
    rate = scale * LOG2E
    key_in = iota((length, length), 0)
    causal = key_in <= iota((length, length), 1)
    for a in range(in_ref.shape[1]):

        def piece(block, place):
            return in_ref[block, a, place * length : (place + 1) * length, :]

        for i in range(parts):
            kt_ref[i] = flip(piece(i, 1))
            vt_ref[i] = flip(piece(i, 2))
            queries, grads = piece(i, 0), piece(i, 3)
            marks = in_ref[i, a, 4 * length :, :].astype(F32)
            starts = jnp.concatenate(
                [
                    marks[2 * n : 2 * n + 1] * 128.0 + marks[2 * n + 1 : 2 * n + 2]
                    for n in range(length // 128)
                ],
                axis=1,
            ).astype(jnp.int32)
            query_at = i * length + iota((1, length), 1)
            if parts * length > WINDOW:
                starts = jnp.maximum(starts, query_at - (WINDOW - 1))
            top = jnp.full((1, length), MASKED, F32)
            total = jnp.zeros((1, length), F32)
            tops = []
            for j in range(i + 1):
                seen = key_in >= starts - j * length
                if j == i:
                    seen = seen & causal
                raw = jnp.where(seen, dot_nt(piece(j, 1), queries), MASKED)
                new = jnp.maximum(top, jnp.max(raw, axis=0, keepdims=True))
                expo = jnp.exp2((raw - new) * rate)
                expo_ref[j] = expo
                total = total * jnp.exp2((top - new) * rate) + jnp.sum(expo, axis=0, keepdims=True)
                top = new
                tops.append(new)
            out = jnp.zeros((ATT_DIM, length), F32)
            for j in range(i + 1):
                probs = expo_ref[j] * (jnp.exp2((tops[j] - top) * rate) / total)
                expo_ref[j] = probs
                weights = probs.astype(BF16)
                dvalue = dot(weights, grads)
                dv_ref[j] = dvalue if j == i else dv_ref[j] + dvalue
                out = out + dot(vt_ref[j], weights)
            delta = jnp.sum(out * grads.astype(F32).T, axis=0, keepdims=True)
            dquery = jnp.zeros((ATT_DIM, length), F32)
            for j in range(i + 1):
                dprobs = dot_nt(piece(j, 2), grads)
                dscore = (expo_ref[j] * ((dprobs - delta) * scale)).astype(BF16)
                dkey = dot(dscore, queries)
                dk_ref[j] = dkey if j == i else dk_ref[j] + dkey
                dquery = dquery + dot(kt_ref[j], dscore)
            out_ref[i, a, 0:length, :] = out.T.astype(BF16)
            out_ref[i, a, length : 2 * length, :] = dquery.T.astype(BF16)
        for j in range(parts):
            out_ref[j, a, 2 * length : 3 * length, :] = dk_ref[j].astype(BF16)
            out_ref[j, a, 3 * length :, :] = dv_ref[j].astype(BF16)


def shifted(shard, axis, by):
    devices = lax.axis_size(axis)
    pairs = [(i, i + by) for i in range(devices) if 0 <= i + by < devices]
    return lax.ppermute(shard, axis, pairs)


def head_cols(array, head_index):
    return lax.dynamic_slice_in_dim(array, head_index * ATT_DIM, ATT_DIM, 1)


def ring_attention(att_queries, att_keys, att_values, att_grad, doc_start):
    length = att_queries.shape[0]
    shard_index = lax.axis_index("ctx")
    halo_shards = WINDOW // length
    att_count = att_queries.shape[1] // ATT_DIM
    att_width = att_queries.shape[1]
    score_scale = ATT_DIM ** (-0.5)

    def pass_keys(running, unused):
        moved = shifted((running[0], running[1]), "ctx", 1)
        return (moved, moved)

    _, earlier = lax.scan(pass_keys, (att_keys, att_values), None, length=halo_shards)
    key_all = jnp.concatenate(
        [earlier[0][::-1].reshape(halo_shards * length, att_width), att_keys], axis=0
    )
    value_all = jnp.concatenate(
        [earlier[1][::-1].reshape(halo_shards * length, att_width), att_values], axis=0
    )
    spread_rows = (halo_shards + 1) * length
    query_pos = shard_index * length + jnp.arange(length, dtype=jnp.int32)
    key_pos = (shard_index - halo_shards) * length + jnp.arange(spread_rows, dtype=jnp.int32)
    visible = (
        (key_pos[None, :] <= query_pos[:, None])
        & (query_pos[:, None] - key_pos[None, :] < WINDOW)
        & (key_pos[None, :] >= doc_start[:, None])
    )

    def forward_head(head_index, running):
        out_buf, max_buf, total_buf, delta_buf = running
        query_head = head_cols(att_queries, head_index)
        key_head = head_cols(key_all, head_index)
        value_head = head_cols(value_all, head_index)
        score = (
            jnp.einsum("td,sd->ts", query_head, key_head, preferred_element_type=jnp.float32)
            * score_scale
        )
        row_max = jnp.max(jnp.where(visible, score, -jnp.inf), axis=1)
        expo = jnp.where(visible, jnp.exp(score - row_max[:, None]), 0.0)
        row_total = jnp.sum(expo, axis=1)
        weights = (expo / row_total[:, None]).astype(jnp.bfloat16)
        attended = jnp.dot(weights, value_head, preferred_element_type=jnp.float32)
        delta = jnp.sum(head_cols(att_grad, head_index).astype(jnp.float32) * attended, axis=1)
        out_buf = lax.dynamic_update_slice_in_dim(
            out_buf, attended.astype(jnp.bfloat16), head_index * ATT_DIM, 1
        )
        return (
            out_buf,
            max_buf.at[:, head_index].set(row_max),
            total_buf.at[:, head_index].set(row_total),
            delta_buf.at[:, head_index].set(delta),
        )

    stats_zero = jnp.zeros((length, att_count), jnp.float32)
    window_out, row_maxes, row_totals, row_deltas = lax.fori_loop(
        0,
        att_count,
        forward_head,
        (jnp.zeros((length, att_width), jnp.bfloat16), stats_zero, stats_zero, stats_zero),
    )

    def query_terms(head_index):
        query_head = head_cols(att_queries, head_index)
        key_head = head_cols(key_all, head_index)
        value_head = head_cols(value_all, head_index)
        grad_head = head_cols(att_grad, head_index)
        score = (
            jnp.einsum("td,sd->ts", query_head, key_head, preferred_element_type=jnp.float32)
            * score_scale
        )
        probs = (
            jnp.where(visible, jnp.exp(score - row_maxes[:, head_index][:, None]), 0.0)
            / row_totals[:, head_index][:, None]
        )
        weights = probs.astype(jnp.bfloat16)
        dprobs = jnp.einsum("td,sd->ts", grad_head, value_head, preferred_element_type=jnp.float32)
        dscore = (probs * (dprobs - row_deltas[:, head_index][:, None]) * score_scale).astype(
            jnp.bfloat16
        )
        query_part = jnp.dot(dscore, key_head, preferred_element_type=jnp.float32)
        return (query_head, grad_head, weights, dscore, query_part)

    def backward_head(head_index, running):
        query_buf, key_buf, value_buf = running
        query_head, grad_head, weights, dscore, query_part = query_terms(head_index)
        key_part = jnp.einsum("ts,td->sd", dscore, query_head, preferred_element_type=jnp.float32)
        value_part = jnp.einsum("ts,td->sd", weights, grad_head, preferred_element_type=jnp.float32)
        query_buf = lax.dynamic_update_slice_in_dim(query_buf, query_part, head_index * ATT_DIM, 1)
        key_buf = lax.dynamic_update_slice_in_dim(key_buf, key_part, head_index * ATT_DIM, 1)
        value_buf = lax.dynamic_update_slice_in_dim(value_buf, value_part, head_index * ATT_DIM, 1)
        return (query_buf, key_buf, value_buf)

    part_zero = jnp.zeros((spread_rows, att_width), jnp.float32)
    query_sum, key_parts, value_parts = lax.fori_loop(
        0,
        att_count,
        backward_head,
        (jnp.zeros((length, att_width), jnp.float32), part_zero, part_zero),
    )
    key_blocks = key_parts.reshape(halo_shards + 1, length, att_width)
    value_blocks = value_parts.reshape(halo_shards + 1, length, att_width)

    def send_back(running, block_index):
        moved = shifted((running[0], running[1]), "ctx", -1)
        return ((moved[0] + key_blocks[block_index], moved[1] + value_blocks[block_index]), None)

    (key_sum, value_sum), _ = lax.scan(
        send_back, (key_blocks[0], value_blocks[0]), jnp.arange(1, halo_shards + 1, dtype=jnp.int32)
    )
    return (
        window_out,
        query_sum.astype(jnp.bfloat16),
        key_sum.astype(jnp.bfloat16),
        value_sum.astype(jnp.bfloat16),
    )


def body(
    ssm_input,
    gate_input,
    write_map,
    read_map,
    log_decay,
    doc_start,
    ssm_grad,
    att_queries,
    att_keys,
    att_values,
    att_grad,
):
    length, width = ssm_input.shape
    heads = width // HEAD_DIM
    parts = lax.axis_size("ctx")
    shares = parts // 2
    rows = width // shares
    full_width = width * lax.axis_size("head")
    att_width = att_queries.shape[1]
    per = att_width // ATT_DIM // parts
    dealt = att_width // ATT_DIM % parts == 0
    place = lax.axis_index("ctx")
    starts = doc_start.reshape(1, length)
    me = place.reshape(1).astype(jnp.int32)
    tailed = [shape((rows + TAIL, 128), BF16)] * shares
    plain = [shape((rows, 128), BF16)] * shares
    held_tails = pltpu.VMEM((shares, rows + TAIL, 128), BF16)
    held_plain = pltpu.VMEM((shares, rows, 128), BF16)

    def carry_total(backward, *blocks):
        return call(
            lambda *refs: total_kernel(backward, shares, *refs),
            shape((rows, 128), BF16), me, *blocks,
            specs=[SMEM] + [VMEM] * len(blocks),
            scratch=[held_tails, held_plain] if backward else [held_tails],
            vmem=SMALL, name="ssm_total",
        )

    def carry_states(backward, start, *blocks):
        return call(
            lambda *refs: carry_kernel(backward, shares, *refs),
            plain, me, start, *blocks,
            specs=[SMEM] + [VMEM] * (1 + len(blocks)),
            scratch=[held_tails, held_plain, held_plain] if backward else [held_tails, held_plain],
            vmem=SMALL, name="ssm_carry",
        )

    lcol, lrow, *sent = call(
        lambda *refs: first_kernel(shares, *refs),
        [shape((length, heads), F32), shape((heads, length), F32)] + tailed,
        me, log_decay.T, starts, write_map, ssm_input,
        specs=[SMEM] + [VMEM] * 4, scratch=[held_tails], name="ssm_first",
    )
    tails = [pass_block(block, n) for n, block in enumerate(sent)]
    total = carry_total(False, *tails)
    start = cross(total, False)
    if dealt:
        marks = doc_start.reshape(length // 128, 128)
        marks = jnp.stack([marks // 128, marks % 128], axis=1).reshape(length // 64, 128)
        marks = jnp.pad(marks, ((0, TAIL - length // 64), (0, 0))).astype(BF16)
        marks, total = lax.optimization_barrier((marks, total))
        packed = call(
            pack_kernel, [shape((per, 4 * length + TAIL, 128), BF16)] * parts,
            me, marks, att_queries, att_keys, att_values, att_grad,
            specs=[SMEM] + [VMEM] * 5, vmem=SMALL, name="att_pack",
        )
        packed, start = lax.optimization_barrier((packed, start))
        att_got = {n: pass_block(packed[n], n) for n in (0, shares)}
    else:
        att_out = ring_attention(att_queries, att_keys, att_values, att_grad, doc_start)
    state = [
        pass_block(block, n) for n, block in enumerate(carry_states(False, start, *tails))
    ]
    if dealt:
        att_got[shares], state = lax.optimization_barrier((att_got[shares], state))
    if dealt:
        packed, att_got[shares], state = lax.optimization_barrier((packed, att_got[shares], state))
        soon = [*range(shares + 1, parts), 1]
        att_got.update((n, pass_block(packed[n], n)) for n in soon)
    mixed, sums, state = call(
        lambda *refs: mix_kernel(shares, *refs),
        (shape((length, width), F32), shape((8, length), F32), shape((width, 128), BF16)),
        me, ssm_input, gate_input, ssm_grad, write_map, read_map, starts, lcol, lrow, *state,
        specs=[SMEM] + [VMEM] * (8 + shares), name="ssm_mix",
    )
    sums = lax.psum(sums, "head")
    mixer_out, gate_grad, dmixed, *sent = call(
        lambda *refs: gate_kernel(full_width, shares, *refs),
        [shape((length, width), BF16)] * 3 + plain,
        me, sums, mixed, gate_input, ssm_grad, read_map, starts, lrow,
        specs=[SMEM] + [VMEM] * 7, scratch=[held_plain], name="ssm_gate",
    )

    if dealt:
        rest = [*range(shares + 1, parts - 1), 1]
        done, sent = lax.optimization_barrier(([att_got[n] for n in rest], sent))
        att_got.update(zip(rest, done))
    blocks = [pass_block(block, n) for n, block in enumerate(sent)]
    if dealt:
        packed, blocks = lax.optimization_barrier((packed, blocks))
        att_got.update((n, pass_block(packed[n], n)) for n in range(2, shares))
    gin, read_part, write_part = call(
        inner_kernel,
        (shape((length, width), F32), shape((length, 128), F32), shape((length, 128), F32)),
        me, dmixed, ssm_input, write_map, read_map, starts, lcol, lrow, state,
        specs=[SMEM] + [VMEM] * 8, name="ssm_inner",
    )
    blocks, gin = lax.optimization_barrier((blocks, gin))
    total = carry_total(True, *tails, *blocks)
    start = cross(total, True)
    if dealt:
        att_in, total = lax.optimization_barrier(([att_got[n] for n in range(parts)], total))
        att_done = call(
            lambda *refs: attend_blocks(length, parts, *refs),
            [shape((per, 4 * length, 128), BF16)] * parts, me, *att_in,
            specs=[SMEM] + [VMEM] * parts,
            scratch=[
                pltpu.VMEM((parts, per, 4 * length + TAIL, 128), BF16),
                pltpu.VMEM((parts, per, 4 * length, 128), BF16),
                pltpu.VMEM((parts, length, length), F32),
                pltpu.VMEM((parts, ATT_DIM, length), BF16),
                pltpu.VMEM((parts, ATT_DIM, length), BF16),
                pltpu.VMEM((parts, length, ATT_DIM), F32),
                pltpu.VMEM((parts, length, ATT_DIM), F32),
            ],
            flops=6 * per * (parts * length) ** 2 * ATT_DIM, name="att_attend",
        )
        start, att_done = lax.optimization_barrier((start, att_done))
    carried = carry_states(True, start, *tails, *blocks)
    back = [pass_block(block, n) for n, block in enumerate(carried)]
    if dealt:
        held, carried = lax.optimization_barrier((att_done, carried))
        att_back = {n: pass_block(held[n], n) for n in (0, shares)}
        held, back = lax.optimization_barrier((att_done, back))
        late = [*range(shares + 1, parts), *range(1, shares)]
        att_back.update((n, pass_block(held[n], n)) for n in late)
        att_out = call(
            unpack_kernel, (shape((length, att_width), BF16),) * 4,
            me, *[att_back[n] for n in range(parts)],
            specs=[SMEM] + [VMEM] * parts, vmem=SMALL, name="att_unpack",
        )

    input_grad, write_part = call(
        lambda *refs: last_kernel(shares, *refs),
        (shape((length, width), BF16), shape((length, 128), F32)),
        me, gin, ssm_input, write_map, starts, lcol, write_part, *back,
        specs=[SMEM] + [VMEM] * (6 + shares),
        scratch=[pltpu.VMEM((width, 128), BF16)], name="ssm_last",
    )
    write_sum, read_sum = lax.psum((write_part, read_part), "head")
    window_out, query_grad, key_grad, value_grad = att_out
    return (
        mixer_out,
        window_out,
        input_grad,
        gate_grad,
        write_sum.astype(BF16),
        read_sum.astype(BF16),
        query_grad,
        key_grad,
        value_grad,
    )


def solution(mesh):
    in_specs = (
        P("ctx", "head"),
        P("ctx", "head"),
        P("ctx", None),
        P("ctx", None),
        P("ctx", "head"),
        P("ctx"),
        P("ctx", "head"),
        P("ctx", "head"),
        P("ctx", "head"),
        P("ctx", "head"),
        P("ctx", "head"),
    )
    out_specs = (
        P("ctx", "head"),
        P("ctx", "head"),
        P("ctx", "head"),
        P("ctx", "head"),
        P("ctx", None),
        P("ctx", None),
        P("ctx", "head"),
        P("ctx", "head"),
        P("ctx", "head"),
    )
    return jax.shard_map(body, mesh=mesh, in_specs=in_specs, out_specs=out_specs, check_vma=False)
```

```python
import jax
import jax.numpy as jnp
from jax import lax
from jax.experimental import pallas as pl
from jax.experimental.pallas import tpu as pltpu
from jax.sharding import PartitionSpec as P

HEAD_DIM = 128
ATT_DIM = 128
WINDOW = 4096
EPSILON = 1e-05
LOG2E = 1.4426950408889634
TAIL = 16
MASKED = -1e30
HIGH = lax.Precision.HIGHEST
F32 = jnp.float32
BF16 = jnp.bfloat16
VMEM_BYTES = 56 * 1024 * 1024


VMEM = pl.BlockSpec(memory_space=pltpu.VMEM)
SMEM = pl.BlockSpec(memory_space=pltpu.SMEM)
SMALL = 16 * 1024 * 1024


def call(kernel, out_shape, *operands, specs=None, scratch=(), flops=0, vmem=VMEM_BYTES, name=None):
    moved = sum(a.size * a.dtype.itemsize for a in jax.tree.leaves((operands, out_shape)))
    return pl.pallas_call(
        kernel,
        out_shape=out_shape,
        in_specs=specs or [VMEM] * len(operands),
        out_specs=jax.tree.map(lambda _: VMEM, out_shape),
        scratch_shapes=scratch,
        compiler_params=pltpu.CompilerParams(vmem_limit_bytes=vmem),
        cost_estimate=pl.CostEstimate(flops=flops, bytes_accessed=moved, transcendentals=0),
        name=name,
    )(*operands)


def shape(dims, dtype):
    return jax.ShapeDtypeStruct(dims, dtype)


def dot(a, b):
    return jnp.dot(a, b, preferred_element_type=F32)


def dot_nt(a, b, precision=None):
    return lax.dot_general(
        a, b, (((1,), (1,)), ((), ())), preferred_element_type=F32, precision=precision
    )


def iota(dims, axis):
    return lax.broadcasted_iota(jnp.int32, dims, axis)


def flip(a):
    return a.astype(F32).T.astype(BF16)


def column(row):
    return jnp.broadcast_to(row, (128, row.shape[1])).T


def cols(h):
    return slice(h * HEAD_DIM, (h + 1) * HEAD_DIM)


def shifted_starts(me_ref, starts_ref):
    return starts_ref[...] - me_ref[0] * starts_ref.shape[1]


def deal(me_ref, held, out_refs):
    share = me_ref[0] & (len(out_refs) - 1)
    for n, out_ref in enumerate(out_refs):
        out_ref[...] = held[share ^ n]


def collect(me_ref, in_refs, held):
    share = me_ref[0] & (len(in_refs) - 1)
    for n, in_ref in enumerate(in_refs):
        held[share ^ n] = in_ref[...]


def gather_state(me_ref, in_refs, state_ref):
    rows = in_refs[0].shape[0]
    share = me_ref[0] & (len(in_refs) - 1)
    for n, in_ref in enumerate(in_refs):
        here = pl.ds(pl.multiple_of((share ^ n) * rows, rows), rows)
        state_ref[here, :] = in_ref[...]


def first_kernel(shares, me_ref, ld_ref, rel_ref, w_ref, x_ref, lcol_ref, lrow_ref, *refs):
    out_refs, out_ref = refs[:shares], refs[shares]
    heads, length = ld_ref.shape
    rel_row = shifted_starts(me_ref, rel_ref)
    parts, rows = out_ref.shape[0], out_ref.shape[1] - TAIL
    rates = ld_ref[...] * LOG2E
    lower = jnp.where(iota((length, length), 0) >= iota((length, length), 1), 1.0, 0.0)
    upper = jnp.where(iota((length, length), 0) <= iota((length, length), 1), 1.0, 0.0)
    lcol_ref[...] = dot_nt(lower, rates, HIGH)
    lrow = jnp.dot(rates, upper, preferred_element_type=F32, precision=HIGH)
    lrow_ref[...] = lrow
    rel_last = rel_row[:, length - 1 :]
    last_doc = iota((1, length), 1) >= rel_last
    keeps = rel_last < 0
    writes = w_ref[...].astype(F32).T
    tail_row = iota((TAIL, 128), 0)
    for h in range(heads):
        line = lrow[h : h + 1, :]
        total = line[:, length - 1 :]
        to_end = jnp.where(last_doc, jnp.exp2(total - line), 0.0)
        state = dot((writes * to_end).astype(BF16), x_ref[:, cols(h)]).astype(BF16)
        factor = jnp.where(keeps, jnp.exp2(total), 0.0)
        high = factor.astype(BF16).astype(F32)
        low = factor - high
        first = h * HEAD_DIM
        for part in range(first // rows, (first + HEAD_DIM - 1) // rows + 1):
            begin = max(first, part * rows)
            end = min(first + HEAD_DIM, (part + 1) * rows)
            out_ref[part, begin - part * rows : end - part * rows, :] = state[
                begin - first : end - first, :
            ]
            place = 2 * (begin - part * rows) // HEAD_DIM
            tail = jnp.where(tail_row == place, high, jnp.where(tail_row == place + 1, low, 0.0))
            if place:
                tail = tail + out_ref[part, rows:, :].astype(F32)
            out_ref[part, rows:, :] = tail.astype(BF16)
    deal(me_ref, out_ref, out_refs)


def carry(backward, start_ref, tails, held, total_ref, out):
    shares, rows = tails.shape[0], tails.shape[1] - TAIL
    step = min(rows, HEAD_DIM)
    for k in range(rows // step):
        here = slice(k * step, (k + 1) * step)
        state = jnp.zeros((step, 128), F32) if start_ref is None else start_ref[here, :].astype(F32)
        for c in range(shares)[:: -1 if backward else 1]:
            if out is not None:
                out[c, here, :] = state.astype(BF16)
            tail = tails[c, rows:, :].astype(F32)
            factor = tail[2 * k : 2 * k + 1, :] + tail[2 * k + 1 : 2 * k + 2, :]
            state = factor * state + held[c, here, :].astype(F32)
        if total_ref is not None:
            total_ref[here, :] = state.astype(BF16)


def total_kernel(backward, shares, me_ref, *refs):
    count = 2 if backward else 1
    in_refs, (total_ref, *held) = refs[: count * shares], refs[count * shares :]
    for n in range(count):
        collect(me_ref, in_refs[n * shares : (n + 1) * shares], held[n])
    carry(backward, None, held[0], held[-1], total_ref, None)


def carry_kernel(backward, shares, me_ref, start_ref, *refs):
    count = 2 if backward else 1
    in_refs, out_refs = refs[: count * shares], refs[count * shares : (count + 1) * shares]
    *held, out = refs[(count + 1) * shares :]
    for n in range(count):
        collect(me_ref, in_refs[n * shares : (n + 1) * shares], held[n])
    carry(backward, start_ref, held[0], held[-1], None, out)
    deal(me_ref, out, out_refs)


def mix_kernel(
    shares, me_ref, x_ref, gate_ref, grad_ref, w_ref, r_ref, rel_ref, lcol_ref, lrow_ref, *refs
):
    state_refs, (mixed_ref, sums_ref, s_ref) = refs[:shares], refs[shares:]
    gather_state(me_ref, state_refs, s_ref)
    length, heads = lcol_ref.shape
    reads = r_ref[...]
    rel = column(shifted_starts(me_ref, rel_ref).astype(F32))
    wide = jnp.concatenate([rel] * (length // 128), axis=1)
    seen = (iota((length, length), 1).astype(F32) >= wide) & (
        iota((length, length), 1) <= iota((length, length), 0)
    )
    scores = jnp.where(seen, dot_nt(reads, w_ref[...]), 0.0)
    squares = jnp.zeros((length, 128), F32)
    inners = jnp.zeros((length, 128), F32)
    for h in range(heads):
        lc = lcol_ref[:, h : h + 1]
        decay = jnp.exp2(jnp.minimum(lc - lrow_ref[h : h + 1, :], 0.0))
        enter = jnp.where(rel < 0, jnp.exp2(jnp.broadcast_to(lc, rel.shape)), 0.0)
        mixed = dot((scores * decay).astype(BF16), x_ref[:, cols(h)]) + enter * dot(
            reads, s_ref[cols(h), :]
        )
        mixed_ref[:, cols(h)] = mixed
        gate = gate_ref[:, cols(h)].astype(F32)
        gated = mixed * (gate / (1.0 + jnp.exp(-gate)))
        squares = squares + gated * gated
        inners = inners + grad_ref[:, cols(h)].astype(F32) * gated
    ones = jnp.ones((8, 128), F32)
    square_row = dot_nt(ones, squares, HIGH)
    inner_row = dot_nt(ones, inners, HIGH)
    sums_ref[...] = jnp.where(iota((8, length), 0) == 0, square_row, inner_row)


def gate_kernel(
    width, shares, me_ref, sums_ref, mixed_ref, gate_ref, grad_ref, r_ref, rel_ref, lrow_ref,
    mixer_ref, ggrad_ref, dmixed_ref, *refs,
):
    out_refs, out_ref = refs[:shares], refs[shares]
    length = mixed_ref.shape[0]
    heads = lrow_ref.shape[0]
    rows = out_ref.shape[1]
    scale = lax.rsqrt(sums_ref[0:1, :] / width + EPSILON)
    rms = column(scale)
    pull = column(scale * scale * scale * sums_ref[1:2, :] / width)
    reads = r_ref[...].astype(F32).T
    enters = shifted_starts(me_ref, rel_ref) < 0
    for h in range(heads):
        mixed = mixed_ref[:, cols(h)]
        gate = gate_ref[:, cols(h)].astype(F32)
        sigma = 1.0 / (1.0 + jnp.exp(-gate))
        swish = gate * sigma
        gated = mixed * swish
        mixer_ref[:, cols(h)] = (gated * rms).astype(BF16)
        dgated = rms * grad_ref[:, cols(h)].astype(F32) - pull * gated
        dmixed = (dgated * swish).astype(BF16)
        dmixed_ref[:, cols(h)] = dmixed
        ggrad_ref[:, cols(h)] = (
            dgated * mixed * sigma * (1.0 + gate * (1.0 - sigma))
        ).astype(BF16)
        enter = jnp.where(enters, jnp.exp2(lrow_ref[h : h + 1, :]), 0.0)
        state = dot((reads * enter).astype(BF16), dmixed).astype(BF16)
        first = h * HEAD_DIM
        for part in range(first // rows, (first + HEAD_DIM - 1) // rows + 1):
            begin = max(first, part * rows)
            end = min(first + HEAD_DIM, (part + 1) * rows)
            out_ref[part, begin - part * rows : end - part * rows, :] = state[
                begin - first : end - first, :
            ]
    deal(me_ref, out_ref, out_refs)


def inner_kernel(
    me_ref, dmixed_ref, x_ref, w_ref, r_ref, rel_ref, lcol_ref, lrow_ref, s_ref, gin_ref, read_ref, write_ref
):
    length, heads = lcol_ref.shape
    rel_row = shifted_starts(me_ref, rel_ref)
    rel = column(rel_row.astype(F32))
    seen = (iota((length, length), 0) >= rel_row) & (
        iota((length, length), 0) <= iota((length, length), 1)
    )
    scores = jnp.where(seen, dot_nt(w_ref[...], r_ref[...]), 0.0)
    total = jnp.zeros((length, length), F32)
    read = jnp.zeros((length, 128), F32)
    for h in range(heads):
        lc = lcol_ref[:, h : h + 1]
        decay = jnp.exp2(jnp.minimum(lrow_ref[h : h + 1, :] - lc, 0.0))
        dmixed = dmixed_ref[:, cols(h)]
        gin_ref[:, cols(h)] = dot((scores * decay).astype(BF16), dmixed)
        total = total + decay * dot_nt(x_ref[:, cols(h)], dmixed)
        enter = jnp.where(rel < 0, jnp.exp2(jnp.broadcast_to(lc, rel.shape)), 0.0)
        read = read + enter * dot_nt(dmixed, s_ref[cols(h), :])
    total = jnp.where(seen, total, 0.0)
    write_ref[...] = dot(total.astype(BF16), r_ref[...])
    read_ref[...] = read + dot(total.T.astype(BF16), w_ref[...])


def last_kernel(shares, me_ref, gin_ref, x_ref, w_ref, rel_ref, lcol_ref, part_ref, *refs):
    state_refs, (out_ref, write_ref, back_ref) = refs[:shares], refs[shares:]
    gather_state(me_ref, state_refs, back_ref)
    length, heads = lcol_ref.shape
    rel_last = shifted_starts(me_ref, rel_ref)[:, length - 1 :]
    last_doc = iota((length, 128), 0) >= rel_last
    writes = w_ref[...]
    write = part_ref[...]
    for h in range(heads):
        lc = lcol_ref[:, h : h + 1]
        line = jnp.broadcast_to(lc[length - 1 :, :] - lc, (length, 128))
        to_end = jnp.where(last_doc, jnp.exp2(line), 0.0)
        back = back_ref[cols(h), :]
        out_ref[:, cols(h)] = (gin_ref[:, cols(h)] + to_end * dot(writes, back)).astype(BF16)
        write = write + to_end * dot_nt(x_ref[:, cols(h)], back)
    write_ref[...] = write


def pass_block(block, n):
    if n == 0:
        return block
    return lax.ppermute(block, "ctx", [(i, i ^ n) for i in range(lax.axis_size("ctx"))])


def cross(total, backward):
    count = lax.axis_size("ctx")
    half = count // 2
    pairs = [(i + half, i) if backward else (i, i + half) for i in range(half)]
    return lax.ppermute(total, "ctx", pairs)


def pack_kernel(me_ref, marks_ref, q_ref, k_ref, v_ref, g_ref, *out_refs):
    length = q_ref.shape[0]
    for n, out_ref in enumerate(out_refs):
        for a in range(out_ref.shape[0]):
            head = (me_ref[0] ^ n) * out_ref.shape[0] + a
            here = pl.ds(pl.multiple_of(head * ATT_DIM, ATT_DIM), ATT_DIM)
            for place, ref in enumerate((q_ref, k_ref, v_ref, g_ref)):
                out_ref[a, place * length : (place + 1) * length, :] = ref[:, here]
            out_ref[a, 4 * length :, :] = marks_ref[...]


def unpack_kernel(me_ref, *refs):
    in_refs, out_refs = refs[:-4], refs[-4:]
    length = out_refs[0].shape[0]
    for n, in_ref in enumerate(in_refs):
        for a in range(in_ref.shape[0]):
            head = (me_ref[0] ^ n) * in_ref.shape[0] + a
            here = pl.ds(pl.multiple_of(head * ATT_DIM, ATT_DIM), ATT_DIM)
            for place, ref in enumerate(out_refs):
                ref[:, here] = in_ref[a, place * length : (place + 1) * length, :]


def attend_blocks(length, parts, me_ref, *refs):
    in_refs, out_refs = refs[:parts], refs[parts : 2 * parts]
    all_in, all_out = refs[2 * parts : 2 * parts + 2]
    for n in range(parts):
        all_in[me_ref[0] ^ n] = in_refs[n][...]
    attend_kernel(length, all_in, all_out, *refs[2 * parts + 2 :])
    for n in range(parts):
        out_refs[n][...] = all_out[me_ref[0] ^ n]


def attend_kernel(length, in_ref, out_ref, expo_ref, kt_ref, vt_ref, dk_ref, dv_ref):
    parts = in_ref.shape[0]
    scale = ATT_DIM ** (-0.5)
    rate = scale * LOG2E
    key_in = iota((length, length), 0)
    causal = key_in <= iota((length, length), 1)
    for a in range(in_ref.shape[1]):

        def piece(block, place):
            return in_ref[block, a, place * length : (place + 1) * length, :]

        for i in range(parts):
            kt_ref[i] = flip(piece(i, 1))
            vt_ref[i] = flip(piece(i, 2))
            queries, grads = piece(i, 0), piece(i, 3)
            marks = in_ref[i, a, 4 * length :, :].astype(F32)
            starts = jnp.concatenate(
                [
                    marks[2 * n : 2 * n + 1] * 128.0 + marks[2 * n + 1 : 2 * n + 2]
                    for n in range(length // 128)
                ],
                axis=1,
            ).astype(jnp.int32)
            query_at = i * length + iota((1, length), 1)
            if parts * length > WINDOW:
                starts = jnp.maximum(starts, query_at - (WINDOW - 1))
            top = jnp.full((1, length), MASKED, F32)
            total = jnp.zeros((1, length), F32)
            tops = []
            for j in range(i + 1):
                seen = key_in >= starts - j * length
                if j == i:
                    seen = seen & causal
                raw = jnp.where(seen, dot_nt(piece(j, 1), queries), MASKED)
                new = jnp.maximum(top, jnp.max(raw, axis=0, keepdims=True))
                expo = jnp.exp2((raw - new) * rate)
                expo_ref[j] = expo
                total = total * jnp.exp2((top - new) * rate) + jnp.sum(expo, axis=0, keepdims=True)
                top = new
                tops.append(new)
            out = jnp.zeros((ATT_DIM, length), F32)
            factors = [jnp.exp2((tops[j] - top) * rate) / total for j in range(i + 1)]
            for j in range(i + 1):
                weights = (expo_ref[j] * factors[j]).astype(BF16)
                dvalue = dot(weights, grads)
                dv_ref[j] = dvalue if j == i else dv_ref[j] + dvalue
                out = out + dot(vt_ref[j], weights)
            delta = jnp.sum(out * grads.astype(F32).T, axis=0, keepdims=True)
            dquery = jnp.zeros((ATT_DIM, length), F32)
            for j in range(i + 1):
                dprobs = dot_nt(piece(j, 2), grads)
                dscore = (expo_ref[j] * ((dprobs - delta) * (factors[j] * scale))).astype(BF16)
                dkey = dot(dscore, queries)
                dk_ref[j] = dkey if j == i else dk_ref[j] + dkey
                dquery = dquery + dot(kt_ref[j], dscore)
            out_ref[i, a, 0:length, :] = out.T.astype(BF16)
            out_ref[i, a, length : 2 * length, :] = dquery.T.astype(BF16)
        for j in range(parts):
            out_ref[j, a, 2 * length : 3 * length, :] = dk_ref[j].astype(BF16)
            out_ref[j, a, 3 * length :, :] = dv_ref[j].astype(BF16)


def shifted(shard, axis, by):
    devices = lax.axis_size(axis)
    pairs = [(i, i + by) for i in range(devices) if 0 <= i + by < devices]
    return lax.ppermute(shard, axis, pairs)


def head_cols(array, head_index):
    return lax.dynamic_slice_in_dim(array, head_index * ATT_DIM, ATT_DIM, 1)


def ring_attention(att_queries, att_keys, att_values, att_grad, doc_start):
    length = att_queries.shape[0]
    shard_index = lax.axis_index("ctx")
    halo_shards = WINDOW // length
    att_count = att_queries.shape[1] // ATT_DIM
    att_width = att_queries.shape[1]
    score_scale = ATT_DIM ** (-0.5)

    def pass_keys(running, unused):
        moved = shifted((running[0], running[1]), "ctx", 1)
        return (moved, moved)

    _, earlier = lax.scan(pass_keys, (att_keys, att_values), None, length=halo_shards)
    key_all = jnp.concatenate(
        [earlier[0][::-1].reshape(halo_shards * length, att_width), att_keys], axis=0
    )
    value_all = jnp.concatenate(
        [earlier[1][::-1].reshape(halo_shards * length, att_width), att_values], axis=0
    )
    spread_rows = (halo_shards + 1) * length
    query_pos = shard_index * length + jnp.arange(length, dtype=jnp.int32)
    key_pos = (shard_index - halo_shards) * length + jnp.arange(spread_rows, dtype=jnp.int32)
    visible = (
        (key_pos[None, :] <= query_pos[:, None])
        & (query_pos[:, None] - key_pos[None, :] < WINDOW)
        & (key_pos[None, :] >= doc_start[:, None])
    )

    def forward_head(head_index, running):
        out_buf, max_buf, total_buf, delta_buf = running
        query_head = head_cols(att_queries, head_index)
        key_head = head_cols(key_all, head_index)
        value_head = head_cols(value_all, head_index)
        score = (
            jnp.einsum("td,sd->ts", query_head, key_head, preferred_element_type=jnp.float32)
            * score_scale
        )
        row_max = jnp.max(jnp.where(visible, score, -jnp.inf), axis=1)
        expo = jnp.where(visible, jnp.exp(score - row_max[:, None]), 0.0)
        row_total = jnp.sum(expo, axis=1)
        weights = (expo / row_total[:, None]).astype(jnp.bfloat16)
        attended = jnp.dot(weights, value_head, preferred_element_type=jnp.float32)
        delta = jnp.sum(head_cols(att_grad, head_index).astype(jnp.float32) * attended, axis=1)
        out_buf = lax.dynamic_update_slice_in_dim(
            out_buf, attended.astype(jnp.bfloat16), head_index * ATT_DIM, 1
        )
        return (
            out_buf,
            max_buf.at[:, head_index].set(row_max),
            total_buf.at[:, head_index].set(row_total),
            delta_buf.at[:, head_index].set(delta),
        )

    stats_zero = jnp.zeros((length, att_count), jnp.float32)
    window_out, row_maxes, row_totals, row_deltas = lax.fori_loop(
        0,
        att_count,
        forward_head,
        (jnp.zeros((length, att_width), jnp.bfloat16), stats_zero, stats_zero, stats_zero),
    )

    def query_terms(head_index):
        query_head = head_cols(att_queries, head_index)
        key_head = head_cols(key_all, head_index)
        value_head = head_cols(value_all, head_index)
        grad_head = head_cols(att_grad, head_index)
        score = (
            jnp.einsum("td,sd->ts", query_head, key_head, preferred_element_type=jnp.float32)
            * score_scale
        )
        probs = (
            jnp.where(visible, jnp.exp(score - row_maxes[:, head_index][:, None]), 0.0)
            / row_totals[:, head_index][:, None]
        )
        weights = probs.astype(jnp.bfloat16)
        dprobs = jnp.einsum("td,sd->ts", grad_head, value_head, preferred_element_type=jnp.float32)
        dscore = (probs * (dprobs - row_deltas[:, head_index][:, None]) * score_scale).astype(
            jnp.bfloat16
        )
        query_part = jnp.dot(dscore, key_head, preferred_element_type=jnp.float32)
        return (query_head, grad_head, weights, dscore, query_part)

    def backward_head(head_index, running):
        query_buf, key_buf, value_buf = running
        query_head, grad_head, weights, dscore, query_part = query_terms(head_index)
        key_part = jnp.einsum("ts,td->sd", dscore, query_head, preferred_element_type=jnp.float32)
        value_part = jnp.einsum("ts,td->sd", weights, grad_head, preferred_element_type=jnp.float32)
        query_buf = lax.dynamic_update_slice_in_dim(query_buf, query_part, head_index * ATT_DIM, 1)
        key_buf = lax.dynamic_update_slice_in_dim(key_buf, key_part, head_index * ATT_DIM, 1)
        value_buf = lax.dynamic_update_slice_in_dim(value_buf, value_part, head_index * ATT_DIM, 1)
        return (query_buf, key_buf, value_buf)

    part_zero = jnp.zeros((spread_rows, att_width), jnp.float32)
    query_sum, key_parts, value_parts = lax.fori_loop(
        0,
        att_count,
        backward_head,
        (jnp.zeros((length, att_width), jnp.float32), part_zero, part_zero),
    )
    key_blocks = key_parts.reshape(halo_shards + 1, length, att_width)
    value_blocks = value_parts.reshape(halo_shards + 1, length, att_width)

    def send_back(running, block_index):
        moved = shifted((running[0], running[1]), "ctx", -1)
        return ((moved[0] + key_blocks[block_index], moved[1] + value_blocks[block_index]), None)

    (key_sum, value_sum), _ = lax.scan(
        send_back, (key_blocks[0], value_blocks[0]), jnp.arange(1, halo_shards + 1, dtype=jnp.int32)
    )
    return (
        window_out,
        query_sum.astype(jnp.bfloat16),
        key_sum.astype(jnp.bfloat16),
        value_sum.astype(jnp.bfloat16),
    )


def body(
    ssm_input,
    gate_input,
    write_map,
    read_map,
    log_decay,
    doc_start,
    ssm_grad,
    att_queries,
    att_keys,
    att_values,
    att_grad,
):
    length, width = ssm_input.shape
    heads = width // HEAD_DIM
    parts = lax.axis_size("ctx")
    shares = parts // 2
    rows = width // shares
    full_width = width * lax.axis_size("head")
    att_width = att_queries.shape[1]
    per = att_width // ATT_DIM // parts
    dealt = att_width // ATT_DIM % parts == 0
    place = lax.axis_index("ctx")
    starts = doc_start.reshape(1, length)
    me = place.reshape(1).astype(jnp.int32)
    tailed = [shape((rows + TAIL, 128), BF16)] * shares
    plain = [shape((rows, 128), BF16)] * shares
    held_tails = pltpu.VMEM((shares, rows + TAIL, 128), BF16)
    held_plain = pltpu.VMEM((shares, rows, 128), BF16)

    def carry_total(backward, *blocks):
        return call(
            lambda *refs: total_kernel(backward, shares, *refs),
            shape((rows, 128), BF16), me, *blocks,
            specs=[SMEM] + [VMEM] * len(blocks),
            scratch=[held_tails, held_plain] if backward else [held_tails],
            vmem=SMALL, name="ssm_total",
        )

    def carry_states(backward, start, *blocks):
        return call(
            lambda *refs: carry_kernel(backward, shares, *refs),
            plain, me, start, *blocks,
            specs=[SMEM] + [VMEM] * (1 + len(blocks)),
            scratch=[held_tails, held_plain, held_plain] if backward else [held_tails, held_plain],
            vmem=SMALL, name="ssm_carry",
        )

    lcol, lrow, *sent = call(
        lambda *refs: first_kernel(shares, *refs),
        [shape((length, heads), F32), shape((heads, length), F32)] + tailed,
        me, log_decay.T, starts, write_map, ssm_input,
        specs=[SMEM] + [VMEM] * 4, scratch=[held_tails], name="ssm_first",
    )
    tails = [pass_block(block, n) for n, block in enumerate(sent)]
    total = carry_total(False, *tails)
    start = cross(total, False)
    if dealt:
        marks = doc_start.reshape(length // 128, 128)
        marks = jnp.stack([marks // 128, marks % 128], axis=1).reshape(length // 64, 128)
        marks = jnp.pad(marks, ((0, TAIL - length // 64), (0, 0))).astype(BF16)
        marks, total = lax.optimization_barrier((marks, total))
        packed = call(
            pack_kernel, [shape((per, 4 * length + TAIL, 128), BF16)] * parts,
            me, marks, att_queries, att_keys, att_values, att_grad,
            specs=[SMEM] + [VMEM] * 5, vmem=SMALL, name="att_pack",
        )
        packed, start = lax.optimization_barrier((packed, start))
        att_got = {n: pass_block(block, n) for n, block in enumerate(packed)}
    else:
        att_out = ring_attention(att_queries, att_keys, att_values, att_grad, doc_start)
    state = [
        pass_block(block, n) for n, block in enumerate(carry_states(False, start, *tails))
    ]
    if dealt:
        att_got[shares], state = lax.optimization_barrier((att_got[shares], state))
    mixed, sums, state = call(
        lambda *refs: mix_kernel(shares, *refs),
        (shape((length, width), F32), shape((8, length), F32), shape((width, 128), BF16)),
        me, ssm_input, gate_input, ssm_grad, write_map, read_map, starts, lcol, lrow, *state,
        specs=[SMEM] + [VMEM] * (8 + shares), name="ssm_mix",
    )
    sums = lax.psum(sums, "head")
    mixer_out, gate_grad, dmixed, *sent = call(
        lambda *refs: gate_kernel(full_width, shares, *refs),
        [shape((length, width), BF16)] * 3 + plain,
        me, sums, mixed, gate_input, ssm_grad, read_map, starts, lrow,
        specs=[SMEM] + [VMEM] * 7, scratch=[held_plain], name="ssm_gate",
    )

    if dealt:
        rest = [n for n in range(1, parts - 1) if n != shares]
        done, sent = lax.optimization_barrier(([att_got[n] for n in rest], sent))
        att_got.update(zip(rest, done))
    blocks = [pass_block(block, n) for n, block in enumerate(sent)]
    gin, read_part, write_part = call(
        inner_kernel,
        (shape((length, width), F32), shape((length, 128), F32), shape((length, 128), F32)),
        me, dmixed, ssm_input, write_map, read_map, starts, lcol, lrow, state,
        specs=[SMEM] + [VMEM] * 8, name="ssm_inner",
    )
    blocks, gin = lax.optimization_barrier((blocks, gin))
    total = carry_total(True, *tails, *blocks)
    start = cross(total, True)
    if dealt:
        att_in, total = lax.optimization_barrier(([att_got[n] for n in range(parts)], total))
        att_done = call(
            lambda *refs: attend_blocks(length, parts, *refs),
            [shape((per, 4 * length, 128), BF16)] * parts, me, *att_in,
            specs=[SMEM] + [VMEM] * parts,
            scratch=[
                pltpu.VMEM((parts, per, 4 * length + TAIL, 128), BF16),
                pltpu.VMEM((parts, per, 4 * length, 128), BF16),
                pltpu.VMEM((parts, length, length), F32),
                pltpu.VMEM((parts, ATT_DIM, length), BF16),
                pltpu.VMEM((parts, ATT_DIM, length), BF16),
                pltpu.VMEM((parts, length, ATT_DIM), F32),
                pltpu.VMEM((parts, length, ATT_DIM), F32),
            ],
            flops=6 * per * (parts * length) ** 2 * ATT_DIM, name="att_attend",
        )
        start, att_done = lax.optimization_barrier((start, att_done))
    carried = carry_states(True, start, *tails, *blocks)
    back = [pass_block(block, n) for n, block in enumerate(carried)]
    if dealt:
        held, carried = lax.optimization_barrier((att_done, carried))
        att_back = {n: pass_block(held[n], n) for n in (0, shares)}
        held, back = lax.optimization_barrier((att_done, back))
        late = [*range(shares + 1, parts), *range(1, shares)]
        att_back.update((n, pass_block(held[n], n)) for n in late)
        att_out = call(
            unpack_kernel, (shape((length, att_width), BF16),) * 4,
            me, *[att_back[n] for n in range(parts)],
            specs=[SMEM] + [VMEM] * parts, vmem=SMALL, name="att_unpack",
        )

    input_grad, write_part = call(
        lambda *refs: last_kernel(shares, *refs),
        (shape((length, width), BF16), shape((length, 128), F32)),
        me, gin, ssm_input, write_map, starts, lcol, write_part, *back,
        specs=[SMEM] + [VMEM] * (6 + shares),
        scratch=[pltpu.VMEM((width, 128), BF16)], name="ssm_last",
    )
    write_sum, read_sum = lax.psum((write_part, read_part), "head")
    window_out, query_grad, key_grad, value_grad = att_out
    return (
        mixer_out,
        window_out,
        input_grad,
        gate_grad,
        write_sum.astype(BF16),
        read_sum.astype(BF16),
        query_grad,
        key_grad,
        value_grad,
    )


def solution(mesh):
    in_specs = (
        P("ctx", "head"),
        P("ctx", "head"),
        P("ctx", None),
        P("ctx", None),
        P("ctx", "head"),
        P("ctx"),
        P("ctx", "head"),
        P("ctx", "head"),
        P("ctx", "head"),
        P("ctx", "head"),
        P("ctx", "head"),
    )
    out_specs = (
        P("ctx", "head"),
        P("ctx", "head"),
        P("ctx", "head"),
        P("ctx", "head"),
        P("ctx", None),
        P("ctx", None),
        P("ctx", "head"),
        P("ctx", "head"),
        P("ctx", "head"),
    )
    return jax.shard_map(body, mesh=mesh, in_specs=in_specs, out_specs=out_specs, check_vma=False)
```
